32 devices in a mesh: samples: 8 (over z, y), params: 4 (over x, core).
Axes of the slice: x: 2, y: 2, z: 4, core: 2. Of those that a mesh axis runs over, the one named last changes fastest.
Arguments:
- occupations: int32 [512, 152], P('samples'), may hold values from 0 to 1, as said below
- connection_counts: int32 [512], P('samples'), may hold values from 0 to 3072, as said below
- connection_orbitals: int32 [4, 24576], P(None, ('samples', 'params')), may hold values from 0 to 151, as said below
- connection_elements: float32 [2, 24576], P(None, ('samples', 'params')), may hold values from -2 to 2
- laser_step: int32 [], replicated, may hold values from 0 to 3999
- first_weight: bfloat16 [152, 1024], replicated, may hold values from -4 to 4
- first_bias: float32 [1024], replicated, may hold values from -3 to 3
- second_weight: bfloat16 [1024, 256], P('params'), may hold values from -1.25 to 1.25
- readout: float32 [2, 256], replicated, may hold values from -0.375 to 0.375
Outputs:
- local_energy: float32 [2, 512], P(None, 'samples')
- change: float32 [2, 512], P(None, 'samples')
The draws below stay inside these ranges and needn't reach their ends.
Inputs may be any that keep to these rules, and one draw needn't show every extreme that they name: `occupations`: each row has exactly 76 ones. `connection_counts`: the connections of block b of 64 consecutive samples fill the first slots q of that block in order of sample; the counts of a block sum to at most 3072, and to exactly 3072 in some block. `connection_orbitals`: the 4 orbitals of a slot are distinct; unused slots hold arbitrary orbitals in the range.
All inputs are finite; a program needn't handle non-finite values.
Results may differ from the reference program's by a relative error of at most 0.0099.
Values may be sent and summed in bfloat16 or wider, within the bound.
No kernel may reach another device: no remote copies, remote signals or barrier semaphores. Data moves between devices by JAX's collectives and lax.ppermute only.
A program may use at most 64 MiB of HBM per device.

```python
import jax
import jax.numpy as jnp
from jax import lax

SO = 152
NEL = 76
HID = 1024
HID2 = 256
UPD = 4
ITERS = 2
S_DEV = 64
CAP = 768
SAMPLES = 512
GSLOTS = 3072
SLOTS = 24576
N_PARAMS = 4


def draw_occupations(key, part):
    keys = jax.random.split(jax.random.fold_in(key, 11), SAMPLES)
    orders = jax.vmap(lambda single: jax.random.permutation(single, SO))(keys)
    return (orders < NEL).astype(jnp.int32)


def draw_connection_counts(key, part):
    blocks = SAMPLES // S_DEV
    first_key, second_key, third_key = jax.random.split(jax.random.fold_in(key, 23), 3)
    totals = jax.random.randint(first_key, (blocks,), GSLOTS // 4, GSLOTS + 1)
    fullest = jax.random.randint(second_key, (), 0, blocks)
    is_fullest = jnp.arange(blocks) == fullest
    totals = jnp.where(is_fullest, GSLOTS, totals).astype(jnp.int32)
    cuts = jax.random.randint(third_key, (blocks, S_DEV - 1), 0, totals[:, None] + 1)
    cuts = jnp.sort(cuts, axis=1).astype(jnp.int32)
    cuts = jnp.where(is_fullest[:, None], GSLOTS, cuts).astype(jnp.int32)
    bounds = jnp.concatenate([jnp.zeros((blocks, 1), jnp.int32), cuts, totals[:, None]], axis=1)
    return (bounds[:, 1:] - bounds[:, :-1]).reshape(-1).astype(jnp.int32)


def draw_connection_orbitals(key, part):
    first_key, second_key = jax.random.split(jax.random.fold_in(key, 37), 2)
    anchor = jax.random.randint(first_key, (1, SLOTS), 0, SO)
    stride = jax.random.randint(second_key, (1, SLOTS), 1, SO // UPD)
    offsets = jnp.arange(UPD, dtype=jnp.int32)[:, None]
    return ((anchor + offsets * stride) % SO).astype(jnp.int32)


def shard_levels(key, dims, shards, smallest, largest):
    gain, own = 1.0, jax.random.fold_in(key, 6)
    for position, parts in shards:
        draws = jnp.exp(jax.random.uniform(jax.random.fold_in(own, position), (parts,), jnp.float32, smallest / len(shards), largest / len(shards)))
        gain = gain * jnp.repeat(draws, dims[position] // parts).reshape([-1 if axis == position else 1 for axis in range(len(dims))])
    return gain


def normal_values(key, shape, scale, limit, cuts=(), held_as=jnp.bfloat16):
    level = shard_levels(key, shape, cuts, -0.22, 0.18) if cuts else 1.0
    entries = jax.random.normal(key, shape, jnp.float32) * scale * level
    return jnp.minimum(jnp.maximum(entries, -limit), limit).astype(held_as)


def setup_inputs(seed: int = 0) -> dict:
    seeds = jax.random.split(jax.random.key(seed), 10)
    occupations = draw_occupations(jax.random.fold_in(seeds[9], 71), 0)
    connection_counts = draw_connection_counts(jax.random.fold_in(seeds[9], 71), 0)
    connection_orbitals = draw_connection_orbitals(jax.random.fold_in(seeds[9], 71), 0)
    connection_elements = normal_values(seeds[3], (2, SLOTS), 0.15, 2.0, ((1, 32),), jnp.float32)
    laser_step = jax.random.randint(seeds[4], (), 0, 4000).astype(jnp.int32)
    first_weight = normal_values(seeds[5], (SO, HID), (2.6 * NEL ** -0.5), 4.0)
    first_bias = normal_values(seeds[6], (HID,), 0.5, 3.0, (), jnp.float32)
    second_weight = normal_values(seeds[7], (HID, HID2), (2.6 * HID ** -0.5), 1.25, ((0, 4),))
    readout = normal_values(seeds[8], (2, HID2), HID2 ** -0.5, 0.375, (), jnp.float32)
    return dict(occupations=occupations, connection_counts=connection_counts, connection_orbitals=connection_orbitals, connection_elements=connection_elements, laser_step=laser_step, first_weight=first_weight, first_bias=first_bias, second_weight=second_weight, readout=readout)


PRECISE = lax.Precision.HIGHEST
FIELD_SCALE = 0.8
FIELD_RATE = 0.0123
DIAG_SHIFT = 0.01


def slot_values(base_pre, orbitals, deltas, first_weight, second_weight, readout):
    columns = jnp.arange(first_weight.shape[0], dtype=jnp.int32)
    flips = jnp.sum(deltas[:, :, None] * (orbitals[:, :, None] == columns[None, None, :]).astype(jnp.float32), axis=0)
    slot_pre = base_pre + jnp.dot(flips.astype(jnp.bfloat16), first_weight, preferred_element_type=jnp.float32)
    slot_hidden = jnp.tanh(slot_pre).astype(jnp.bfloat16)
    slot_mid = jnp.tanh(jnp.dot(slot_hidden, second_weight, preferred_element_type=jnp.float32))
    return jnp.dot(slot_mid, readout.T, precision=PRECISE)


def reference(occupations, connection_counts, connection_orbitals, connection_elements, laser_step, first_weight, first_bias, second_weight, readout):
    field = FIELD_SCALE * jnp.sin(FIELD_RATE * laser_step.astype(jnp.float32))
    pre = jnp.dot(occupations.astype(jnp.bfloat16), first_weight, preferred_element_type=jnp.float32) + first_bias
    hidden = jnp.tanh(pre).astype(jnp.bfloat16)
    mid = jnp.tanh(jnp.dot(hidden, second_weight, preferred_element_type=jnp.float32))
    logs = jnp.dot(mid, readout.T, precision=PRECISE)
    blocks = SAMPLES // S_DEV
    cumulative = jnp.cumsum(connection_counts.reshape(blocks, S_DEV), axis=1, dtype=jnp.int32)
    orbital_blocks = connection_orbitals.reshape(UPD, blocks * N_PARAMS, CAP).transpose(1, 0, 2)
    element_blocks = connection_elements.reshape(2, blocks * N_PARAMS, CAP).transpose(1, 0, 2)

    def one_device(index):
        block = index // N_PARAMS
        place = index % N_PARAMS
        positions = (place + N_PARAMS * jnp.arange(CAP, dtype=jnp.int32)).astype(jnp.int32)
        ends = cumulative[block]
        parent = jnp.sum((ends[None, :] <= positions[:, None]).astype(jnp.int32), axis=1, dtype=jnp.int32)
        parent = jnp.minimum(parent, S_DEV - 1)
        used = positions < ends[-1]
        global_parent = (block * S_DEV + parent).astype(jnp.int32)
        orbitals = orbital_blocks[index]
        elements = element_blocks[index]
        picked = jnp.take_along_axis(jnp.take(occupations, global_parent, axis=0), orbitals.T, axis=1).T
        deltas = 1.0 - 2.0 * picked.astype(jnp.float32)
        slot_logs = slot_values(jnp.take(pre, global_parent, axis=0), orbitals, deltas, first_weight, second_weight, readout)
        diff = slot_logs - jnp.take(logs, global_parent, axis=0)
        magnitude = jnp.exp(diff[:, 0])
        ratio = jnp.stack([magnitude * jnp.cos(diff[:, 1]), magnitude * jnp.sin(diff[:, 1])])
        weight = elements[0] + field * elements[1]
        contrib = jnp.where(used[None, :], weight[None, :] * ratio, 0.0)
        target = jnp.where(used, global_parent, SAMPLES).astype(jnp.int32)
        return contrib, target

    contribs, targets = lax.map(one_device, jnp.arange(blocks * N_PARAMS, dtype=jnp.int32))
    summed = jax.ops.segment_sum(contribs.transpose(0, 2, 1).reshape(-1, 2), targets.reshape(-1), num_segments=SAMPLES + 1)
    local_energy = summed[:SAMPLES].T

    hidden_full = hidden.astype(jnp.float32)
    slope = 1.0 - mid * mid
    slope_re = slope * readout[0]
    slope_im = slope * readout[1]
    total = float(SAMPLES)
    obar_re = jnp.dot(hidden_full.T, slope_re, precision=PRECISE) / total
    obar_im = jnp.dot(hidden_full.T, slope_im, precision=PRECISE) / total
    emean = jnp.sum(local_energy, axis=1) / total
    centered = local_energy - emean[:, None]
    force = jnp.dot(hidden_full.T, slope_re * centered[1][:, None] - slope_im * centered[0][:, None], precision=PRECISE) / total

    def project(vector):
        lifted = jnp.dot(hidden_full, vector, precision=PRECISE)
        raw = jnp.stack([jnp.sum(lifted * slope_re, axis=1), jnp.sum(lifted * slope_im, axis=1)])
        means = jnp.stack([jnp.sum(obar_re * vector), jnp.sum(obar_im * vector)])
        return raw - means[:, None]

    def metric(vector):
        coeffs = project(vector)
        back = slope_re * coeffs[0][:, None] + slope_im * coeffs[1][:, None]
        return jnp.dot(hidden_full.T, back, precision=PRECISE) / total + DIAG_SHIFT * vector

    solution = jnp.zeros_like(force)
    residual = force
    direction = force
    norm_now = jnp.sum(residual * residual)
    for turn in range(ITERS):
        image = metric(direction)
        alpha = norm_now / jnp.sum(direction * image)
        solution = solution + alpha * direction
        residual = residual - alpha * image
        norm_next = jnp.sum(residual * residual)
        direction = residual + (norm_next / norm_now) * direction
        norm_now = norm_next
    change = project(solution)
    return local_energy, change
```

```python
import jax
import jax.numpy as jnp
from jax import lax
from jax.sharding import PartitionSpec as P

ITERS = 2


PRECISE = lax.Precision.HIGHEST
FIELD_SCALE = 0.8
FIELD_RATE = 0.0123
DIAG_SHIFT = 0.01
F32 = jnp.float32
BF16 = jnp.bfloat16


def dot(a, b, dims, precision=None):
    return lax.dot_general(a, b, (dims, ((), ())), precision=precision, preferred_element_type=F32)


def split(x):
    high = lax.reduce_precision(x, 8, 7)
    return high.astype(BF16), (x - high).astype(BF16)


def forward(occupied, first_weight, bias_row, second_weight):
    pre = dot(occupied, first_weight, ((1,), (0,))) + bias_row
    hidden = jnp.tanh(pre).astype(BF16)
    return hidden, jnp.tanh(dot(second_weight, hidden, ((0,), (1,))))


def body(
    occupations,
    connection_counts,
    connection_orbitals,
    connection_elements,
    laser_step,
    first_weight,
    first_bias,
    second_weight,
    readout,
):
    here = occupations.shape[0]
    slots = connection_orbitals.shape[1]
    orbitals = first_weight.shape[0]
    place = lax.axis_index("params")
    spread = lax.axis_size("params")
    block = lax.axis_index("samples")
    total = here * lax.axis_size("samples")
    field = FIELD_SCALE * jnp.sin(FIELD_RATE * laser_step.astype(F32))
    bias_row = first_bias[None, :]

    occupied = occupations.astype(BF16)
    full_second = lax.all_gather(second_weight, "params", axis=0, tiled=True)
    all_occupied = lax.all_gather(occupied, "samples", axis=0, tiled=True)

    ends = jnp.cumsum(connection_counts, dtype=jnp.int32)[:, None]
    starts = ends - connection_counts[:, None]
    positions = (place + spread * jnp.arange(slots, dtype=jnp.int32))[None, :]
    owner = (starts <= positions) & (positions < ends)
    owner_bf16 = owner.astype(BF16)
    parent_occ = dot(occupied, owner_bf16, ((0,), (0,)))
    columns = jnp.arange(orbitals, dtype=jnp.int32)[:, None]
    flipped = columns == connection_orbitals[0][None, :]
    for u in range(1, connection_orbitals.shape[0]):
        flipped = flipped | (columns == connection_orbitals[u][None, :])
    slot_occ = jnp.where(flipped, 1.0 - parent_occ, parent_occ).astype(BF16)
    _, slot_mid = forward(slot_occ.T, first_weight, bias_row, full_second)
    slot_logs = dot(readout, slot_mid, ((1,), (0,)), PRECISE)
    _, own_mid = forward(occupied, first_weight, bias_row, full_second)
    logs = dot(readout, own_mid, ((1,), (0,)), PRECISE)
    diff = slot_logs - dot(logs, owner.astype(F32), ((1,), (0,)), PRECISE)
    weight = connection_elements[0] + field * connection_elements[1]
    scale = weight * jnp.exp(diff[0])
    contrib = jnp.stack([scale * jnp.cos(diff[1]), scale * jnp.sin(diff[1])])
    contrib = jnp.where(jnp.any(owner, axis=0)[None, :], contrib, 0.0)
    partial = dot(contrib, owner.astype(F32), ((1,), (1,)), PRECISE)

    hidden, mid = forward(all_occupied, first_weight, bias_row, full_second)
    slope = 1.0 - mid * mid
    slope_re = slope * readout[0][:, None]
    slope_im = slope * readout[1][:, None]

    if total <= first_weight.shape[1]:
        overlap_high, overlap_low = split(dot(hidden, hidden, ((1,), (1,))))

        def lift(back):
            high, low = split(back)
            return (
                dot(high, overlap_high, ((1,), (0,)))
                + dot(low, overlap_high, ((1,), (0,)))
                + dot(high, overlap_low, ((1,), (0,)))
            )
    else:

        def lift(back):
            high, low = split(back)
            vector = dot(high, hidden, ((1,), (0,))) + dot(low, hidden, ((1,), (0,)))
            high, low = split(vector)
            return dot(high, hidden, ((1,), (1,))) + dot(low, hidden, ((1,), (1,)))

    def gram(c):
        lifted = lift(slope_re * c[0][None, :] + slope_im * c[1][None, :])
        raw = jnp.stack([jnp.sum(lifted * slope_re, axis=0), jnp.sum(lifted * slope_im, axis=0)])
        return raw - jnp.mean(raw, axis=1, keepdims=True)

    gathered = lax.all_gather(partial, ("samples", "params"), axis=0, tiled=False)
    energy = jnp.sum(gathered.reshape(-1, spread, 2, here), axis=1)
    energy = energy.transpose(1, 0, 2).reshape(2, total)
    local_energy = lax.dynamic_slice_in_dim(energy, block * here, here, 1)
    centered = energy - jnp.mean(energy, axis=1, keepdims=True)

    res_c = jnp.stack([centered[1], -centered[0]]) / total
    res_y = gram(res_c)
    dir_c, dir_y = res_c, res_y
    norm_now = jnp.sum(res_c * res_y)
    change = jnp.zeros_like(res_y)
    for turn in range(ITERS):
        img_c = dir_y / total + DIAG_SHIFT * dir_c
        alpha = norm_now / jnp.sum(img_c * dir_y)
        change = change + alpha * dir_y
        if turn + 1 < ITERS:
            img_y = gram(dir_y) / total + DIAG_SHIFT * dir_y
            res_c = res_c - alpha * img_c
            res_y = res_y - alpha * img_y
            norm_next = jnp.sum(res_c * res_y)
            beta = norm_next / norm_now
            dir_c = res_c + beta * dir_c
            dir_y = res_y + beta * dir_y
            norm_now = norm_next
    return local_energy, lax.dynamic_slice_in_dim(change, block * here, here, 1)


def solution(mesh):
    return jax.shard_map(
        body,
        mesh=mesh,
        in_specs=(
            P("samples", None),
            P("samples"),
            P(None, ("samples", "params")),
            P(None, ("samples", "params")),
            P(),
            P(),
            P(),
            P("params", None),
            P(),
        ),
        out_specs=(P(None, "samples"), P(None, "samples")),
        check_vma=False,
    )
```

```python
import jax
import jax.numpy as jnp
from jax import lax
from jax.sharding import PartitionSpec as P

ITERS = 2


PRECISE = lax.Precision.HIGHEST
FIELD_SCALE = 0.8
FIELD_RATE = 0.0123
DIAG_SHIFT = 0.01
F32 = jnp.float32
BF16 = jnp.bfloat16


def dot(a, b, dims, precision=None):
    return lax.dot_general(a, b, (dims, ((), ())), precision=precision, preferred_element_type=F32)


def split(x):
    high = lax.reduce_precision(x, 8, 7)
    return high.astype(BF16), (x - high).astype(BF16)


def gather_by_permutes(shard, axis):
    size = lax.axis_size(axis)
    me = lax.axis_index(axis)
    rows = shard.shape[0]
    whole = jnp.zeros((size * rows,) + shard.shape[1:], shard.dtype)
    whole = lax.dynamic_update_slice_in_dim(whole, shard, me * rows, 0)
    for step in range(1, size):
        moved = lax.ppermute(shard, axis, [(i, (i + step) % size) for i in range(size)])
        whole = lax.dynamic_update_slice_in_dim(whole, moved, (me + size - step) % size * rows, 0)
    return whole


def forward(occupied, first_weight, bias_row, second_weight):
    pre = dot(occupied, first_weight, ((1,), (0,))) + bias_row
    hidden = jnp.tanh(pre).astype(BF16)
    return hidden, jnp.tanh(dot(second_weight, hidden, ((0,), (1,))))


def body(
    occupations,
    connection_counts,
    connection_orbitals,
    connection_elements,
    laser_step,
    first_weight,
    first_bias,
    second_weight,
    readout,
):
    here = occupations.shape[0]
    slots = connection_orbitals.shape[1]
    orbitals = first_weight.shape[0]
    place = lax.axis_index("params")
    spread = lax.axis_size("params")
    block = lax.axis_index("samples")
    total = here * lax.axis_size("samples")
    field = FIELD_SCALE * jnp.sin(FIELD_RATE * laser_step.astype(F32))
    bias_row = first_bias[None, :]

    occupied = occupations.astype(BF16)
    full_second = gather_by_permutes(second_weight, "params")
    all_occupied = gather_by_permutes(occupied, "samples")

    ends = jnp.cumsum(connection_counts, dtype=jnp.int32)[:, None]
    starts = ends - connection_counts[:, None]
    positions = (place + spread * jnp.arange(slots, dtype=jnp.int32))[None, :]
    owner = (starts <= positions) & (positions < ends)
    owner_bf16 = owner.astype(BF16)
    parent_occ = dot(occupied, owner_bf16, ((0,), (0,)))
    columns = jnp.arange(orbitals, dtype=jnp.int32)[:, None]
    flipped = columns == connection_orbitals[0][None, :]
    for u in range(1, connection_orbitals.shape[0]):
        flipped = flipped | (columns == connection_orbitals[u][None, :])
    slot_occ = jnp.where(flipped, 1.0 - parent_occ, parent_occ).astype(BF16)
    _, slot_mid = forward(slot_occ.T, first_weight, bias_row, full_second)
    slot_logs = dot(readout, slot_mid, ((1,), (0,)), PRECISE)
    _, own_mid = forward(occupied, first_weight, bias_row, full_second)
    logs = dot(readout, own_mid, ((1,), (0,)), PRECISE)
    diff = slot_logs - dot(logs, owner.astype(F32), ((1,), (0,)), PRECISE)
    weight = connection_elements[0] + field * connection_elements[1]
    scale = weight * jnp.exp(diff[0])
    contrib = jnp.stack([scale * jnp.cos(diff[1]), scale * jnp.sin(diff[1])])
    contrib = jnp.where(jnp.any(owner, axis=0)[None, :], contrib, 0.0)
    partial = dot(contrib, owner.astype(F32), ((1,), (1,)), PRECISE)

    hidden, mid = forward(all_occupied, first_weight, bias_row, full_second)
    slope = 1.0 - mid * mid
    slope_re = slope * readout[0][:, None]
    slope_im = slope * readout[1][:, None]

    if total <= first_weight.shape[1]:
        overlap_high, overlap_low = split(dot(hidden, hidden, ((1,), (1,))))

        def lift(back):
            high, low = split(back)
            return (
                dot(high, overlap_high, ((1,), (0,)))
                + dot(low, overlap_high, ((1,), (0,)))
                + dot(high, overlap_low, ((1,), (0,)))
            )
    else:

        def lift(back):
            high, low = split(back)
            vector = dot(high, hidden, ((1,), (0,))) + dot(low, hidden, ((1,), (0,)))
            high, low = split(vector)
            return dot(high, hidden, ((1,), (1,))) + dot(low, hidden, ((1,), (1,)))

    def gram(c):
        lifted = lift(slope_re * c[0][None, :] + slope_im * c[1][None, :])
        raw = jnp.stack([jnp.sum(lifted * slope_re, axis=0), jnp.sum(lifted * slope_im, axis=0)])
        return raw - jnp.mean(raw, axis=1, keepdims=True)

    ranks = spread * lax.axis_size("samples")
    gathered = lax.all_to_all(
        jnp.broadcast_to(partial[None], (ranks, 2, here)), ("samples", "params"), 0, 0, tiled=True
    )
    energy = jnp.sum(gathered.reshape(-1, spread, 2, here), axis=1)
    energy = energy.transpose(1, 0, 2).reshape(2, total)
    local_energy = lax.dynamic_slice_in_dim(energy, block * here, here, 1)
    centered = energy - jnp.mean(energy, axis=1, keepdims=True)

    res_c = jnp.stack([centered[1], -centered[0]]) / total
    res_y = gram(res_c)
    dir_c, dir_y = res_c, res_y
    norm_now = jnp.sum(res_c * res_y)
    change = jnp.zeros_like(res_y)
    for turn in range(ITERS):
        img_c = dir_y / total + DIAG_SHIFT * dir_c
        alpha = norm_now / jnp.sum(img_c * dir_y)
        change = change + alpha * dir_y
        if turn + 1 < ITERS:
            img_y = gram(dir_y) / total + DIAG_SHIFT * dir_y
            res_c = res_c - alpha * img_c
            res_y = res_y - alpha * img_y
            norm_next = jnp.sum(res_c * res_y)
            beta = norm_next / norm_now
            dir_c = res_c + beta * dir_c
            dir_y = res_y + beta * dir_y
            norm_now = norm_next
    return local_energy, lax.dynamic_slice_in_dim(change, block * here, here, 1)


def solution(mesh):
    return jax.shard_map(
        body,
        mesh=mesh,
        in_specs=(
            P("samples", None),
            P("samples"),
            P(None, ("samples", "params")),
            P(None, ("samples", "params")),
            P(),
            P(),
            P(),
            P("params", None),
            P(),
        ),
        out_specs=(P(None, "samples"), P(None, "samples")),
        check_vma=False,
    )
```

```python
import functools

import jax
import jax.numpy as jnp
from jax import lax
from jax.experimental import pallas as pl
from jax.experimental.pallas import tpu as pltpu
from jax.sharding import PartitionSpec as P

ITERS = 2


FIELD_SCALE = 0.8
FIELD_RATE = 0.0123
DIAG_SHIFT = 0.01
F32 = jnp.float32
BF16 = jnp.bfloat16
ROWS = 256
VMEM_LIMIT = 48 * 1024 * 1024


def dot(a, b, dims):
    return lax.dot_general(a, b, (dims, ((), ())), preferred_element_type=F32)


def split(x):
    high = lax.reduce_precision(x, 8, 7)
    return high.astype(BF16), (x - high).astype(BF16)


def parts(x):
    high = x.astype(BF16)
    rest = x - high.astype(F32)
    middle = rest.astype(BF16)
    return high, middle, (rest - middle.astype(F32)).astype(BF16)


def iota(shape, dim):
    return lax.broadcasted_iota(jnp.int32, shape, dim)


def call(kernel, out_shape, scratch=(), name=None):
    return pl.pallas_call(
        kernel,
        out_shape=out_shape,
        scratch_shapes=scratch,
        compiler_params=pltpu.CompilerParams(vmem_limit_bytes=VMEM_LIMIT),
        name=name,
    )


def slot_hidden_kernel(spread, counts_ref, orbitals_ref, occ_ref, w1_ref, bias_ref, hidden_ref, owner_ref):
    here, orbitals = occ_ref.shape
    updates, slots = orbitals_ref.shape
    place = lax.axis_index("params")
    counts = counts_ref[...].astype(F32)
    row, col = iota((here, here), 0), iota((here, here), 1)
    ends = jnp.sum(jnp.where(col <= row, counts, 0.0), axis=1, keepdims=True)
    starts = jnp.sum(jnp.where(col < row, counts, 0.0), axis=1, keepdims=True)
    positions = (place + spread * iota((1, slots), 1)).astype(F32)
    owner = jnp.where((starts <= positions) & (positions < ends), 1.0, 0.0).astype(BF16)
    owner_ref[...] = owner
    occupied = occ_ref[...].astype(F32).astype(BF16)
    w1 = w1_ref[...]
    bias = bias_ref[...]
    hidden_ref[slots:, :] = jnp.tanh(dot(occupied, w1, ((1,), (0,))) + bias).astype(BF16)
    for start in range(0, slots, ROWS):
        stop = min(start + ROWS, slots)
        parent_occ = dot(occupied, owner[:, start:stop], ((0,), (0,)))
        columns = iota((orbitals, stop - start), 0)
        flipped = columns == orbitals_ref[0:1, start:stop]
        for u in range(1, updates):
            flipped = flipped | (columns == orbitals_ref[u : u + 1, start:stop])
        slot_occ = jnp.where(flipped, 1.0 - parent_occ, parent_occ).astype(BF16)
        pre = dot(slot_occ, w1, ((0,), (0,))) + bias
        hidden_ref[start:stop, :] = jnp.tanh(pre).astype(BF16)


def slot_energy_kernel(
    spread,
    laser_ref,
    hidden_ref,
    owner_ref,
    w2_0,
    w2_1,
    w2_2,
    w2_3,
    readout_ref,
    elements_ref,
    energy_ref,
    second_ref,
):
    here, slots = owner_ref.shape
    place = lax.axis_index("params")
    block = lax.axis_index("samples")
    for step, shard in enumerate((w2_0, w2_1, w2_2, w2_3)):
        rows = shard.shape[0]
        second_ref[pl.ds(pl.multiple_of((place ^ step) * rows, rows), rows), :] = shard[...]
    mid = jnp.tanh(dot(second_ref[...], hidden_ref[...], ((0,), (1,))))
    readout = readout_ref[...].T
    logs_re = jnp.sum(mid * readout[:, 0:1], axis=0, keepdims=True)
    logs_im = jnp.sum(mid * readout[:, 1:2], axis=0, keepdims=True)
    owner = owner_ref[...]
    own = jnp.concatenate(parts(logs_re[:, slots:]) + parts(logs_im[:, slots:]), axis=0)
    parent = dot(own, owner, ((1,), (0,)))
    diff_re = logs_re[:, :slots] - (parent[0:1] + parent[1:2] + parent[2:3])
    diff_im = logs_im[:, :slots] - (parent[3:4] + parent[4:5] + parent[5:6])
    laser = jnp.full((1, slots), laser_ref[0], jnp.int32).astype(F32)
    field = FIELD_SCALE * jnp.sin(FIELD_RATE * laser)
    weight = elements_ref[0:1, :] + field * elements_ref[1:2, :]
    used = jnp.sum(owner.astype(F32), axis=0, keepdims=True) > 0.0
    scale = weight * jnp.exp(diff_re)
    contrib_re = jnp.where(used, scale * jnp.cos(diff_im), 0.0)
    contrib_im = jnp.where(used, scale * jnp.sin(diff_im), 0.0)
    contrib = jnp.concatenate(parts(contrib_re) + parts(contrib_im), axis=0)
    sums = dot(contrib, owner, ((1,), (1,)))
    partial = jnp.concatenate(
        [sums[0:1] + sums[1:2] + sums[2:3], sums[3:4] + sums[4:5] + sums[5:6]], axis=0
    )
    energy_ref[...] = spread_blocks(partial, block, energy_ref.shape[1] // here)


def spread_blocks(partial, block, blocks):
    zero = jnp.zeros_like(partial)
    return jnp.concatenate([jnp.where(block == b, partial, zero) for b in range(blocks)], axis=1)


def pick_block(whole, block, width):
    blocks = whole.shape[1] // width
    picked = jnp.zeros((whole.shape[0], width), F32)
    for b in range(blocks):
        picked = jnp.where(block == b, whole[:, b * width : (b + 1) * width], picked)
    return picked


def overlap_kernel(
    occ_ref, w1_ref, bias_ref, second_ref, readout_ref, high_ref, low_ref, re_ref, im_ref, occ_all, hidden_ref
):
    blocks, here, _ = occ_ref.shape
    total = blocks * here
    block = lax.axis_index("samples")
    for step in range(blocks):
        occ_all[pl.ds(pl.multiple_of((block ^ step) * here, here), here), :] = occ_ref[step]
    w1 = w1_ref[...]
    bias = bias_ref[...]
    for start in range(0, total, ROWS):
        pre = dot(occ_all[start : start + ROWS, :], w1, ((1,), (0,))) + bias
        hidden_ref[start : start + ROWS, :] = jnp.tanh(pre).astype(BF16)
    hidden = hidden_ref[...]
    overlap = dot(hidden, hidden, ((1,), (1,)))
    high = overlap.astype(BF16)
    high_ref[...] = high
    low_ref[...] = (overlap - high.astype(F32)).astype(BF16)
    mid = jnp.tanh(dot(second_ref[...], hidden, ((0,), (1,))))
    slope = 1.0 - mid * mid
    readout = readout_ref[...].T
    re_ref[...] = slope * readout[:, 0:1]
    im_ref[...] = slope * readout[:, 1:2]


def solve(energy, gram):
    total = energy.shape[1]
    centered = energy - jnp.mean(energy, axis=1, keepdims=True)
    res_c = jnp.concatenate([centered[1:2], -centered[0:1]], axis=0) / total
    res_y = gram(res_c)
    dir_c, dir_y = res_c, res_y
    norm_now = full_sum(res_c * res_y)
    change = jnp.zeros_like(res_y)
    for turn in range(ITERS):
        img_c = dir_y / total + DIAG_SHIFT * dir_c
        alpha = norm_now / full_sum(img_c * dir_y)
        change = change + alpha * dir_y
        if turn + 1 < ITERS:
            img_y = gram(dir_y) / total + DIAG_SHIFT * dir_y
            res_c = res_c - alpha * img_c
            res_y = res_y - alpha * img_y
            norm_next = full_sum(res_c * res_y)
            beta = norm_next / norm_now
            dir_c = res_c + beta * dir_c
            dir_y = res_y + beta * dir_y
            norm_now = norm_next
    return change


def full_sum(x):
    return jnp.sum(jnp.sum(x, axis=1, keepdims=True), axis=0, keepdims=True)


def project(lifted, slope_re, slope_im):
    raw = jnp.concatenate(
        [jnp.sum(lifted * slope_re, axis=0, keepdims=True), jnp.sum(lifted * slope_im, axis=0, keepdims=True)],
        axis=0,
    )
    return raw - jnp.mean(raw, axis=1, keepdims=True)


def solve_kernel(energy_ref, high_ref, low_ref, re_ref, im_ref, local_ref, change_ref):
    width = local_ref.shape[1]
    block = lax.axis_index("samples")
    energy = energy_ref[...]
    local_ref[...] = pick_block(energy, block, width)

    def gram(c):
        back = re_ref[...] * c[0:1] + im_ref[...] * c[1:2]
        high = back.astype(BF16)
        low = (back - high.astype(F32)).astype(BF16)
        lifted = dot(high, high_ref[...], ((1,), (0,)))
        lifted += dot(low, high_ref[...], ((1,), (0,)))
        lifted += dot(high, low_ref[...], ((1,), (0,)))
        return project(lifted, re_ref[...], im_ref[...])

    change_ref[...] = pick_block(solve(energy, gram), block, width)


def wide_solve(energy, occ_stack, first_weight, bias_row, second, readout, block, here):
    order = block ^ jnp.arange(occ_stack.shape[0], dtype=jnp.int32)
    occupied = jnp.take(occ_stack, order, axis=0).reshape(-1, occ_stack.shape[2])
    pre = dot(occupied, first_weight, ((1,), (0,))) + bias_row
    hidden = jnp.tanh(pre).astype(BF16)
    mid = jnp.tanh(dot(second, hidden, ((0,), (1,))))
    slope = 1.0 - mid * mid
    slope_re = slope * readout[0][:, None]
    slope_im = slope * readout[1][:, None]

    def gram(c):
        high, low = split(slope_re * c[0:1] + slope_im * c[1:2])
        high, low = split(dot(high, hidden, ((1,), (0,))) + dot(low, hidden, ((1,), (0,))))
        lifted = dot(high, hidden, ((1,), (1,))) + dot(low, hidden, ((1,), (1,)))
        return project(lifted, slope_re, slope_im)

    change = solve(energy, gram)
    return (
        lax.dynamic_slice_in_dim(energy, block * here, here, 1),
        lax.dynamic_slice_in_dim(change, block * here, here, 1),
    )


def swap(x, axis, bit):
    return lax.ppermute(x, axis, [(i, i ^ bit) for i in range(lax.axis_size(axis))])


def body(
    occupations,
    connection_counts,
    connection_orbitals,
    connection_elements,
    laser_step,
    first_weight,
    first_bias,
    second_weight,
    readout,
):
    here, orbitals = occupations.shape
    slots = connection_orbitals.shape[1]
    wide, narrow = first_weight.shape[1], second_weight.shape[1]
    spread = lax.axis_size("params")
    blocks = lax.axis_size("samples")
    total = here * blocks
    bias_row = first_bias[None, :]

    shards = [second_weight] + [swap(second_weight, "params", bit) for bit in range(1, spread)]
    occ_stack = occupations.astype(BF16)[None]
    bit = 1
    while bit < blocks:
        occ_stack = jnp.concatenate([occ_stack, swap(occ_stack, "samples", bit)], axis=0)
        bit *= 2

    hidden, owner = call(
        functools.partial(slot_hidden_kernel, spread),
        (
            jax.ShapeDtypeStruct((slots + here, wide), BF16),
            jax.ShapeDtypeStruct((here, slots), BF16),
        ),
        name="slot_hidden",
    )(connection_counts[None, :], connection_orbitals, occupations, first_weight, bias_row)

    vmem = pl.BlockSpec(memory_space=pltpu.VMEM)
    energy, second = pl.pallas_call(
        functools.partial(slot_energy_kernel, spread),
        out_shape=(
            jax.ShapeDtypeStruct((2, total), F32),
            jax.ShapeDtypeStruct((wide, narrow), BF16),
        ),
        in_specs=[pl.BlockSpec(memory_space=pltpu.SMEM)] + [vmem] * 8,
        compiler_params=pltpu.CompilerParams(vmem_limit_bytes=VMEM_LIMIT),
        name="slot_energy",
    )(laser_step[None], hidden, owner, *shards, readout, connection_elements)

    bit = 1
    while bit < spread:
        energy = energy + swap(energy, "params", bit)
        bit *= 2
    bit = 1
    while bit < blocks:
        energy = energy + swap(energy, "samples", bit)
        bit *= 2

    if total > wide:
        block = lax.axis_index("samples")
        return wide_solve(energy, occ_stack, first_weight, bias_row, second, readout, block, here)

    overlap = call(
        overlap_kernel,
        (jax.ShapeDtypeStruct((total, total), BF16),) * 2 + (jax.ShapeDtypeStruct((narrow, total), F32),) * 2,
        [pltpu.VMEM((total, orbitals), BF16), pltpu.VMEM((total, wide), BF16)],
        name="overlap",
    )(occ_stack, first_weight, bias_row, second, readout)
    return call(
        solve_kernel,
        (jax.ShapeDtypeStruct((2, here), F32),) * 2,
        name="solve",
    )(energy, *overlap)


def solution(mesh):
    return jax.shard_map(
        body,
        mesh=mesh,
        in_specs=(
            P("samples", None),
            P("samples"),
            P(None, ("samples", "params")),
            P(None, ("samples", "params")),
            P(),
            P(),
            P(),
            P("params", None),
            P(),
        ),
        out_specs=(P(None, "samples"), P(None, "samples")),
        check_vma=False,
    )
```

```python
import functools

import jax
import jax.numpy as jnp
from jax import lax
from jax.experimental import pallas as pl
from jax.experimental.pallas import tpu as pltpu
from jax.sharding import Mesh, PartitionSpec as P

ITERS = 2


FIELD_SCALE = 0.8
FIELD_RATE = 0.0123
DIAG_SHIFT = 0.01
F32 = jnp.float32
BF16 = jnp.bfloat16
ROWS = 256
VMEM_LIMIT = 48 * 1024 * 1024


def dot(a, b, dims):
    return lax.dot_general(a, b, (dims, ((), ())), preferred_element_type=F32)


def split(x):
    high = lax.reduce_precision(x, 8, 7)
    return high.astype(BF16), (x - high).astype(BF16)


def parts(x):
    high = x.astype(BF16)
    rest = x - high.astype(F32)
    middle = rest.astype(BF16)
    return high, middle, (rest - middle.astype(F32)).astype(BF16)


def iota(shape, dim):
    return lax.broadcasted_iota(jnp.int32, shape, dim)


def call(kernel, count, out_shape, scratch=(), name=None, in_specs=None):
    vmem = pl.BlockSpec(memory_space=pltpu.VMEM)
    return pl.pallas_call(
        kernel,
        out_shape=out_shape,
        in_specs=in_specs if in_specs else [vmem] * count,
        out_specs=jax.tree.map(lambda _: vmem, out_shape),
        scratch_shapes=scratch,
        compiler_params=pltpu.CompilerParams(vmem_limit_bytes=VMEM_LIMIT),
        name=name,
    )


def slot_hidden_kernel(
    spread,
    counts_hbm,
    orbitals_hbm,
    occ_hbm,
    w1_hbm,
    bias_hbm,
    laser_hbm,
    elements_hbm,
    readout_hbm,
    own_hbm,
    hidden_ref,
    owner_ref,
    weight_ref,
    carry_ref,
    w1_ref,
    bias_ref,
    readout_ref,
    own_ref,
    counts_ref,
    orbitals_ref,
    occ_ref,
    laser_ref,
    elements_ref,
    sems,
):
    here, orbitals = occ_ref.shape
    updates, slots = orbitals_ref.shape
    pairs = (
        (counts_hbm, counts_ref),
        (occ_hbm, occ_ref),
        (w1_hbm, w1_ref),
        (bias_hbm, bias_ref),
        (orbitals_hbm, orbitals_ref),
        (laser_hbm, laser_ref),
        (elements_hbm, elements_ref),
        (readout_hbm, readout_ref),
        (own_hbm, own_ref),
    )
    copies = [pltpu.make_async_copy(a, b, sems.at[i]) for i, (a, b) in enumerate(pairs)]
    for copy in copies:
        copy.start()
    chip, core = lax.axis_index("chip"), lax.axis_index("core")
    place = chip * 2 + core
    copies[0].wait()
    counts = counts_ref[...].astype(F32)
    row, col = iota((here, here), 0), iota((here, here), 1)
    ends = jnp.sum(jnp.where(col <= row, counts, 0.0), axis=1, keepdims=True)
    starts = jnp.sum(jnp.where(col < row, counts, 0.0), axis=1, keepdims=True)
    positions = (place + spread * iota((1, slots), 1)).astype(F32)
    owner = jnp.where((starts <= positions) & (positions < ends), 1.0, 0.0).astype(BF16)
    owner_ref[...] = owner
    copies[1].wait()
    occupied = occ_ref[...].astype(F32).astype(BF16)
    copies[2].wait()
    copies[3].wait()
    w1 = w1_ref[...]
    bias = bias_ref[...]
    hidden_ref[slots:, :] = jnp.tanh(dot(occupied, w1, ((1,), (0,))) + bias).astype(BF16)
    copies[4].wait()
    for start in range(0, slots, ROWS):
        stop = min(start + ROWS, slots)
        parent_occ = dot(occupied, owner[:, start:stop], ((0,), (0,)))
        columns = iota((orbitals, stop - start), 0)
        flipped = columns == orbitals_ref[0:1, start:stop]
        for u in range(1, updates):
            flipped = flipped | (columns == orbitals_ref[u : u + 1, start:stop])
        slot_occ = jnp.where(flipped, 1.0 - parent_occ, parent_occ).astype(BF16)
        pre = dot(slot_occ, w1, ((0,), (0,))) + bias
        hidden_ref[start:stop, :] = jnp.tanh(pre).astype(BF16)
    copies[5].wait()
    copies[6].wait()
    laser = jnp.full((1, slots), laser_ref[0], jnp.int32).astype(F32)
    field = FIELD_SCALE * jnp.sin(FIELD_RATE * laser)
    weight_ref[...] = elements_ref[0:1, :] + field * elements_ref[1:2, :]
    rows, lanes = carry_ref.shape
    share = occ_ref[pl.ds(pl.multiple_of(chip * rows, rows), rows), :].astype(F32)
    carry_ref[...] = jnp.concatenate([share, jnp.zeros((rows, lanes - orbitals), F32)], axis=1)
    copies[7].wait()
    copies[8].wait()


def slot_energy_kernel(shifts, hidden_ref, owner_ref, weight_ref, carry_ref, readout_ref, *refs):
    shard_refs, (send_ref, second_ref) = refs[: len(shifts)], refs[len(shifts) :]
    here, slots = owner_ref.shape
    chips = lax.axis_size("chip")
    chip, core = lax.axis_index("chip"), lax.axis_index("core")
    for (step, other), shard in zip(shifts, shard_refs):
        rows = shard.shape[0]
        source = lax.rem(chip + chips - step, chips) * 2 + (core ^ other)
        second_ref[pl.ds(pl.multiple_of(source * rows, rows), rows), :] = shard[...]
    mid = jnp.tanh(dot(second_ref[...], hidden_ref[...], ((0,), (1,))))
    readout = readout_ref[...].T
    logs_re = jnp.sum(mid * readout[:, 0:1], axis=0, keepdims=True)
    logs_im = jnp.sum(mid * readout[:, 1:2], axis=0, keepdims=True)
    owner = owner_ref[...]
    own = jnp.concatenate(parts(logs_re[:, slots:]) + parts(logs_im[:, slots:]), axis=0)
    parent = dot(own, owner, ((1,), (0,)))
    diff_re = logs_re[:, :slots] - (parent[0:1] + parent[1:2] + parent[2:3])
    diff_im = logs_im[:, :slots] - (parent[3:4] + parent[4:5] + parent[5:6])
    used = jnp.sum(owner.astype(F32), axis=0, keepdims=True) > 0.0
    scale = weight_ref[...] * jnp.exp(diff_re)
    contrib_re = jnp.where(used, scale * jnp.cos(diff_im), 0.0)
    contrib_im = jnp.where(used, scale * jnp.sin(diff_im), 0.0)
    contrib = jnp.concatenate(parts(contrib_re) + parts(contrib_im), axis=0)
    sums = dot(contrib, owner, ((1,), (1,)))
    partial_re = sums[0:1] + sums[1:2] + sums[2:3]
    partial_im = sums[3:4] + sums[4:5] + sums[5:6]
    carry = carry_ref[...]
    rows, lanes = carry.shape
    pieces = [x.astype(F32) for x in parts(partial_re) + parts(partial_im)]
    block = jnp.concatenate(pieces + [jnp.zeros((rows - len(pieces), here), F32)], axis=0)
    carry = carry + jnp.concatenate([jnp.zeros((rows, lanes - here), F32), block], axis=1)
    send_ref[...] = jnp.broadcast_to(carry.astype(BF16)[None], send_ref.shape)


def collect_kernel(here, chips, received_ref, energy_ref):
    lanes = received_ref.shape[2]
    out_re, out_im = [], []
    for start in range(0, received_ref.shape[0], chips):
        tile = received_ref[start, 0:16, lanes - here :].astype(F32)
        re = tile[0:1] + tile[1:2] + tile[2:3]
        im = tile[3:4] + tile[4:5] + tile[5:6]
        for k in range(1, chips):
            tile = received_ref[start + k, 0:16, lanes - here :].astype(F32)
            re = re + (tile[0:1] + tile[1:2] + tile[2:3])
            im = im + (tile[3:4] + tile[4:5] + tile[5:6])
        out_re.append(re)
        out_im.append(im)
    energy_ref[...] = jnp.concatenate(
        [jnp.concatenate(out_re, axis=1), jnp.concatenate(out_im, axis=1)], axis=0
    )


def pick_block(whole, block, width):
    blocks = whole.shape[1] // width
    picked = jnp.zeros((whole.shape[0], width), F32)
    for b in range(blocks):
        picked = jnp.where(block == b, whole[:, b * width : (b + 1) * width], picked)
    return picked


def overlap_kernel(
    received_ref, w1_ref, bias_ref, second_ref, readout_ref, high_ref, low_ref, re_ref, im_ref, hidden_ref
):
    peers, share, _ = received_ref.shape
    orbitals = w1_ref.shape[0]
    w1 = w1_ref[...]
    bias = bias_ref[...]
    step = max(1, ROWS // share)
    for start in range(0, peers, step):
        occupied = received_ref[start : start + step, :, 0:orbitals].reshape(step * share, orbitals)
        pre = dot(occupied, w1, ((1,), (0,))) + bias
        hidden_ref[start * share : (start + step) * share, :] = jnp.tanh(pre).astype(BF16)
    hidden = hidden_ref[...]
    overlap = dot(hidden, hidden, ((1,), (1,)))
    high = overlap.astype(BF16)
    high_ref[...] = high
    low_ref[...] = (overlap - high.astype(F32)).astype(BF16)
    mid = jnp.tanh(dot(second_ref[...], hidden, ((0,), (1,))))
    slope = 1.0 - mid * mid
    readout = readout_ref[...].T
    re_ref[...] = slope * readout[:, 0:1]
    im_ref[...] = slope * readout[:, 1:2]


def solve(energy, gram):
    total = energy.shape[1]
    centered = energy - jnp.mean(energy, axis=1, keepdims=True)
    res_c = jnp.concatenate([centered[1:2], -centered[0:1]], axis=0) / total
    res_y = gram(res_c)
    dir_c, dir_y = res_c, res_y
    norm_now = full_sum(res_c * res_y)
    change = jnp.zeros_like(res_y)
    for turn in range(ITERS):
        img_c = dir_y / total + DIAG_SHIFT * dir_c
        alpha = norm_now / full_sum(img_c * dir_y)
        change = change + alpha * dir_y
        if turn + 1 < ITERS:
            img_y = gram(dir_y) / total + DIAG_SHIFT * dir_y
            res_c = res_c - alpha * img_c
            res_y = res_y - alpha * img_y
            norm_next = full_sum(res_c * res_y)
            beta = norm_next / norm_now
            dir_c = res_c + beta * dir_c
            dir_y = res_y + beta * dir_y
            norm_now = norm_next
    return change


def full_sum(x):
    return jnp.sum(jnp.sum(x, axis=1, keepdims=True), axis=0, keepdims=True)


def project(lifted, slope_re, slope_im):
    raw = jnp.concatenate(
        [jnp.sum(lifted * slope_re, axis=0, keepdims=True), jnp.sum(lifted * slope_im, axis=0, keepdims=True)],
        axis=0,
    )
    return raw - jnp.mean(raw, axis=1, keepdims=True)


def solve_kernel(mine_ref, other_ref, high_ref, low_ref, re_ref, im_ref, local_ref, change_ref):
    width = local_ref.shape[1]
    block = lax.axis_index("samples")
    energy = mine_ref[...] + other_ref[...]
    local_ref[...] = pick_block(energy, block, width)

    def gram(c):
        back = re_ref[...] * c[0:1] + im_ref[...] * c[1:2]
        high = back.astype(BF16)
        low = (back - high.astype(F32)).astype(BF16)
        lifted = dot(high, high_ref[...], ((1,), (0,)))
        lifted += dot(low, high_ref[...], ((1,), (0,)))
        lifted += dot(high, low_ref[...], ((1,), (0,)))
        return project(lifted, re_ref[...], im_ref[...])

    change_ref[...] = pick_block(solve(energy, gram), block, width)


def wide_solve(energy, occupied, first_weight, bias_row, second, readout, here):
    block = lax.axis_index("samples")
    pre = dot(occupied, first_weight, ((1,), (0,))) + bias_row
    hidden = jnp.tanh(pre).astype(BF16)
    mid = jnp.tanh(dot(second, hidden, ((0,), (1,))))
    slope = 1.0 - mid * mid
    slope_re = slope * readout[0][:, None]
    slope_im = slope * readout[1][:, None]

    def gram(c):
        high, low = split(slope_re * c[0:1] + slope_im * c[1:2])
        high, low = split(dot(high, hidden, ((1,), (0,))) + dot(low, hidden, ((1,), (0,))))
        lifted = dot(high, hidden, ((1,), (1,))) + dot(low, hidden, ((1,), (1,)))
        return project(lifted, slope_re, slope_im)

    change = solve(energy, gram)
    return (
        lax.dynamic_slice_in_dim(energy, block * here, here, 1),
        lax.dynamic_slice_in_dim(change, block * here, here, 1),
    )


def shift(x, axis, step):
    size = lax.axis_size(axis)
    return lax.ppermute(x, axis, [(i, (i + step) % size) for i in range(size)])


def body(
    occupations,
    connection_counts,
    connection_orbitals,
    connection_elements,
    laser_step,
    first_weight,
    first_bias,
    second_weight,
    readout,
):
    here, orbitals = occupations.shape
    slots = connection_orbitals.shape[1]
    wide, narrow = first_weight.shape[1], second_weight.shape[1]
    chips = lax.axis_size("chip")
    spread = chips * lax.axis_size("core")
    blocks = lax.axis_size("samples")
    total = here * blocks
    peers = blocks * chips
    share = here // chips
    lanes = -(-(orbitals + here) // 128) * 128
    bias_row = first_bias[None, :]

    shifts, shards = [], []
    for step in range(1, chips):
        shifts.append((step, 0))
        shards.append(shift(second_weight, "chip", step))
    shifts.append((0, 1))
    shards.append(shift(second_weight, "core", 1))
    for step in range(1, chips):
        shifts.append((step, 1))
        shards.append(shift(shards[step - 1], "core", 1))
    shifts.append((0, 0))

    hbm = pl.BlockSpec(memory_space=pltpu.HBM)
    hidden, owner, weight, carry, w1, bias, readout_near, own_shard = call(
        functools.partial(slot_hidden_kernel, spread),
        9,
        (
            jax.ShapeDtypeStruct((slots + here, wide), BF16),
            jax.ShapeDtypeStruct((here, slots), BF16),
            jax.ShapeDtypeStruct((1, slots), F32),
            jax.ShapeDtypeStruct((share, lanes), F32),
            jax.ShapeDtypeStruct(first_weight.shape, BF16),
            jax.ShapeDtypeStruct(bias_row.shape, F32),
            jax.ShapeDtypeStruct(readout.shape, F32),
            jax.ShapeDtypeStruct(second_weight.shape, BF16),
        ),
        [
            pltpu.VMEM((1, here), jnp.int32),
            pltpu.VMEM(connection_orbitals.shape, jnp.int32),
            pltpu.VMEM(occupations.shape, jnp.int32),
            pltpu.SMEM((1,), jnp.int32),
            pltpu.VMEM(connection_elements.shape, F32),
            pltpu.SemaphoreType.DMA((9,)),
        ],
        name="slot_hidden",
        in_specs=[hbm] * 9,
    )(
        connection_counts[None, :],
        connection_orbitals,
        occupations,
        first_weight,
        bias_row,
        laser_step[None],
        connection_elements,
        readout,
        second_weight,
    )

    send, second = call(
        functools.partial(slot_energy_kernel, tuple(shifts)),
        5 + len(shifts),
        (
            jax.ShapeDtypeStruct((peers, share, lanes), BF16),
            jax.ShapeDtypeStruct((wide, narrow), BF16),
        ),
        name="slot_energy",
    )(hidden, owner, weight, carry, readout_near, *shards, own_shard)

    received = lax.all_to_all(send, ("samples", "chip"), 0, 0, tiled=True)
    mine = call(
        functools.partial(collect_kernel, here, chips),
        1,
        jax.ShapeDtypeStruct((2, total), F32),
        name="collect",
    )(received)
    other = shift(mine, "core", 1)

    if total > wide:
        occupied = received[:, :, :orbitals].reshape(total, orbitals)
        return wide_solve(mine + other, occupied, first_weight, bias_row, second, readout, here)

    overlap = call(
        overlap_kernel,
        5,
        (jax.ShapeDtypeStruct((total, total), BF16),) * 2 + (jax.ShapeDtypeStruct((narrow, total), F32),) * 2,
        [pltpu.VMEM((total, wide), BF16)],
        name="overlap",
    )(received, w1, bias, second, readout_near)
    return call(
        solve_kernel,
        6,
        (jax.ShapeDtypeStruct((2, here), F32),) * 2,
        name="solve",
    )(mine, other, *overlap)


def solution(mesh):
    blocks, spread = mesh.shape["samples"], mesh.shape["params"]
    fine = Mesh(mesh.devices.reshape(blocks, spread // 2, 2), ("samples", "chip", "core"))
    return jax.shard_map(
        body,
        mesh=fine,
        in_specs=(
            P("samples", None),
            P("samples"),
            P(None, ("samples", "chip", "core")),
            P(None, ("samples", "chip", "core")),
            P(),
            P(),
            P(),
            P(("chip", "core"), None),
            P(),
        ),
        out_specs=(P(None, "samples"), P(None, "samples")),
        check_vma=False,
    )
```

```python
import functools

import jax
import jax.numpy as jnp
from jax import lax
from jax.experimental import pallas as pl
from jax.experimental.pallas import tpu as pltpu
from jax.sharding import Mesh, PartitionSpec as P

ITERS = 2


FIELD_SCALE = 0.8
FIELD_RATE = 0.0123
DIAG_SHIFT = 0.01
F32 = jnp.float32
BF16 = jnp.bfloat16
ROWS = 256
VMEM_LIMIT = 48 * 1024 * 1024


def dot(a, b, dims):
    return lax.dot_general(a, b, (dims, ((), ())), preferred_element_type=F32)


def split(x):
    high = lax.reduce_precision(x, 8, 7)
    return high.astype(BF16), (x - high).astype(BF16)


def parts(x):
    high = x.astype(BF16)
    rest = x - high.astype(F32)
    middle = rest.astype(BF16)
    return high, middle, (rest - middle.astype(F32)).astype(BF16)


def iota(shape, dim):
    return lax.broadcasted_iota(jnp.int32, shape, dim)


def call(kernel, count, out_shape, scratch=(), name=None, scalars=False, flops=0, transcendentals=0):
    vmem = pl.BlockSpec(memory_space=pltpu.VMEM)
    far = pl.BlockSpec(memory_space=pltpu.HBM)
    scalar = pl.BlockSpec(memory_space=pltpu.SMEM)
    return pl.pallas_call(
        kernel,
        out_shape=out_shape,
        in_specs=[scalar] + [far] * (count - 1) if scalars else [vmem] * count,
        out_specs=jax.tree.map(lambda _: vmem, out_shape),
        scratch_shapes=scratch,
        compiler_params=pltpu.CompilerParams(vmem_limit_bytes=VMEM_LIMIT),
        cost_estimate=pl.CostEstimate(
            flops=int(flops),
            transcendentals=int(transcendentals),
            bytes_accessed=sum(x.size * x.dtype.itemsize for x in jax.tree.leaves(out_shape)),
        ),
        name=name,
    )


def slot_hidden_kernel(
    spread,
    laser_ref,
    counts_hbm,
    orbitals_hbm,
    occ_hbm,
    w1_hbm,
    bias_hbm,
    elements_hbm,
    readout_hbm,
    own_hbm,
    hidden_ref,
    owner_ref,
    weight_ref,
    w1_ref,
    bias_ref,
    readout_ref,
    own_ref,
    occupied_ref,
    counts_ref,
    orbitals_ref,
    occ_ref,
    elements_ref,
    sems,
):
    here, orbitals = occ_ref.shape
    updates, slots = orbitals_ref.shape
    pairs = (
        (counts_hbm, counts_ref),
        (occ_hbm, occ_ref),
        (w1_hbm, w1_ref),
        (bias_hbm, bias_ref),
        (orbitals_hbm, orbitals_ref),
        (elements_hbm, elements_ref),
        (readout_hbm, readout_ref),
        (own_hbm, own_ref),
    )
    copies = [pltpu.make_async_copy(a, b, sems.at[i]) for i, (a, b) in enumerate(pairs)]
    for copy in copies:
        copy.start()
    chip, core = lax.axis_index("chip"), lax.axis_index("core")
    place = chip * 2 + core
    copies[0].wait()
    counts = counts_ref[...].astype(F32)
    row, col = iota((here, here), 0), iota((here, here), 1)
    ends = jnp.sum(jnp.where(col <= row, counts, 0.0), axis=1, keepdims=True)
    starts = jnp.sum(jnp.where(col < row, counts, 0.0), axis=1, keepdims=True)
    positions = (place + spread * iota((1, slots), 1)).astype(F32)
    owner = jnp.where((starts <= positions) & (positions < ends), 1.0, 0.0).astype(BF16)
    owner_ref[...] = owner
    copies[1].wait()
    occupied = occ_ref[...].astype(F32).astype(BF16)
    occupied_ref[...] = occupied
    copies[2].wait()
    copies[3].wait()
    w1 = w1_ref[...]
    bias = bias_ref[...]
    hidden_ref[slots:, :] = jnp.tanh(dot(occupied, w1, ((1,), (0,))) + bias).astype(BF16)
    copies[4].wait()
    for start in range(0, slots, ROWS):
        stop = min(start + ROWS, slots)
        parent_occ = dot(occupied, owner[:, start:stop], ((0,), (0,)))
        columns = iota((orbitals, stop - start), 0)
        flipped = columns == orbitals_ref[0:1, start:stop]
        for u in range(1, updates):
            flipped = flipped | (columns == orbitals_ref[u : u + 1, start:stop])
        slot_occ = jnp.where(flipped, 1.0 - parent_occ, parent_occ).astype(BF16)
        pre = dot(slot_occ, w1, ((0,), (0,))) + bias
        hidden_ref[start:stop, :] = jnp.tanh(pre).astype(BF16)
    copies[5].wait()
    laser = jnp.full((1, slots), laser_ref[0], jnp.int32).astype(F32)
    field = FIELD_SCALE * jnp.sin(FIELD_RATE * laser)
    weight_ref[...] = elements_ref[0:1, :] + field * elements_ref[1:2, :]
    copies[6].wait()
    copies[7].wait()


def slot_energy_kernel(shifts, hidden_ref, owner_ref, weight_ref, readout_ref, occupied_ref, *refs):
    shard_refs, (send_ref, second_ref, again_ref) = refs[: len(shifts)], refs[len(shifts) :]
    here, slots = owner_ref.shape
    chips = lax.axis_size("chip")
    chip, core = lax.axis_index("chip"), lax.axis_index("core")
    for (step, other), shard in zip(shifts, shard_refs):
        rows = shard.shape[0]
        source = lax.rem(chip + chips - step, chips) * 2 + (core ^ other)
        second_ref[pl.ds(pl.multiple_of(source * rows, rows), rows), :] = shard[...]
    mid = jnp.tanh(dot(second_ref[...], hidden_ref[...], ((0,), (1,))))
    readout = readout_ref[...].T
    logs_re = jnp.sum(mid * readout[:, 0:1], axis=0, keepdims=True)
    logs_im = jnp.sum(mid * readout[:, 1:2], axis=0, keepdims=True)
    owner = owner_ref[...]
    own = jnp.concatenate(parts(logs_re[:, slots:]) + parts(logs_im[:, slots:]), axis=0)
    parent = dot(own, owner, ((1,), (0,)))
    diff_re = logs_re[:, :slots] - (parent[0:1] + parent[1:2] + parent[2:3])
    diff_im = logs_im[:, :slots] - (parent[3:4] + parent[4:5] + parent[5:6])
    used = jnp.sum(owner.astype(F32), axis=0, keepdims=True) > 0.0
    scale = weight_ref[...] * jnp.exp(diff_re)
    contrib_re = jnp.where(used, scale * jnp.cos(diff_im), 0.0)
    contrib_im = jnp.where(used, scale * jnp.sin(diff_im), 0.0)
    contrib = jnp.concatenate(parts(contrib_re) + parts(contrib_im), axis=0)
    sums = dot(contrib, owner, ((1,), (1,)))
    partial_re = sums[0:1] + sums[1:2] + sums[2:3]
    partial_im = sums[3:4] + sums[4:5] + sums[5:6]
    row = jnp.concatenate([partial_re, partial_im], axis=1)
    send_ref[...] = jnp.broadcast_to(row[None], send_ref.shape)
    again_ref[...] = occupied_ref[...]


def collect_kernel(here, chips, received_ref, energy_ref):
    out_re, out_im = [], []
    for start in range(0, received_ref.shape[0], chips):
        row = received_ref[start]
        for k in range(1, chips):
            row = row + received_ref[start + k]
        out_re.append(row[:, :here])
        out_im.append(row[:, here:])
    energy_ref[...] = jnp.concatenate(
        [jnp.concatenate(out_re, axis=1), jnp.concatenate(out_im, axis=1)], axis=0
    )


def pick_block(whole, block, width):
    blocks = whole.shape[1] // width
    picked = jnp.zeros((whole.shape[0], width), F32)
    for b in range(blocks):
        picked = jnp.where(block == b, whole[:, b * width : (b + 1) * width], picked)
    return picked


def overlap_kernel(
    entries, occ_ref, w1_ref, bias_ref, second_ref, readout_ref, high_ref, low_ref, re_ref, im_ref, occ_all, hidden_ref
):
    blocks, here, _ = occ_ref.shape
    block = lax.axis_index("samples")
    for step, entry in enumerate(entries):
        occ_all[pl.ds(pl.multiple_of((block ^ entry) * here, here), here), :] = occ_ref[step]
    w1 = w1_ref[...]
    bias = bias_ref[...]
    for start in range(0, blocks * here, ROWS):
        pre = dot(occ_all[start : start + ROWS, :], w1, ((1,), (0,))) + bias
        hidden_ref[start : start + ROWS, :] = jnp.tanh(pre).astype(BF16)
    hidden = hidden_ref[...]
    overlap = dot(hidden, hidden, ((1,), (1,)))
    high = overlap.astype(BF16)
    high_ref[...] = high
    low_ref[...] = (overlap - high.astype(F32)).astype(BF16)
    mid = jnp.tanh(dot(second_ref[...], hidden, ((0,), (1,))))
    slope = 1.0 - mid * mid
    readout = readout_ref[...].T
    re_ref[...] = slope * readout[:, 0:1]
    im_ref[...] = slope * readout[:, 1:2]


def solve(energy, gram):
    total = energy.shape[1]
    centered = energy - jnp.mean(energy, axis=1, keepdims=True)
    res_c = jnp.concatenate([centered[1:2], -centered[0:1]], axis=0) / total
    res_y = gram(res_c)
    dir_c, dir_y = res_c, res_y
    norm_now = full_sum(res_c * res_y)
    change = jnp.zeros_like(res_y)
    for turn in range(ITERS):
        img_c = dir_y / total + DIAG_SHIFT * dir_c
        alpha = norm_now / full_sum(img_c * dir_y)
        change = change + alpha * dir_y
        if turn + 1 < ITERS:
            img_y = gram(dir_y) / total + DIAG_SHIFT * dir_y
            res_c = res_c - alpha * img_c
            res_y = res_y - alpha * img_y
            norm_next = full_sum(res_c * res_y)
            beta = norm_next / norm_now
            dir_c = res_c + beta * dir_c
            dir_y = res_y + beta * dir_y
            norm_now = norm_next
    return change


def full_sum(x):
    return jnp.sum(jnp.sum(x, axis=1, keepdims=True), axis=0, keepdims=True)


def project(lifted, slope_re, slope_im):
    raw = jnp.concatenate(
        [jnp.sum(lifted * slope_re, axis=0, keepdims=True), jnp.sum(lifted * slope_im, axis=0, keepdims=True)],
        axis=0,
    )
    return raw - jnp.mean(raw, axis=1, keepdims=True)


def solve_kernel(mine_ref, other_ref, high_ref, low_ref, re_ref, im_ref, local_ref, change_ref):
    width = local_ref.shape[1]
    block = lax.axis_index("samples")
    energy = mine_ref[...] + other_ref[...]
    local_ref[...] = pick_block(energy, block, width)

    def gram(c):
        back = re_ref[...] * c[0:1] + im_ref[...] * c[1:2]
        high = back.astype(BF16)
        low = (back - high.astype(F32)).astype(BF16)
        lifted = dot(high, high_ref[...], ((1,), (0,)))
        lifted += dot(low, high_ref[...], ((1,), (0,)))
        lifted += dot(high, low_ref[...], ((1,), (0,)))
        return project(lifted, re_ref[...], im_ref[...])

    change_ref[...] = pick_block(solve(energy, gram), block, width)


def wide_solve(energy, occ_stack, entries, first_weight, bias_row, second, readout):
    block = lax.axis_index("samples")
    here = occ_stack.shape[1]
    where = sorted(range(len(entries)), key=lambda k: entries[k])
    order = jnp.take(jnp.array(where, jnp.int32), block ^ jnp.arange(len(entries), dtype=jnp.int32))
    occupied = jnp.take(occ_stack, order, axis=0).reshape(-1, occ_stack.shape[2])
    pre = dot(occupied, first_weight, ((1,), (0,))) + bias_row
    hidden = jnp.tanh(pre).astype(BF16)
    mid = jnp.tanh(dot(second, hidden, ((0,), (1,))))
    slope = 1.0 - mid * mid
    slope_re = slope * readout[0][:, None]
    slope_im = slope * readout[1][:, None]

    def gram(c):
        high, low = split(slope_re * c[0:1] + slope_im * c[1:2])
        high, low = split(dot(high, hidden, ((1,), (0,))) + dot(low, hidden, ((1,), (0,))))
        lifted = dot(high, hidden, ((1,), (1,))) + dot(low, hidden, ((1,), (1,)))
        return project(lifted, slope_re, slope_im)

    change = solve(energy, gram)
    return (
        lax.dynamic_slice_in_dim(energy, block * here, here, 1),
        lax.dynamic_slice_in_dim(change, block * here, here, 1),
    )


def shift(x, axis, step):
    size = lax.axis_size(axis)
    return lax.ppermute(x, axis, [(i, (i + step) % size) for i in range(size)])


def double(stack, bit):
    blocks = lax.axis_size("samples")
    return lax.ppermute(stack, "samples", [(i, i ^ bit) for i in range(blocks)])


def body(
    occupations,
    connection_counts,
    connection_orbitals,
    connection_elements,
    laser_step,
    first_weight,
    first_bias,
    second_weight,
    readout,
):
    here, orbitals = occupations.shape
    slots = connection_orbitals.shape[1]
    wide, narrow = first_weight.shape[1], second_weight.shape[1]
    chips = lax.axis_size("chip")
    spread = chips * lax.axis_size("core")
    blocks = lax.axis_size("samples")
    total = here * blocks
    peers = blocks * chips
    bias_row = first_bias[None, :]

    bits = [1 << k for k in reversed(range((blocks - 1).bit_length()))]
    entries = [0]
    for bit in bits:
        entries = entries + [e ^ bit for e in entries]
    moved = double(occupations.astype(BF16)[None], bits[0])

    shifts, shards = [], []
    for step in range(1, chips):
        shifts.append((step, 0))
        shards.append(shift(second_weight, "chip", step))
    shifts.append((0, 1))
    shards.append(shift(second_weight, "core", 1))
    for step in range(1, chips):
        shifts.append((step, 1))
        shards.append(shift(shards[step - 1], "core", 1))
    shifts.append((0, 0))

    hidden, owner, weight, w1, bias, readout_near, own_shard, occupied = call(
        functools.partial(slot_hidden_kernel, spread),
        9,
        (
            jax.ShapeDtypeStruct((slots + here, wide), BF16),
            jax.ShapeDtypeStruct((here, slots), BF16),
            jax.ShapeDtypeStruct((1, slots), F32),
            jax.ShapeDtypeStruct(first_weight.shape, BF16),
            jax.ShapeDtypeStruct(bias_row.shape, F32),
            jax.ShapeDtypeStruct(readout.shape, F32),
            jax.ShapeDtypeStruct(second_weight.shape, BF16),
            jax.ShapeDtypeStruct(occupations.shape, BF16),
        ),
        [
            pltpu.VMEM((1, here), jnp.int32),
            pltpu.VMEM(connection_orbitals.shape, jnp.int32),
            pltpu.VMEM(occupations.shape, jnp.int32),
            pltpu.VMEM(connection_elements.shape, F32),
            pltpu.SemaphoreType.DMA((8,)),
        ],
        name="slot_hidden",
        scalars=True,
        flops=2 * (slots + here) * orbitals * wide,
        transcendentals=(slots + here) * wide,
    )(
        laser_step[None],
        *(
            pltpu.with_memory_space_constraint(x, pltpu.HBM)
            for x in (
                connection_counts[None, :],
                connection_orbitals,
                occupations,
                first_weight,
                bias_row,
                connection_elements,
                readout,
                second_weight,
            )
        ),
    )
    stack = jnp.concatenate([occupied[None], moved], axis=0)
    moved = double(stack, bits[1])

    send, second, occupied = call(
        functools.partial(slot_energy_kernel, tuple(shifts)),
        5 + len(shifts),
        (
            jax.ShapeDtypeStruct((peers, 1, 2 * here), F32),
            jax.ShapeDtypeStruct((wide, narrow), BF16),
            jax.ShapeDtypeStruct(occupations.shape, BF16),
        ),
        name="slot_energy",
        flops=2 * (slots + here) * wide * narrow,
        transcendentals=(slots + here) * narrow,
    )(hidden, owner, weight, readout_near, occupied, *shards, own_shard)
    stack = jnp.concatenate([occupied[None], stack[1:], moved], axis=0)
    for bit in bits[2:]:
        stack = jnp.concatenate([stack, double(stack, bit)], axis=0)

    received = lax.all_to_all(send, ("samples", "chip"), 0, 0, tiled=True)
    mine = call(
        functools.partial(collect_kernel, here, chips),
        1,
        jax.ShapeDtypeStruct((2, total), F32),
        name="collect",
    )(received)
    other = shift(mine, "core", 1)

    if total > wide:
        return wide_solve(mine + other, stack, entries, first_weight, bias_row, second, readout)

    overlap = call(
        functools.partial(overlap_kernel, entries),
        5,
        (jax.ShapeDtypeStruct((total, total), BF16),) * 2 + (jax.ShapeDtypeStruct((narrow, total), F32),) * 2,
        [pltpu.VMEM((total, orbitals), BF16), pltpu.VMEM((total, wide), BF16)],
        name="overlap",
        flops=2 * total * wide * (orbitals + narrow + total),
        transcendentals=total * (wide + narrow),
    )(stack, w1, bias, second, readout_near)
    return call(
        solve_kernel,
        6,
        (jax.ShapeDtypeStruct((2, here), F32),) * 2,
        name="solve",
        flops=ITERS * 6 * total * total * narrow,
    )(mine, other, *overlap)


def solution(mesh):
    blocks, spread = mesh.shape["samples"], mesh.shape["params"]
    fine = Mesh(mesh.devices.reshape(blocks, spread // 2, 2), ("samples", "chip", "core"))
    return jax.shard_map(
        body,
        mesh=fine,
        in_specs=(
            P("samples", None),
            P("samples"),
            P(None, ("samples", "chip", "core")),
            P(None, ("samples", "chip", "core")),
            P(),
            P(),
            P(),
            P(("chip", "core"), None),
            P(),
        ),
        out_specs=(P(None, "samples"), P(None, "samples")),
        check_vma=False,
    )
```

```python
import functools

import jax
import jax.numpy as jnp
from jax import lax
from jax.experimental import pallas as pl
from jax.experimental.pallas import tpu as pltpu
from jax.sharding import Mesh, PartitionSpec as P

ITERS = 2


FIELD_SCALE = 0.8
FIELD_RATE = 0.0123
DIAG_SHIFT = 0.01
F32 = jnp.float32
BF16 = jnp.bfloat16
ROWS = 256
VMEM_LIMIT = 48 * 1024 * 1024


def dot(a, b, dims):
    return lax.dot_general(a, b, (dims, ((), ())), preferred_element_type=F32)


def split(x):
    high = lax.reduce_precision(x, 8, 7)
    return high.astype(BF16), (x - high).astype(BF16)


def parts(x):
    high = x.astype(BF16)
    rest = x - high.astype(F32)
    middle = rest.astype(BF16)
    return high, middle, (rest - middle.astype(F32)).astype(BF16)


def iota(shape, dim):
    return lax.broadcasted_iota(jnp.int32, shape, dim)


def call(kernel, count, out_shape, scratch=(), name=None, copies=False, flops=0, transcendentals=0):
    vmem = pl.BlockSpec(memory_space=pltpu.VMEM)
    far = pl.BlockSpec(memory_space=pltpu.HBM)
    return pl.pallas_call(
        kernel,
        out_shape=out_shape,
        in_specs=[far if copies else vmem] * count,
        out_specs=jax.tree.map(lambda _: vmem, out_shape),
        scratch_shapes=scratch,
        compiler_params=pltpu.CompilerParams(vmem_limit_bytes=VMEM_LIMIT),
        cost_estimate=pl.CostEstimate(
            flops=int(flops),
            transcendentals=int(transcendentals),
            bytes_accessed=sum(x.size * x.dtype.itemsize for x in jax.tree.leaves(out_shape)),
        ),
        name=name,
    )


def slot_hidden_kernel(
    spread,
    counts_hbm,
    orbitals_hbm,
    occ_hbm,
    w1_hbm,
    bias_hbm,
    elements_hbm,
    readout_hbm,
    own_hbm,
    hidden_ref,
    owner_ref,
    elements_ref,
    w1_ref,
    bias_ref,
    readout_ref,
    own_ref,
    occupied_ref,
    counts_ref,
    orbitals_ref,
    occ_ref,
    sems,
):
    here, orbitals = occ_ref.shape
    updates, slots = orbitals_ref.shape
    pairs = (
        (counts_hbm, counts_ref),
        (occ_hbm, occ_ref),
        (w1_hbm, w1_ref),
        (bias_hbm, bias_ref),
        (orbitals_hbm, orbitals_ref),
        (elements_hbm, elements_ref),
        (readout_hbm, readout_ref),
        (own_hbm, own_ref),
    )
    copies = [pltpu.make_async_copy(a, b, sems.at[i]) for i, (a, b) in enumerate(pairs)]
    for copy in copies:
        copy.start()
    chip, core = lax.axis_index("chip"), lax.axis_index("core")
    place = chip * 2 + core
    copies[0].wait()
    counts = counts_ref[...].astype(F32)
    row, col = iota((here, here), 0), iota((here, here), 1)
    ends = jnp.sum(jnp.where(col <= row, counts, 0.0), axis=1, keepdims=True)
    starts = jnp.sum(jnp.where(col < row, counts, 0.0), axis=1, keepdims=True)
    positions = (place + spread * iota((1, slots), 1)).astype(F32)
    owner = jnp.where((starts <= positions) & (positions < ends), 1.0, 0.0).astype(BF16)
    owner_ref[...] = owner
    copies[1].wait()
    occupied = occ_ref[...].astype(F32).astype(BF16)
    occupied_ref[...] = occupied
    copies[2].wait()
    copies[3].wait()
    w1 = w1_ref[...]
    bias = bias_ref[...]
    hidden_ref[slots:, :] = jnp.tanh(dot(occupied, w1, ((1,), (0,))) + bias).astype(BF16)
    copies[4].wait()
    for start in range(0, slots, ROWS):
        stop = min(start + ROWS, slots)
        parent_occ = dot(occupied, owner[:, start:stop], ((0,), (0,)))
        columns = iota((orbitals, stop - start), 0)
        flipped = columns == orbitals_ref[0:1, start:stop]
        for u in range(1, updates):
            flipped = flipped | (columns == orbitals_ref[u : u + 1, start:stop])
        slot_occ = jnp.where(flipped, 1.0 - parent_occ, parent_occ).astype(BF16)
        pre = dot(slot_occ, w1, ((0,), (0,))) + bias
        hidden_ref[start:stop, :] = jnp.tanh(pre).astype(BF16)
    copies[5].wait()
    copies[6].wait()
    copies[7].wait()


def slot_energy_kernel(
    shifts, field_ref, hidden_ref, owner_ref, elements_ref, readout_ref, occupied_ref, *refs
):
    shard_refs, (energy_ref, second_ref, again_ref) = refs[: len(shifts)], refs[len(shifts) :]
    here, slots = owner_ref.shape
    chips = lax.axis_size("chip")
    chip, core = lax.axis_index("chip"), lax.axis_index("core")
    for (step, other), shard in zip(shifts, shard_refs):
        rows = shard.shape[0]
        source = lax.rem(chip + chips - step, chips) * 2 + (core ^ other)
        second_ref[pl.ds(pl.multiple_of(source * rows, rows), rows), :] = shard[...]
    mid = jnp.tanh(dot(second_ref[...], hidden_ref[...], ((0,), (1,))))
    readout = readout_ref[...].T
    logs_re = jnp.sum(mid * readout[:, 0:1], axis=0, keepdims=True)
    logs_im = jnp.sum(mid * readout[:, 1:2], axis=0, keepdims=True)
    owner = owner_ref[...]
    own = jnp.concatenate(parts(logs_re[:, slots:]) + parts(logs_im[:, slots:]), axis=0)
    parent = dot(own, owner, ((1,), (0,)))
    diff_re = logs_re[:, :slots] - (parent[0:1] + parent[1:2] + parent[2:3])
    diff_im = logs_im[:, :slots] - (parent[3:4] + parent[4:5] + parent[5:6])
    used = jnp.sum(owner.astype(F32), axis=0, keepdims=True) > 0.0
    weight = elements_ref[0:1, :] + field_ref[...] * elements_ref[1:2, :]
    scale = weight * jnp.exp(diff_re)
    contrib_re = jnp.where(used, scale * jnp.cos(diff_im), 0.0)
    contrib_im = jnp.where(used, scale * jnp.sin(diff_im), 0.0)
    contrib = jnp.concatenate(parts(contrib_re) + parts(contrib_im), axis=0)
    sums = dot(contrib, owner, ((1,), (1,)))
    partial_re = sums[0:1] + sums[1:2] + sums[2:3]
    partial_im = sums[3:4] + sums[4:5] + sums[5:6]
    partial = jnp.concatenate([partial_re, partial_im], axis=0)
    energy_ref[...] = spread_blocks(partial, lax.axis_index("samples"), energy_ref.shape[1] // here)
    again_ref[...] = occupied_ref[...]


def spread_blocks(partial, block, blocks):
    zero = jnp.zeros_like(partial)
    return jnp.concatenate([jnp.where(block == b, partial, zero) for b in range(blocks)], axis=1)


def pick_block(whole, block, width):
    blocks = whole.shape[1] // width
    picked = jnp.zeros((whole.shape[0], width), F32)
    for b in range(blocks):
        picked = jnp.where(block == b, whole[:, b * width : (b + 1) * width], picked)
    return picked


def overlap_kernel(
    entries, occ_ref, other_ref, w1_ref, bias_ref, second_ref, readout_ref, high_ref, low_ref, re_ref, im_ref, occ_all, hidden_ref
):
    blocks, here, _ = occ_ref.shape
    block = lax.axis_index("samples")
    odd = lax.axis_index("core") == 1
    for step, entry in enumerate(entries):
        picked = jnp.where(odd, other_ref[step], occ_ref[step])
        occ_all[pl.ds(pl.multiple_of((block ^ entry) * here, here), here), :] = picked
    w1 = w1_ref[...]
    bias = bias_ref[...]
    for start in range(0, blocks * here, ROWS):
        pre = dot(occ_all[start : start + ROWS, :], w1, ((1,), (0,))) + bias
        hidden_ref[start : start + ROWS, :] = jnp.tanh(pre).astype(BF16)
    hidden = hidden_ref[...]
    overlap = dot(hidden, hidden, ((1,), (1,)))
    high = overlap.astype(BF16)
    high_ref[...] = high
    low_ref[...] = (overlap - high.astype(F32)).astype(BF16)
    mid = jnp.tanh(dot(second_ref[...], hidden, ((0,), (1,))))
    slope = 1.0 - mid * mid
    readout = readout_ref[...].T
    re_ref[...] = slope * readout[:, 0:1]
    im_ref[...] = slope * readout[:, 1:2]


def solve(energy, gram):
    total = energy.shape[1]
    centered = energy - jnp.mean(energy, axis=1, keepdims=True)
    res_c = jnp.concatenate([centered[1:2], -centered[0:1]], axis=0) / total
    res_y = gram(res_c)
    dir_c, dir_y = res_c, res_y
    norm_now = full_sum(res_c * res_y)
    change = jnp.zeros_like(res_y)
    for turn in range(ITERS):
        img_c = dir_y / total + DIAG_SHIFT * dir_c
        alpha = norm_now / full_sum(img_c * dir_y)
        change = change + alpha * dir_y
        if turn + 1 < ITERS:
            img_y = gram(dir_y) / total + DIAG_SHIFT * dir_y
            res_c = res_c - alpha * img_c
            res_y = res_y - alpha * img_y
            norm_next = full_sum(res_c * res_y)
            beta = norm_next / norm_now
            dir_c = res_c + beta * dir_c
            dir_y = res_y + beta * dir_y
            norm_now = norm_next
    return change


def full_sum(x):
    return jnp.sum(jnp.sum(x, axis=1, keepdims=True), axis=0, keepdims=True)


def project(lifted, slope_re, slope_im):
    raw = jnp.concatenate(
        [jnp.sum(lifted * slope_re, axis=0, keepdims=True), jnp.sum(lifted * slope_im, axis=0, keepdims=True)],
        axis=0,
    )
    return raw - jnp.mean(raw, axis=1, keepdims=True)


def solve_kernel(mine_ref, other_ref, high_ref, low_ref, re_ref, im_ref, local_ref, change_ref):
    width = local_ref.shape[1]
    block = lax.axis_index("samples")
    energy = jnp.where(lax.axis_index("core") == 1, mine_ref[...], other_ref[...])
    local_ref[...] = pick_block(energy, block, width)

    def gram(c):
        back = re_ref[...] * c[0:1] + im_ref[...] * c[1:2]
        high = back.astype(BF16)
        low = (back - high.astype(F32)).astype(BF16)
        lifted = dot(high, high_ref[...], ((1,), (0,)))
        lifted += dot(low, high_ref[...], ((1,), (0,)))
        lifted += dot(high, low_ref[...], ((1,), (0,)))
        return project(lifted, re_ref[...], im_ref[...])

    change_ref[...] = pick_block(solve(energy, gram), block, width)


def wide_solve(energy, occ_stack, entries, first_weight, bias_row, second, readout):
    block = lax.axis_index("samples")
    here = occ_stack.shape[1]
    where = sorted(range(len(entries)), key=lambda k: entries[k])
    order = jnp.take(jnp.array(where, jnp.int32), block ^ jnp.arange(len(entries), dtype=jnp.int32))
    occupied = jnp.take(occ_stack, order, axis=0).reshape(-1, occ_stack.shape[2])
    pre = dot(occupied, first_weight, ((1,), (0,))) + bias_row
    hidden = jnp.tanh(pre).astype(BF16)
    mid = jnp.tanh(dot(second, hidden, ((0,), (1,))))
    slope = 1.0 - mid * mid
    slope_re = slope * readout[0][:, None]
    slope_im = slope * readout[1][:, None]

    def gram(c):
        high, low = split(slope_re * c[0:1] + slope_im * c[1:2])
        high, low = split(dot(high, hidden, ((1,), (0,))) + dot(low, hidden, ((1,), (0,))))
        lifted = dot(high, hidden, ((1,), (1,))) + dot(low, hidden, ((1,), (1,)))
        return project(lifted, slope_re, slope_im)

    change = solve(energy, gram)
    return (
        lax.dynamic_slice_in_dim(energy, block * here, here, 1),
        lax.dynamic_slice_in_dim(change, block * here, here, 1),
    )


def shift(x, axis, step):
    size = lax.axis_size(axis)
    return lax.ppermute(x, axis, [(i, (i + step) % size) for i in range(size)])


def exchange(x, cores, partner):
    blocks, chips = lax.axis_size("samples"), lax.axis_size("chip")

    def rank(block, chip, core):
        return (block * chips + chip) * 2 + core

    pairs = [
        (rank(block, chip, core), rank(*partner(block, chip, core)))
        for block in range(blocks)
        for chip in range(chips)
        for core in cores
    ]
    return lax.ppermute(x, ("samples", "chip", "core"), pairs)


def across_blocks(bit):
    return lambda block, chip, core: (block ^ bit, chip, core)


def across_chips(bit):
    return lambda block, chip, core: (block, chip ^ bit, core)


def across_cores(block, chip, core):
    return block, chip, core ^ 1


def powers(size):
    return [1 << k for k in reversed(range((size - 1).bit_length()))]


def body(
    occupations,
    connection_counts,
    connection_orbitals,
    connection_elements,
    laser_step,
    first_weight,
    first_bias,
    second_weight,
    readout,
):
    here, orbitals = occupations.shape
    slots = connection_orbitals.shape[1]
    wide, narrow = first_weight.shape[1], second_weight.shape[1]
    chips = lax.axis_size("chip")
    spread = chips * lax.axis_size("core")
    blocks = lax.axis_size("samples")
    total = here * blocks
    bias_row = first_bias[None, :]
    field = FIELD_SCALE * jnp.sin(FIELD_RATE * laser_step.astype(F32)[None, None])

    bits = powers(blocks)
    entries = [0]
    for bit in bits:
        entries = entries + [e ^ bit for e in entries]
    moved = exchange(occupations.astype(BF16)[None], (0,), across_blocks(bits[0]))

    shifts, shards = [], []
    for step in range(1, chips):
        shifts.append((step, 0))
        shards.append(shift(second_weight, "chip", step))
    shifts.append((0, 1))
    shards.append(shift(second_weight, "core", 1))

    hidden, owner, elements, w1, bias, readout_near, own_shard, occupied = call(
        functools.partial(slot_hidden_kernel, spread),
        8,
        (
            jax.ShapeDtypeStruct((slots + here, wide), BF16),
            jax.ShapeDtypeStruct((here, slots), BF16),
            jax.ShapeDtypeStruct(connection_elements.shape, F32),
            jax.ShapeDtypeStruct(first_weight.shape, BF16),
            jax.ShapeDtypeStruct(bias_row.shape, F32),
            jax.ShapeDtypeStruct(readout.shape, F32),
            jax.ShapeDtypeStruct(second_weight.shape, BF16),
            jax.ShapeDtypeStruct(occupations.shape, BF16),
        ),
        [
            pltpu.VMEM((1, here), jnp.int32),
            pltpu.VMEM(connection_orbitals.shape, jnp.int32),
            pltpu.VMEM(occupations.shape, jnp.int32),
            pltpu.SemaphoreType.DMA((8,)),
        ],
        name="slot_hidden",
        copies=True,
        flops=2 * (slots + here) * orbitals * wide,
        transcendentals=(slots + here) * wide,
    )(
        *(
            pltpu.with_memory_space_constraint(x, pltpu.HBM)
            for x in (
                connection_counts[None, :],
                connection_orbitals,
                occupations,
                first_weight,
                bias_row,
                connection_elements,
                readout,
                second_weight,
            )
        ),
    )
    relayed, occupied = lax.optimization_barrier((shards[: chips - 1], occupied))
    for step in range(1, chips):
        shifts.append((step, 1))
        shards.append(shift(relayed[step - 1], "core", 1))
    shifts.append((0, 0))
    stack = jnp.concatenate([occupied[None], moved], axis=0)
    moved = exchange(stack, (0,), across_blocks(bits[1]))

    energy, second, occupied = call(
        functools.partial(slot_energy_kernel, tuple(shifts)),
        6 + len(shifts),
        (
            jax.ShapeDtypeStruct((2, total), F32),
            jax.ShapeDtypeStruct((wide, narrow), BF16),
            jax.ShapeDtypeStruct(occupations.shape, BF16),
        ),
        name="slot_energy",
        flops=2 * (slots + here) * wide * narrow,
        transcendentals=(slots + here) * narrow,
    )(field, hidden, owner, elements, readout_near, occupied, *shards, own_shard)
    mine = energy + exchange(energy, (0, 1), across_cores)
    moved, mine = lax.optimization_barrier((moved, mine))
    stack = jnp.concatenate([occupied[None], stack[1:], moved], axis=0)

    left = bits[2:]
    moved, age = None, 0
    for partner in [across_chips(bit) for bit in powers(chips)] + [across_blocks(bit) for bit in bits]:
        if moved is None and left:
            moved, age = exchange(stack, (0,), across_blocks(left.pop(0))), 0
        mine = mine + exchange(mine, (1,), partner)
        age += 1
        if moved is not None and age == 2:
            moved, mine = lax.optimization_barrier((moved, mine))
            stack, moved = jnp.concatenate([stack, moved], axis=0), None
    if moved is not None:
        stack = jnp.concatenate([stack, moved], axis=0)
    for bit in left:
        stack = jnp.concatenate([stack, exchange(stack, (0,), across_blocks(bit))], axis=0)
    other_stack = exchange(stack, (0,), across_cores)
    other = exchange(mine, (1,), across_cores)

    if total > wide:
        odd = lax.axis_index("core") == 1
        stack = jnp.where(odd, other_stack, stack)
        energy = jnp.where(odd, mine, other)
        return wide_solve(energy, stack, entries, first_weight, bias_row, second, readout)

    overlap = call(
        functools.partial(overlap_kernel, entries),
        6,
        (jax.ShapeDtypeStruct((total, total), BF16),) * 2 + (jax.ShapeDtypeStruct((narrow, total), F32),) * 2,
        [pltpu.VMEM((total, orbitals), BF16), pltpu.VMEM((total, wide), BF16)],
        name="overlap",
        flops=2 * total * wide * (orbitals + narrow + total),
        transcendentals=total * (wide + narrow),
    )(stack, other_stack, w1, bias, second, readout_near)
    return call(
        solve_kernel,
        6,
        (jax.ShapeDtypeStruct((2, here), F32),) * 2,
        name="solve",
        flops=ITERS * 6 * total * total * narrow,
    )(mine, other, *overlap)


def solution(mesh):
    blocks, spread = mesh.shape["samples"], mesh.shape["params"]
    fine = Mesh(mesh.devices.reshape(blocks, spread // 2, 2), ("samples", "chip", "core"))
    return jax.shard_map(
        body,
        mesh=fine,
        in_specs=(
            P("samples", None),
            P("samples"),
            P(None, ("samples", "chip", "core")),
            P(None, ("samples", "chip", "core")),
            P(),
            P(),
            P(),
            P(("chip", "core"), None),
            P(),
        ),
        out_specs=(P(None, "samples"), P(None, "samples")),
        check_vma=False,
    )
```

```python
import functools

import jax
import jax.numpy as jnp
from jax import lax
from jax.experimental import pallas as pl
from jax.experimental.pallas import tpu as pltpu
from jax.sharding import Mesh, PartitionSpec as P

ITERS = 2


FIELD_SCALE = 0.8
FIELD_RATE = 0.0123
DIAG_SHIFT = 0.01
F32 = jnp.float32
BF16 = jnp.bfloat16
ROWS = 256
VMEM_LIMIT = 48 * 1024 * 1024


def dot(a, b, dims):
    return lax.dot_general(a, b, (dims, ((), ())), preferred_element_type=F32)


def split(x):
    high = lax.reduce_precision(x, 8, 7)
    return high.astype(BF16), (x - high).astype(BF16)


def parts(x):
    high = x.astype(BF16)
    rest = x - high.astype(F32)
    middle = rest.astype(BF16)
    return high, middle, (rest - middle.astype(F32)).astype(BF16)


def iota(shape, dim):
    return lax.broadcasted_iota(jnp.int32, shape, dim)


def call(kernel, count, out_shape, scratch=(), name=None, copies=False, flops=0, transcendentals=0):
    vmem = pl.BlockSpec(memory_space=pltpu.VMEM)
    far = pl.BlockSpec(memory_space=pltpu.HBM)
    return pl.pallas_call(
        kernel,
        out_shape=out_shape,
        in_specs=[far if copies else vmem] * count,
        out_specs=jax.tree.map(lambda _: vmem, out_shape),
        scratch_shapes=scratch,
        compiler_params=pltpu.CompilerParams(vmem_limit_bytes=VMEM_LIMIT),
        cost_estimate=pl.CostEstimate(
            flops=int(flops),
            transcendentals=int(transcendentals),
            bytes_accessed=sum(x.size * x.dtype.itemsize for x in jax.tree.leaves(out_shape)),
        ),
        name=name,
    )


def slot_hidden_kernel(
    spread,
    counts_hbm,
    orbitals_hbm,
    occ_hbm,
    w1_hbm,
    bias_hbm,
    elements_hbm,
    readout_hbm,
    own_hbm,
    hidden_ref,
    owner_ref,
    elements_ref,
    w1_ref,
    bias_ref,
    readout_ref,
    own_ref,
    occupied_ref,
    counts_ref,
    orbitals_ref,
    occ_ref,
    sems,
):
    here, orbitals = occ_ref.shape
    updates, slots = orbitals_ref.shape
    pairs = (
        (counts_hbm, counts_ref),
        (occ_hbm, occ_ref),
        (w1_hbm, w1_ref),
        (bias_hbm, bias_ref),
        (orbitals_hbm, orbitals_ref),
        (elements_hbm, elements_ref),
        (readout_hbm, readout_ref),
        (own_hbm, own_ref),
    )
    copies = [pltpu.make_async_copy(a, b, sems.at[i]) for i, (a, b) in enumerate(pairs)]
    for copy in copies:
        copy.start()
    chip, core = lax.axis_index("chip"), lax.axis_index("core")
    place = chip * 2 + core
    copies[0].wait()
    counts = counts_ref[...].astype(F32)
    row, col = iota((here, here), 0), iota((here, here), 1)
    ends = jnp.sum(jnp.where(col <= row, counts, 0.0), axis=1, keepdims=True)
    starts = jnp.sum(jnp.where(col < row, counts, 0.0), axis=1, keepdims=True)
    positions = (place + spread * iota((1, slots), 1)).astype(F32)
    owner = jnp.where((starts <= positions) & (positions < ends), 1.0, 0.0).astype(BF16)
    owner_ref[...] = owner
    copies[1].wait()
    occupied = occ_ref[...].astype(F32).astype(BF16)
    occupied_ref[...] = occupied
    copies[2].wait()
    copies[3].wait()
    w1 = w1_ref[...]
    bias = bias_ref[...]
    hidden_ref[slots:, :] = jnp.tanh(dot(occupied, w1, ((1,), (0,))) + bias).astype(BF16)
    copies[4].wait()
    for start in range(0, slots, ROWS):
        stop = min(start + ROWS, slots)
        parent_occ = dot(occupied, owner[:, start:stop], ((0,), (0,)))
        columns = iota((orbitals, stop - start), 0)
        flipped = columns == orbitals_ref[0:1, start:stop]
        for u in range(1, updates):
            flipped = flipped | (columns == orbitals_ref[u : u + 1, start:stop])
        slot_occ = jnp.where(flipped, 1.0 - parent_occ, parent_occ).astype(BF16)
        pre = dot(slot_occ, w1, ((0,), (0,))) + bias
        hidden_ref[start:stop, :] = jnp.tanh(pre).astype(BF16)
    copies[5].wait()
    copies[6].wait()
    copies[7].wait()


def slot_energy_kernel(
    shifts, field_ref, hidden_ref, owner_ref, elements_ref, readout_ref, occupied_ref, *refs
):
    shard_refs, (energy_ref, second_ref, again_ref) = refs[: len(shifts)], refs[len(shifts) :]
    here, slots = owner_ref.shape
    chips = lax.axis_size("chip")
    chip, core = lax.axis_index("chip"), lax.axis_index("core")
    for (step, other), shard in zip(shifts, shard_refs):
        rows = shard.shape[0]
        source = lax.rem(chip + chips - step, chips) * 2 + (core ^ other)
        second_ref[pl.ds(pl.multiple_of(source * rows, rows), rows), :] = shard[...]
    mid = jnp.tanh(dot(second_ref[...], hidden_ref[...], ((0,), (1,))))
    readout = readout_ref[...].T
    logs_re = jnp.sum(mid * readout[:, 0:1], axis=0, keepdims=True)
    logs_im = jnp.sum(mid * readout[:, 1:2], axis=0, keepdims=True)
    owner = owner_ref[...]
    own = jnp.concatenate(parts(logs_re[:, slots:]) + parts(logs_im[:, slots:]), axis=0)
    parent = dot(own, owner, ((1,), (0,)))
    diff_re = logs_re[:, :slots] - (parent[0:1] + parent[1:2] + parent[2:3])
    diff_im = logs_im[:, :slots] - (parent[3:4] + parent[4:5] + parent[5:6])
    used = jnp.sum(owner.astype(F32), axis=0, keepdims=True) > 0.0
    weight = elements_ref[0:1, :] + field_ref[...] * elements_ref[1:2, :]
    scale = weight * jnp.exp(diff_re)
    contrib_re = jnp.where(used, scale * jnp.cos(diff_im), 0.0)
    contrib_im = jnp.where(used, scale * jnp.sin(diff_im), 0.0)
    contrib = jnp.concatenate(parts(contrib_re) + parts(contrib_im), axis=0)
    sums = dot(contrib, owner, ((1,), (1,)))
    partial_re = sums[0:1] + sums[1:2] + sums[2:3]
    partial_im = sums[3:4] + sums[4:5] + sums[5:6]
    partial = jnp.concatenate([partial_re, partial_im], axis=0)
    energy_ref[...] = spread_blocks(partial, lax.axis_index("samples"), energy_ref.shape[1] // here)
    again_ref[...] = occupied_ref[...]


def spread_blocks(partial, block, blocks):
    zero = jnp.zeros_like(partial)
    return jnp.concatenate([jnp.where(block == b, partial, zero) for b in range(blocks)], axis=1)


def pick_block(whole, block, width):
    blocks = whole.shape[1] // width
    picked = jnp.zeros((whole.shape[0], width), F32)
    for b in range(blocks):
        picked = jnp.where(block == b, whole[:, b * width : (b + 1) * width], picked)
    return picked


def overlap_kernel(
    entries, occ_ref, other_ref, w1_ref, bias_ref, second_ref, readout_ref, high_ref, low_ref, re_ref, im_ref, occ_all, hidden_ref
):
    blocks, here, _ = occ_ref.shape
    block = lax.axis_index("samples")
    odd = lax.axis_index("core") == 1
    for step, entry in enumerate(entries):
        picked = jnp.where(odd, other_ref[step], occ_ref[step])
        occ_all[pl.ds(pl.multiple_of((block ^ entry) * here, here), here), :] = picked
    w1 = w1_ref[...]
    bias = bias_ref[...]
    for start in range(0, blocks * here, ROWS):
        pre = dot(occ_all[start : start + ROWS, :], w1, ((1,), (0,))) + bias
        hidden_ref[start : start + ROWS, :] = jnp.tanh(pre).astype(BF16)
    hidden = hidden_ref[...]
    overlap = dot(hidden, hidden, ((1,), (1,)))
    high = overlap.astype(BF16)
    high_ref[...] = high
    low_ref[...] = (overlap - high.astype(F32)).astype(BF16)
    mid = jnp.tanh(dot(second_ref[...], hidden, ((0,), (1,))))
    slope = 1.0 - mid * mid
    readout = readout_ref[...].T
    re_ref[...] = slope * readout[:, 0:1]
    im_ref[...] = slope * readout[:, 1:2]


def solve(energy, gram):
    total = energy.shape[1]
    centered = energy - jnp.mean(energy, axis=1, keepdims=True)
    res_c = jnp.concatenate([centered[1:2], -centered[0:1]], axis=0) / total
    res_y = gram(res_c)
    dir_c, dir_y = res_c, res_y
    norm_now = full_sum(res_c * res_y)
    change = jnp.zeros_like(res_y)
    for turn in range(ITERS):
        img_c = dir_y / total + DIAG_SHIFT * dir_c
        alpha = norm_now / full_sum(img_c * dir_y)
        change = change + alpha * dir_y
        if turn + 1 < ITERS:
            img_y = gram(dir_y) / total + DIAG_SHIFT * dir_y
            res_c = res_c - alpha * img_c
            res_y = res_y - alpha * img_y
            norm_next = full_sum(res_c * res_y)
            beta = norm_next / norm_now
            dir_c = res_c + beta * dir_c
            dir_y = res_y + beta * dir_y
            norm_now = norm_next
    return change


def full_sum(x):
    return jnp.sum(jnp.sum(x, axis=1, keepdims=True), axis=0, keepdims=True)


def project(lifted, slope_re, slope_im):
    raw = jnp.concatenate(
        [jnp.sum(lifted * slope_re, axis=0, keepdims=True), jnp.sum(lifted * slope_im, axis=0, keepdims=True)],
        axis=0,
    )
    return raw - jnp.mean(raw, axis=1, keepdims=True)


def solve_kernel(mine_ref, other_ref, high_ref, low_ref, re_ref, im_ref, local_ref, change_ref):
    width = local_ref.shape[1]
    block = lax.axis_index("samples")
    energy = jnp.where(lax.axis_index("core") == 1, mine_ref[...], other_ref[...])
    local_ref[...] = pick_block(energy, block, width)

    def gram(c):
        back = re_ref[...] * c[0:1] + im_ref[...] * c[1:2]
        high = back.astype(BF16)
        low = (back - high.astype(F32)).astype(BF16)
        lifted = dot(high, high_ref[...], ((1,), (0,)))
        lifted += dot(low, high_ref[...], ((1,), (0,)))
        lifted += dot(high, low_ref[...], ((1,), (0,)))
        return project(lifted, re_ref[...], im_ref[...])

    change_ref[...] = pick_block(solve(energy, gram), block, width)


def wide_solve(energy, occ_stack, entries, first_weight, bias_row, second, readout):
    block = lax.axis_index("samples")
    here = occ_stack.shape[1]
    where = sorted(range(len(entries)), key=lambda k: entries[k])
    order = jnp.take(jnp.array(where, jnp.int32), block ^ jnp.arange(len(entries), dtype=jnp.int32))
    occupied = jnp.take(occ_stack, order, axis=0).reshape(-1, occ_stack.shape[2])
    pre = dot(occupied, first_weight, ((1,), (0,))) + bias_row
    hidden = jnp.tanh(pre).astype(BF16)
    mid = jnp.tanh(dot(second, hidden, ((0,), (1,))))
    slope = 1.0 - mid * mid
    slope_re = slope * readout[0][:, None]
    slope_im = slope * readout[1][:, None]

    def gram(c):
        high, low = split(slope_re * c[0:1] + slope_im * c[1:2])
        high, low = split(dot(high, hidden, ((1,), (0,))) + dot(low, hidden, ((1,), (0,))))
        lifted = dot(high, hidden, ((1,), (1,))) + dot(low, hidden, ((1,), (1,)))
        return project(lifted, slope_re, slope_im)

    change = solve(energy, gram)
    return (
        lax.dynamic_slice_in_dim(energy, block * here, here, 1),
        lax.dynamic_slice_in_dim(change, block * here, here, 1),
    )


def shift(x, axis, step):
    size = lax.axis_size(axis)
    return lax.ppermute(x, axis, [(i, (i + step) % size) for i in range(size)])


def exchange(x, cores, partner):
    blocks, chips = lax.axis_size("samples"), lax.axis_size("chip")

    def rank(block, chip, core):
        return (block * chips + chip) * 2 + core

    pairs = []
    for block in range(blocks):
        for chip in range(chips):
            for core in range(2):
                target = partner(block, chip, core) if core in cores else (block, chip, core)
                pairs.append((rank(block, chip, core), rank(*target)))
    return lax.ppermute(x, ("samples", "chip", "core"), pairs)


def across_blocks(bit):
    return lambda block, chip, core: (block ^ bit, chip, core)


def across_chips(bit):
    return lambda block, chip, core: (block, chip ^ bit, core)


def across_cores(block, chip, core):
    return block, chip, core ^ 1


def powers(size):
    return [1 << k for k in reversed(range((size - 1).bit_length()))]


def body(
    occupations,
    connection_counts,
    connection_orbitals,
    connection_elements,
    laser_step,
    first_weight,
    first_bias,
    second_weight,
    readout,
):
    here, orbitals = occupations.shape
    slots = connection_orbitals.shape[1]
    wide, narrow = first_weight.shape[1], second_weight.shape[1]
    chips = lax.axis_size("chip")
    spread = chips * lax.axis_size("core")
    blocks = lax.axis_size("samples")
    total = here * blocks
    bias_row = first_bias[None, :]
    field = FIELD_SCALE * jnp.sin(FIELD_RATE * laser_step.astype(F32)[None, None])

    bits = powers(blocks)
    entries = [0]
    for bit in bits:
        entries = entries + [e ^ bit for e in entries]
    moved = exchange(occupations.astype(BF16)[None], (0,), across_blocks(bits[0]))

    shifts, shards = [], []
    for step in range(1, chips):
        shifts.append((step, 0))
        shards.append(shift(second_weight, "chip", step))
    shifts.append((0, 1))
    shards.append(shift(second_weight, "core", 1))

    hidden, owner, elements, w1, bias, readout_near, own_shard, occupied = call(
        functools.partial(slot_hidden_kernel, spread),
        8,
        (
            jax.ShapeDtypeStruct((slots + here, wide), BF16),
            jax.ShapeDtypeStruct((here, slots), BF16),
            jax.ShapeDtypeStruct(connection_elements.shape, F32),
            jax.ShapeDtypeStruct(first_weight.shape, BF16),
            jax.ShapeDtypeStruct(bias_row.shape, F32),
            jax.ShapeDtypeStruct(readout.shape, F32),
            jax.ShapeDtypeStruct(second_weight.shape, BF16),
            jax.ShapeDtypeStruct(occupations.shape, BF16),
        ),
        [
            pltpu.VMEM((1, here), jnp.int32),
            pltpu.VMEM(connection_orbitals.shape, jnp.int32),
            pltpu.VMEM(occupations.shape, jnp.int32),
            pltpu.SemaphoreType.DMA((8,)),
        ],
        name="slot_hidden",
        copies=True,
        flops=2 * (slots + here) * orbitals * wide,
        transcendentals=(slots + here) * wide,
    )(
        *(
            pltpu.with_memory_space_constraint(x, pltpu.HBM)
            for x in (
                connection_counts[None, :],
                connection_orbitals,
                occupations,
                first_weight,
                bias_row,
                connection_elements,
                readout,
                second_weight,
            )
        ),
    )
    relayed, occupied = lax.optimization_barrier((shards[: chips - 1], occupied))
    for step in range(1, chips):
        shifts.append((step, 1))
        shards.append(shift(relayed[step - 1], "core", 1))
    shifts.append((0, 0))
    stack = jnp.concatenate([occupied[None], moved], axis=0)
    moved = exchange(stack, (0,), across_blocks(bits[1]))

    energy, second, occupied = call(
        functools.partial(slot_energy_kernel, tuple(shifts)),
        6 + len(shifts),
        (
            jax.ShapeDtypeStruct((2, total), F32),
            jax.ShapeDtypeStruct((wide, narrow), BF16),
            jax.ShapeDtypeStruct(occupations.shape, BF16),
        ),
        name="slot_energy",
        flops=2 * (slots + here) * wide * narrow,
        transcendentals=(slots + here) * narrow,
    )(field, hidden, owner, elements, readout_near, occupied, *shards, own_shard)
    mine = energy + exchange(energy, (0, 1), across_cores)
    moved, mine = lax.optimization_barrier((moved, mine))
    stack = jnp.concatenate([occupied[None], stack[1:], moved], axis=0)

    left = bits[2:]
    moved, age = None, 0
    for partner in [across_chips(bit) for bit in powers(chips)] + [across_blocks(bit) for bit in bits]:
        if moved is None and left:
            moved, age = exchange(stack, (0,), across_blocks(left.pop(0))), 0
        mine = mine + exchange(mine, (1,), partner)
        age += 1
        if moved is not None and age == 2:
            moved, mine = lax.optimization_barrier((moved, mine))
            stack, moved = jnp.concatenate([stack, moved], axis=0), None
    if moved is not None:
        stack = jnp.concatenate([stack, moved], axis=0)
    for bit in left:
        stack = jnp.concatenate([stack, exchange(stack, (0,), across_blocks(bit))], axis=0)
    other_stack = exchange(stack, (0, 1), across_cores)
    other = exchange(mine, (0, 1), across_cores)

    if total > wide:
        odd = lax.axis_index("core") == 1
        stack = jnp.where(odd, other_stack, stack)
        energy = jnp.where(odd, mine, other)
        return wide_solve(energy, stack, entries, first_weight, bias_row, second, readout)

    overlap = call(
        functools.partial(overlap_kernel, entries),
        6,
        (jax.ShapeDtypeStruct((total, total), BF16),) * 2 + (jax.ShapeDtypeStruct((narrow, total), F32),) * 2,
        [pltpu.VMEM((total, orbitals), BF16), pltpu.VMEM((total, wide), BF16)],
        name="overlap",
        flops=2 * total * wide * (orbitals + narrow + total),
        transcendentals=total * (wide + narrow),
    )(stack, other_stack, w1, bias, second, readout_near)
    return call(
        solve_kernel,
        6,
        (jax.ShapeDtypeStruct((2, here), F32),) * 2,
        name="solve",
        flops=ITERS * 6 * total * total * narrow,
    )(mine, other, *overlap)


def solution(mesh):
    blocks, spread = mesh.shape["samples"], mesh.shape["params"]
    fine = Mesh(mesh.devices.reshape(blocks, spread // 2, 2), ("samples", "chip", "core"))
    return jax.shard_map(
        body,
        mesh=fine,
        in_specs=(
            P("samples", None),
            P("samples"),
            P(None, ("samples", "chip", "core")),
            P(None, ("samples", "chip", "core")),
            P(),
            P(),
            P(),
            P(("chip", "core"), None),
            P(),
        ),
        out_specs=(P(None, "samples"), P(None, "samples")),
        check_vma=False,
    )
```

```python
import functools

import jax
import jax.numpy as jnp
from jax import lax
from jax.experimental import pallas as pl
from jax.experimental.pallas import tpu as pltpu
from jax.sharding import Mesh, PartitionSpec as P

ITERS = 2


FIELD_SCALE = 0.8
FIELD_RATE = 0.0123
DIAG_SHIFT = 0.01
F32 = jnp.float32
BF16 = jnp.bfloat16
ROWS = 256
COLLECT_WEIGHT = 1e10
VMEM_LIMIT = 48 * 1024 * 1024


def dot(a, b, dims):
    return lax.dot_general(a, b, (dims, ((), ())), preferred_element_type=F32)


def split(x):
    high = lax.reduce_precision(x, 8, 7)
    return high.astype(BF16), (x - high).astype(BF16)


def parts(x):
    high = x.astype(BF16)
    rest = x - high.astype(F32)
    middle = rest.astype(BF16)
    return high, middle, (rest - middle.astype(F32)).astype(BF16)


def iota(shape, dim):
    return lax.broadcasted_iota(jnp.int32, shape, dim)


def call(kernel, count, out_shape, scratch=(), name=None, copies=False, flops=0, transcendentals=0):
    vmem = pl.BlockSpec(memory_space=pltpu.VMEM)
    far = pl.BlockSpec(memory_space=pltpu.HBM)
    return pl.pallas_call(
        kernel,
        out_shape=out_shape,
        in_specs=[far if copies else vmem] * count,
        out_specs=jax.tree.map(lambda _: vmem, out_shape),
        scratch_shapes=scratch,
        compiler_params=pltpu.CompilerParams(vmem_limit_bytes=VMEM_LIMIT),
        cost_estimate=pl.CostEstimate(
            flops=int(flops),
            transcendentals=int(transcendentals),
            bytes_accessed=sum(x.size * x.dtype.itemsize for x in jax.tree.leaves(out_shape)),
        ),
        name=name,
    )


def slot_hidden_kernel(
    spread,
    counts_hbm,
    orbitals_hbm,
    occ_hbm,
    w1_hbm,
    bias_hbm,
    elements_hbm,
    readout_hbm,
    own_hbm,
    hidden_ref,
    owner_ref,
    elements_ref,
    w1_ref,
    bias_ref,
    readout_ref,
    own_ref,
    occupied_ref,
    counts_ref,
    orbitals_ref,
    occ_ref,
    sems,
):
    here, orbitals = occ_ref.shape
    updates, slots = orbitals_ref.shape
    pairs = (
        (counts_hbm, counts_ref),
        (occ_hbm, occ_ref),
        (w1_hbm, w1_ref),
        (bias_hbm, bias_ref),
        (orbitals_hbm, orbitals_ref),
        (elements_hbm, elements_ref),
        (readout_hbm, readout_ref),
        (own_hbm, own_ref),
    )
    copies = [pltpu.make_async_copy(a, b, sems.at[i]) for i, (a, b) in enumerate(pairs)]
    for copy in copies:
        copy.start()
    chip, core = lax.axis_index("chip"), lax.axis_index("core")
    place = chip * 2 + core
    copies[0].wait()
    counts = counts_ref[...].astype(F32)
    row, col = iota((here, here), 0), iota((here, here), 1)
    ends = jnp.sum(jnp.where(col <= row, counts, 0.0), axis=1, keepdims=True)
    starts = jnp.sum(jnp.where(col < row, counts, 0.0), axis=1, keepdims=True)
    positions = (place + spread * iota((1, slots), 1)).astype(F32)
    owner = jnp.where((starts <= positions) & (positions < ends), 1.0, 0.0).astype(BF16)
    owner_ref[...] = owner
    copies[1].wait()
    occupied = occ_ref[...].astype(F32).astype(BF16)
    occupied_ref[...] = occupied
    copies[2].wait()
    copies[3].wait()
    w1 = w1_ref[...]
    bias = bias_ref[...]
    hidden_ref[slots:, :] = jnp.tanh(dot(occupied, w1, ((1,), (0,))) + bias).astype(BF16)
    copies[4].wait()
    for start in range(0, slots, ROWS):
        stop = min(start + ROWS, slots)
        parent_occ = dot(occupied, owner[:, start:stop], ((0,), (0,)))
        columns = iota((orbitals, stop - start), 0)
        flipped = columns == orbitals_ref[0:1, start:stop]
        for u in range(1, updates):
            flipped = flipped | (columns == orbitals_ref[u : u + 1, start:stop])
        slot_occ = jnp.where(flipped, 1.0 - parent_occ, parent_occ).astype(BF16)
        pre = dot(slot_occ, w1, ((0,), (0,))) + bias
        hidden_ref[start:stop, :] = jnp.tanh(pre).astype(BF16)
    copies[5].wait()
    copies[6].wait()
    copies[7].wait()


def slot_energy_kernel(
    shifts, field_ref, hidden_ref, owner_ref, elements_ref, readout_ref, *refs
):
    shard_refs, (send_ref, second_ref) = refs[: len(shifts)], refs[len(shifts) :]
    here, slots = owner_ref.shape
    chips = lax.axis_size("chip")
    chip, core = lax.axis_index("chip"), lax.axis_index("core")
    for (step, other), shard in zip(shifts, shard_refs):
        rows = shard.shape[0]
        source = lax.rem(chip + chips - step, chips) * 2 + (core ^ other)
        second_ref[pl.ds(pl.multiple_of(source * rows, rows), rows), :] = shard[...]
    mid = jnp.tanh(dot(second_ref[...], hidden_ref[...], ((0,), (1,))))
    readout = readout_ref[...].T
    logs_re = jnp.sum(mid * readout[:, 0:1], axis=0, keepdims=True)
    logs_im = jnp.sum(mid * readout[:, 1:2], axis=0, keepdims=True)
    owner = owner_ref[...]
    own = jnp.concatenate(parts(logs_re[:, slots:]) + parts(logs_im[:, slots:]), axis=0)
    parent = dot(own, owner, ((1,), (0,)))
    diff_re = logs_re[:, :slots] - (parent[0:1] + parent[1:2] + parent[2:3])
    diff_im = logs_im[:, :slots] - (parent[3:4] + parent[4:5] + parent[5:6])
    used = jnp.sum(owner.astype(F32), axis=0, keepdims=True) > 0.0
    weight = elements_ref[0:1, :] + field_ref[...] * elements_ref[1:2, :]
    scale = weight * jnp.exp(diff_re)
    contrib_re = jnp.where(used, scale * jnp.cos(diff_im), 0.0)
    contrib_im = jnp.where(used, scale * jnp.sin(diff_im), 0.0)
    contrib = jnp.concatenate(parts(contrib_re) + parts(contrib_im), axis=0)
    sums = dot(contrib, owner, ((1,), (1,)))
    partial_re = sums[0:1] + sums[1:2] + sums[2:3]
    partial_im = sums[3:4] + sums[4:5] + sums[5:6]
    row = jnp.concatenate([partial_re, partial_im], axis=1)
    send_ref[...] = jnp.broadcast_to(row[None], send_ref.shape)


def collect_kernel(entries, chips, received_ref, energy_ref):
    here = received_ref.shape[2] // 2
    block = lax.axis_index("samples")
    out_re, out_im = [], []
    for entry in entries:
        first = (block ^ entry) * chips
        row = received_ref[first]
        for k in range(1, chips):
            row = row + received_ref[first + k]
        out_re.append(row[:, :here])
        out_im.append(row[:, here:])
    energy_ref[...] = jnp.concatenate(
        [jnp.concatenate(out_re, axis=1), jnp.concatenate(out_im, axis=1)], axis=0
    )


def sample_values(occupied, w1_ref, bias_ref, second_ref, readout_ref):
    hidden = jnp.tanh(dot(occupied, w1_ref[...], ((1,), (0,))) + bias_ref[...]).astype(BF16)
    mid = jnp.tanh(dot(second_ref[...], hidden, ((0,), (1,))))
    slope = 1.0 - mid * mid
    readout = readout_ref[...].T
    return hidden, slope * readout[:, 0:1], slope * readout[:, 1:2]


def near_half_kernel(
    mine_ref,
    moved_ref,
    w1_ref,
    bias_ref,
    second_ref,
    readout_ref,
    hidden_ref,
    overlap_ref,
    re_ref,
    im_ref,
    both_ref,
):
    blocks, here, orbitals = both_ref.shape
    both_ref[: blocks // 2] = mine_ref[...]
    both_ref[blocks // 2 :] = moved_ref[...]
    occupied = both_ref[...].reshape(blocks * here, orbitals)
    hidden, re_ref[...], im_ref[...] = sample_values(occupied, w1_ref, bias_ref, second_ref, readout_ref)
    hidden_ref[...] = hidden
    overlap_ref[...] = dot(hidden, hidden, ((1,), (1,)))


def far_half_kernel(
    half_ref,
    w1_ref,
    bias_ref,
    second_ref,
    readout_ref,
    hidden_ref,
    overlap_ref,
    near_re_ref,
    near_im_ref,
    high_ref,
    low_ref,
    re_ref,
    im_ref,
):
    blocks, here, orbitals = half_ref.shape
    size = blocks * here
    occupied = half_ref[...].reshape(size, orbitals)
    hidden, re, im = sample_values(occupied, w1_ref, bias_ref, second_ref, readout_ref)
    re_ref[:, :size] = near_re_ref[...]
    im_ref[:, :size] = near_im_ref[...]
    re_ref[:, size:] = re
    im_ref[:, size:] = im
    near = hidden_ref[...]

    def put(row, col, overlap):
        high = overlap.astype(BF16)
        high_ref[row * size : (row + 1) * size, col * size : (col + 1) * size] = high
        low = (overlap - high.astype(F32)).astype(BF16)
        low_ref[row * size : (row + 1) * size, col * size : (col + 1) * size] = low

    put(0, 0, overlap_ref[...])
    put(0, 1, dot(near, hidden, ((1,), (1,))))
    put(1, 0, dot(hidden, near, ((1,), (1,))))
    put(1, 1, dot(hidden, hidden, ((1,), (1,))))


def solve(energy, gram):
    total = energy.shape[1]
    centered = energy - jnp.mean(energy, axis=1, keepdims=True)
    res_c = jnp.concatenate([centered[1:2], -centered[0:1]], axis=0) / total
    res_y = gram(res_c)
    dir_c, dir_y = res_c, res_y
    norm_now = full_sum(res_c * res_y)
    change = jnp.zeros_like(res_y)
    for turn in range(ITERS):
        img_c = dir_y / total + DIAG_SHIFT * dir_c
        alpha = norm_now / full_sum(img_c * dir_y)
        change = change + alpha * dir_y
        if turn + 1 < ITERS:
            img_y = gram(dir_y) / total + DIAG_SHIFT * dir_y
            res_c = res_c - alpha * img_c
            res_y = res_y - alpha * img_y
            norm_next = full_sum(res_c * res_y)
            beta = norm_next / norm_now
            dir_c = res_c + beta * dir_c
            dir_y = res_y + beta * dir_y
            norm_now = norm_next
    return change


def full_sum(x):
    return jnp.sum(jnp.sum(x, axis=1, keepdims=True), axis=0, keepdims=True)


def project(lifted, slope_re, slope_im):
    raw = jnp.concatenate(
        [jnp.sum(lifted * slope_re, axis=0, keepdims=True), jnp.sum(lifted * slope_im, axis=0, keepdims=True)],
        axis=0,
    )
    return raw - jnp.mean(raw, axis=1, keepdims=True)


def solve_kernel(mine_ref, other_ref, high_ref, low_ref, re_ref, im_ref, local_ref, change_ref):
    width = local_ref.shape[1]
    energy = mine_ref[...] + other_ref[...]
    local_ref[...] = energy[:, :width]

    def gram(c):
        back = re_ref[...] * c[0:1] + im_ref[...] * c[1:2]
        high = back.astype(BF16)
        low = (back - high.astype(F32)).astype(BF16)
        lifted = dot(high, high_ref[...], ((1,), (0,)))
        lifted += dot(low, high_ref[...], ((1,), (0,)))
        lifted += dot(high, low_ref[...], ((1,), (0,)))
        return project(lifted, re_ref[...], im_ref[...])

    change_ref[...] = solve(energy, gram)[:, :width]


def wide_solve(energy, occ_stack, first_weight, bias_row, second, readout):
    here = occ_stack.shape[1]
    occupied = occ_stack.reshape(-1, occ_stack.shape[2])
    pre = dot(occupied, first_weight, ((1,), (0,))) + bias_row
    hidden = jnp.tanh(pre).astype(BF16)
    mid = jnp.tanh(dot(second, hidden, ((0,), (1,))))
    slope = 1.0 - mid * mid
    slope_re = slope * readout[0][:, None]
    slope_im = slope * readout[1][:, None]

    def gram(c):
        high, low = split(slope_re * c[0:1] + slope_im * c[1:2])
        high, low = split(dot(high, hidden, ((1,), (0,))) + dot(low, hidden, ((1,), (0,))))
        lifted = dot(high, hidden, ((1,), (1,))) + dot(low, hidden, ((1,), (1,)))
        return project(lifted, slope_re, slope_im)

    return energy[:, :here], solve(energy, gram)[:, :here]


def swap(x, axis, bit):
    return lax.ppermute(x, axis, [(i, i ^ bit) for i in range(lax.axis_size(axis))])


def shift(x, axis, step):
    size = lax.axis_size(axis)
    return lax.ppermute(x, axis, [(i, (i + step) % size) for i in range(size)])


def powers(size):
    return [1 << k for k in reversed(range((size - 1).bit_length()))]


def body(
    occupations,
    connection_counts,
    connection_orbitals,
    connection_elements,
    laser_step,
    first_weight,
    first_bias,
    second_weight,
    readout,
):
    here, orbitals = occupations.shape
    slots = connection_orbitals.shape[1]
    wide, narrow = first_weight.shape[1], second_weight.shape[1]
    chips = lax.axis_size("chip")
    spread = chips * lax.axis_size("core")
    blocks = lax.axis_size("samples")
    total = here * blocks
    bias_row = first_bias[None, :]
    field = FIELD_SCALE * jnp.sin(FIELD_RATE * laser_step.astype(F32)[None, None])

    bits = powers(blocks)
    entries = [0]
    for bit in bits:
        entries = entries + [e ^ bit for e in entries]
    moved = swap(occupations.astype(BF16)[None], "samples", bits[0])

    shifts, shards = [], []
    for step in range(1, chips):
        shifts.append((step, 0))
        shards.append(shift(second_weight, "chip", step))
    shifts.append((0, 1))
    shards.append(shift(second_weight, "core", 1))

    hidden, owner, elements, w1, bias, readout_near, own_shard, occupied = call(
        functools.partial(slot_hidden_kernel, spread),
        8,
        (
            jax.ShapeDtypeStruct((slots + here, wide), BF16),
            jax.ShapeDtypeStruct((here, slots), BF16),
            jax.ShapeDtypeStruct(connection_elements.shape, F32),
            jax.ShapeDtypeStruct(first_weight.shape, BF16),
            jax.ShapeDtypeStruct(bias_row.shape, F32),
            jax.ShapeDtypeStruct(readout.shape, F32),
            jax.ShapeDtypeStruct(second_weight.shape, BF16),
            jax.ShapeDtypeStruct(occupations.shape, BF16),
        ),
        [
            pltpu.VMEM((1, here), jnp.int32),
            pltpu.VMEM(connection_orbitals.shape, jnp.int32),
            pltpu.VMEM(occupations.shape, jnp.int32),
            pltpu.SemaphoreType.DMA((8,)),
        ],
        name="slot_hidden",
        copies=True,
        flops=2 * (slots + here) * orbitals * wide,
        transcendentals=(slots + here) * wide,
    )(
        *(
            pltpu.with_memory_space_constraint(x, pltpu.HBM)
            for x in (
                connection_counts[None, :],
                connection_orbitals,
                occupations,
                first_weight,
                bias_row,
                connection_elements,
                readout,
                second_weight,
            )
        ),
    )
    relayed, occupied = lax.optimization_barrier((shards[: chips - 1], occupied))
    for step in range(1, chips):
        shifts.append((step, 1))
        shards.append(shift(relayed[step - 1], "core", 1))
    shifts.append((0, 0))
    stack = jnp.concatenate([occupied[None], moved], axis=0)
    moved = swap(stack, "samples", bits[1])

    send, second = call(
        functools.partial(slot_energy_kernel, tuple(shifts)),
        5 + len(shifts),
        (
            jax.ShapeDtypeStruct((blocks * chips, 1, 2 * here), F32),
            jax.ShapeDtypeStruct((wide, narrow), BF16),
        ),
        name="slot_energy",
        flops=2 * (slots + here) * wide * narrow,
        transcendentals=(slots + here) * narrow,
    )(field, hidden, owner, elements, readout_near, *shards, own_shard)
    received = lax.all_to_all(send, ("samples", "chip"), 0, 0, tiled=True)
    mine = call(
        functools.partial(collect_kernel, entries, chips),
        1,
        jax.ShapeDtypeStruct((2, total), F32),
        name="collect",
        flops=COLLECT_WEIGHT,
    )(received)
    other = swap(mine, "core", 1)

    for bit in bits[2:-1]:
        stack = jnp.concatenate([stack, moved], axis=0)
        moved = swap(stack, "samples", bit)
    if total > wide:
        stack = jnp.concatenate([stack, moved], axis=0)
        stack = jnp.concatenate([stack, swap(stack, "samples", bits[-1])], axis=0)
        return wide_solve(mine + other, stack, first_weight, bias_row, second, readout)

    half = total // 2
    weights = (w1, bias, second, readout_near)
    near_hidden, near_overlap, near_re, near_im, both = call(
        near_half_kernel,
        6,
        (
            jax.ShapeDtypeStruct((half, wide), BF16),
            jax.ShapeDtypeStruct((half, half), F32),
            jax.ShapeDtypeStruct((narrow, half), F32),
            jax.ShapeDtypeStruct((narrow, half), F32),
            jax.ShapeDtypeStruct((blocks // 2, here, orbitals), BF16),
        ),
        name="near_half",
        flops=2 * half * wide * (orbitals + narrow + half),
        transcendentals=half * (wide + narrow),
    )(stack, moved, *weights)
    overlap = call(
        far_half_kernel,
        9,
        (jax.ShapeDtypeStruct((total, total), BF16),) * 2 + (jax.ShapeDtypeStruct((narrow, total), F32),) * 2,
        name="far_half",
        flops=2 * half * wide * (orbitals + narrow + 3 * half),
        transcendentals=half * (wide + narrow),
    )(swap(both, "samples", bits[-1]), *weights, near_hidden, near_overlap, near_re, near_im)
    return call(
        solve_kernel,
        6,
        (jax.ShapeDtypeStruct((2, here), F32),) * 2,
        name="solve",
        flops=ITERS * 6 * total * total * narrow,
    )(mine, other, *overlap)


def solution(mesh):
    blocks, spread = mesh.shape["samples"], mesh.shape["params"]
    fine = Mesh(mesh.devices.reshape(blocks, spread // 2, 2), ("samples", "chip", "core"))
    return jax.shard_map(
        body,
        mesh=fine,
        in_specs=(
            P("samples", None),
            P("samples"),
            P(None, ("samples", "chip", "core")),
            P(None, ("samples", "chip", "core")),
            P(),
            P(),
            P(),
            P(("chip", "core"), None),
            P(),
        ),
        out_specs=(P(None, "samples"), P(None, "samples")),
        check_vma=False,
    )
```

```python
import functools

import jax
import jax.numpy as jnp
from jax import lax
from jax.experimental import pallas as pl
from jax.experimental.pallas import tpu as pltpu
from jax.sharding import Mesh, PartitionSpec as P

ITERS = 2


FIELD_SCALE = 0.8
FIELD_RATE = 0.0123
DIAG_SHIFT = 0.01
F32 = jnp.float32
BF16 = jnp.bfloat16
ROWS = 256
COLLECT_WEIGHT = 1e10
VMEM_LIMIT = 48 * 1024 * 1024


def dot(a, b, dims):
    return lax.dot_general(a, b, (dims, ((), ())), preferred_element_type=F32)


def split(x):
    high = lax.reduce_precision(x, 8, 7)
    return high.astype(BF16), (x - high).astype(BF16)


def parts(x):
    high = x.astype(BF16)
    rest = x - high.astype(F32)
    middle = rest.astype(BF16)
    return high, middle, (rest - middle.astype(F32)).astype(BF16)


def iota(shape, dim):
    return lax.broadcasted_iota(jnp.int32, shape, dim)


def call(kernel, count, out_shape, scratch=(), name=None, copies=False, flops=0, transcendentals=0):
    vmem = pl.BlockSpec(memory_space=pltpu.VMEM)
    far = pl.BlockSpec(memory_space=pltpu.HBM)
    return pl.pallas_call(
        kernel,
        out_shape=out_shape,
        in_specs=[far if copies else vmem] * count,
        out_specs=jax.tree.map(lambda _: vmem, out_shape),
        scratch_shapes=scratch,
        compiler_params=pltpu.CompilerParams(vmem_limit_bytes=VMEM_LIMIT),
        cost_estimate=pl.CostEstimate(
            flops=int(flops),
            transcendentals=int(transcendentals),
            bytes_accessed=sum(x.size * x.dtype.itemsize for x in jax.tree.leaves(out_shape)),
        ),
        name=name,
    )


def slot_hidden_kernel(
    spread,
    counts_hbm,
    orbitals_hbm,
    occ_hbm,
    w1_hbm,
    bias_hbm,
    elements_hbm,
    readout_hbm,
    own_hbm,
    hidden_ref,
    owner_ref,
    elements_ref,
    w1_ref,
    bias_ref,
    readout_ref,
    own_ref,
    occupied_ref,
    counts_ref,
    orbitals_ref,
    occ_ref,
    sems,
):
    here, orbitals = occ_ref.shape
    updates, slots = orbitals_ref.shape
    pairs = (
        (counts_hbm, counts_ref),
        (occ_hbm, occ_ref),
        (w1_hbm, w1_ref),
        (bias_hbm, bias_ref),
        (orbitals_hbm, orbitals_ref),
        (elements_hbm, elements_ref),
        (readout_hbm, readout_ref),
        (own_hbm, own_ref),
    )
    copies = [pltpu.make_async_copy(a, b, sems.at[i]) for i, (a, b) in enumerate(pairs)]
    for copy in copies:
        copy.start()
    chip, core = lax.axis_index("chip"), lax.axis_index("core")
    place = chip * 2 + core
    copies[0].wait()
    counts = counts_ref[...].astype(F32)
    row, col = iota((here, here), 0), iota((here, here), 1)
    ends = jnp.sum(jnp.where(col <= row, counts, 0.0), axis=1, keepdims=True)
    starts = jnp.sum(jnp.where(col < row, counts, 0.0), axis=1, keepdims=True)
    positions = (place + spread * iota((1, slots), 1)).astype(F32)
    owner = jnp.where((starts <= positions) & (positions < ends), 1.0, 0.0).astype(BF16)
    owner_ref[...] = owner
    copies[1].wait()
    occupied = occ_ref[...].astype(F32).astype(BF16)
    occupied_ref[...] = occupied
    copies[2].wait()
    copies[3].wait()
    w1 = w1_ref[...]
    bias = bias_ref[...]
    hidden_ref[slots:, :] = jnp.tanh(dot(occupied, w1, ((1,), (0,))) + bias).astype(BF16)
    copies[4].wait()
    for start in range(0, slots, ROWS):
        stop = min(start + ROWS, slots)
        parent_occ = dot(occupied, owner[:, start:stop], ((0,), (0,)))
        columns = iota((orbitals, stop - start), 0)
        flipped = columns == orbitals_ref[0:1, start:stop]
        for u in range(1, updates):
            flipped = flipped | (columns == orbitals_ref[u : u + 1, start:stop])
        slot_occ = jnp.where(flipped, 1.0 - parent_occ, parent_occ).astype(BF16)
        pre = dot(slot_occ, w1, ((0,), (0,))) + bias
        hidden_ref[start:stop, :] = jnp.tanh(pre).astype(BF16)
    copies[5].wait()
    copies[6].wait()
    copies[7].wait()


def slot_energy_kernel(
    shifts, field_ref, hidden_ref, owner_ref, elements_ref, readout_ref, *refs
):
    shard_refs, (send_ref, second_ref) = refs[: len(shifts)], refs[len(shifts) :]
    here, slots = owner_ref.shape
    chips = lax.axis_size("chip")
    chip, core = lax.axis_index("chip"), lax.axis_index("core")
    for (step, other), shard in zip(shifts, shard_refs):
        rows = shard.shape[0]
        source = lax.rem(chip + chips - step, chips) * 2 + (core ^ other)
        second_ref[pl.ds(pl.multiple_of(source * rows, rows), rows), :] = shard[...]
    mid = jnp.tanh(dot(second_ref[...], hidden_ref[...], ((0,), (1,))))
    readout = readout_ref[...].T
    logs_re = jnp.sum(mid * readout[:, 0:1], axis=0, keepdims=True)
    logs_im = jnp.sum(mid * readout[:, 1:2], axis=0, keepdims=True)
    owner = owner_ref[...]
    own = jnp.concatenate(parts(logs_re[:, slots:]) + parts(logs_im[:, slots:]), axis=0)
    parent = dot(own, owner, ((1,), (0,)))
    diff_re = logs_re[:, :slots] - (parent[0:1] + parent[1:2] + parent[2:3])
    diff_im = logs_im[:, :slots] - (parent[3:4] + parent[4:5] + parent[5:6])
    used = jnp.sum(owner.astype(F32), axis=0, keepdims=True) > 0.0
    weight = elements_ref[0:1, :] + field_ref[...] * elements_ref[1:2, :]
    scale = weight * jnp.exp(diff_re)
    contrib_re = jnp.where(used, scale * jnp.cos(diff_im), 0.0)
    contrib_im = jnp.where(used, scale * jnp.sin(diff_im), 0.0)
    contrib = jnp.concatenate(parts(contrib_re) + parts(contrib_im), axis=0)
    sums = dot(contrib, owner, ((1,), (1,)))
    partial_re = sums[0:1] + sums[1:2] + sums[2:3]
    partial_im = sums[3:4] + sums[4:5] + sums[5:6]
    row = jnp.concatenate([partial_re, partial_im], axis=1)
    send_ref[...] = jnp.broadcast_to(row[None], send_ref.shape)


def collect_kernel(entries, chips, received_ref, energy_ref):
    here = received_ref.shape[2] // 2
    block = lax.axis_index("samples")
    out_re, out_im = [], []
    for entry in entries:
        first = (block ^ entry) * chips
        row = received_ref[first]
        for k in range(1, chips):
            row = row + received_ref[first + k]
        out_re.append(row[:, :here])
        out_im.append(row[:, here:])
    energy_ref[...] = jnp.concatenate(
        [jnp.concatenate(out_re, axis=1), jnp.concatenate(out_im, axis=1)], axis=0
    )


def sample_values(packed_ref, w1_ref, bias_ref, second_ref, readout_ref, size):
    hidden = jnp.tanh(sample_pre(packed_ref, w1_ref, bias_ref, size)).astype(BF16)
    mid = jnp.tanh(dot(second_ref[...], hidden, ((0,), (1,))))
    slope = 1.0 - mid * mid
    readout = readout_ref[...].T
    return hidden, slope * readout[:, 0:1], slope * readout[:, 1:2]


def pack_kernel(mine_ref, moved_ref, after_ref, packed_ref):
    del after_ref
    blocks, here, orbitals = mine_ref.shape
    full = packed_ref.shape[1]
    pieces = [mine_ref[k] for k in range(blocks)] + [moved_ref[k] for k in range(blocks)]
    rest = orbitals - full
    for k, piece in enumerate(pieces):
        packed_ref[k * here : (k + 1) * here, :] = piece[:, :full]
    rests = [piece[:, full:].astype(F32) for piece in pieces]
    rests.append(jnp.zeros((here, full - rest * len(pieces)), F32))
    packed_ref[len(pieces) * here :, :] = jnp.concatenate(rests, axis=1).astype(BF16)


def sample_pre(packed_ref, w1_ref, bias_ref, size):
    full = packed_ref.shape[1]
    here = packed_ref.shape[0] - size
    rest = w1_ref.shape[0] - full
    tail = packed_ref[size:, :].astype(F32)
    rests = [tail[:, k * rest : (k + 1) * rest] for k in range(size // here)]
    tail = jnp.concatenate(rests, axis=0).astype(BF16)
    pre = dot(packed_ref[:size, :], w1_ref[:full, :], ((1,), (0,)))
    return pre + dot(tail, w1_ref[full:, :], ((1,), (0,))) + bias_ref[...]


def near_half_kernel(packed_ref, w1_ref, bias_ref, second_ref, readout_ref, hidden_ref, overlap_ref, re_ref, im_ref):
    size = hidden_ref.shape[0]
    hidden, re_ref[...], im_ref[...] = sample_values(packed_ref, w1_ref, bias_ref, second_ref, readout_ref, size)
    hidden_ref[...] = hidden
    overlap_ref[...] = dot(hidden, hidden, ((1,), (1,)))


def far_half_kernel(
    packed_ref,
    w1_ref,
    bias_ref,
    second_ref,
    readout_ref,
    hidden_ref,
    overlap_ref,
    near_re_ref,
    near_im_ref,
    high_ref,
    low_ref,
    re_ref,
    im_ref,
):
    size = hidden_ref.shape[0]
    hidden, re, im = sample_values(packed_ref, w1_ref, bias_ref, second_ref, readout_ref, size)
    re_ref[:, :size] = near_re_ref[...]
    im_ref[:, :size] = near_im_ref[...]
    re_ref[:, size:] = re
    im_ref[:, size:] = im
    near = hidden_ref[...]

    def put(row, col, overlap):
        high = overlap.astype(BF16)
        high_ref[row * size : (row + 1) * size, col * size : (col + 1) * size] = high
        low = (overlap - high.astype(F32)).astype(BF16)
        low_ref[row * size : (row + 1) * size, col * size : (col + 1) * size] = low

    put(0, 0, overlap_ref[...])
    put(0, 1, dot(near, hidden, ((1,), (1,))))
    put(1, 0, dot(hidden, near, ((1,), (1,))))
    put(1, 1, dot(hidden, hidden, ((1,), (1,))))


def solve(energy, gram):
    total = energy.shape[1]
    centered = energy - jnp.mean(energy, axis=1, keepdims=True)
    res_c = jnp.concatenate([centered[1:2], -centered[0:1]], axis=0) / total
    res_y = gram(res_c)
    dir_c, dir_y = res_c, res_y
    norm_now = full_sum(res_c * res_y)
    change = jnp.zeros_like(res_y)
    for turn in range(ITERS):
        img_c = dir_y / total + DIAG_SHIFT * dir_c
        alpha = norm_now / full_sum(img_c * dir_y)
        change = change + alpha * dir_y
        if turn + 1 < ITERS:
            img_y = gram(dir_y) / total + DIAG_SHIFT * dir_y
            res_c = res_c - alpha * img_c
            res_y = res_y - alpha * img_y
            norm_next = full_sum(res_c * res_y)
            beta = norm_next / norm_now
            dir_c = res_c + beta * dir_c
            dir_y = res_y + beta * dir_y
            norm_now = norm_next
    return change


def full_sum(x):
    return jnp.sum(jnp.sum(x, axis=1, keepdims=True), axis=0, keepdims=True)


def project(lifted, slope_re, slope_im):
    raw = jnp.concatenate(
        [jnp.sum(lifted * slope_re, axis=0, keepdims=True), jnp.sum(lifted * slope_im, axis=0, keepdims=True)],
        axis=0,
    )
    return raw - jnp.mean(raw, axis=1, keepdims=True)


def solve_kernel(mine_ref, other_ref, high_ref, low_ref, re_ref, im_ref, local_ref, change_ref):
    width = local_ref.shape[1]
    energy = mine_ref[...] + other_ref[...]
    local_ref[...] = energy[:, :width]

    def gram(c):
        back = re_ref[...] * c[0:1] + im_ref[...] * c[1:2]
        high = back.astype(BF16)
        low = (back - high.astype(F32)).astype(BF16)
        lifted = dot(high, high_ref[...], ((1,), (0,)))
        lifted += dot(low, high_ref[...], ((1,), (0,)))
        lifted += dot(high, low_ref[...], ((1,), (0,)))
        return project(lifted, re_ref[...], im_ref[...])

    change_ref[...] = solve(energy, gram)[:, :width]


def wide_solve(energy, occ_stack, first_weight, bias_row, second, readout):
    here = occ_stack.shape[1]
    occupied = occ_stack.reshape(-1, occ_stack.shape[2])
    pre = dot(occupied, first_weight, ((1,), (0,))) + bias_row
    hidden = jnp.tanh(pre).astype(BF16)
    mid = jnp.tanh(dot(second, hidden, ((0,), (1,))))
    slope = 1.0 - mid * mid
    slope_re = slope * readout[0][:, None]
    slope_im = slope * readout[1][:, None]

    def gram(c):
        high, low = split(slope_re * c[0:1] + slope_im * c[1:2])
        high, low = split(dot(high, hidden, ((1,), (0,))) + dot(low, hidden, ((1,), (0,))))
        lifted = dot(high, hidden, ((1,), (1,))) + dot(low, hidden, ((1,), (1,)))
        return project(lifted, slope_re, slope_im)

    return energy[:, :here], solve(energy, gram)[:, :here]


def swap(x, axis, bit):
    return lax.ppermute(x, axis, [(i, i ^ bit) for i in range(lax.axis_size(axis))])


def shift(x, axis, step):
    size = lax.axis_size(axis)
    return lax.ppermute(x, axis, [(i, (i + step) % size) for i in range(size)])


def powers(size):
    return [1 << k for k in reversed(range((size - 1).bit_length()))]


def body(
    occupations,
    connection_counts,
    connection_orbitals,
    connection_elements,
    laser_step,
    first_weight,
    first_bias,
    second_weight,
    readout,
):
    here, orbitals = occupations.shape
    slots = connection_orbitals.shape[1]
    wide, narrow = first_weight.shape[1], second_weight.shape[1]
    chips = lax.axis_size("chip")
    spread = chips * lax.axis_size("core")
    blocks = lax.axis_size("samples")
    total = here * blocks
    bias_row = first_bias[None, :]
    field = FIELD_SCALE * jnp.sin(FIELD_RATE * laser_step.astype(F32)[None, None])

    bits = powers(blocks)
    entries = [0]
    for bit in bits:
        entries = entries + [e ^ bit for e in entries]
    moved = swap(occupations.astype(BF16)[None], "samples", bits[0])

    shifts, shards = [], []
    for step in range(1, chips):
        shifts.append((step, 0))
        shards.append(shift(second_weight, "chip", step))
    shifts.append((0, 1))
    shards.append(shift(second_weight, "core", 1))

    hidden, owner, elements, w1, bias, readout_near, own_shard, occupied = call(
        functools.partial(slot_hidden_kernel, spread),
        8,
        (
            jax.ShapeDtypeStruct((slots + here, wide), BF16),
            jax.ShapeDtypeStruct((here, slots), BF16),
            jax.ShapeDtypeStruct(connection_elements.shape, F32),
            jax.ShapeDtypeStruct(first_weight.shape, BF16),
            jax.ShapeDtypeStruct(bias_row.shape, F32),
            jax.ShapeDtypeStruct(readout.shape, F32),
            jax.ShapeDtypeStruct(second_weight.shape, BF16),
            jax.ShapeDtypeStruct(occupations.shape, BF16),
        ),
        [
            pltpu.VMEM((1, here), jnp.int32),
            pltpu.VMEM(connection_orbitals.shape, jnp.int32),
            pltpu.VMEM(occupations.shape, jnp.int32),
            pltpu.SemaphoreType.DMA((8,)),
        ],
        name="slot_hidden",
        copies=True,
        flops=2 * (slots + here) * orbitals * wide,
        transcendentals=(slots + here) * wide,
    )(
        *(
            pltpu.with_memory_space_constraint(x, pltpu.HBM)
            for x in (
                connection_counts[None, :],
                connection_orbitals,
                occupations,
                first_weight,
                bias_row,
                connection_elements,
                readout,
                second_weight,
            )
        ),
    )
    relayed, occupied = lax.optimization_barrier((shards[: chips - 1], occupied))
    for step in range(1, chips):
        shifts.append((step, 1))
        shards.append(shift(relayed[step - 1], "core", 1))
    shifts.append((0, 0))
    stack = jnp.concatenate([occupied[None], moved], axis=0)
    moved = swap(stack, "samples", bits[1])

    send, second = call(
        functools.partial(slot_energy_kernel, tuple(shifts)),
        5 + len(shifts),
        (
            jax.ShapeDtypeStruct((blocks * chips, 1, 2 * here), F32),
            jax.ShapeDtypeStruct((wide, narrow), BF16),
        ),
        name="slot_energy",
        flops=2 * (slots + here) * wide * narrow,
        transcendentals=(slots + here) * narrow,
    )(field, hidden, owner, elements, readout_near, *shards, own_shard)
    received = lax.all_to_all(send, ("samples", "chip"), 0, 0, tiled=True)
    mine = call(
        functools.partial(collect_kernel, entries, chips),
        1,
        jax.ShapeDtypeStruct((2, total), F32),
        name="collect",
        flops=COLLECT_WEIGHT,
    )(received)
    other = swap(mine, "core", 1)

    for bit in bits[2:-1]:
        stack = jnp.concatenate([stack, moved], axis=0)
        moved = swap(stack, "samples", bit)
    if total > wide:
        stack = jnp.concatenate([stack, moved], axis=0)
        stack = jnp.concatenate([stack, swap(stack, "samples", bits[-1])], axis=0)
        return wide_solve(mine + other, stack, first_weight, bias_row, second, readout)

    half = total // 2
    weights = (w1, bias, second, readout_near)
    full = orbitals // 128 * 128
    packed = call(
        pack_kernel,
        3,
        jax.ShapeDtypeStruct((half + here, full), BF16),
        name="pack",
    )(stack, moved, second)
    far_packed = swap(packed, "samples", bits[-1])
    near = call(
        near_half_kernel,
        5,
        (
            jax.ShapeDtypeStruct((half, wide), BF16),
            jax.ShapeDtypeStruct((half, half), F32),
            jax.ShapeDtypeStruct((narrow, half), F32),
            jax.ShapeDtypeStruct((narrow, half), F32),
        ),
        name="near_half",
        flops=2 * half * wide * (orbitals + narrow + half),
        transcendentals=half * (wide + narrow),
    )(packed, *weights)
    overlap = call(
        far_half_kernel,
        9,
        (jax.ShapeDtypeStruct((total, total), BF16),) * 2 + (jax.ShapeDtypeStruct((narrow, total), F32),) * 2,
        name="far_half",
        flops=2 * half * wide * (orbitals + narrow + 3 * half),
        transcendentals=half * (wide + narrow),
    )(far_packed, *weights, *near)
    return call(
        solve_kernel,
        6,
        (jax.ShapeDtypeStruct((2, here), F32),) * 2,
        name="solve",
        flops=ITERS * 6 * total * total * narrow,
    )(mine, other, *overlap)


def solution(mesh):
    blocks, spread = mesh.shape["samples"], mesh.shape["params"]
    fine = Mesh(mesh.devices.reshape(blocks, spread // 2, 2), ("samples", "chip", "core"))
    return jax.shard_map(
        body,
        mesh=fine,
        in_specs=(
            P("samples", None),
            P("samples"),
            P(None, ("samples", "chip", "core")),
            P(None, ("samples", "chip", "core")),
            P(),
            P(),
            P(),
            P(("chip", "core"), None),
            P(),
        ),
        out_specs=(P(None, "samples"), P(None, "samples")),
        check_vma=False,
    )
```

```python
import functools

import jax
import jax.numpy as jnp
from jax import lax
from jax.experimental import pallas as pl
from jax.experimental.pallas import tpu as pltpu
from jax.sharding import Mesh, PartitionSpec as P

ITERS = 2


FIELD_SCALE = 0.8
FIELD_RATE = 0.0123
DIAG_SHIFT = 0.01
F32 = jnp.float32
BF16 = jnp.bfloat16
ROWS = 256
COLLECT_WEIGHT = 1e10
VMEM_LIMIT = 48 * 1024 * 1024


def dot(a, b, dims):
    return lax.dot_general(a, b, (dims, ((), ())), preferred_element_type=F32)


def split(x):
    high = lax.reduce_precision(x, 8, 7)
    return high.astype(BF16), (x - high).astype(BF16)


def parts(x):
    high = x.astype(BF16)
    rest = x - high.astype(F32)
    middle = rest.astype(BF16)
    return high, middle, (rest - middle.astype(F32)).astype(BF16)


def iota(shape, dim):
    return lax.broadcasted_iota(jnp.int32, shape, dim)


def call(kernel, count, out_shape, scratch=(), name=None, copies=False, flops=0, transcendentals=0):
    vmem = pl.BlockSpec(memory_space=pltpu.VMEM)
    far = pl.BlockSpec(memory_space=pltpu.HBM)
    return pl.pallas_call(
        kernel,
        out_shape=out_shape,
        in_specs=[far if copies else vmem] * count,
        out_specs=jax.tree.map(lambda _: vmem, out_shape),
        scratch_shapes=scratch,
        compiler_params=pltpu.CompilerParams(vmem_limit_bytes=VMEM_LIMIT),
        cost_estimate=pl.CostEstimate(
            flops=int(flops),
            transcendentals=int(transcendentals),
            bytes_accessed=sum(x.size * x.dtype.itemsize for x in jax.tree.leaves(out_shape)),
        ),
        name=name,
    )


def slot_hidden_kernel(
    spread,
    counts_hbm,
    orbitals_hbm,
    occ_hbm,
    w1_hbm,
    bias_hbm,
    elements_hbm,
    readout_hbm,
    own_hbm,
    hidden_ref,
    owner_ref,
    elements_ref,
    w1_ref,
    bias_ref,
    readout_ref,
    own_ref,
    occupied_ref,
    counts_ref,
    orbitals_ref,
    occ_ref,
    sems,
):
    here, orbitals = occ_ref.shape
    updates, slots = orbitals_ref.shape
    pairs = (
        (counts_hbm, counts_ref),
        (occ_hbm, occ_ref),
        (w1_hbm, w1_ref),
        (bias_hbm, bias_ref),
        (orbitals_hbm, orbitals_ref),
        (elements_hbm, elements_ref),
        (readout_hbm, readout_ref),
        (own_hbm, own_ref),
    )
    copies = [pltpu.make_async_copy(a, b, sems.at[i]) for i, (a, b) in enumerate(pairs)]
    for copy in copies:
        copy.start()
    chip, core = lax.axis_index("chip"), lax.axis_index("core")
    place = chip * 2 + core
    copies[0].wait()
    counts = counts_ref[...].astype(F32)
    row, col = iota((here, here), 0), iota((here, here), 1)
    ends = jnp.sum(jnp.where(col <= row, counts, 0.0), axis=1, keepdims=True)
    starts = jnp.sum(jnp.where(col < row, counts, 0.0), axis=1, keepdims=True)
    positions = (place + spread * iota((1, slots), 1)).astype(F32)
    owner = jnp.where((starts <= positions) & (positions < ends), 1.0, 0.0).astype(BF16)
    owner_ref[...] = owner
    copies[1].wait()
    occupied = occ_ref[...].astype(F32).astype(BF16)
    occupied_ref[...] = occupied
    copies[2].wait()
    copies[3].wait()
    w1 = w1_ref[...]
    bias = bias_ref[...]
    hidden_ref[slots:, :] = jnp.tanh(dot(occupied, w1, ((1,), (0,))) + bias).astype(BF16)
    copies[4].wait()
    for start in range(0, slots, ROWS):
        stop = min(start + ROWS, slots)
        parent_occ = dot(occupied, owner[:, start:stop], ((0,), (0,)))
        columns = iota((orbitals, stop - start), 0)
        flipped = columns == orbitals_ref[0:1, start:stop]
        for u in range(1, updates):
            flipped = flipped | (columns == orbitals_ref[u : u + 1, start:stop])
        slot_occ = jnp.where(flipped, 1.0 - parent_occ, parent_occ).astype(BF16)
        pre = dot(slot_occ, w1, ((0,), (0,))) + bias
        hidden_ref[start:stop, :] = jnp.tanh(pre).astype(BF16)
    copies[5].wait()
    copies[6].wait()
    copies[7].wait()


def slot_energy_kernel(
    shifts, field_ref, hidden_ref, owner_ref, elements_ref, readout_ref, *refs
):
    shard_refs, (send_ref, second_ref) = refs[: len(shifts)], refs[len(shifts) :]
    here, slots = owner_ref.shape
    chips = lax.axis_size("chip")
    chip, core = lax.axis_index("chip"), lax.axis_index("core")
    for (step, other), shard in zip(shifts, shard_refs):
        rows = shard.shape[0]
        source = lax.rem(chip + chips - step, chips) * 2 + (core ^ other)
        second_ref[pl.ds(pl.multiple_of(source * rows, rows), rows), :] = shard[...]
    mid = jnp.tanh(dot(second_ref[...], hidden_ref[...], ((0,), (1,))))
    readout = readout_ref[...].T
    logs_re = jnp.sum(mid * readout[:, 0:1], axis=0, keepdims=True)
    logs_im = jnp.sum(mid * readout[:, 1:2], axis=0, keepdims=True)
    owner = owner_ref[...]
    own = jnp.concatenate(parts(logs_re[:, slots:]) + parts(logs_im[:, slots:]), axis=0)
    parent = dot(own, owner, ((1,), (0,)))
    diff_re = logs_re[:, :slots] - (parent[0:1] + parent[1:2] + parent[2:3])
    diff_im = logs_im[:, :slots] - (parent[3:4] + parent[4:5] + parent[5:6])
    used = jnp.sum(owner.astype(F32), axis=0, keepdims=True) > 0.0
    weight = elements_ref[0:1, :] + field_ref[...] * elements_ref[1:2, :]
    scale = weight * jnp.exp(diff_re)
    contrib_re = jnp.where(used, scale * jnp.cos(diff_im), 0.0)
    contrib_im = jnp.where(used, scale * jnp.sin(diff_im), 0.0)
    contrib = jnp.concatenate(parts(contrib_re) + parts(contrib_im), axis=0)
    sums = dot(contrib, owner, ((1,), (1,)))
    partial_re = sums[0:1] + sums[1:2] + sums[2:3]
    partial_im = sums[3:4] + sums[4:5] + sums[5:6]
    row = jnp.concatenate([partial_re, partial_im], axis=1)
    send_ref[...] = jnp.broadcast_to(row[None], send_ref.shape)


def collect_kernel(entries, chips, received_ref, after_ref, energy_ref):
    del after_ref
    here = received_ref.shape[2] // 2
    block = lax.axis_index("samples")
    out_re, out_im = [], []
    last = received_ref.shape[0] - 1
    for entry in entries:
        first = last - (block ^ entry) * chips
        row = received_ref[first]
        for k in range(1, chips):
            row = row + received_ref[first - k]
        out_re.append(row[:, :here])
        out_im.append(row[:, here:])
    energy_ref[...] = jnp.concatenate(
        [jnp.concatenate(out_re, axis=1), jnp.concatenate(out_im, axis=1)], axis=0
    )


def sample_values(packed_ref, w1_ref, bias_ref, second_ref, readout_ref, size):
    hidden = jnp.tanh(sample_pre(packed_ref, w1_ref, bias_ref, size)).astype(BF16)
    mid = jnp.tanh(dot(second_ref[...], hidden, ((0,), (1,))))
    slope = 1.0 - mid * mid
    readout = readout_ref[...].T
    return hidden, slope * readout[:, 0:1], slope * readout[:, 1:2]


def pack_kernel(*refs):
    pieces, packed_ref = [ref[...] for ref in refs[:-1]], refs[-1]
    here, orbitals = pieces[0].shape
    full = packed_ref.shape[1]
    rest = orbitals - full
    for k, piece in enumerate(pieces):
        packed_ref[k * here : (k + 1) * here, :] = piece[:, :full]
    rests = [piece[:, full:].astype(F32) for piece in pieces]
    rests.append(jnp.zeros((here, full - rest * len(pieces)), F32))
    packed_ref[len(pieces) * here :, :] = jnp.concatenate(rests, axis=1).astype(BF16)


def sample_pre(packed_ref, w1_ref, bias_ref, size):
    full = packed_ref.shape[1]
    here = packed_ref.shape[0] - size
    rest = w1_ref.shape[0] - full
    tail = packed_ref[size:, :].astype(F32)
    rests = [tail[:, k * rest : (k + 1) * rest] for k in range(size // here)]
    tail = jnp.concatenate(rests, axis=0).astype(BF16)
    pre = dot(packed_ref[:size, :], w1_ref[:full, :], ((1,), (0,)))
    return pre + dot(tail, w1_ref[full:, :], ((1,), (0,))) + bias_ref[...]


def near_half_kernel(packed_ref, w1_ref, bias_ref, second_ref, readout_ref, hidden_ref, overlap_ref, re_ref, im_ref):
    size = hidden_ref.shape[0]
    hidden, re_ref[...], im_ref[...] = sample_values(packed_ref, w1_ref, bias_ref, second_ref, readout_ref, size)
    hidden_ref[...] = hidden
    overlap_ref[...] = dot(hidden, hidden, ((1,), (1,)))


def far_half_kernel(
    packed_ref,
    w1_ref,
    bias_ref,
    second_ref,
    readout_ref,
    hidden_ref,
    overlap_ref,
    near_re_ref,
    near_im_ref,
    high_ref,
    low_ref,
    re_ref,
    im_ref,
):
    size = hidden_ref.shape[0]
    hidden, re, im = sample_values(packed_ref, w1_ref, bias_ref, second_ref, readout_ref, size)
    re_ref[:, :size] = near_re_ref[...]
    im_ref[:, :size] = near_im_ref[...]
    re_ref[:, size:] = re
    im_ref[:, size:] = im
    near = hidden_ref[...]

    def put(row, col, overlap):
        high = overlap.astype(BF16)
        high_ref[row * size : (row + 1) * size, col * size : (col + 1) * size] = high
        low = (overlap - high.astype(F32)).astype(BF16)
        low_ref[row * size : (row + 1) * size, col * size : (col + 1) * size] = low

    put(0, 0, overlap_ref[...])
    put(0, 1, dot(near, hidden, ((1,), (1,))))
    put(1, 0, dot(hidden, near, ((1,), (1,))))
    put(1, 1, dot(hidden, hidden, ((1,), (1,))))


def solve(energy, gram):
    total = energy.shape[1]
    centered = energy - jnp.mean(energy, axis=1, keepdims=True)
    res_c = jnp.concatenate([centered[1:2], -centered[0:1]], axis=0) / total
    res_y = gram(res_c)
    dir_c, dir_y = res_c, res_y
    norm_now = full_sum(res_c * res_y)
    change = jnp.zeros_like(res_y)
    for turn in range(ITERS):
        img_c = dir_y / total + DIAG_SHIFT * dir_c
        alpha = norm_now / full_sum(img_c * dir_y)
        change = change + alpha * dir_y
        if turn + 1 < ITERS:
            img_y = gram(dir_y) / total + DIAG_SHIFT * dir_y
            res_c = res_c - alpha * img_c
            res_y = res_y - alpha * img_y
            norm_next = full_sum(res_c * res_y)
            beta = norm_next / norm_now
            dir_c = res_c + beta * dir_c
            dir_y = res_y + beta * dir_y
            norm_now = norm_next
    return change


def full_sum(x):
    return jnp.sum(jnp.sum(x, axis=1, keepdims=True), axis=0, keepdims=True)


def project(lifted, slope_re, slope_im):
    raw = jnp.concatenate(
        [jnp.sum(lifted * slope_re, axis=0, keepdims=True), jnp.sum(lifted * slope_im, axis=0, keepdims=True)],
        axis=0,
    )
    return raw - jnp.mean(raw, axis=1, keepdims=True)


def solve_kernel(mine_ref, other_ref, high_ref, low_ref, re_ref, im_ref, local_ref, change_ref):
    width = local_ref.shape[1]
    energy = mine_ref[...] + other_ref[...]
    local_ref[...] = energy[:, :width]

    def gram(c):
        back = re_ref[...] * c[0:1] + im_ref[...] * c[1:2]
        high = back.astype(BF16)
        low = (back - high.astype(F32)).astype(BF16)
        lifted = dot(high, high_ref[...], ((1,), (0,)))
        lifted += dot(low, high_ref[...], ((1,), (0,)))
        lifted += dot(high, low_ref[...], ((1,), (0,)))
        return project(lifted, re_ref[...], im_ref[...])

    change_ref[...] = solve(energy, gram)[:, :width]


def wide_solve(energy, occ_stack, first_weight, bias_row, second, readout):
    here = occ_stack.shape[1]
    occupied = occ_stack.reshape(-1, occ_stack.shape[2])
    pre = dot(occupied, first_weight, ((1,), (0,))) + bias_row
    hidden = jnp.tanh(pre).astype(BF16)
    mid = jnp.tanh(dot(second, hidden, ((0,), (1,))))
    slope = 1.0 - mid * mid
    slope_re = slope * readout[0][:, None]
    slope_im = slope * readout[1][:, None]

    def gram(c):
        high, low = split(slope_re * c[0:1] + slope_im * c[1:2])
        high, low = split(dot(high, hidden, ((1,), (0,))) + dot(low, hidden, ((1,), (0,))))
        lifted = dot(high, hidden, ((1,), (1,))) + dot(low, hidden, ((1,), (1,)))
        return project(lifted, slope_re, slope_im)

    return energy[:, :here], solve(energy, gram)[:, :here]


def swap(x, axis, bit):
    return lax.ppermute(x, axis, [(i, i ^ bit) for i in range(lax.axis_size(axis))])


def shift(x, axis, step):
    size = lax.axis_size(axis)
    return lax.ppermute(x, axis, [(i, (i + step) % size) for i in range(size)])


def exchange_all(send):
    peers = send.shape[0]
    return lax.all_to_all(
        send,
        ("samples", "chip"),
        0,
        0,
        axis_index_groups=[list(reversed(range(peers)))],
        tiled=True,
    )


def powers(size):
    return [1 << k for k in reversed(range((size - 1).bit_length()))]


def body(
    occupations,
    connection_counts,
    connection_orbitals,
    connection_elements,
    laser_step,
    first_weight,
    first_bias,
    second_weight,
    readout,
):
    here, orbitals = occupations.shape
    slots = connection_orbitals.shape[1]
    wide, narrow = first_weight.shape[1], second_weight.shape[1]
    chips = lax.axis_size("chip")
    spread = chips * lax.axis_size("core")
    blocks = lax.axis_size("samples")
    total = here * blocks
    bias_row = first_bias[None, :]
    field = FIELD_SCALE * jnp.sin(FIELD_RATE * laser_step.astype(F32)[None, None])

    bits = powers(blocks)
    entries = [0]
    for bit in bits:
        entries = entries + [e ^ bit for e in entries]
    sent = occupations.astype(BF16)
    moved = [swap(sent, "samples", entry) for entry in entries[1:4]]

    shifts, shards = [], []
    for step in range(1, chips):
        shifts.append((step, 0))
        shards.append(shift(second_weight, "chip", step))
    shifts.append((0, 1))
    shards.append(shift(second_weight, "core", 1))

    hidden, owner, elements, w1, bias, readout_near, own_shard, occupied = call(
        functools.partial(slot_hidden_kernel, spread),
        8,
        (
            jax.ShapeDtypeStruct((slots + here, wide), BF16),
            jax.ShapeDtypeStruct((here, slots), BF16),
            jax.ShapeDtypeStruct(connection_elements.shape, F32),
            jax.ShapeDtypeStruct(first_weight.shape, BF16),
            jax.ShapeDtypeStruct(bias_row.shape, F32),
            jax.ShapeDtypeStruct(readout.shape, F32),
            jax.ShapeDtypeStruct(second_weight.shape, BF16),
            jax.ShapeDtypeStruct(occupations.shape, BF16),
        ),
        [
            pltpu.VMEM((1, here), jnp.int32),
            pltpu.VMEM(connection_orbitals.shape, jnp.int32),
            pltpu.VMEM(occupations.shape, jnp.int32),
            pltpu.SemaphoreType.DMA((8,)),
        ],
        name="slot_hidden",
        copies=True,
        flops=2 * (slots + here) * orbitals * wide,
        transcendentals=(slots + here) * wide,
    )(
        *(
            pltpu.with_memory_space_constraint(x, pltpu.HBM)
            for x in (
                connection_counts[None, :],
                connection_orbitals,
                occupations,
                first_weight,
                bias_row,
                connection_elements,
                readout,
                second_weight,
            )
        ),
    )
    relayed, occupied, moved = lax.optimization_barrier((shards[: chips - 1], occupied, moved))
    for step in range(1, chips):
        shifts.append((step, 1))
        shards.append(shift(relayed[step - 1], "core", 1))
    shifts.append((0, 0))
    wide_path = total > wide
    if not wide_path:
        full = orbitals // 128 * 128
        packed = call(
            pack_kernel,
            len(moved) + 1,
            jax.ShapeDtypeStruct((total // 2 + here, full), BF16),
            name="pack",
        )(occupied, *moved)
        far_packed = swap(packed, "samples", bits[-1])

    send, second = call(
        functools.partial(slot_energy_kernel, tuple(shifts)),
        5 + len(shifts),
        (
            jax.ShapeDtypeStruct((blocks * chips, 1, 2 * here), F32),
            jax.ShapeDtypeStruct((wide, narrow), BF16),
        ),
        name="slot_energy",
        flops=2 * (slots + here) * wide * narrow,
        transcendentals=(slots + here) * narrow,
    )(field, hidden, owner, elements, readout_near, *shards, own_shard)
    received = exchange_all(send)
    if wide_path:
        stack = jnp.stack([occupied] + moved)
        for bit in bits[2:]:
            stack = jnp.concatenate([stack, swap(stack, "samples", bit)], axis=0)
        overlap = (stack,)
    else:
        half = total // 2
        weights = (w1, bias, second, readout_near)
        near = call(
            near_half_kernel,
            5,
            (
                jax.ShapeDtypeStruct((half, wide), BF16),
                jax.ShapeDtypeStruct((half, half), F32),
                jax.ShapeDtypeStruct((narrow, half), F32),
                jax.ShapeDtypeStruct((narrow, half), F32),
            ),
            name="near_half",
            flops=2 * half * wide * (orbitals + narrow + half),
            transcendentals=half * (wide + narrow),
        )(packed, *weights)
        overlap = call(
            far_half_kernel,
            9,
            (jax.ShapeDtypeStruct((total, total), BF16),) * 2 + (jax.ShapeDtypeStruct((narrow, total), F32),) * 2,
            name="far_half",
            flops=2 * half * wide * (orbitals + narrow + 3 * half),
            transcendentals=half * (wide + narrow),
        )(far_packed, *weights, *near)

    mine = call(
        functools.partial(collect_kernel, entries, chips),
        2,
        jax.ShapeDtypeStruct((2, total), F32),
        name="collect",
        flops=COLLECT_WEIGHT,
    )(received, overlap[0])
    other = swap(mine, "core", 1)
    if wide_path:
        return wide_solve(mine + other, stack, first_weight, bias_row, second, readout)
    return call(
        solve_kernel,
        6,
        (jax.ShapeDtypeStruct((2, here), F32),) * 2,
        name="solve",
        flops=ITERS * 6 * total * total * narrow,
    )(mine, other, *overlap)


def solution(mesh):
    blocks, spread = mesh.shape["samples"], mesh.shape["params"]
    fine = Mesh(mesh.devices.reshape(blocks, spread // 2, 2), ("samples", "chip", "core"))
    return jax.shard_map(
        body,
        mesh=fine,
        in_specs=(
            P("samples", None),
            P("samples"),
            P(None, ("samples", "chip", "core")),
            P(None, ("samples", "chip", "core")),
            P(),
            P(),
            P(),
            P(("chip", "core"), None),
            P(),
        ),
        out_specs=(P(None, "samples"), P(None, "samples")),
        check_vma=False,
    )
```

```python
import functools

import jax
import jax.numpy as jnp
from jax import lax
from jax.experimental import pallas as pl
from jax.experimental.pallas import tpu as pltpu
from jax.sharding import Mesh, PartitionSpec as P

ITERS = 2


FIELD_SCALE = 0.8
FIELD_RATE = 0.0123
DIAG_SHIFT = 0.01
F32 = jnp.float32
BF16 = jnp.bfloat16
ROWS = 256
COLLECT_WEIGHT = 1e10
VMEM_LIMIT = 48 * 1024 * 1024


def dot(a, b, dims):
    return lax.dot_general(a, b, (dims, ((), ())), preferred_element_type=F32)


def split(x):
    high = lax.reduce_precision(x, 8, 7)
    return high.astype(BF16), (x - high).astype(BF16)


def parts(x):
    high = x.astype(BF16)
    rest = x - high.astype(F32)
    middle = rest.astype(BF16)
    return high, middle, (rest - middle.astype(F32)).astype(BF16)


def iota(shape, dim):
    return lax.broadcasted_iota(jnp.int32, shape, dim)


def call(kernel, count, out_shape, scratch=(), name=None, copies=False, flops=0, transcendentals=0):
    vmem = pl.BlockSpec(memory_space=pltpu.VMEM)
    far = pl.BlockSpec(memory_space=pltpu.HBM)
    return pl.pallas_call(
        kernel,
        out_shape=out_shape,
        in_specs=[far if copies else vmem] * count,
        out_specs=jax.tree.map(lambda _: vmem, out_shape),
        scratch_shapes=scratch,
        compiler_params=pltpu.CompilerParams(vmem_limit_bytes=VMEM_LIMIT),
        cost_estimate=pl.CostEstimate(
            flops=int(flops),
            transcendentals=int(transcendentals),
            bytes_accessed=sum(x.size * x.dtype.itemsize for x in jax.tree.leaves(out_shape)),
        ),
        name=name,
    )


def slot_hidden_kernel(
    spread,
    counts_hbm,
    orbitals_hbm,
    occ_hbm,
    w1_hbm,
    bias_hbm,
    elements_hbm,
    readout_hbm,
    own_hbm,
    hidden_ref,
    owner_ref,
    elements_ref,
    w1_ref,
    bias_ref,
    readout_ref,
    own_ref,
    occupied_ref,
    counts_ref,
    orbitals_ref,
    occ_ref,
    sems,
):
    here, orbitals = occ_ref.shape
    updates, slots = orbitals_ref.shape
    pairs = (
        (counts_hbm, counts_ref),
        (occ_hbm, occ_ref),
        (w1_hbm, w1_ref),
        (bias_hbm, bias_ref),
        (orbitals_hbm, orbitals_ref),
        (elements_hbm, elements_ref),
        (readout_hbm, readout_ref),
        (own_hbm, own_ref),
    )
    copies = [pltpu.make_async_copy(a, b, sems.at[i]) for i, (a, b) in enumerate(pairs)]
    for copy in copies:
        copy.start()
    chip, core = lax.axis_index("chip"), lax.axis_index("core")
    place = chip * 2 + core
    copies[0].wait()
    counts = counts_ref[...].astype(F32)
    row, col = iota((here, here), 0), iota((here, here), 1)
    ends = jnp.sum(jnp.where(col <= row, counts, 0.0), axis=1, keepdims=True)
    starts = jnp.sum(jnp.where(col < row, counts, 0.0), axis=1, keepdims=True)
    positions = (place + spread * iota((1, slots), 1)).astype(F32)
    owner = jnp.where((starts <= positions) & (positions < ends), 1.0, 0.0).astype(BF16)
    owner_ref[...] = owner
    copies[1].wait()
    occupied = occ_ref[...].astype(F32).astype(BF16)
    occupied_ref[...] = occupied
    copies[2].wait()
    copies[3].wait()
    w1 = w1_ref[...]
    bias = bias_ref[...]
    hidden_ref[slots:, :] = jnp.tanh(dot(occupied, w1, ((1,), (0,))) + bias).astype(BF16)
    copies[4].wait()
    for start in range(0, slots, ROWS):
        stop = min(start + ROWS, slots)
        parent_occ = dot(occupied, owner[:, start:stop], ((0,), (0,)))
        columns = iota((orbitals, stop - start), 0)
        flipped = columns == orbitals_ref[0:1, start:stop]
        for u in range(1, updates):
            flipped = flipped | (columns == orbitals_ref[u : u + 1, start:stop])
        slot_occ = jnp.where(flipped, 1.0 - parent_occ, parent_occ).astype(BF16)
        pre = dot(slot_occ, w1, ((0,), (0,))) + bias
        hidden_ref[start:stop, :] = jnp.tanh(pre).astype(BF16)
    copies[5].wait()
    copies[6].wait()
    copies[7].wait()


def slot_energy_kernel(
    shifts, field_ref, hidden_ref, owner_ref, elements_ref, readout_ref, *refs
):
    shard_refs, (send_ref, second_ref) = refs[: len(shifts)], refs[len(shifts) :]
    here, slots = owner_ref.shape
    chips = lax.axis_size("chip")
    chip, core = lax.axis_index("chip"), lax.axis_index("core")
    for (step, other), shard in zip(shifts, shard_refs):
        rows = shard.shape[0]
        source = lax.rem(chip + chips - step, chips) * 2 + (core ^ other)
        second_ref[pl.ds(pl.multiple_of(source * rows, rows), rows), :] = shard[...]
    mid = jnp.tanh(dot(second_ref[...], hidden_ref[...], ((0,), (1,))))
    readout = readout_ref[...].T
    logs_re = jnp.sum(mid * readout[:, 0:1], axis=0, keepdims=True)
    logs_im = jnp.sum(mid * readout[:, 1:2], axis=0, keepdims=True)
    owner = owner_ref[...]
    own = jnp.concatenate(parts(logs_re[:, slots:]) + parts(logs_im[:, slots:]), axis=0)
    parent = dot(own, owner, ((1,), (0,)))
    diff_re = logs_re[:, :slots] - (parent[0:1] + parent[1:2] + parent[2:3])
    diff_im = logs_im[:, :slots] - (parent[3:4] + parent[4:5] + parent[5:6])
    used = jnp.sum(owner.astype(F32), axis=0, keepdims=True) > 0.0
    weight = elements_ref[0:1, :] + field_ref[...] * elements_ref[1:2, :]
    scale = weight * jnp.exp(diff_re)
    contrib_re = jnp.where(used, scale * jnp.cos(diff_im), 0.0)
    contrib_im = jnp.where(used, scale * jnp.sin(diff_im), 0.0)
    contrib = jnp.concatenate(parts(contrib_re) + parts(contrib_im), axis=0)
    sums = dot(contrib, owner, ((1,), (1,)))
    partial_re = sums[0:1] + sums[1:2] + sums[2:3]
    partial_im = sums[3:4] + sums[4:5] + sums[5:6]
    row = jnp.concatenate([partial_re, partial_im], axis=1)
    send_ref[...] = jnp.broadcast_to(row[None], send_ref.shape)


def collect_kernel(entries, chips, received_ref, energy_ref):
    here = received_ref.shape[2] // 2
    block = lax.axis_index("samples")
    out_re, out_im = [], []
    peers = received_ref.shape[0]
    for entry in entries:
        first = lax.rem((block ^ entry) * chips + peers // 2, peers)
        row = received_ref[first]
        for k in range(1, chips):
            row = row + received_ref[first + k]
        out_re.append(row[:, :here])
        out_im.append(row[:, here:])
    energy_ref[...] = jnp.concatenate(
        [jnp.concatenate(out_re, axis=1), jnp.concatenate(out_im, axis=1)], axis=0
    )


def sample_values(packed_ref, w1_ref, bias_ref, second_ref, readout_ref, size):
    hidden = jnp.tanh(sample_pre(packed_ref, w1_ref, bias_ref, size)).astype(BF16)
    mid = jnp.tanh(dot(second_ref[...], hidden, ((0,), (1,))))
    slope = 1.0 - mid * mid
    readout = readout_ref[...].T
    return hidden, slope * readout[:, 0:1], slope * readout[:, 1:2]


def pack_kernel(mine_ref, moved_ref, after_ref, packed_ref):
    del after_ref
    blocks, here, orbitals = mine_ref.shape
    full = packed_ref.shape[1]
    pieces = [mine_ref[k] for k in range(blocks)] + [moved_ref[k] for k in range(blocks)]
    rest = orbitals - full
    for k, piece in enumerate(pieces):
        packed_ref[k * here : (k + 1) * here, :] = piece[:, :full]
    rests = [piece[:, full:].astype(F32) for piece in pieces]
    rests.append(jnp.zeros((here, full - rest * len(pieces)), F32))
    packed_ref[len(pieces) * here :, :] = jnp.concatenate(rests, axis=1).astype(BF16)


def sample_pre(packed_ref, w1_ref, bias_ref, size):
    full = packed_ref.shape[1]
    here = packed_ref.shape[0] - size
    rest = w1_ref.shape[0] - full
    tail = packed_ref[size:, :].astype(F32)
    rests = [tail[:, k * rest : (k + 1) * rest] for k in range(size // here)]
    tail = jnp.concatenate(rests, axis=0).astype(BF16)
    pre = dot(packed_ref[:size, :], w1_ref[:full, :], ((1,), (0,)))
    return pre + dot(tail, w1_ref[full:, :], ((1,), (0,))) + bias_ref[...]


def near_half_kernel(packed_ref, w1_ref, bias_ref, second_ref, readout_ref, hidden_ref, overlap_ref, re_ref, im_ref):
    size = hidden_ref.shape[0]
    hidden, re_ref[...], im_ref[...] = sample_values(packed_ref, w1_ref, bias_ref, second_ref, readout_ref, size)
    hidden_ref[...] = hidden
    overlap_ref[...] = dot(hidden, hidden, ((1,), (1,)))


def far_half_kernel(
    packed_ref,
    w1_ref,
    bias_ref,
    second_ref,
    readout_ref,
    hidden_ref,
    overlap_ref,
    near_re_ref,
    near_im_ref,
    overlap_out_ref,
    re_ref,
    im_ref,
):
    size = hidden_ref.shape[0]
    total = 2 * size
    hidden, re, im = sample_values(packed_ref, w1_ref, bias_ref, second_ref, readout_ref, size)
    re_ref[:, :size] = near_re_ref[...]
    im_ref[:, :size] = near_im_ref[...]
    re_ref[:, size:] = re
    im_ref[:, size:] = im
    near = hidden_ref[...]

    def put(row, col, overlap):
        high = overlap.astype(BF16)
        columns = slice(col * size, (col + 1) * size)
        overlap_out_ref[row * size : (row + 1) * size, columns] = high
        low = (overlap - high.astype(F32)).astype(BF16)
        overlap_out_ref[total + row * size : total + (row + 1) * size, columns] = low
        overlap_out_ref[2 * total + row * size : 2 * total + (row + 1) * size, columns] = high

    put(0, 0, overlap_ref[...])
    put(0, 1, dot(near, hidden, ((1,), (1,))))
    put(1, 0, dot(hidden, near, ((1,), (1,))))
    put(1, 1, dot(hidden, hidden, ((1,), (1,))))


def solve(energy, gram):
    total = energy.shape[1]
    centered = energy - jnp.mean(energy, axis=1, keepdims=True)
    res_c = jnp.concatenate([centered[1:2], -centered[0:1]], axis=0) / total
    res_y = gram(res_c)
    dir_c, dir_y = res_c, res_y
    norm_now = full_sum(res_c * res_y)
    change = jnp.zeros_like(res_y)
    for turn in range(ITERS):
        img_c = dir_y / total + DIAG_SHIFT * dir_c
        alpha = norm_now / full_sum(img_c * dir_y)
        change = change + alpha * dir_y
        if turn + 1 < ITERS:
            img_y = gram(dir_y) / total + DIAG_SHIFT * dir_y
            res_c = res_c - alpha * img_c
            res_y = res_y - alpha * img_y
            norm_next = full_sum(res_c * res_y)
            beta = norm_next / norm_now
            dir_c = res_c + beta * dir_c
            dir_y = res_y + beta * dir_y
            norm_now = norm_next
    return change


def full_sum(x):
    return jnp.sum(jnp.sum(x, axis=1, keepdims=True), axis=0, keepdims=True)


def project(lifted, slope_re, slope_im):
    raw = jnp.concatenate(
        [jnp.sum(lifted * slope_re, axis=0, keepdims=True), jnp.sum(lifted * slope_im, axis=0, keepdims=True)],
        axis=0,
    )
    return raw - jnp.mean(raw, axis=1, keepdims=True)


def solve_kernel(mine_ref, other_ref, overlap_ref, re_ref, im_ref, local_ref, change_ref):
    width = local_ref.shape[1]
    energy = mine_ref[...] + other_ref[...]
    local_ref[...] = energy[:, :width]

    def gram(c):
        back = re_ref[...] * c[0:1] + im_ref[...] * c[1:2]
        high = back.astype(BF16)
        low = (back - high.astype(F32)).astype(BF16)
        lifted = dot(jnp.concatenate([high, high, low], axis=1), overlap_ref[...], ((1,), (0,)))
        return project(lifted, re_ref[...], im_ref[...])

    change_ref[...] = solve(energy, gram)[:, :width]


def wide_solve(energy, occ_stack, first_weight, bias_row, second, readout):
    here = occ_stack.shape[1]
    occupied = occ_stack.reshape(-1, occ_stack.shape[2])
    pre = dot(occupied, first_weight, ((1,), (0,))) + bias_row
    hidden = jnp.tanh(pre).astype(BF16)
    mid = jnp.tanh(dot(second, hidden, ((0,), (1,))))
    slope = 1.0 - mid * mid
    slope_re = slope * readout[0][:, None]
    slope_im = slope * readout[1][:, None]

    def gram(c):
        high, low = split(slope_re * c[0:1] + slope_im * c[1:2])
        high, low = split(dot(high, hidden, ((1,), (0,))) + dot(low, hidden, ((1,), (0,))))
        lifted = dot(high, hidden, ((1,), (1,))) + dot(low, hidden, ((1,), (1,)))
        return project(lifted, slope_re, slope_im)

    return energy[:, :here], solve(energy, gram)[:, :here]


def swap(x, axis, bit):
    return lax.ppermute(x, axis, [(i, i ^ bit) for i in range(lax.axis_size(axis))])


def shift(x, axis, step):
    size = lax.axis_size(axis)
    return lax.ppermute(x, axis, [(i, (i + step) % size) for i in range(size)])


def exchange_all(send):
    peers = send.shape[0]
    return lax.all_to_all(
        send,
        ("samples", "chip"),
        0,
        0,
        axis_index_groups=[[(k + peers // 2) % peers for k in range(peers)]],
        tiled=True,
    )


def powers(size):
    return [1 << k for k in reversed(range((size - 1).bit_length()))]


def body(
    occupations,
    connection_counts,
    connection_orbitals,
    connection_elements,
    laser_step,
    first_weight,
    first_bias,
    second_weight,
    readout,
):
    here, orbitals = occupations.shape
    slots = connection_orbitals.shape[1]
    wide, narrow = first_weight.shape[1], second_weight.shape[1]
    chips = lax.axis_size("chip")
    spread = chips * lax.axis_size("core")
    blocks = lax.axis_size("samples")
    total = here * blocks
    bias_row = first_bias[None, :]
    field = FIELD_SCALE * jnp.sin(FIELD_RATE * laser_step.astype(F32)[None, None])

    bits = powers(blocks)
    entries = [0]
    for bit in bits:
        entries = entries + [e ^ bit for e in entries]
    moved = swap(occupations.astype(BF16)[None], "samples", bits[0])

    shifts, shards = [], []
    for step in range(1, chips):
        shifts.append((step, 0))
        shards.append(shift(second_weight, "chip", step))
    shifts.append((0, 1))
    shards.append(shift(second_weight, "core", 1))

    hidden, owner, elements, w1, bias, readout_near, own_shard, occupied = call(
        functools.partial(slot_hidden_kernel, spread),
        8,
        (
            jax.ShapeDtypeStruct((slots + here, wide), BF16),
            jax.ShapeDtypeStruct((here, slots), BF16),
            jax.ShapeDtypeStruct(connection_elements.shape, F32),
            jax.ShapeDtypeStruct(first_weight.shape, BF16),
            jax.ShapeDtypeStruct(bias_row.shape, F32),
            jax.ShapeDtypeStruct(readout.shape, F32),
            jax.ShapeDtypeStruct(second_weight.shape, BF16),
            jax.ShapeDtypeStruct(occupations.shape, BF16),
        ),
        [
            pltpu.VMEM((1, here), jnp.int32),
            pltpu.VMEM(connection_orbitals.shape, jnp.int32),
            pltpu.VMEM(occupations.shape, jnp.int32),
            pltpu.SemaphoreType.DMA((8,)),
        ],
        name="slot_hidden",
        copies=True,
        flops=2 * (slots + here) * orbitals * wide,
        transcendentals=(slots + here) * wide,
    )(
        *(
            pltpu.with_memory_space_constraint(x, pltpu.HBM)
            for x in (
                connection_counts[None, :],
                connection_orbitals,
                occupations,
                first_weight,
                bias_row,
                connection_elements,
                readout,
                second_weight,
            )
        ),
    )
    relayed, occupied = lax.optimization_barrier((shards[: chips - 1], occupied))
    for step in range(1, chips):
        shifts.append((step, 1))
        shards.append(shift(relayed[step - 1], "core", 1))
    shifts.append((0, 0))
    stack = jnp.concatenate([occupied[None], moved], axis=0)
    moved = swap(stack, "samples", bits[1])

    send, second = call(
        functools.partial(slot_energy_kernel, tuple(shifts)),
        5 + len(shifts),
        (
            jax.ShapeDtypeStruct((blocks * chips, 1, 2 * here), F32),
            jax.ShapeDtypeStruct((wide, narrow), BF16),
        ),
        name="slot_energy",
        flops=2 * (slots + here) * wide * narrow,
        transcendentals=(slots + here) * narrow,
    )(field, hidden, owner, elements, readout_near, *shards, own_shard)
    received = exchange_all(send)
    mine = call(
        functools.partial(collect_kernel, entries, chips),
        1,
        jax.ShapeDtypeStruct((2, total), F32),
        name="collect",
        flops=COLLECT_WEIGHT,
    )(received)
    other = swap(mine, "core", 1)

    for bit in bits[2:-1]:
        stack = jnp.concatenate([stack, moved], axis=0)
        moved = swap(stack, "samples", bit)
    if total > wide:
        stack = jnp.concatenate([stack, moved], axis=0)
        stack = jnp.concatenate([stack, swap(stack, "samples", bits[-1])], axis=0)
        return wide_solve(mine + other, stack, first_weight, bias_row, second, readout)

    half = total // 2
    weights = (w1, bias, second, readout_near)
    full = orbitals // 128 * 128
    packed = call(
        pack_kernel,
        3,
        jax.ShapeDtypeStruct((half + here, full), BF16),
        name="pack",
    )(stack, moved, second)
    far_packed = swap(packed, "samples", bits[-1])
    near = call(
        near_half_kernel,
        5,
        (
            jax.ShapeDtypeStruct((half, wide), BF16),
            jax.ShapeDtypeStruct((half, half), F32),
            jax.ShapeDtypeStruct((narrow, half), F32),
            jax.ShapeDtypeStruct((narrow, half), F32),
        ),
        name="near_half",
        flops=2 * half * wide * (orbitals + narrow + half),
        transcendentals=half * (wide + narrow),
    )(packed, *weights)
    overlap = call(
        far_half_kernel,
        9,
        (jax.ShapeDtypeStruct((3 * total, total), BF16),) + (jax.ShapeDtypeStruct((narrow, total), F32),) * 2,
        name="far_half",
        flops=2 * half * wide * (orbitals + narrow + 3 * half),
        transcendentals=half * (wide + narrow),
    )(far_packed, *weights, *near)
    return call(
        solve_kernel,
        5,
        (jax.ShapeDtypeStruct((2, here), F32),) * 2,
        name="solve",
        flops=ITERS * 6 * total * total * narrow,
    )(mine, other, *overlap)


def solution(mesh):
    blocks, spread = mesh.shape["samples"], mesh.shape["params"]
    fine = Mesh(mesh.devices.reshape(blocks, spread // 2, 2), ("samples", "chip", "core"))
    return jax.shard_map(
        body,
        mesh=fine,
        in_specs=(
            P("samples", None),
            P("samples"),
            P(None, ("samples", "chip", "core")),
            P(None, ("samples", "chip", "core")),
            P(),
            P(),
            P(),
            P(("chip", "core"), None),
            P(),
        ),
        out_specs=(P(None, "samples"), P(None, "samples")),
        check_vma=False,
    )
```

```python
import functools

import jax
import jax.numpy as jnp
from jax import lax
from jax.experimental import pallas as pl
from jax.experimental.pallas import tpu as pltpu
from jax.sharding import Mesh, PartitionSpec as P

ITERS = 2


FIELD_SCALE = 0.8
FIELD_RATE = 0.0123
DIAG_SHIFT = 0.01
F32 = jnp.float32
BF16 = jnp.bfloat16
ROWS = 256
COLLECT_WEIGHT = 1e10
VMEM_LIMIT = 48 * 1024 * 1024


def dot(a, b, dims):
    return lax.dot_general(a, b, (dims, ((), ())), preferred_element_type=F32)


def split(x):
    high = lax.reduce_precision(x, 8, 7)
    return high.astype(BF16), (x - high).astype(BF16)


def parts(x):
    high = x.astype(BF16)
    rest = x - high.astype(F32)
    middle = rest.astype(BF16)
    return high, middle, (rest - middle.astype(F32)).astype(BF16)


def iota(shape, dim):
    return lax.broadcasted_iota(jnp.int32, shape, dim)


def call(kernel, count, out_shape, scratch=(), name=None, copies=False, flops=0, transcendentals=0):
    vmem = pl.BlockSpec(memory_space=pltpu.VMEM)
    far = pl.BlockSpec(memory_space=pltpu.HBM)
    return pl.pallas_call(
        kernel,
        out_shape=out_shape,
        in_specs=[far if copies else vmem] * count,
        out_specs=jax.tree.map(lambda _: vmem, out_shape),
        scratch_shapes=scratch,
        compiler_params=pltpu.CompilerParams(vmem_limit_bytes=VMEM_LIMIT),
        cost_estimate=pl.CostEstimate(
            flops=int(flops),
            transcendentals=int(transcendentals),
            bytes_accessed=sum(x.size * x.dtype.itemsize for x in jax.tree.leaves(out_shape)),
        ),
        name=name,
    )


def slot_hidden_kernel(
    spread,
    counts_hbm,
    orbitals_hbm,
    occ_hbm,
    w1_hbm,
    bias_hbm,
    elements_hbm,
    readout_hbm,
    own_hbm,
    hidden_ref,
    owner_ref,
    elements_ref,
    w1_ref,
    bias_ref,
    readout_ref,
    own_ref,
    occupied_ref,
    counts_ref,
    orbitals_ref,
    occ_ref,
    sems,
):
    here, orbitals = occ_ref.shape
    updates, slots = orbitals_ref.shape
    pairs = (
        (counts_hbm, counts_ref),
        (occ_hbm, occ_ref),
        (w1_hbm, w1_ref),
        (bias_hbm, bias_ref),
        (orbitals_hbm, orbitals_ref),
        (elements_hbm, elements_ref),
        (readout_hbm, readout_ref),
        (own_hbm, own_ref),
    )
    copies = [pltpu.make_async_copy(a, b, sems.at[i]) for i, (a, b) in enumerate(pairs)]
    for copy in copies:
        copy.start()
    chip, core = lax.axis_index("chip"), lax.axis_index("core")
    place = chip * 2 + core
    copies[0].wait()
    counts = counts_ref[...].astype(F32)
    row, col = iota((here, here), 0), iota((here, here), 1)
    ends = jnp.sum(jnp.where(col <= row, counts, 0.0), axis=1, keepdims=True)
    starts = jnp.sum(jnp.where(col < row, counts, 0.0), axis=1, keepdims=True)
    positions = (place + spread * iota((1, slots), 1)).astype(F32)
    owner = jnp.where((starts <= positions) & (positions < ends), 1.0, 0.0).astype(BF16)
    owner_ref[...] = owner
    copies[1].wait()
    occupied = occ_ref[...].astype(F32).astype(BF16)
    occupied_ref[...] = occupied
    copies[2].wait()
    copies[3].wait()
    w1 = w1_ref[...]
    bias = bias_ref[...]
    hidden_ref[slots:, :] = jnp.tanh(dot(occupied, w1, ((1,), (0,))) + bias).astype(BF16)
    copies[4].wait()
    for start in range(0, slots, ROWS):
        stop = min(start + ROWS, slots)
        parent_occ = dot(occupied, owner[:, start:stop], ((0,), (0,)))
        columns = iota((orbitals, stop - start), 0)
        flipped = columns == orbitals_ref[0:1, start:stop]
        for u in range(1, updates):
            flipped = flipped | (columns == orbitals_ref[u : u + 1, start:stop])
        slot_occ = jnp.where(flipped, 1.0 - parent_occ, parent_occ).astype(BF16)
        pre = dot(slot_occ, w1, ((0,), (0,))) + bias
        hidden_ref[start:stop, :] = jnp.tanh(pre).astype(BF16)
    copies[5].wait()
    copies[6].wait()
    copies[7].wait()


def slot_energy_kernel(
    shifts, field_ref, hidden_ref, owner_ref, elements_ref, readout_ref, *refs
):
    shard_refs, (send_ref, second_ref) = refs[: len(shifts)], refs[len(shifts) :]
    here, slots = owner_ref.shape
    chips = lax.axis_size("chip")
    chip, core = lax.axis_index("chip"), lax.axis_index("core")
    for (step, other), shard in zip(shifts, shard_refs):
        rows = shard.shape[0]
        source = lax.rem(chip + chips - step, chips) * 2 + (core ^ other)
        second_ref[pl.ds(pl.multiple_of(source * rows, rows), rows), :] = shard[...]
    mid = jnp.tanh(dot(second_ref[...], hidden_ref[...], ((0,), (1,))))
    readout = readout_ref[...].T
    logs_re = jnp.sum(mid * readout[:, 0:1], axis=0, keepdims=True)
    logs_im = jnp.sum(mid * readout[:, 1:2], axis=0, keepdims=True)
    owner = owner_ref[...]
    own = jnp.concatenate(parts(logs_re[:, slots:]) + parts(logs_im[:, slots:]), axis=0)
    parent = dot(own, owner, ((1,), (0,)))
    diff_re = logs_re[:, :slots] - (parent[0:1] + parent[1:2] + parent[2:3])
    diff_im = logs_im[:, :slots] - (parent[3:4] + parent[4:5] + parent[5:6])
    used = jnp.sum(owner.astype(F32), axis=0, keepdims=True) > 0.0
    weight = elements_ref[0:1, :] + field_ref[...] * elements_ref[1:2, :]
    scale = weight * jnp.exp(diff_re)
    contrib_re = jnp.where(used, scale * jnp.cos(diff_im), 0.0)
    contrib_im = jnp.where(used, scale * jnp.sin(diff_im), 0.0)
    contrib = jnp.concatenate(parts(contrib_re) + parts(contrib_im), axis=0)
    sums = dot(contrib, owner, ((1,), (1,)))
    partial_re = sums[0:1] + sums[1:2] + sums[2:3]
    partial_im = sums[3:4] + sums[4:5] + sums[5:6]
    row = jnp.concatenate([partial_re, partial_im], axis=1)
    send_ref[...] = jnp.broadcast_to(row[None], send_ref.shape)


def collect_kernel(entries, chips, received_ref, energy_ref):
    here = received_ref.shape[2] // 2
    block = lax.axis_index("samples")
    out_re, out_im = [], []
    peers = received_ref.shape[0]
    for entry in entries:
        first = lax.rem((block ^ entry) * chips + peers // 2, peers)
        row = received_ref[first]
        for k in range(1, chips):
            row = row + received_ref[first + k]
        out_re.append(row[:, :here])
        out_im.append(row[:, here:])
    energy_ref[...] = jnp.concatenate(
        [jnp.concatenate(out_re, axis=1), jnp.concatenate(out_im, axis=1)], axis=0
    )


def sample_values(packed_ref, w1_ref, bias_ref, second_ref, readout_ref, size):
    hidden = jnp.tanh(sample_pre(packed_ref, w1_ref, bias_ref, size)).astype(BF16)
    mid = jnp.tanh(dot(second_ref[...], hidden, ((0,), (1,))))
    slope = 1.0 - mid * mid
    readout = readout_ref[...].T
    return hidden, slope * readout[:, 0:1], slope * readout[:, 1:2]


def pack_kernel(mine_ref, moved_ref, after_ref, packed_ref):
    del after_ref
    blocks, here, orbitals = mine_ref.shape
    full = packed_ref.shape[1]
    pieces = [mine_ref[k] for k in range(blocks)] + [moved_ref[k] for k in range(blocks)]
    rest = orbitals - full
    for k, piece in enumerate(pieces):
        packed_ref[k * here : (k + 1) * here, :] = piece[:, :full]
    rests = [piece[:, full:].astype(F32) for piece in pieces]
    rests.append(jnp.zeros((here, full - rest * len(pieces)), F32))
    packed_ref[len(pieces) * here :, :] = jnp.concatenate(rests, axis=1).astype(BF16)


def sample_pre(packed_ref, w1_ref, bias_ref, size):
    full = packed_ref.shape[1]
    here = packed_ref.shape[0] - size
    rest = w1_ref.shape[0] - full
    tail = packed_ref[size:, :].astype(F32)
    rests = [tail[:, k * rest : (k + 1) * rest] for k in range(size // here)]
    tail = jnp.concatenate(rests, axis=0).astype(BF16)
    pre = dot(packed_ref[:size, :], w1_ref[:full, :], ((1,), (0,)))
    return pre + dot(tail, w1_ref[full:, :], ((1,), (0,))) + bias_ref[...]


def near_half_kernel(packed_ref, w1_ref, bias_ref, second_ref, readout_ref, hidden_ref, overlap_ref, re_ref, im_ref):
    size = hidden_ref.shape[0]
    hidden, re_ref[...], im_ref[...] = sample_values(packed_ref, w1_ref, bias_ref, second_ref, readout_ref, size)
    hidden_ref[...] = hidden
    overlap_ref[...] = dot(hidden, hidden, ((1,), (1,)))


def far_half_kernel(
    packed_ref,
    w1_ref,
    bias_ref,
    second_ref,
    readout_ref,
    hidden_ref,
    overlap_ref,
    near_re_ref,
    near_im_ref,
    overlap_out_ref,
    re_ref,
    im_ref,
):
    size = hidden_ref.shape[0]
    total = 2 * size
    hidden, re, im = sample_values(packed_ref, w1_ref, bias_ref, second_ref, readout_ref, size)
    re_ref[:, :size] = near_re_ref[...]
    im_ref[:, :size] = near_im_ref[...]
    re_ref[:, size:] = re
    im_ref[:, size:] = im
    near = hidden_ref[...]

    def put(row, col, overlap):
        high = overlap.astype(BF16)
        columns = slice(col * size, (col + 1) * size)
        overlap_out_ref[row * size : (row + 1) * size, columns] = high
        low = (overlap - high.astype(F32)).astype(BF16)
        overlap_out_ref[total + row * size : total + (row + 1) * size, columns] = low
        overlap_out_ref[2 * total + row * size : 2 * total + (row + 1) * size, columns] = high

    put(0, 0, overlap_ref[...])
    put(0, 1, dot(near, hidden, ((1,), (1,))))
    put(1, 0, dot(hidden, near, ((1,), (1,))))
    put(1, 1, dot(hidden, hidden, ((1,), (1,))))


def solve(energy, gram):
    total = energy.shape[1]
    centered = energy - jnp.mean(energy, axis=1, keepdims=True)
    res_c = jnp.concatenate([centered[1:2], -centered[0:1]], axis=0) / total
    res_y = gram(res_c)
    dir_c, dir_y = res_c, res_y
    norm_now = full_sum(res_c * res_y)
    cross, square = norm_now, full_sum(res_y * res_y)
    change = jnp.zeros_like(res_y)
    for turn in range(ITERS):
        alpha = norm_now / (square / total + DIAG_SHIFT * cross)
        change = change + alpha * dir_y
        if turn + 1 < ITERS:
            img_c = dir_y / total + DIAG_SHIFT * dir_c
            img_y = gram(dir_y) / total + DIAG_SHIFT * dir_y
            res_c = res_c - alpha * img_c
            res_y = res_y - alpha * img_y
            norm_next = full_sum(res_c * res_y)
            mixed = full_sum(res_c * dir_y) + full_sum(dir_c * res_y)
            squares = full_sum(res_y * res_y), full_sum(res_y * dir_y)
            beta = norm_next / norm_now
            cross = norm_next + beta * mixed + beta * beta * cross
            square = squares[0] + 2.0 * beta * squares[1] + beta * beta * square
            dir_c = res_c + beta * dir_c
            dir_y = res_y + beta * dir_y
            norm_now = norm_next
    return change


def full_sum(x):
    return jnp.sum(jnp.sum(x, axis=1, keepdims=True), axis=0, keepdims=True)


def project(lifted, slope_re, slope_im):
    raw = jnp.concatenate(
        [jnp.sum(lifted * slope_re, axis=0, keepdims=True), jnp.sum(lifted * slope_im, axis=0, keepdims=True)],
        axis=0,
    )
    return raw - jnp.mean(raw, axis=1, keepdims=True)


def solve_kernel(mine_ref, other_ref, overlap_ref, re_ref, im_ref, local_ref, change_ref):
    width = local_ref.shape[1]
    energy = mine_ref[...] + other_ref[...]
    local_ref[...] = energy[:, :width]

    def gram(c):
        back = re_ref[...] * c[0:1] + im_ref[...] * c[1:2]
        high = back.astype(BF16)
        low = (back - high.astype(F32)).astype(BF16)
        lifted = dot(jnp.concatenate([high, high, low], axis=1), overlap_ref[...], ((1,), (0,)))
        return project(lifted, re_ref[...], im_ref[...])

    change_ref[...] = solve(energy, gram)[:, :width]


def wide_solve(energy, occ_stack, first_weight, bias_row, second, readout):
    here = occ_stack.shape[1]
    occupied = occ_stack.reshape(-1, occ_stack.shape[2])
    pre = dot(occupied, first_weight, ((1,), (0,))) + bias_row
    hidden = jnp.tanh(pre).astype(BF16)
    mid = jnp.tanh(dot(second, hidden, ((0,), (1,))))
    slope = 1.0 - mid * mid
    slope_re = slope * readout[0][:, None]
    slope_im = slope * readout[1][:, None]

    def gram(c):
        high, low = split(slope_re * c[0:1] + slope_im * c[1:2])
        high, low = split(dot(high, hidden, ((1,), (0,))) + dot(low, hidden, ((1,), (0,))))
        lifted = dot(high, hidden, ((1,), (1,))) + dot(low, hidden, ((1,), (1,)))
        return project(lifted, slope_re, slope_im)

    return energy[:, :here], solve(energy, gram)[:, :here]


def swap(x, axis, bit):
    return lax.ppermute(x, axis, [(i, i ^ bit) for i in range(lax.axis_size(axis))])


def shift(x, axis, step):
    size = lax.axis_size(axis)
    return lax.ppermute(x, axis, [(i, (i + step) % size) for i in range(size)])


def exchange_all(send):
    peers = send.shape[0]
    return lax.all_to_all(
        send,
        ("samples", "chip"),
        0,
        0,
        axis_index_groups=[[(k + peers // 2) % peers for k in range(peers)]],
        tiled=True,
    )


def powers(size):
    return [1 << k for k in reversed(range((size - 1).bit_length()))]


def body(
    occupations,
    connection_counts,
    connection_orbitals,
    connection_elements,
    laser_step,
    first_weight,
    first_bias,
    second_weight,
    readout,
):
    here, orbitals = occupations.shape
    slots = connection_orbitals.shape[1]
    wide, narrow = first_weight.shape[1], second_weight.shape[1]
    chips = lax.axis_size("chip")
    spread = chips * lax.axis_size("core")
    blocks = lax.axis_size("samples")
    total = here * blocks
    bias_row = first_bias[None, :]
    field = FIELD_SCALE * jnp.sin(FIELD_RATE * laser_step.astype(F32)[None, None])

    bits = powers(blocks)
    entries = [0]
    for bit in bits:
        entries = entries + [e ^ bit for e in entries]
    moved = swap(occupations[None], "samples", bits[0])

    shifts, shards = [], []
    for step in range(1, chips):
        shifts.append((step, 0))
        shards.append(shift(second_weight, "chip", step))
    shifts.append((0, 1))
    shards.append(shift(second_weight, "core", 1))

    hidden, owner, elements, w1, bias, readout_near, own_shard, occupied = call(
        functools.partial(slot_hidden_kernel, spread),
        8,
        (
            jax.ShapeDtypeStruct((slots + here, wide), BF16),
            jax.ShapeDtypeStruct((here, slots), BF16),
            jax.ShapeDtypeStruct(connection_elements.shape, F32),
            jax.ShapeDtypeStruct(first_weight.shape, BF16),
            jax.ShapeDtypeStruct(bias_row.shape, F32),
            jax.ShapeDtypeStruct(readout.shape, F32),
            jax.ShapeDtypeStruct(second_weight.shape, BF16),
            jax.ShapeDtypeStruct(occupations.shape, BF16),
        ),
        [
            pltpu.VMEM((1, here), jnp.int32),
            pltpu.VMEM(connection_orbitals.shape, jnp.int32),
            pltpu.VMEM(occupations.shape, jnp.int32),
            pltpu.SemaphoreType.DMA((8,)),
        ],
        name="slot_hidden",
        copies=True,
        flops=2 * (slots + here) * orbitals * wide,
        transcendentals=(slots + here) * wide,
    )(
        *(
            pltpu.with_memory_space_constraint(x, pltpu.HBM)
            for x in (
                connection_counts[None, :],
                connection_orbitals,
                occupations,
                first_weight,
                bias_row,
                connection_elements,
                readout,
                second_weight,
            )
        ),
    )
    relayed, occupied, field = lax.optimization_barrier((shards[: chips - 1], occupied, field))
    for step in range(1, chips):
        shifts.append((step, 1))
        shards.append(shift(relayed[step - 1], "core", 1))
    shifts.append((0, 0))
    stack = jnp.concatenate([occupied[None], moved.astype(BF16)], axis=0)
    moved = swap(stack, "samples", bits[1])

    send, second = call(
        functools.partial(slot_energy_kernel, tuple(shifts)),
        5 + len(shifts),
        (
            jax.ShapeDtypeStruct((blocks * chips, 1, 2 * here), F32),
            jax.ShapeDtypeStruct((wide, narrow), BF16),
        ),
        name="slot_energy",
        flops=2 * (slots + here) * wide * narrow,
        transcendentals=(slots + here) * narrow,
    )(field, hidden, owner, elements, readout_near, *shards, own_shard)
    received = exchange_all(send)
    mine = call(
        functools.partial(collect_kernel, entries, chips),
        1,
        jax.ShapeDtypeStruct((2, total), F32),
        name="collect",
        flops=COLLECT_WEIGHT,
    )(received)
    other = swap(mine, "core", 1)

    for bit in bits[2:-1]:
        stack = jnp.concatenate([stack, moved], axis=0)
        moved = swap(stack, "samples", bit)
    if total > wide:
        stack = jnp.concatenate([stack, moved], axis=0)
        stack = jnp.concatenate([stack, swap(stack, "samples", bits[-1])], axis=0)
        return wide_solve(mine + other, stack, first_weight, bias_row, second, readout)

    half = total // 2
    weights = (w1, bias, second, readout_near)
    full = orbitals // 128 * 128
    packed = call(
        pack_kernel,
        3,
        jax.ShapeDtypeStruct((half + here, full), BF16),
        name="pack",
    )(stack, moved, second)
    far_packed = swap(packed, "samples", bits[-1])
    near = call(
        near_half_kernel,
        5,
        (
            jax.ShapeDtypeStruct((half, wide), BF16),
            jax.ShapeDtypeStruct((half, half), F32),
            jax.ShapeDtypeStruct((narrow, half), F32),
            jax.ShapeDtypeStruct((narrow, half), F32),
        ),
        name="near_half",
        flops=2 * half * wide * (orbitals + narrow + half),
        transcendentals=half * (wide + narrow),
    )(packed, *weights)
    overlap = call(
        far_half_kernel,
        9,
        (jax.ShapeDtypeStruct((3 * total, total), BF16),) + (jax.ShapeDtypeStruct((narrow, total), F32),) * 2,
        name="far_half",
        flops=2 * half * wide * (orbitals + narrow + 3 * half),
        transcendentals=half * (wide + narrow),
    )(far_packed, *weights, *near)
    return call(
        solve_kernel,
        5,
        (jax.ShapeDtypeStruct((2, here), F32),) * 2,
        name="solve",
        flops=ITERS * 6 * total * total * narrow,
    )(mine, other, *overlap)


def solution(mesh):
    blocks, spread = mesh.shape["samples"], mesh.shape["params"]
    fine = Mesh(mesh.devices.reshape(blocks, spread // 2, 2), ("samples", "chip", "core"))
    return jax.shard_map(
        body,
        mesh=fine,
        in_specs=(
            P("samples", None),
            P("samples"),
            P(None, ("samples", "chip", "core")),
            P(None, ("samples", "chip", "core")),
            P(),
            P(),
            P(),
            P(("chip", "core"), None),
            P(),
        ),
        out_specs=(P(None, "samples"), P(None, "samples")),
        check_vma=False,
    )
```

```python
import functools

import jax
import jax.numpy as jnp
from jax import lax
from jax.experimental import pallas as pl
from jax.experimental.pallas import tpu as pltpu
from jax.sharding import Mesh, PartitionSpec as P

ITERS = 2


FIELD_SCALE = 0.8
FIELD_RATE = 0.0123
DIAG_SHIFT = 0.01
F32 = jnp.float32
BF16 = jnp.bfloat16
ROWS = 256
COLLECT_WEIGHT = 1e10
VMEM_LIMIT = 48 * 1024 * 1024


def dot(a, b, dims):
    return lax.dot_general(a, b, (dims, ((), ())), preferred_element_type=F32)


def split(x):
    high = lax.reduce_precision(x, 8, 7)
    return high.astype(BF16), (x - high).astype(BF16)


def parts(x):
    high = x.astype(BF16)
    rest = x - high.astype(F32)
    middle = rest.astype(BF16)
    return high, middle, (rest - middle.astype(F32)).astype(BF16)


def iota(shape, dim):
    return lax.broadcasted_iota(jnp.int32, shape, dim)


def call(kernel, count, out_shape, scratch=(), name=None, copies=False, flops=0, transcendentals=0):
    vmem = pl.BlockSpec(memory_space=pltpu.VMEM)
    far = pl.BlockSpec(memory_space=pltpu.HBM)
    return pl.pallas_call(
        kernel,
        out_shape=out_shape,
        in_specs=[far if copies else vmem] * count,
        out_specs=jax.tree.map(lambda _: vmem, out_shape),
        scratch_shapes=scratch,
        compiler_params=pltpu.CompilerParams(vmem_limit_bytes=VMEM_LIMIT),
        cost_estimate=pl.CostEstimate(
            flops=int(flops),
            transcendentals=int(transcendentals),
            bytes_accessed=sum(x.size * x.dtype.itemsize for x in jax.tree.leaves(out_shape)),
        ),
        name=name,
    )


def slot_hidden_kernel(
    spread,
    counts_hbm,
    orbitals_hbm,
    occ_hbm,
    w1_hbm,
    bias_hbm,
    elements_hbm,
    readout_hbm,
    own_hbm,
    hidden_ref,
    owner_ref,
    elements_ref,
    w1_ref,
    bias_ref,
    readout_ref,
    own_ref,
    occupied_ref,
    counts_ref,
    orbitals_ref,
    occ_ref,
    sems,
):
    here, orbitals = occ_ref.shape
    updates, slots = orbitals_ref.shape
    pairs = (
        (counts_hbm, counts_ref),
        (occ_hbm, occ_ref),
        (w1_hbm, w1_ref),
        (bias_hbm, bias_ref),
        (orbitals_hbm, orbitals_ref),
        (elements_hbm, elements_ref),
        (readout_hbm, readout_ref),
        (own_hbm, own_ref),
    )
    copies = [pltpu.make_async_copy(a, b, sems.at[i]) for i, (a, b) in enumerate(pairs)]
    for copy in copies:
        copy.start()
    chip, core = lax.axis_index("chip"), lax.axis_index("core")
    place = chip * 2 + core
    copies[0].wait()
    counts = counts_ref[...].astype(F32)
    row, col = iota((here, here), 0), iota((here, here), 1)
    ends = jnp.sum(jnp.where(col <= row, counts, 0.0), axis=1, keepdims=True)
    starts = jnp.sum(jnp.where(col < row, counts, 0.0), axis=1, keepdims=True)
    positions = (place + spread * iota((1, slots), 1)).astype(F32)
    owner = jnp.where((starts <= positions) & (positions < ends), 1.0, 0.0).astype(BF16)
    owner_ref[...] = owner
    copies[1].wait()
    occupied = occ_ref[...].astype(F32).astype(BF16)
    occupied_ref[...] = occupied
    copies[2].wait()
    copies[3].wait()
    w1 = w1_ref[...]
    bias = bias_ref[...]
    hidden_ref[slots:, :] = jnp.tanh(dot(occupied, w1, ((1,), (0,))) + bias).astype(BF16)
    copies[4].wait()
    for start in range(0, slots, ROWS):
        stop = min(start + ROWS, slots)
        parent_occ = dot(occupied, owner[:, start:stop], ((0,), (0,)))
        columns = iota((orbitals, stop - start), 0)
        flipped = columns == orbitals_ref[0:1, start:stop]
        for u in range(1, updates):
            flipped = flipped | (columns == orbitals_ref[u : u + 1, start:stop])
        slot_occ = jnp.where(flipped, 1.0 - parent_occ, parent_occ).astype(BF16)
        pre = dot(slot_occ, w1, ((0,), (0,))) + bias
        hidden_ref[start:stop, :] = jnp.tanh(pre).astype(BF16)
    copies[5].wait()
    copies[6].wait()
    copies[7].wait()


def slot_energy_kernel(
    shifts, field_ref, hidden_ref, owner_ref, elements_ref, readout_ref, *refs
):
    shard_refs, (send_ref, second_ref) = refs[: len(shifts)], refs[len(shifts) :]
    here, slots = owner_ref.shape
    chips = lax.axis_size("chip")
    chip, core = lax.axis_index("chip"), lax.axis_index("core")
    for (step, other), shard in zip(shifts, shard_refs):
        rows = shard.shape[0]
        source = lax.rem(chip + chips - step, chips) * 2 + (core ^ other)
        second_ref[pl.ds(pl.multiple_of(source * rows, rows), rows), :] = shard[...]
    mid = jnp.tanh(dot(second_ref[...], hidden_ref[...], ((0,), (1,))))
    readout = readout_ref[...].T
    logs_re = jnp.sum(mid * readout[:, 0:1], axis=0, keepdims=True)
    logs_im = jnp.sum(mid * readout[:, 1:2], axis=0, keepdims=True)
    owner = owner_ref[...]
    own = jnp.concatenate(parts(logs_re[:, slots:]) + parts(logs_im[:, slots:]), axis=0)
    parent = dot(own, owner, ((1,), (0,)))
    diff_re = logs_re[:, :slots] - (parent[0:1] + parent[1:2] + parent[2:3])
    diff_im = logs_im[:, :slots] - (parent[3:4] + parent[4:5] + parent[5:6])
    used = jnp.sum(owner.astype(F32), axis=0, keepdims=True) > 0.0
    weight = elements_ref[0:1, :] + field_ref[...] * elements_ref[1:2, :]
    scale = weight * jnp.exp(diff_re)
    contrib_re = jnp.where(used, scale * jnp.cos(diff_im), 0.0)
    contrib_im = jnp.where(used, scale * jnp.sin(diff_im), 0.0)
    contrib = jnp.concatenate(parts(contrib_re) + parts(contrib_im), axis=0)
    sums = dot(contrib, owner, ((1,), (1,)))
    partial_re = sums[0:1] + sums[1:2] + sums[2:3]
    partial_im = sums[3:4] + sums[4:5] + sums[5:6]
    row = jnp.concatenate([partial_re, partial_im], axis=1)
    send_ref[...] = jnp.broadcast_to(row[None], send_ref.shape)


def collect_kernel(entries, chips, received_ref, energy_ref):
    here = received_ref.shape[2] // 2
    block = lax.axis_index("samples")
    out_re, out_im = [], []
    peers = received_ref.shape[0]
    for entry in entries:
        first = lax.rem((block ^ entry) * chips + peers // 2, peers)
        row = received_ref[first]
        for k in range(1, chips):
            row = row + received_ref[first + k]
        out_re.append(row[:, :here])
        out_im.append(row[:, here:])
    energy_ref[...] = jnp.concatenate(
        [jnp.concatenate(out_re, axis=1), jnp.concatenate(out_im, axis=1)], axis=0
    )


def sample_values(packed_ref, w1_ref, bias_ref, second_ref, readout_ref, size):
    hidden = jnp.tanh(sample_pre(packed_ref, w1_ref, bias_ref, size)).astype(BF16)
    mid = jnp.tanh(dot(second_ref[...], hidden, ((0,), (1,))))
    slope = 1.0 - mid * mid
    readout = readout_ref[...].T
    return hidden, slope * readout[:, 0:1], slope * readout[:, 1:2]


def pack_kernel(mine_ref, moved_ref, after_ref, packed_ref):
    del after_ref
    blocks, here, orbitals = mine_ref.shape
    full = packed_ref.shape[1]
    pieces = [mine_ref[k] for k in range(blocks)] + [moved_ref[k] for k in range(blocks)]
    rest = orbitals - full
    for k, piece in enumerate(pieces):
        packed_ref[k * here : (k + 1) * here, :] = piece[:, :full]
    rests = [piece[:, full:].astype(F32) for piece in pieces]
    rests.append(jnp.zeros((here, full - rest * len(pieces)), F32))
    packed_ref[len(pieces) * here :, :] = jnp.concatenate(rests, axis=1).astype(BF16)


def sample_pre(packed_ref, w1_ref, bias_ref, size):
    full = packed_ref.shape[1]
    here = packed_ref.shape[0] - size
    rest = w1_ref.shape[0] - full
    tail = packed_ref[size:, :].astype(F32)
    rests = [tail[:, k * rest : (k + 1) * rest] for k in range(size // here)]
    tail = jnp.concatenate(rests, axis=0).astype(BF16)
    pre = dot(packed_ref[:size, :], w1_ref[:full, :], ((1,), (0,)))
    return pre + dot(tail, w1_ref[full:, :], ((1,), (0,))) + bias_ref[...]


def near_half_kernel(packed_ref, w1_ref, bias_ref, second_ref, readout_ref, hidden_ref, overlap_ref, re_ref, im_ref):
    size = hidden_ref.shape[0]
    hidden, re_ref[...], im_ref[...] = sample_values(packed_ref, w1_ref, bias_ref, second_ref, readout_ref, size)
    hidden_ref[...] = hidden
    overlap_ref[...] = dot(hidden, hidden, ((1,), (1,)))


def far_half_kernel(
    packed_ref,
    w1_ref,
    bias_ref,
    second_ref,
    readout_ref,
    hidden_ref,
    overlap_ref,
    near_re_ref,
    near_im_ref,
    overlap_out_ref,
    re_ref,
    im_ref,
):
    size = hidden_ref.shape[0]
    total = 2 * size
    hidden, re, im = sample_values(packed_ref, w1_ref, bias_ref, second_ref, readout_ref, size)
    re_ref[:, :size] = near_re_ref[...]
    im_ref[:, :size] = near_im_ref[...]
    re_ref[:, size:] = re
    im_ref[:, size:] = im
    near = hidden_ref[...]

    def put(row, col, overlap):
        high = overlap.astype(BF16)
        columns = slice(col * size, (col + 1) * size)
        overlap_out_ref[row * size : (row + 1) * size, columns] = high
        low = (overlap - high.astype(F32)).astype(BF16)
        overlap_out_ref[total + row * size : total + (row + 1) * size, columns] = low
        overlap_out_ref[2 * total + row * size : 2 * total + (row + 1) * size, columns] = high

    put(0, 0, overlap_ref[...])
    put(0, 1, dot(near, hidden, ((1,), (1,))))
    put(1, 0, dot(hidden, near, ((1,), (1,))))
    put(1, 1, dot(hidden, hidden, ((1,), (1,))))


def solve(energy, gram):
    total = energy.shape[1]
    centered = energy - jnp.mean(energy, axis=1, keepdims=True)
    res_c = jnp.concatenate([centered[1:2], -centered[0:1]], axis=0) / total
    res_y = gram(res_c)
    dir_c, dir_y = res_c, res_y
    norm_now = full_sum(res_c * res_y)
    cross, square = norm_now, full_sum(res_y * res_y)
    change = jnp.zeros_like(res_y)
    for turn in range(ITERS):
        alpha = norm_now / (square / total + DIAG_SHIFT * cross)
        change = change + alpha * dir_y
        if turn + 1 < ITERS:
            img_c = dir_y / total + DIAG_SHIFT * dir_c
            img_y = gram(dir_y) / total + DIAG_SHIFT * dir_y
            res_c = res_c - alpha * img_c
            res_y = res_y - alpha * img_y
            norm_next = full_sum(res_c * res_y)
            mixed = full_sum(res_c * dir_y) + full_sum(dir_c * res_y)
            squares = full_sum(res_y * res_y), full_sum(res_y * dir_y)
            beta = norm_next / norm_now
            cross = norm_next + beta * mixed + beta * beta * cross
            square = squares[0] + 2.0 * beta * squares[1] + beta * beta * square
            dir_c = res_c + beta * dir_c
            dir_y = res_y + beta * dir_y
            norm_now = norm_next
    return change


def full_sum(x):
    return jnp.sum(jnp.sum(x, axis=1, keepdims=True), axis=0, keepdims=True)


def project(lifted, slope_re, slope_im):
    raw = jnp.concatenate(
        [jnp.sum(lifted * slope_re, axis=0, keepdims=True), jnp.sum(lifted * slope_im, axis=0, keepdims=True)],
        axis=0,
    )
    return raw - jnp.mean(raw, axis=1, keepdims=True)


def solve_kernel(mine_ref, other_ref, overlap_ref, re_ref, im_ref, local_ref, change_ref):
    width = local_ref.shape[1]
    energy = mine_ref[...] + other_ref[...]
    local_ref[...] = energy[:, :width]

    def gram(c):
        back = re_ref[...] * c[0:1] + im_ref[...] * c[1:2]
        high = back.astype(BF16)
        low = (back - high.astype(F32)).astype(BF16)
        lifted = dot(jnp.concatenate([high, high, low], axis=1), overlap_ref[...], ((1,), (0,)))
        return project(lifted, re_ref[...], im_ref[...])

    change_ref[...] = solve(energy, gram)[:, :width]


def wide_solve(energy, occ_stack, first_weight, bias_row, second, readout):
    here = occ_stack.shape[1]
    occupied = occ_stack.reshape(-1, occ_stack.shape[2])
    pre = dot(occupied, first_weight, ((1,), (0,))) + bias_row
    hidden = jnp.tanh(pre).astype(BF16)
    mid = jnp.tanh(dot(second, hidden, ((0,), (1,))))
    slope = 1.0 - mid * mid
    slope_re = slope * readout[0][:, None]
    slope_im = slope * readout[1][:, None]

    def gram(c):
        high, low = split(slope_re * c[0:1] + slope_im * c[1:2])
        high, low = split(dot(high, hidden, ((1,), (0,))) + dot(low, hidden, ((1,), (0,))))
        lifted = dot(high, hidden, ((1,), (1,))) + dot(low, hidden, ((1,), (1,)))
        return project(lifted, slope_re, slope_im)

    return energy[:, :here], solve(energy, gram)[:, :here]


def swap(x, axis, bit):
    return lax.ppermute(x, axis, [(i, i ^ bit) for i in range(lax.axis_size(axis))])


def shift(x, axis, step):
    size = lax.axis_size(axis)
    return lax.ppermute(x, axis, [(i, (i + step) % size) for i in range(size)])


def exchange_all(send):
    peers = send.shape[0]
    return lax.all_to_all(
        send,
        ("samples", "chip"),
        0,
        0,
        axis_index_groups=[[(k + peers // 2) % peers for k in range(peers)]],
        tiled=True,
    )


def powers(size):
    return [1 << k for k in reversed(range((size - 1).bit_length()))]


def body(
    occupations,
    connection_counts,
    connection_orbitals,
    connection_elements,
    laser_step,
    first_weight,
    first_bias,
    second_weight,
    readout,
):
    here, orbitals = occupations.shape
    slots = connection_orbitals.shape[1]
    wide, narrow = first_weight.shape[1], second_weight.shape[1]
    chips = lax.axis_size("chip")
    spread = chips * lax.axis_size("core")
    blocks = lax.axis_size("samples")
    total = here * blocks
    bias_row = first_bias[None, :]
    field = FIELD_SCALE * jnp.sin(FIELD_RATE * laser_step.astype(F32)[None, None])

    bits = powers(blocks)
    bits = bits[-1:] + bits[:-1]
    entries = [0]
    for bit in bits:
        entries = entries + [e ^ bit for e in entries]
    moved = swap(occupations.astype(BF16)[None], "samples", bits[0])

    shifts, shards = [], []
    for step in range(1, chips):
        shifts.append((step, 0))
        shards.append(shift(second_weight, "chip", step))
    shifts.append((0, 1))
    shards.append(shift(second_weight, "core", 1))

    hidden, owner, elements, w1, bias, readout_near, own_shard, occupied = call(
        functools.partial(slot_hidden_kernel, spread),
        8,
        (
            jax.ShapeDtypeStruct((slots + here, wide), BF16),
            jax.ShapeDtypeStruct((here, slots), BF16),
            jax.ShapeDtypeStruct(connection_elements.shape, F32),
            jax.ShapeDtypeStruct(first_weight.shape, BF16),
            jax.ShapeDtypeStruct(bias_row.shape, F32),
            jax.ShapeDtypeStruct(readout.shape, F32),
            jax.ShapeDtypeStruct(second_weight.shape, BF16),
            jax.ShapeDtypeStruct(occupations.shape, BF16),
        ),
        [
            pltpu.VMEM((1, here), jnp.int32),
            pltpu.VMEM(connection_orbitals.shape, jnp.int32),
            pltpu.VMEM(occupations.shape, jnp.int32),
            pltpu.SemaphoreType.DMA((8,)),
        ],
        name="slot_hidden",
        copies=True,
        flops=2 * (slots + here) * orbitals * wide,
        transcendentals=(slots + here) * wide,
    )(
        *(
            pltpu.with_memory_space_constraint(x, pltpu.HBM)
            for x in (
                connection_counts[None, :],
                connection_orbitals,
                occupations,
                first_weight,
                bias_row,
                connection_elements,
                readout,
                second_weight,
            )
        ),
    )
    relayed, occupied, field = lax.optimization_barrier((shards[: chips - 1], occupied, field))
    for step in range(1, chips):
        shifts.append((step, 1))
        shards.append(shift(relayed[step - 1], "core", 1))
    shifts.append((0, 0))
    stack = jnp.concatenate([occupied[None], moved], axis=0)
    moved = swap(stack, "samples", bits[1])

    send, second = call(
        functools.partial(slot_energy_kernel, tuple(shifts)),
        5 + len(shifts),
        (
            jax.ShapeDtypeStruct((blocks * chips, 1, 2 * here), F32),
            jax.ShapeDtypeStruct((wide, narrow), BF16),
        ),
        name="slot_energy",
        flops=2 * (slots + here) * wide * narrow,
        transcendentals=(slots + here) * narrow,
    )(field, hidden, owner, elements, readout_near, *shards, own_shard)
    received = exchange_all(send)
    mine = call(
        functools.partial(collect_kernel, entries, chips),
        1,
        jax.ShapeDtypeStruct((2, total), F32),
        name="collect",
        flops=COLLECT_WEIGHT,
    )(received)
    other = swap(mine, "core", 1)

    for bit in bits[2:-1]:
        stack = jnp.concatenate([stack, moved], axis=0)
        moved = swap(stack, "samples", bit)
    if total > wide:
        stack = jnp.concatenate([stack, moved], axis=0)
        stack = jnp.concatenate([stack, swap(stack, "samples", bits[-1])], axis=0)
        return wide_solve(mine + other, stack, first_weight, bias_row, second, readout)

    half = total // 2
    weights = (w1, bias, second, readout_near)
    full = orbitals // 128 * 128
    packed = call(
        pack_kernel,
        3,
        jax.ShapeDtypeStruct((half + here, full), BF16),
        name="pack",
    )(stack, moved, second)
    far_packed = swap(packed, "samples", bits[-1])
    near = call(
        near_half_kernel,
        5,
        (
            jax.ShapeDtypeStruct((half, wide), BF16),
            jax.ShapeDtypeStruct((half, half), F32),
            jax.ShapeDtypeStruct((narrow, half), F32),
            jax.ShapeDtypeStruct((narrow, half), F32),
        ),
        name="near_half",
        flops=2 * half * wide * (orbitals + narrow + half),
        transcendentals=half * (wide + narrow),
    )(packed, *weights)
    overlap = call(
        far_half_kernel,
        9,
        (jax.ShapeDtypeStruct((3 * total, total), BF16),) + (jax.ShapeDtypeStruct((narrow, total), F32),) * 2,
        name="far_half",
        flops=2 * half * wide * (orbitals + narrow + 3 * half),
        transcendentals=half * (wide + narrow),
    )(far_packed, *weights, *near)
    return call(
        solve_kernel,
        5,
        (jax.ShapeDtypeStruct((2, here), F32),) * 2,
        name="solve",
        flops=ITERS * 6 * total * total * narrow,
    )(mine, other, *overlap)


def solution(mesh):
    blocks, spread = mesh.shape["samples"], mesh.shape["params"]
    fine = Mesh(mesh.devices.reshape(blocks, spread // 2, 2), ("samples", "chip", "core"))
    return jax.shard_map(
        body,
        mesh=fine,
        in_specs=(
            P("samples", None),
            P("samples"),
            P(None, ("samples", "chip", "core")),
            P(None, ("samples", "chip", "core")),
            P(),
            P(),
            P(),
            P(("chip", "core"), None),
            P(),
        ),
        out_specs=(P(None, "samples"), P(None, "samples")),
        check_vma=False,
    )
```

```python
import functools
import math

import jax
import jax.numpy as jnp
from jax import lax
from jax.experimental import pallas as pl
from jax.experimental.pallas import tpu as pltpu
from jax.sharding import Mesh, PartitionSpec as P

ITERS = 2


FIELD_SCALE = 0.8
FIELD_RATE = 0.0123
DIAG_SHIFT = 0.01
F32 = jnp.float32
BF16 = jnp.bfloat16
ROWS = 256
COLLECT_WEIGHT = 1e10
VMEM_LIMIT = 48 * 1024 * 1024


def dot(a, b, dims):
    return lax.dot_general(a, b, (dims, ((), ())), preferred_element_type=F32)


def split(x):
    high = lax.reduce_precision(x, 8, 7)
    return high.astype(BF16), (x - high).astype(BF16)


def parts(x):
    high = x.astype(BF16)
    rest = x - high.astype(F32)
    middle = rest.astype(BF16)
    return high, middle, (rest - middle.astype(F32)).astype(BF16)


def iota(shape, dim):
    return lax.broadcasted_iota(jnp.int32, shape, dim)


def call(kernel, count, out_shape, scratch=(), name=None, copies=False, flops=0, transcendentals=0):
    vmem = pl.BlockSpec(memory_space=pltpu.VMEM)
    far = pl.BlockSpec(memory_space=pltpu.HBM)
    return pl.pallas_call(
        kernel,
        out_shape=out_shape,
        in_specs=[far if copies else vmem] * count,
        out_specs=jax.tree.map(lambda _: vmem, out_shape),
        scratch_shapes=scratch,
        compiler_params=pltpu.CompilerParams(vmem_limit_bytes=VMEM_LIMIT),
        cost_estimate=pl.CostEstimate(
            flops=int(flops),
            transcendentals=int(transcendentals),
            bytes_accessed=sum(x.size * x.dtype.itemsize for x in jax.tree.leaves(out_shape)),
        ),
        name=name,
    )


def slot_hidden_kernel(
    spread,
    counts_hbm,
    orbitals_hbm,
    occ_hbm,
    w1_hbm,
    bias_hbm,
    elements_hbm,
    readout_hbm,
    own_hbm,
    hidden_ref,
    owner_ref,
    elements_ref,
    w1_ref,
    bias_ref,
    readout_ref,
    own_ref,
    occupied_ref,
    counts_ref,
    orbitals_ref,
    occ_ref,
    sems,
):
    here, orbitals = occ_ref.shape
    updates, slots = orbitals_ref.shape
    pairs = (
        (counts_hbm, counts_ref),
        (occ_hbm, occ_ref),
        (w1_hbm, w1_ref),
        (bias_hbm, bias_ref),
        (orbitals_hbm, orbitals_ref),
        (elements_hbm, elements_ref),
        (readout_hbm, readout_ref),
        (own_hbm, own_ref),
    )
    copies = [pltpu.make_async_copy(a, b, sems.at[i]) for i, (a, b) in enumerate(pairs)]
    for copy in copies:
        copy.start()
    chip, core = lax.axis_index("chip"), lax.axis_index("core")
    place = chip * 2 + core
    copies[0].wait()
    counts = counts_ref[...].astype(F32)
    row, col = iota((here, here), 0), iota((here, here), 1)
    ends = jnp.sum(jnp.where(col <= row, counts, 0.0), axis=1, keepdims=True)
    starts = jnp.sum(jnp.where(col < row, counts, 0.0), axis=1, keepdims=True)
    positions = (place + spread * iota((1, slots), 1)).astype(F32)
    owner = jnp.where((starts <= positions) & (positions < ends), 1.0, 0.0).astype(BF16)
    owner_ref[...] = owner
    copies[1].wait()
    occupied = occ_ref[...].astype(F32).astype(BF16)
    occupied_ref[...] = occupied
    copies[2].wait()
    copies[3].wait()
    w1 = w1_ref[...]
    bias = bias_ref[...]
    hidden_ref[slots:, :] = jnp.tanh(dot(occupied, w1, ((1,), (0,))) + bias).astype(BF16)
    copies[4].wait()
    for start in range(0, slots, ROWS):
        stop = min(start + ROWS, slots)
        parent_occ = dot(occupied, owner[:, start:stop], ((0,), (0,)))
        columns = iota((orbitals, stop - start), 0)
        flipped = columns == orbitals_ref[0:1, start:stop]
        for u in range(1, updates):
            flipped = flipped | (columns == orbitals_ref[u : u + 1, start:stop])
        slot_occ = jnp.where(flipped, 1.0 - parent_occ, parent_occ).astype(BF16)
        pre = dot(slot_occ, w1, ((0,), (0,))) + bias
        hidden_ref[start:stop, :] = jnp.tanh(pre).astype(BF16)
    copies[5].wait()
    copies[6].wait()
    copies[7].wait()


def sine_cosine(x):
    turns = jnp.floor(x * (2.0 / math.pi) + 0.5)
    rest = ((x - turns * 1.5703125) - turns * 4.837512969970703125e-4) - turns * 7.549789948768648e-8
    square = rest * rest
    sine = (-1.9515295891e-4 * square + 8.3321608736e-3) * square - 1.6666654611e-1
    sine = rest + rest * square * sine
    cosine = (2.443315711809948e-5 * square - 1.388731625493765e-3) * square + 4.166664568298827e-2
    cosine = 1.0 - 0.5 * square + square * square * cosine
    quarter = turns.astype(jnp.int32) & 3
    odd = (quarter & 1) == 1
    high_sine = jnp.where(odd, cosine, sine)
    high_cosine = jnp.where(odd, sine, cosine)
    sine = jnp.where(quarter >= 2, -high_sine, high_sine)
    cosine = jnp.where((quarter == 1) | (quarter == 2), -high_cosine, high_cosine)
    return sine, cosine


def slot_energy_kernel(
    shifts, field_ref, hidden_ref, owner_ref, elements_ref, readout_ref, *refs
):
    shard_refs, (send_ref, turned_ref, second_scratch) = refs[: len(shifts)], refs[len(shifts) :]
    here, slots = owner_ref.shape
    chips = lax.axis_size("chip")
    chip, core = lax.axis_index("chip"), lax.axis_index("core")
    for (step, other), shard in zip(shifts, shard_refs):
        rows = shard.shape[0]
        source = lax.rem(chip + chips - step, chips) * 2 + (core ^ other)
        second_scratch[pl.ds(pl.multiple_of(source * rows, rows), rows), :] = shard[...]
    turned = second_scratch[...].T
    turned_ref[...] = turned
    readout = readout_ref[...].T
    readout_re, readout_im = readout[:, 0:1], readout[:, 1:2]
    owner = owner_ref[...]
    field = field_ref[...]

    def logs(start, stop):
        mid = jnp.tanh(dot(turned, hidden_ref[start:stop, :], ((1,), (1,))))
        re = jnp.sum(mid * readout_re, axis=0, keepdims=True)
        return re, jnp.sum(mid * readout_im, axis=0, keepdims=True)

    own_re, own_im = logs(slots, slots + here)
    parent = dot(jnp.concatenate(parts(own_re) + parts(own_im), axis=0), owner, ((1,), (0,)))
    parent_re = parent[0:1] + parent[1:2] + parent[2:3]
    parent_im = parent[3:4] + parent[4:5] + parent[5:6]
    used = jnp.sum(owner.astype(F32), axis=0, keepdims=True) > 0.0
    weight = elements_ref[0:1, :] + field * elements_ref[1:2, :]
    sums = jnp.zeros((6, here), F32)
    for start in range(0, slots, ROWS):
        stop = min(start + ROWS, slots)
        log_re, log_im = logs(start, stop)
        scale = weight[:, start:stop] * jnp.exp(log_re - parent_re[:, start:stop])
        sine, cosine = sine_cosine(log_im - parent_im[:, start:stop])
        inside = used[:, start:stop]
        contrib_re = jnp.where(inside, scale * cosine, 0.0)
        contrib_im = jnp.where(inside, scale * sine, 0.0)
        contrib = jnp.concatenate(parts(contrib_re) + parts(contrib_im), axis=0)
        sums = sums + dot(contrib, owner[:, start:stop], ((1,), (1,)))
    partial_re = sums[0:1] + sums[1:2] + sums[2:3]
    partial_im = sums[3:4] + sums[4:5] + sums[5:6]
    row = jnp.concatenate([partial_re, partial_im], axis=1)
    send_ref[...] = jnp.broadcast_to(row[None], send_ref.shape)


def collect_kernel(entries, chips, received_ref, energy_ref):
    here = received_ref.shape[2] // 2
    block = lax.axis_index("samples")
    out_re, out_im = [], []
    peers = received_ref.shape[0]
    for entry in entries:
        first = lax.rem((block ^ entry) * chips + peers // 2, peers)
        row = received_ref[first]
        for k in range(1, chips):
            row = row + received_ref[first + k]
        out_re.append(row[:, :here])
        out_im.append(row[:, here:])
    energy_ref[...] = jnp.concatenate(
        [jnp.concatenate(out_re, axis=1), jnp.concatenate(out_im, axis=1)], axis=0
    )


def sample_values(packed_ref, w1_ref, bias_ref, turned_ref, readout_ref, size):
    hidden = jnp.tanh(sample_pre(packed_ref, w1_ref, bias_ref, size)).astype(BF16)
    mid = jnp.tanh(dot(turned_ref[...], hidden, ((1,), (1,))))
    slope = 1.0 - mid * mid
    readout = readout_ref[...].T
    return hidden, slope * readout[:, 0:1], slope * readout[:, 1:2]


def pack_kernel(mine_ref, moved_ref, after_ref, packed_ref):
    del after_ref
    blocks, here, orbitals = mine_ref.shape
    full = packed_ref.shape[1]
    pieces = [mine_ref[k] for k in range(blocks)] + [moved_ref[k] for k in range(blocks)]
    rest = orbitals - full
    for k, piece in enumerate(pieces):
        packed_ref[k * here : (k + 1) * here, :] = piece[:, :full]
    rests = [piece[:, full:].astype(F32) for piece in pieces]
    rests.append(jnp.zeros((here, full - rest * len(pieces)), F32))
    packed_ref[len(pieces) * here :, :] = jnp.concatenate(rests, axis=1).astype(BF16)


def sample_pre(packed_ref, w1_ref, bias_ref, size):
    full = packed_ref.shape[1]
    here = packed_ref.shape[0] - size
    rest = w1_ref.shape[0] - full
    tail = packed_ref[size:, :].astype(F32)
    rests = [tail[:, k * rest : (k + 1) * rest] for k in range(size // here)]
    tail = jnp.concatenate(rests, axis=0).astype(BF16)
    pre = dot(packed_ref[:size, :], w1_ref[:full, :], ((1,), (0,)))
    return pre + dot(tail, w1_ref[full:, :], ((1,), (0,))) + bias_ref[...]


def near_half_kernel(packed_ref, w1_ref, bias_ref, turned_ref, readout_ref, hidden_ref, overlap_ref, re_ref, im_ref):
    size = hidden_ref.shape[0]
    hidden, re_ref[...], im_ref[...] = sample_values(packed_ref, w1_ref, bias_ref, turned_ref, readout_ref, size)
    hidden_ref[...] = hidden
    overlap_ref[...] = dot(hidden, hidden, ((1,), (1,)))


def far_half_kernel(
    packed_ref,
    w1_ref,
    bias_ref,
    turned_ref,
    readout_ref,
    hidden_ref,
    overlap_ref,
    near_re_ref,
    near_im_ref,
    overlap_out_ref,
    re_ref,
    im_ref,
):
    size = hidden_ref.shape[0]
    total = 2 * size
    hidden, re, im = sample_values(packed_ref, w1_ref, bias_ref, turned_ref, readout_ref, size)
    re_ref[:, :size] = near_re_ref[...]
    im_ref[:, :size] = near_im_ref[...]
    re_ref[:, size:] = re
    im_ref[:, size:] = im
    near = hidden_ref[...]

    def put(row, col, overlap):
        high = overlap.astype(BF16)
        columns = slice(col * size, (col + 1) * size)
        overlap_out_ref[row * size : (row + 1) * size, columns] = high
        low = (overlap - high.astype(F32)).astype(BF16)
        overlap_out_ref[total + row * size : total + (row + 1) * size, columns] = low
        overlap_out_ref[2 * total + row * size : 2 * total + (row + 1) * size, columns] = high

    put(0, 0, overlap_ref[...])
    put(0, 1, dot(near, hidden, ((1,), (1,))))
    put(1, 0, dot(hidden, near, ((1,), (1,))))
    put(1, 1, dot(hidden, hidden, ((1,), (1,))))


def solve(energy, gram):
    total = energy.shape[1]
    centered = energy - jnp.mean(energy, axis=1, keepdims=True)
    res_c = jnp.concatenate([centered[1:2], -centered[0:1]], axis=0) / total
    res_y = gram(res_c)
    dir_c, dir_y = res_c, res_y
    norm_now = full_sum(res_c * res_y)
    cross, square = norm_now, full_sum(res_y * res_y)
    change = jnp.zeros_like(res_y)
    for turn in range(ITERS):
        alpha = norm_now / (square / total + DIAG_SHIFT * cross)
        change = change + alpha * dir_y
        if turn + 1 < ITERS:
            img_c = dir_y / total + DIAG_SHIFT * dir_c
            img_y = gram(dir_y) / total + DIAG_SHIFT * dir_y
            res_c = res_c - alpha * img_c
            res_y = res_y - alpha * img_y
            norm_next = full_sum(res_c * res_y)
            mixed = full_sum(res_c * dir_y) + full_sum(dir_c * res_y)
            squares = full_sum(res_y * res_y), full_sum(res_y * dir_y)
            beta = norm_next / norm_now
            cross = norm_next + beta * mixed + beta * beta * cross
            square = squares[0] + 2.0 * beta * squares[1] + beta * beta * square
            dir_c = res_c + beta * dir_c
            dir_y = res_y + beta * dir_y
            norm_now = norm_next
    return change


def full_sum(x):
    return jnp.sum(jnp.sum(x, axis=1, keepdims=True), axis=0, keepdims=True)


def project(lifted, slope_re, slope_im):
    raw = jnp.concatenate(
        [jnp.sum(lifted * slope_re, axis=0, keepdims=True), jnp.sum(lifted * slope_im, axis=0, keepdims=True)],
        axis=0,
    )
    return raw - jnp.mean(raw, axis=1, keepdims=True)


def solve_kernel(mine_ref, other_ref, overlap_ref, re_ref, im_ref, local_ref, change_ref):
    width = local_ref.shape[1]
    energy = mine_ref[...] + other_ref[...]
    local_ref[...] = energy[:, :width]

    def gram(c):
        back = re_ref[...] * c[0:1] + im_ref[...] * c[1:2]
        high = back.astype(BF16)
        low = (back - high.astype(F32)).astype(BF16)
        lifted = dot(jnp.concatenate([high, high, low], axis=1), overlap_ref[...], ((1,), (0,)))
        return project(lifted, re_ref[...], im_ref[...])

    change_ref[...] = solve(energy, gram)[:, :width]


def wide_solve(energy, occ_stack, first_weight, bias_row, turned, readout):
    here = occ_stack.shape[1]
    occupied = occ_stack.reshape(-1, occ_stack.shape[2])
    pre = dot(occupied, first_weight, ((1,), (0,))) + bias_row
    hidden = jnp.tanh(pre).astype(BF16)
    mid = jnp.tanh(dot(turned, hidden, ((1,), (1,))))
    slope = 1.0 - mid * mid
    slope_re = slope * readout[0][:, None]
    slope_im = slope * readout[1][:, None]

    def gram(c):
        high, low = split(slope_re * c[0:1] + slope_im * c[1:2])
        high, low = split(dot(high, hidden, ((1,), (0,))) + dot(low, hidden, ((1,), (0,))))
        lifted = dot(high, hidden, ((1,), (1,))) + dot(low, hidden, ((1,), (1,)))
        return project(lifted, slope_re, slope_im)

    return energy[:, :here], solve(energy, gram)[:, :here]


def swap(x, axis, bit):
    return lax.ppermute(x, axis, [(i, i ^ bit) for i in range(lax.axis_size(axis))])


def shift(x, axis, step):
    size = lax.axis_size(axis)
    return lax.ppermute(x, axis, [(i, (i + step) % size) for i in range(size)])


def exchange_all(send):
    peers = send.shape[0]
    return lax.all_to_all(
        send,
        ("samples", "chip"),
        0,
        0,
        axis_index_groups=[[(k + peers // 2) % peers for k in range(peers)]],
        tiled=True,
    )


def powers(size):
    return [1 << k for k in reversed(range((size - 1).bit_length()))]


def body(
    occupations,
    connection_counts,
    connection_orbitals,
    connection_elements,
    laser_step,
    first_weight,
    first_bias,
    second_weight,
    readout,
):
    here, orbitals = occupations.shape
    slots = connection_orbitals.shape[1]
    wide, narrow = first_weight.shape[1], second_weight.shape[1]
    chips = lax.axis_size("chip")
    spread = chips * lax.axis_size("core")
    blocks = lax.axis_size("samples")
    total = here * blocks
    bias_row = first_bias[None, :]
    field = FIELD_SCALE * jnp.sin(FIELD_RATE * laser_step.astype(F32)[None, None])

    bits = powers(blocks)
    bits = bits[-1:] + bits[:-1]
    entries = [0]
    for bit in bits:
        entries = entries + [e ^ bit for e in entries]
    moved = swap(occupations.astype(BF16)[None], "samples", bits[0])

    shifts, shards = [], []
    for step in range(1, chips):
        shifts.append((step, 0))
        shards.append(shift(second_weight, "chip", step))
    shifts.append((0, 1))
    shards.append(shift(second_weight, "core", 1))

    hidden, owner, elements, w1, bias, readout_near, own_shard, occupied = call(
        functools.partial(slot_hidden_kernel, spread),
        8,
        (
            jax.ShapeDtypeStruct((slots + here, wide), BF16),
            jax.ShapeDtypeStruct((here, slots), BF16),
            jax.ShapeDtypeStruct(connection_elements.shape, F32),
            jax.ShapeDtypeStruct(first_weight.shape, BF16),
            jax.ShapeDtypeStruct(bias_row.shape, F32),
            jax.ShapeDtypeStruct(readout.shape, F32),
            jax.ShapeDtypeStruct(second_weight.shape, BF16),
            jax.ShapeDtypeStruct(occupations.shape, BF16),
        ),
        [
            pltpu.VMEM((1, here), jnp.int32),
            pltpu.VMEM(connection_orbitals.shape, jnp.int32),
            pltpu.VMEM(occupations.shape, jnp.int32),
            pltpu.SemaphoreType.DMA((8,)),
        ],
        name="slot_hidden",
        copies=True,
        flops=2 * (slots + here) * orbitals * wide,
        transcendentals=(slots + here) * wide,
    )(
        *(
            pltpu.with_memory_space_constraint(x, pltpu.HBM)
            for x in (
                connection_counts[None, :],
                connection_orbitals,
                occupations,
                first_weight,
                bias_row,
                connection_elements,
                readout,
                second_weight,
            )
        ),
    )
    relayed, occupied, field = lax.optimization_barrier((shards[: chips - 1], occupied, field))
    for step in range(1, chips):
        shifts.append((step, 1))
        shards.append(shift(relayed[step - 1], "core", 1))
    shifts.append((0, 0))
    stack = jnp.concatenate([occupied[None], moved], axis=0)
    moved = swap(stack, "samples", bits[1])

    send, turned = call(
        functools.partial(slot_energy_kernel, tuple(shifts)),
        5 + len(shifts),
        (
            jax.ShapeDtypeStruct((blocks * chips, 1, 2 * here), F32),
            jax.ShapeDtypeStruct((narrow, wide), BF16),
        ),
        [pltpu.VMEM((wide, narrow), BF16)],
        name="slot_energy",
        flops=2 * (slots + here) * wide * narrow,
        transcendentals=(slots + here) * narrow,
    )(field, hidden, owner, elements, readout_near, *shards, own_shard)
    received = exchange_all(send)
    mine = call(
        functools.partial(collect_kernel, entries, chips),
        1,
        jax.ShapeDtypeStruct((2, total), F32),
        name="collect",
        flops=COLLECT_WEIGHT,
    )(received)
    other = swap(mine, "core", 1)

    for bit in bits[2:-1]:
        stack = jnp.concatenate([stack, moved], axis=0)
        moved = swap(stack, "samples", bit)
    if total > wide:
        stack = jnp.concatenate([stack, moved], axis=0)
        stack = jnp.concatenate([stack, swap(stack, "samples", bits[-1])], axis=0)
        return wide_solve(mine + other, stack, first_weight, bias_row, turned, readout)

    half = total // 2
    weights = (w1, bias, turned, readout_near)
    full = orbitals // 128 * 128
    packed = call(
        pack_kernel,
        3,
        jax.ShapeDtypeStruct((half + here, full), BF16),
        name="pack",
    )(stack, moved, turned)
    far_packed = swap(packed, "samples", bits[-1])
    near = call(
        near_half_kernel,
        5,
        (
            jax.ShapeDtypeStruct((half, wide), BF16),
            jax.ShapeDtypeStruct((half, half), F32),
            jax.ShapeDtypeStruct((narrow, half), F32),
            jax.ShapeDtypeStruct((narrow, half), F32),
        ),
        name="near_half",
        flops=2 * half * wide * (orbitals + narrow + half),
        transcendentals=half * (wide + narrow),
    )(packed, *weights)
    overlap = call(
        far_half_kernel,
        9,
        (jax.ShapeDtypeStruct((3 * total, total), BF16),) + (jax.ShapeDtypeStruct((narrow, total), F32),) * 2,
        name="far_half",
        flops=2 * half * wide * (orbitals + narrow + 3 * half),
        transcendentals=half * (wide + narrow),
    )(far_packed, *weights, *near)
    return call(
        solve_kernel,
        5,
        (jax.ShapeDtypeStruct((2, here), F32),) * 2,
        name="solve",
        flops=ITERS * 6 * total * total * narrow,
    )(mine, other, *overlap)


def solution(mesh):
    blocks, spread = mesh.shape["samples"], mesh.shape["params"]
    fine = Mesh(mesh.devices.reshape(blocks, spread // 2, 2), ("samples", "chip", "core"))
    return jax.shard_map(
        body,
        mesh=fine,
        in_specs=(
            P("samples", None),
            P("samples"),
            P(None, ("samples", "chip", "core")),
            P(None, ("samples", "chip", "core")),
            P(),
            P(),
            P(),
            P(("chip", "core"), None),
            P(),
        ),
        out_specs=(P(None, "samples"), P(None, "samples")),
        check_vma=False,
    )
```

```python
import functools
import math

import jax
import jax.numpy as jnp
from jax import lax
from jax.experimental import pallas as pl
from jax.experimental.pallas import tpu as pltpu
from jax.sharding import Mesh, PartitionSpec as P

ITERS = 2


FIELD_SCALE = 0.8
FIELD_RATE = 0.0123
DIAG_SHIFT = 0.01
F32 = jnp.float32
BF16 = jnp.bfloat16
ROWS = 256
COLLECT_WEIGHT = 1e10
VMEM_LIMIT = 48 * 1024 * 1024


def dot(a, b, dims):
    return lax.dot_general(a, b, (dims, ((), ())), preferred_element_type=F32)


def split(x):
    high = lax.reduce_precision(x, 8, 7)
    return high.astype(BF16), (x - high).astype(BF16)


def parts(x):
    high = x.astype(BF16)
    rest = x - high.astype(F32)
    middle = rest.astype(BF16)
    return high, middle, (rest - middle.astype(F32)).astype(BF16)


def iota(shape, dim):
    return lax.broadcasted_iota(jnp.int32, shape, dim)


def call(kernel, count, out_shape, scratch=(), name=None, copies=False, flops=0, transcendentals=0):
    vmem = pl.BlockSpec(memory_space=pltpu.VMEM)
    far = pl.BlockSpec(memory_space=pltpu.HBM)
    return pl.pallas_call(
        kernel,
        out_shape=out_shape,
        in_specs=[far if copies else vmem] * count,
        out_specs=jax.tree.map(lambda _: vmem, out_shape),
        scratch_shapes=scratch,
        compiler_params=pltpu.CompilerParams(vmem_limit_bytes=VMEM_LIMIT),
        cost_estimate=pl.CostEstimate(
            flops=int(flops),
            transcendentals=int(transcendentals),
            bytes_accessed=sum(x.size * x.dtype.itemsize for x in jax.tree.leaves(out_shape)),
        ),
        name=name,
    )


def slot_hidden_kernel(
    spread,
    counts_hbm,
    orbitals_hbm,
    occ_hbm,
    w1_hbm,
    bias_hbm,
    elements_hbm,
    readout_hbm,
    own_hbm,
    hidden_ref,
    owner_ref,
    elements_ref,
    w1_ref,
    bias_ref,
    readout_ref,
    own_ref,
    occupied_ref,
    counts_ref,
    orbitals_ref,
    occ_ref,
    sems,
):
    here, orbitals = occ_ref.shape
    updates, slots = orbitals_ref.shape
    pairs = (
        (counts_hbm, counts_ref),
        (occ_hbm, occ_ref),
        (w1_hbm, w1_ref),
        (bias_hbm, bias_ref),
        (orbitals_hbm, orbitals_ref),
        (elements_hbm, elements_ref),
        (readout_hbm, readout_ref),
        (own_hbm, own_ref),
    )
    copies = [pltpu.make_async_copy(a, b, sems.at[i]) for i, (a, b) in enumerate(pairs)]
    for copy in copies:
        copy.start()
    chip, core = lax.axis_index("chip"), lax.axis_index("core")
    place = chip * 2 + core
    copies[0].wait()
    counts = counts_ref[...].astype(F32)
    row, col = iota((here, here), 0), iota((here, here), 1)
    ends = jnp.sum(jnp.where(col <= row, counts, 0.0), axis=1, keepdims=True)
    starts = jnp.sum(jnp.where(col < row, counts, 0.0), axis=1, keepdims=True)
    positions = (place + spread * iota((1, slots), 1)).astype(F32)
    owner = jnp.where((starts <= positions) & (positions < ends), 1.0, 0.0).astype(BF16)
    owner_ref[...] = owner
    copies[1].wait()
    occupied = occ_ref[...].astype(F32).astype(BF16)
    occupied_ref[...] = occupied
    copies[2].wait()
    copies[3].wait()
    w1 = w1_ref[...]
    bias = bias_ref[...]
    hidden_ref[slots:, :] = jnp.tanh(dot(occupied, w1, ((1,), (0,))) + bias).astype(BF16)
    copies[4].wait()
    for start in range(0, slots, ROWS):
        stop = min(start + ROWS, slots)
        parent_occ = dot(occupied, owner[:, start:stop], ((0,), (0,)))
        columns = iota((orbitals, stop - start), 0)
        flipped = columns == orbitals_ref[0:1, start:stop]
        for u in range(1, updates):
            flipped = flipped | (columns == orbitals_ref[u : u + 1, start:stop])
        slot_occ = jnp.where(flipped, 1.0 - parent_occ, parent_occ).astype(BF16)
        pre = dot(slot_occ, w1, ((0,), (0,))) + bias
        hidden_ref[start:stop, :] = jnp.tanh(pre).astype(BF16)
    copies[5].wait()
    copies[6].wait()
    copies[7].wait()


def sine_cosine(x):
    turns = jnp.floor(x * (2.0 / math.pi) + 0.5)
    rest = ((x - turns * 1.5703125) - turns * 4.837512969970703125e-4) - turns * 7.549789948768648e-8
    square = rest * rest
    sine = (-1.9515295891e-4 * square + 8.3321608736e-3) * square - 1.6666654611e-1
    sine = rest + rest * square * sine
    cosine = (2.443315711809948e-5 * square - 1.388731625493765e-3) * square + 4.166664568298827e-2
    cosine = 1.0 - 0.5 * square + square * square * cosine
    quarter = turns.astype(jnp.int32) & 3
    odd = (quarter & 1) == 1
    high_sine = jnp.where(odd, cosine, sine)
    high_cosine = jnp.where(odd, sine, cosine)
    sine = jnp.where(quarter >= 2, -high_sine, high_sine)
    cosine = jnp.where((quarter == 1) | (quarter == 2), -high_cosine, high_cosine)
    return sine, cosine


def slot_energy_kernel(
    shifts, field_ref, hidden_ref, owner_ref, elements_ref, readout_ref, *refs
):
    shard_refs, (send_ref, second_ref) = refs[: len(shifts)], refs[len(shifts) :]
    here, slots = owner_ref.shape
    chips = lax.axis_size("chip")
    chip, core = lax.axis_index("chip"), lax.axis_index("core")
    for (step, other), shard in zip(shifts, shard_refs):
        rows = shard.shape[0]
        source = lax.rem(chip + chips - step, chips) * 2 + (core ^ other)
        second_ref[pl.ds(pl.multiple_of(source * rows, rows), rows), :] = shard[...]
    mid = jnp.tanh(dot(second_ref[...], hidden_ref[...], ((0,), (1,))))
    readout = readout_ref[...].T
    logs_re = jnp.sum(mid * readout[:, 0:1], axis=0, keepdims=True)
    logs_im = jnp.sum(mid * readout[:, 1:2], axis=0, keepdims=True)
    owner = owner_ref[...]
    own = jnp.concatenate(parts(logs_re[:, slots:]) + parts(logs_im[:, slots:]), axis=0)
    parent = dot(own, owner, ((1,), (0,)))
    diff_re = logs_re[:, :slots] - (parent[0:1] + parent[1:2] + parent[2:3])
    diff_im = logs_im[:, :slots] - (parent[3:4] + parent[4:5] + parent[5:6])
    used = jnp.sum(owner.astype(F32), axis=0, keepdims=True) > 0.0
    weight = elements_ref[0:1, :] + field_ref[...] * elements_ref[1:2, :]
    scale = weight * jnp.exp(diff_re)
    sine, cosine = sine_cosine(diff_im)
    contrib_re = jnp.where(used, scale * cosine, 0.0)
    contrib_im = jnp.where(used, scale * sine, 0.0)
    contrib = jnp.concatenate(parts(contrib_re) + parts(contrib_im), axis=0)
    sums = dot(contrib, owner, ((1,), (1,)))
    partial_re = sums[0:1] + sums[1:2] + sums[2:3]
    partial_im = sums[3:4] + sums[4:5] + sums[5:6]
    row = jnp.concatenate([partial_re, partial_im], axis=1)
    send_ref[...] = jnp.broadcast_to(row[None], send_ref.shape)


def collect_kernel(entries, chips, received_ref, energy_ref):
    here = received_ref.shape[2] // 2
    block = lax.axis_index("samples")
    out_re, out_im = [], []
    peers = received_ref.shape[0]
    for entry in entries:
        first = lax.rem((block ^ entry) * chips + first_place(peers), peers)
        row = received_ref[first]
        for k in range(1, chips):
            row = row + received_ref[first + k]
        out_re.append(row[:, :here])
        out_im.append(row[:, here:])
    energy_ref[...] = jnp.concatenate(
        [jnp.concatenate(out_re, axis=1), jnp.concatenate(out_im, axis=1)], axis=0
    )


def sample_values(packed_ref, w1_ref, bias_ref, second_ref, readout_ref, size):
    hidden = jnp.tanh(sample_pre(packed_ref, w1_ref, bias_ref, size)).astype(BF16)
    mid = jnp.tanh(dot(second_ref[...], hidden, ((0,), (1,))))
    slope = 1.0 - mid * mid
    readout = readout_ref[...].T
    return hidden, slope * readout[:, 0:1], slope * readout[:, 1:2]


def pack_kernel(mine_ref, moved_ref, after_ref, packed_ref):
    del after_ref
    blocks, here, orbitals = mine_ref.shape
    full = packed_ref.shape[1]
    pieces = [mine_ref[k] for k in range(blocks)] + [moved_ref[k] for k in range(blocks)]
    rest = orbitals - full
    for k, piece in enumerate(pieces):
        packed_ref[k * here : (k + 1) * here, :] = piece[:, :full]
    rests = [piece[:, full:].astype(F32) for piece in pieces]
    rests.append(jnp.zeros((here, full - rest * len(pieces)), F32))
    packed_ref[len(pieces) * here :, :] = jnp.concatenate(rests, axis=1).astype(BF16)


def sample_pre(packed_ref, w1_ref, bias_ref, size):
    full = packed_ref.shape[1]
    here = packed_ref.shape[0] - size
    rest = w1_ref.shape[0] - full
    tail = packed_ref[size:, :].astype(F32)
    rests = [tail[:, k * rest : (k + 1) * rest] for k in range(size // here)]
    tail = jnp.concatenate(rests, axis=0).astype(BF16)
    pre = dot(packed_ref[:size, :], w1_ref[:full, :], ((1,), (0,)))
    return pre + dot(tail, w1_ref[full:, :], ((1,), (0,))) + bias_ref[...]


def put(overlap_ref, overlap):
    size = overlap.shape[0]
    high = overlap.astype(BF16)
    overlap_ref[:size, :] = high
    overlap_ref[size : 2 * size, :] = (overlap - high.astype(F32)).astype(BF16)
    overlap_ref[2 * size :, :] = high


def near_half_kernel(packed_ref, w1_ref, bias_ref, second_ref, readout_ref, hidden_ref, near_ref, re_ref, im_ref):
    size = hidden_ref.shape[0]
    hidden, re_ref[...], im_ref[...] = sample_values(packed_ref, w1_ref, bias_ref, second_ref, readout_ref, size)
    hidden_ref[...] = hidden
    put(near_ref, dot(hidden, hidden, ((1,), (1,))))


def far_half_kernel(
    packed_ref,
    w1_ref,
    bias_ref,
    second_ref,
    readout_ref,
    hidden_ref,
    near_far_ref,
    far_near_ref,
    far_ref,
    re_ref,
    im_ref,
):
    size = hidden_ref.shape[0]
    hidden, re_ref[...], im_ref[...] = sample_values(packed_ref, w1_ref, bias_ref, second_ref, readout_ref, size)
    near = hidden_ref[...]
    put(near_far_ref, dot(near, hidden, ((1,), (1,))))
    put(far_near_ref, dot(hidden, near, ((1,), (1,))))
    put(far_ref, dot(hidden, hidden, ((1,), (1,))))


def solve(energy, gram):
    total = energy.shape[1]
    centered = energy - jnp.mean(energy, axis=1, keepdims=True)
    res_c = jnp.concatenate([centered[1:2], -centered[0:1]], axis=0) / total
    res_y = gram(res_c)
    dir_c, dir_y = res_c, res_y
    norm_now = full_sum(res_c * res_y)
    cross, square = norm_now, full_sum(res_y * res_y)
    change = jnp.zeros_like(res_y)
    for turn in range(ITERS):
        alpha = norm_now / (square / total + DIAG_SHIFT * cross)
        change = change + alpha * dir_y
        if turn + 1 < ITERS:
            img_c = dir_y / total + DIAG_SHIFT * dir_c
            img_y = gram(dir_y) / total + DIAG_SHIFT * dir_y
            res_c = res_c - alpha * img_c
            res_y = res_y - alpha * img_y
            norm_next = full_sum(res_c * res_y)
            mixed = full_sum(res_c * dir_y) + full_sum(dir_c * res_y)
            squares = full_sum(res_y * res_y), full_sum(res_y * dir_y)
            beta = norm_next / norm_now
            cross = norm_next + beta * mixed + beta * beta * cross
            square = squares[0] + 2.0 * beta * squares[1] + beta * beta * square
            dir_c = res_c + beta * dir_c
            dir_y = res_y + beta * dir_y
            norm_now = norm_next
    return change


def full_sum(x):
    return jnp.sum(jnp.sum(x, axis=1, keepdims=True), axis=0, keepdims=True)


def project(lifted, slope_re, slope_im):
    raw = jnp.concatenate(
        [jnp.sum(lifted * slope_re, axis=0, keepdims=True), jnp.sum(lifted * slope_im, axis=0, keepdims=True)],
        axis=0,
    )
    return raw - jnp.mean(raw, axis=1, keepdims=True)


def solve_kernel(
    mine_ref,
    other_ref,
    near_ref,
    near_re_ref,
    near_im_ref,
    near_far_ref,
    far_near_ref,
    far_ref,
    far_re_ref,
    far_im_ref,
    local_ref,
    change_ref,
):
    width = local_ref.shape[1]
    half = near_ref.shape[1]
    energy = mine_ref[...] + other_ref[...]
    local_ref[...] = energy[:, :width]

    def scaled(c, re_ref, im_ref):
        back = re_ref[...] * c[0:1] + im_ref[...] * c[1:2]
        high = back.astype(BF16)
        low = (back - high.astype(F32)).astype(BF16)
        return jnp.concatenate([high, high, low], axis=1)

    def raw(lifted, re_ref, im_ref):
        re = jnp.sum(lifted * re_ref[...], axis=0, keepdims=True)
        return jnp.concatenate([re, jnp.sum(lifted * im_ref[...], axis=0, keepdims=True)], axis=0)

    def gram(c):
        near = scaled(c[:, :half], near_re_ref, near_im_ref)
        far = scaled(c[:, half:], far_re_ref, far_im_ref)
        to_near = dot(near, near_ref[...], ((1,), (0,))) + dot(far, far_near_ref[...], ((1,), (0,)))
        to_far = dot(near, near_far_ref[...], ((1,), (0,))) + dot(far, far_ref[...], ((1,), (0,)))
        both = jnp.concatenate(
            [raw(to_near, near_re_ref, near_im_ref), raw(to_far, far_re_ref, far_im_ref)], axis=1
        )
        return both - jnp.mean(both, axis=1, keepdims=True)

    change_ref[...] = solve(energy, gram)[:, :width]


def wide_solve(energy, occ_stack, first_weight, bias_row, second, readout):
    here = occ_stack.shape[1]
    occupied = occ_stack.reshape(-1, occ_stack.shape[2])
    pre = dot(occupied, first_weight, ((1,), (0,))) + bias_row
    hidden = jnp.tanh(pre).astype(BF16)
    mid = jnp.tanh(dot(second, hidden, ((0,), (1,))))
    slope = 1.0 - mid * mid
    slope_re = slope * readout[0][:, None]
    slope_im = slope * readout[1][:, None]

    def gram(c):
        high, low = split(slope_re * c[0:1] + slope_im * c[1:2])
        high, low = split(dot(high, hidden, ((1,), (0,))) + dot(low, hidden, ((1,), (0,))))
        lifted = dot(high, hidden, ((1,), (1,))) + dot(low, hidden, ((1,), (1,)))
        return project(lifted, slope_re, slope_im)

    return energy[:, :here], solve(energy, gram)[:, :here]


def swap(x, axis, bit):
    return lax.ppermute(x, axis, [(i, i ^ bit) for i in range(lax.axis_size(axis))])


def shift(x, axis, step):
    size = lax.axis_size(axis)
    return lax.ppermute(x, axis, [(i, (i + step) % size) for i in range(size)])


def first_place(peers):
    return peers // 2 + peers // 8


def exchange_all(send):
    peers = send.shape[0]
    first = first_place(peers)
    return lax.all_to_all(
        send,
        ("samples", "chip"),
        0,
        0,
        axis_index_groups=[[(k - first) % peers for k in range(peers)]],
        tiled=True,
    )


def powers(size):
    return [1 << k for k in reversed(range((size - 1).bit_length()))]


def body(
    occupations,
    connection_counts,
    connection_orbitals,
    connection_elements,
    laser_step,
    first_weight,
    first_bias,
    second_weight,
    readout,
):
    here, orbitals = occupations.shape
    slots = connection_orbitals.shape[1]
    wide, narrow = first_weight.shape[1], second_weight.shape[1]
    chips = lax.axis_size("chip")
    spread = chips * lax.axis_size("core")
    blocks = lax.axis_size("samples")
    total = here * blocks
    bias_row = first_bias[None, :]
    field = FIELD_SCALE * jnp.sin(FIELD_RATE * laser_step.astype(F32)[None, None])

    bits = powers(blocks)
    bits = bits[-1:] + bits[:-1]
    entries = [0]
    for bit in bits:
        entries = entries + [e ^ bit for e in entries]
    moved = swap(occupations.astype(BF16)[None], "samples", bits[0])

    shifts, shards = [], []
    for step in range(1, chips):
        shifts.append((step, 0))
        shards.append(shift(second_weight, "chip", step))
    shifts.append((0, 1))
    shards.append(shift(second_weight, "core", 1))

    hidden, owner, elements, w1, bias, readout_near, own_shard, occupied = call(
        functools.partial(slot_hidden_kernel, spread),
        8,
        (
            jax.ShapeDtypeStruct((slots + here, wide), BF16),
            jax.ShapeDtypeStruct((here, slots), BF16),
            jax.ShapeDtypeStruct(connection_elements.shape, F32),
            jax.ShapeDtypeStruct(first_weight.shape, BF16),
            jax.ShapeDtypeStruct(bias_row.shape, F32),
            jax.ShapeDtypeStruct(readout.shape, F32),
            jax.ShapeDtypeStruct(second_weight.shape, BF16),
            jax.ShapeDtypeStruct(occupations.shape, BF16),
        ),
        [
            pltpu.VMEM((1, here), jnp.int32),
            pltpu.VMEM(connection_orbitals.shape, jnp.int32),
            pltpu.VMEM(occupations.shape, jnp.int32),
            pltpu.SemaphoreType.DMA((8,)),
        ],
        name="slot_hidden",
        copies=True,
        flops=2 * (slots + here) * orbitals * wide,
        transcendentals=(slots + here) * wide,
    )(
        *(
            pltpu.with_memory_space_constraint(x, pltpu.HBM)
            for x in (
                connection_counts[None, :],
                connection_orbitals,
                occupations,
                first_weight,
                bias_row,
                connection_elements,
                readout,
                second_weight,
            )
        ),
    )
    relayed, occupied, field = lax.optimization_barrier((shards[: chips - 1], occupied, field))
    for step in range(1, chips):
        shifts.append((step, 1))
        shards.append(shift(relayed[step - 1], "core", 1))
    shifts.append((0, 0))
    stack = jnp.concatenate([occupied[None], moved], axis=0)
    moved = swap(stack, "samples", bits[1])

    send, second = call(
        functools.partial(slot_energy_kernel, tuple(shifts)),
        5 + len(shifts),
        (
            jax.ShapeDtypeStruct((blocks * chips, 1, 2 * here), F32),
            jax.ShapeDtypeStruct((wide, narrow), BF16),
        ),
        name="slot_energy",
        flops=2 * (slots + here) * wide * narrow,
        transcendentals=(slots + here) * narrow,
    )(field, hidden, owner, elements, readout_near, *shards, own_shard)
    received = exchange_all(send)
    mine = call(
        functools.partial(collect_kernel, entries, chips),
        1,
        jax.ShapeDtypeStruct((2, total), F32),
        name="collect",
        flops=COLLECT_WEIGHT,
    )(received)
    other = swap(mine, "core", 1)

    for bit in bits[2:-1]:
        stack = jnp.concatenate([stack, moved], axis=0)
        moved = swap(stack, "samples", bit)
    if total > wide:
        stack = jnp.concatenate([stack, moved], axis=0)
        stack = jnp.concatenate([stack, swap(stack, "samples", bits[-1])], axis=0)
        return wide_solve(mine + other, stack, first_weight, bias_row, second, readout)

    half = total // 2
    weights = (w1, bias, second, readout_near)
    full = orbitals // 128 * 128
    packed = call(
        pack_kernel,
        3,
        jax.ShapeDtypeStruct((half + here, full), BF16),
        name="pack",
    )(stack, moved, second)
    far_packed = swap(packed, "samples", bits[-1])
    block = jax.ShapeDtypeStruct((3 * half, half), BF16)
    slopes = (jax.ShapeDtypeStruct((narrow, half), F32),) * 2
    near_hidden, *near = call(
        near_half_kernel,
        5,
        (jax.ShapeDtypeStruct((half, wide), BF16), block) + slopes,
        name="near_half",
        flops=2 * half * wide * (orbitals + narrow + half),
        transcendentals=half * (wide + narrow),
    )(packed, *weights)
    far = call(
        far_half_kernel,
        6,
        (block,) * 3 + slopes,
        name="far_half",
        flops=2 * half * wide * (orbitals + narrow + 3 * half),
        transcendentals=half * (wide + narrow),
    )(far_packed, *weights, near_hidden)
    return call(
        solve_kernel,
        10,
        (jax.ShapeDtypeStruct((2, here), F32),) * 2,
        name="solve",
        flops=ITERS * 6 * total * total * narrow,
    )(mine, other, *near, *far)


def solution(mesh):
    blocks, spread = mesh.shape["samples"], mesh.shape["params"]
    fine = Mesh(mesh.devices.reshape(blocks, spread // 2, 2), ("samples", "chip", "core"))
    return jax.shard_map(
        body,
        mesh=fine,
        in_specs=(
            P("samples", None),
            P("samples"),
            P(None, ("samples", "chip", "core")),
            P(None, ("samples", "chip", "core")),
            P(),
            P(),
            P(),
            P(("chip", "core"), None),
            P(),
        ),
        out_specs=(P(None, "samples"), P(None, "samples")),
        check_vma=False,
    )
```

```python
import functools
import math

import jax
import jax.numpy as jnp
from jax import lax
from jax.experimental import pallas as pl
from jax.experimental.pallas import tpu as pltpu
from jax.sharding import Mesh, PartitionSpec as P

ITERS = 2


FIELD_SCALE = 0.8
FIELD_RATE = 0.0123
DIAG_SHIFT = 0.01
F32 = jnp.float32
BF16 = jnp.bfloat16
ROWS = 256
COLLECT_WEIGHT = 1e10
NEAR_WEIGHT = 1e10
VMEM_LIMIT = 48 * 1024 * 1024


def dot(a, b, dims):
    return lax.dot_general(a, b, (dims, ((), ())), preferred_element_type=F32)


def split(x):
    high = lax.reduce_precision(x, 8, 7)
    return high.astype(BF16), (x - high).astype(BF16)


def parts(x):
    high = x.astype(BF16)
    rest = x - high.astype(F32)
    middle = rest.astype(BF16)
    return high, middle, (rest - middle.astype(F32)).astype(BF16)


def iota(shape, dim):
    return lax.broadcasted_iota(jnp.int32, shape, dim)


def call(kernel, count, out_shape, scratch=(), name=None, copies=False, flops=0, transcendentals=0):
    vmem = pl.BlockSpec(memory_space=pltpu.VMEM)
    far = pl.BlockSpec(memory_space=pltpu.HBM)
    return pl.pallas_call(
        kernel,
        out_shape=out_shape,
        in_specs=[far if copies else vmem] * count,
        out_specs=jax.tree.map(lambda _: vmem, out_shape),
        scratch_shapes=scratch,
        compiler_params=pltpu.CompilerParams(vmem_limit_bytes=VMEM_LIMIT),
        cost_estimate=pl.CostEstimate(
            flops=int(flops),
            transcendentals=int(transcendentals),
            bytes_accessed=sum(x.size * x.dtype.itemsize for x in jax.tree.leaves(out_shape)),
        ),
        name=name,
    )


def slot_hidden_kernel(
    spread,
    counts_hbm,
    orbitals_hbm,
    occ_hbm,
    w1_hbm,
    bias_hbm,
    elements_hbm,
    readout_hbm,
    own_hbm,
    hidden_ref,
    owner_ref,
    elements_ref,
    w1_ref,
    bias_ref,
    readout_ref,
    own_ref,
    occupied_ref,
    counts_ref,
    orbitals_ref,
    occ_ref,
    sems,
):
    here, orbitals = occ_ref.shape
    updates, slots = orbitals_ref.shape
    pairs = (
        (counts_hbm, counts_ref),
        (occ_hbm, occ_ref),
        (w1_hbm, w1_ref),
        (bias_hbm, bias_ref),
        (orbitals_hbm, orbitals_ref),
        (elements_hbm, elements_ref),
        (readout_hbm, readout_ref),
        (own_hbm, own_ref),
    )
    copies = [pltpu.make_async_copy(a, b, sems.at[i]) for i, (a, b) in enumerate(pairs)]
    for copy in copies:
        copy.start()
    chip, core = lax.axis_index("chip"), lax.axis_index("core")
    place = chip * 2 + core
    copies[0].wait()
    counts = counts_ref[...].astype(F32)
    row, col = iota((here, here), 0), iota((here, here), 1)
    ends = jnp.sum(jnp.where(col <= row, counts, 0.0), axis=1, keepdims=True)
    starts = jnp.sum(jnp.where(col < row, counts, 0.0), axis=1, keepdims=True)
    positions = (place + spread * iota((1, slots), 1)).astype(F32)
    owner = jnp.where((starts <= positions) & (positions < ends), 1.0, 0.0).astype(BF16)
    owner_ref[...] = owner
    copies[1].wait()
    occupied = occ_ref[...].astype(F32).astype(BF16)
    occupied_ref[...] = occupied
    copies[2].wait()
    copies[3].wait()
    w1 = w1_ref[...]
    bias = bias_ref[...]
    hidden_ref[slots:, :] = jnp.tanh(dot(occupied, w1, ((1,), (0,))) + bias).astype(BF16)
    copies[4].wait()
    for start in range(0, slots, ROWS):
        stop = min(start + ROWS, slots)
        parent_occ = dot(occupied, owner[:, start:stop], ((0,), (0,)))
        columns = iota((orbitals, stop - start), 0)
        flipped = columns == orbitals_ref[0:1, start:stop]
        for u in range(1, updates):
            flipped = flipped | (columns == orbitals_ref[u : u + 1, start:stop])
        slot_occ = jnp.where(flipped, 1.0 - parent_occ, parent_occ).astype(BF16)
        pre = dot(slot_occ, w1, ((0,), (0,))) + bias
        hidden_ref[start:stop, :] = jnp.tanh(pre).astype(BF16)
    copies[5].wait()
    copies[6].wait()
    copies[7].wait()


def sine_cosine(x):
    turns = jnp.floor(x * (2.0 / math.pi) + 0.5)
    rest = ((x - turns * 1.5703125) - turns * 4.837512969970703125e-4) - turns * 7.549789948768648e-8
    square = rest * rest
    sine = (-1.9515295891e-4 * square + 8.3321608736e-3) * square - 1.6666654611e-1
    sine = rest + rest * square * sine
    cosine = (2.443315711809948e-5 * square - 1.388731625493765e-3) * square + 4.166664568298827e-2
    cosine = 1.0 - 0.5 * square + square * square * cosine
    quarter = turns.astype(jnp.int32) & 3
    odd = (quarter & 1) == 1
    high_sine = jnp.where(odd, cosine, sine)
    high_cosine = jnp.where(odd, sine, cosine)
    sine = jnp.where(quarter >= 2, -high_sine, high_sine)
    cosine = jnp.where((quarter == 1) | (quarter == 2), -high_cosine, high_cosine)
    return sine, cosine


def slot_energy_kernel(
    shifts, field_ref, hidden_ref, owner_ref, elements_ref, readout_ref, *refs
):
    shard_refs, (send_ref, second_ref) = refs[: len(shifts)], refs[len(shifts) :]
    here, slots = owner_ref.shape
    chips = lax.axis_size("chip")
    chip, core = lax.axis_index("chip"), lax.axis_index("core")
    for (step, other), shard in zip(shifts, shard_refs):
        rows = shard.shape[0]
        source = lax.rem(chip + chips - step, chips) * 2 + (core ^ other)
        second_ref[pl.ds(pl.multiple_of(source * rows, rows), rows), :] = shard[...]
    mid = jnp.tanh(dot(second_ref[...], hidden_ref[...], ((0,), (1,))))
    readout = readout_ref[...].T
    logs_re = jnp.sum(mid * readout[:, 0:1], axis=0, keepdims=True)
    logs_im = jnp.sum(mid * readout[:, 1:2], axis=0, keepdims=True)
    owner = owner_ref[...]
    own = jnp.concatenate(parts(logs_re[:, slots:]) + parts(logs_im[:, slots:]), axis=0)
    parent = dot(own, owner, ((1,), (0,)))
    diff_re = logs_re[:, :slots] - (parent[0:1] + parent[1:2] + parent[2:3])
    diff_im = logs_im[:, :slots] - (parent[3:4] + parent[4:5] + parent[5:6])
    used = jnp.sum(owner.astype(F32), axis=0, keepdims=True) > 0.0
    weight = elements_ref[0:1, :] + field_ref[...] * elements_ref[1:2, :]
    scale = weight * jnp.exp(diff_re)
    sine, cosine = sine_cosine(diff_im)
    contrib_re = jnp.where(used, scale * cosine, 0.0)
    contrib_im = jnp.where(used, scale * sine, 0.0)
    contrib = jnp.concatenate(parts(contrib_re) + parts(contrib_im), axis=0)
    sums = dot(contrib, owner, ((1,), (1,)))
    partial_re = sums[0:1] + sums[1:2] + sums[2:3]
    partial_im = sums[3:4] + sums[4:5] + sums[5:6]
    row = jnp.concatenate([partial_re, partial_im], axis=1)
    send_ref[...] = jnp.broadcast_to(row[None], send_ref.shape)


def collect(entries, spread, received_ref):
    peers, here = received_ref.shape[0], received_ref.shape[2] // 2
    block = lax.axis_index("samples")
    out_re, out_im = [], []
    for entry in entries:
        first = lax.rem((block ^ entry) * spread + peers // 2, peers)
        row = received_ref[first]
        for k in range(1, spread):
            row = row + received_ref[first + k]
        out_re.append(row[:, :here])
        out_im.append(row[:, here:])
    return jnp.concatenate([jnp.concatenate(out_re, axis=1), jnp.concatenate(out_im, axis=1)], axis=0)


def collect_kernel(entries, spread, received_ref, after_ref, energy_ref):
    del after_ref
    energy_ref[...] = collect(entries, spread, received_ref)


def sample_values(packed_ref, w1_ref, bias_ref, second_ref, readout_ref, size):
    hidden = jnp.tanh(sample_pre(packed_ref, w1_ref, bias_ref, size)).astype(BF16)
    mid = jnp.tanh(dot(second_ref[...], hidden, ((0,), (1,))))
    slope = 1.0 - mid * mid
    readout = readout_ref[...].T
    return hidden, slope * readout[:, 0:1], slope * readout[:, 1:2]


def pack_kernel(mine_ref, moved_ref, after_ref, packed_ref):
    del after_ref
    blocks, here, orbitals = mine_ref.shape
    full = packed_ref.shape[1]
    pieces = [mine_ref[k] for k in range(blocks)] + [moved_ref[k] for k in range(blocks)]
    rest = orbitals - full
    for k, piece in enumerate(pieces):
        packed_ref[k * here : (k + 1) * here, :] = piece[:, :full]
    rests = [piece[:, full:].astype(F32) for piece in pieces]
    rests.append(jnp.zeros((here, full - rest * len(pieces)), F32))
    packed_ref[len(pieces) * here :, :] = jnp.concatenate(rests, axis=1).astype(BF16)


def sample_pre(packed_ref, w1_ref, bias_ref, size):
    full = packed_ref.shape[1]
    here = packed_ref.shape[0] - size
    rest = w1_ref.shape[0] - full
    tail = packed_ref[size:, :].astype(F32)
    rests = [tail[:, k * rest : (k + 1) * rest] for k in range(size // here)]
    tail = jnp.concatenate(rests, axis=0).astype(BF16)
    pre = dot(packed_ref[:size, :], w1_ref[:full, :], ((1,), (0,)))
    return pre + dot(tail, w1_ref[full:, :], ((1,), (0,))) + bias_ref[...]


def put(overlap_ref, overlap):
    size = overlap.shape[0]
    high = overlap.astype(BF16)
    overlap_ref[:size, :] = high
    overlap_ref[size : 2 * size, :] = (overlap - high.astype(F32)).astype(BF16)
    overlap_ref[2 * size :, :] = high


def near_half_kernel(
    packed_ref, w1_ref, bias_ref, second_ref, readout_ref, w1_again, hidden_ref, near_ref, re_ref, im_ref
):
    w1_again[...] = w1_ref[...]
    size = hidden_ref.shape[0]
    hidden, re_ref[...], im_ref[...] = sample_values(packed_ref, w1_ref, bias_ref, second_ref, readout_ref, size)
    hidden_ref[...] = hidden
    put(near_ref, dot(hidden, hidden, ((1,), (1,))))


def far_half_kernel(
    packed_ref,
    w1_ref,
    bias_ref,
    second_ref,
    readout_ref,
    hidden_ref,
    near_far_ref,
    far_near_ref,
    far_ref,
    re_ref,
    im_ref,
):
    size = hidden_ref.shape[0]
    hidden, re_ref[...], im_ref[...] = sample_values(packed_ref, w1_ref, bias_ref, second_ref, readout_ref, size)
    near = hidden_ref[...]
    put(near_far_ref, dot(near, hidden, ((1,), (1,))))
    put(far_near_ref, dot(hidden, near, ((1,), (1,))))
    put(far_ref, dot(hidden, hidden, ((1,), (1,))))


def solve(energy, gram):
    total = energy.shape[1]
    centered = energy - jnp.mean(energy, axis=1, keepdims=True)
    res_c = jnp.concatenate([centered[1:2], -centered[0:1]], axis=0) / total
    res_y = gram(res_c)
    dir_c, dir_y = res_c, res_y
    norm_now = full_sum(res_c * res_y)
    cross, square = norm_now, full_sum(res_y * res_y)
    change = jnp.zeros_like(res_y)
    for turn in range(ITERS):
        alpha = norm_now / (square / total + DIAG_SHIFT * cross)
        change = change + alpha * dir_y
        if turn + 1 < ITERS:
            img_c = dir_y / total + DIAG_SHIFT * dir_c
            img_y = gram(dir_y) / total + DIAG_SHIFT * dir_y
            res_c = res_c - alpha * img_c
            res_y = res_y - alpha * img_y
            norm_next = full_sum(res_c * res_y)
            mixed = full_sum(res_c * dir_y) + full_sum(dir_c * res_y)
            squares = full_sum(res_y * res_y), full_sum(res_y * dir_y)
            beta = norm_next / norm_now
            cross = norm_next + beta * mixed + beta * beta * cross
            square = squares[0] + 2.0 * beta * squares[1] + beta * beta * square
            dir_c = res_c + beta * dir_c
            dir_y = res_y + beta * dir_y
            norm_now = norm_next
    return change


def full_sum(x):
    return jnp.sum(jnp.sum(x, axis=1, keepdims=True), axis=0, keepdims=True)


def project(lifted, slope_re, slope_im):
    raw = jnp.concatenate(
        [jnp.sum(lifted * slope_re, axis=0, keepdims=True), jnp.sum(lifted * slope_im, axis=0, keepdims=True)],
        axis=0,
    )
    return raw - jnp.mean(raw, axis=1, keepdims=True)


def solve_kernel(
    energy_ref,
    near_ref,
    near_re_ref,
    near_im_ref,
    near_far_ref,
    far_near_ref,
    far_ref,
    far_re_ref,
    far_im_ref,
    local_ref,
    change_ref,
):
    width = local_ref.shape[1]
    half = near_ref.shape[1]
    energy = energy_ref[...]
    local_ref[...] = energy[:, :width]

    def scaled(c, re_ref, im_ref):
        back = re_ref[...] * c[0:1] + im_ref[...] * c[1:2]
        high = back.astype(BF16)
        low = (back - high.astype(F32)).astype(BF16)
        return jnp.concatenate([high, high, low], axis=1)

    def raw(lifted, re_ref, im_ref):
        re = jnp.sum(lifted * re_ref[...], axis=0, keepdims=True)
        return jnp.concatenate([re, jnp.sum(lifted * im_ref[...], axis=0, keepdims=True)], axis=0)

    def gram(c):
        near = scaled(c[:, :half], near_re_ref, near_im_ref)
        far = scaled(c[:, half:], far_re_ref, far_im_ref)
        to_near = dot(near, near_ref[...], ((1,), (0,))) + dot(far, far_near_ref[...], ((1,), (0,)))
        to_far = dot(near, near_far_ref[...], ((1,), (0,))) + dot(far, far_ref[...], ((1,), (0,)))
        both = jnp.concatenate(
            [raw(to_near, near_re_ref, near_im_ref), raw(to_far, far_re_ref, far_im_ref)], axis=1
        )
        return both - jnp.mean(both, axis=1, keepdims=True)

    change_ref[...] = solve(energy, gram)[:, :width]


def wide_solve(energy, occ_stack, first_weight, bias_row, second, readout):
    here = occ_stack.shape[1]
    occupied = occ_stack.reshape(-1, occ_stack.shape[2])
    pre = dot(occupied, first_weight, ((1,), (0,))) + bias_row
    hidden = jnp.tanh(pre).astype(BF16)
    mid = jnp.tanh(dot(second, hidden, ((0,), (1,))))
    slope = 1.0 - mid * mid
    slope_re = slope * readout[0][:, None]
    slope_im = slope * readout[1][:, None]

    def gram(c):
        high, low = split(slope_re * c[0:1] + slope_im * c[1:2])
        high, low = split(dot(high, hidden, ((1,), (0,))) + dot(low, hidden, ((1,), (0,))))
        lifted = dot(high, hidden, ((1,), (1,))) + dot(low, hidden, ((1,), (1,)))
        return project(lifted, slope_re, slope_im)

    return energy[:, :here], solve(energy, gram)[:, :here]


def swap(x, axis, bit):
    return lax.ppermute(x, axis, [(i, i ^ bit) for i in range(lax.axis_size(axis))])


def shift(x, axis, step):
    size = lax.axis_size(axis)
    return lax.ppermute(x, axis, [(i, (i + step) % size) for i in range(size)])


def exchange_all(send):
    peers = send.shape[0]
    return lax.all_to_all(
        send,
        ("samples", "chip", "core"),
        0,
        0,
        axis_index_groups=[[(k + peers // 2) % peers for k in range(peers)]],
        tiled=True,
    )


def powers(size):
    return [1 << k for k in reversed(range((size - 1).bit_length()))]


def body(
    occupations,
    connection_counts,
    connection_orbitals,
    connection_elements,
    laser_step,
    first_weight,
    first_bias,
    second_weight,
    readout,
):
    here, orbitals = occupations.shape
    slots = connection_orbitals.shape[1]
    wide, narrow = first_weight.shape[1], second_weight.shape[1]
    chips = lax.axis_size("chip")
    spread = chips * lax.axis_size("core")
    blocks = lax.axis_size("samples")
    total = here * blocks
    bias_row = first_bias[None, :]
    field = FIELD_SCALE * jnp.sin(FIELD_RATE * laser_step.astype(F32)[None, None])

    bits = powers(blocks)
    bits = bits[-1:] + bits[:-1]
    entries = [0]
    for bit in bits:
        entries = entries + [e ^ bit for e in entries]
    moved = swap(occupations.astype(BF16)[None], "samples", bits[0])

    shifts, shards = [], []
    for step in range(1, chips):
        shifts.append((step, 0))
        shards.append(shift(second_weight, "chip", step))
    shifts.append((0, 1))
    shards.append(shift(second_weight, "core", 1))

    hidden, owner, elements, w1, bias, readout_near, own_shard, occupied = call(
        functools.partial(slot_hidden_kernel, spread),
        8,
        (
            jax.ShapeDtypeStruct((slots + here, wide), BF16),
            jax.ShapeDtypeStruct((here, slots), BF16),
            jax.ShapeDtypeStruct(connection_elements.shape, F32),
            jax.ShapeDtypeStruct(first_weight.shape, BF16),
            jax.ShapeDtypeStruct(bias_row.shape, F32),
            jax.ShapeDtypeStruct(readout.shape, F32),
            jax.ShapeDtypeStruct(second_weight.shape, BF16),
            jax.ShapeDtypeStruct(occupations.shape, BF16),
        ),
        [
            pltpu.VMEM((1, here), jnp.int32),
            pltpu.VMEM(connection_orbitals.shape, jnp.int32),
            pltpu.VMEM(occupations.shape, jnp.int32),
            pltpu.SemaphoreType.DMA((8,)),
        ],
        name="slot_hidden",
        copies=True,
        flops=2 * (slots + here) * orbitals * wide,
        transcendentals=(slots + here) * wide,
    )(
        *(
            pltpu.with_memory_space_constraint(x, pltpu.HBM)
            for x in (
                connection_counts[None, :],
                connection_orbitals,
                occupations,
                first_weight,
                bias_row,
                connection_elements,
                readout,
                second_weight,
            )
        ),
    )
    relayed, occupied, field = lax.optimization_barrier((shards[: chips - 1], occupied, field))
    for step in range(1, chips):
        shifts.append((step, 1))
        shards.append(shift(relayed[step - 1], "core", 1))
    shifts.append((0, 0))
    stack = jnp.concatenate([occupied[None], moved], axis=0)
    moved = swap(stack, "samples", bits[1])

    send, second = call(
        functools.partial(slot_energy_kernel, tuple(shifts)),
        5 + len(shifts),
        (
            jax.ShapeDtypeStruct((blocks * spread, 1, 2 * here), F32),
            jax.ShapeDtypeStruct((wide, narrow), BF16),
        ),
        name="slot_energy",
        flops=2 * (slots + here) * wide * narrow,
        transcendentals=(slots + here) * narrow,
    )(field, hidden, owner, elements, readout_near, *shards, own_shard)
    received = exchange_all(send)

    def collected(after):
        return call(
            functools.partial(collect_kernel, entries, spread),
            2,
            jax.ShapeDtypeStruct((2, total), F32),
            name="collect",
            flops=COLLECT_WEIGHT,
        )(received, after)

    for bit in bits[2:-1]:
        stack = jnp.concatenate([stack, moved], axis=0)
        moved = swap(stack, "samples", bit)
    if total > wide:
        stack = jnp.concatenate([stack, moved], axis=0)
        stack = jnp.concatenate([stack, swap(stack, "samples", bits[-1])], axis=0)
        return wide_solve(collected(stack), stack, first_weight, bias_row, second, readout)

    half = total // 2
    weights = (w1, bias, second, readout_near)
    full = orbitals // 128 * 128
    packed = call(
        pack_kernel,
        3,
        jax.ShapeDtypeStruct((half + here, full), BF16),
        name="pack",
    )(stack, moved, second)
    far_packed = swap(packed, "samples", bits[-1])
    block = jax.ShapeDtypeStruct((3 * half, half), BF16)
    slopes = (jax.ShapeDtypeStruct((narrow, half), F32),) * 2
    w1, near_hidden, *near = call(
        near_half_kernel,
        5,
        (jax.ShapeDtypeStruct(w1.shape, BF16), jax.ShapeDtypeStruct((half, wide), BF16), block) + slopes,
        name="near_half",
        flops=NEAR_WEIGHT,
        transcendentals=half * (wide + narrow),
    )(packed, *weights)
    far = call(
        far_half_kernel,
        6,
        (block,) * 3 + slopes,
        name="far_half",
        flops=2 * half * wide * (orbitals + narrow + 3 * half),
        transcendentals=half * (wide + narrow),
    )(far_packed, w1, *weights[1:], near_hidden)
    return call(
        solve_kernel,
        9,
        (jax.ShapeDtypeStruct((2, here), F32),) * 2,
        name="solve",
        flops=ITERS * 6 * total * total * narrow,
    )(collected(far[0]), *near, *far)


def solution(mesh):
    blocks, spread = mesh.shape["samples"], mesh.shape["params"]
    fine = Mesh(mesh.devices.reshape(blocks, spread // 2, 2), ("samples", "chip", "core"))
    return jax.shard_map(
        body,
        mesh=fine,
        in_specs=(
            P("samples", None),
            P("samples"),
            P(None, ("samples", "chip", "core")),
            P(None, ("samples", "chip", "core")),
            P(),
            P(),
            P(),
            P(("chip", "core"), None),
            P(),
        ),
        out_specs=(P(None, "samples"), P(None, "samples")),
        check_vma=False,
    )
```

```python
import functools
import math

import jax
import jax.numpy as jnp
from jax import lax
from jax.experimental import pallas as pl
from jax.experimental.pallas import tpu as pltpu
from jax.sharding import Mesh, PartitionSpec as P

ITERS = 2


FIELD_SCALE = 0.8
FIELD_RATE = 0.0123
DIAG_SHIFT = 0.01
F32 = jnp.float32
BF16 = jnp.bfloat16
ROWS = 256
COLLECT_WEIGHT = 1e10
NEAR_WEIGHT = 1e10
VMEM_LIMIT = 48 * 1024 * 1024


def dot(a, b, dims):
    return lax.dot_general(a, b, (dims, ((), ())), preferred_element_type=F32)


def split(x):
    high = lax.reduce_precision(x, 8, 7)
    return high.astype(BF16), (x - high).astype(BF16)


def parts(x):
    high = x.astype(BF16)
    rest = x - high.astype(F32)
    middle = rest.astype(BF16)
    return high, middle, (rest - middle.astype(F32)).astype(BF16)


def iota(shape, dim):
    return lax.broadcasted_iota(jnp.int32, shape, dim)


def call(kernel, count, out_shape, scratch=(), name=None, copies=False, flops=0, transcendentals=0):
    vmem = pl.BlockSpec(memory_space=pltpu.VMEM)
    far = pl.BlockSpec(memory_space=pltpu.HBM)
    return pl.pallas_call(
        kernel,
        out_shape=out_shape,
        in_specs=[far if copies else vmem] * count,
        out_specs=jax.tree.map(lambda _: vmem, out_shape),
        scratch_shapes=scratch,
        compiler_params=pltpu.CompilerParams(vmem_limit_bytes=VMEM_LIMIT),
        cost_estimate=pl.CostEstimate(
            flops=int(flops),
            transcendentals=int(transcendentals),
            bytes_accessed=sum(x.size * x.dtype.itemsize for x in jax.tree.leaves(out_shape)),
        ),
        name=name,
    )


def slot_hidden_kernel(
    spread,
    counts_hbm,
    orbitals_hbm,
    occ_hbm,
    w1_hbm,
    bias_hbm,
    elements_hbm,
    readout_hbm,
    own_hbm,
    hidden_ref,
    owner_ref,
    elements_ref,
    w1_ref,
    bias_ref,
    readout_ref,
    own_ref,
    occupied_ref,
    counts_ref,
    orbitals_ref,
    occ_ref,
    sems,
):
    here, orbitals = occ_ref.shape
    updates, slots = orbitals_ref.shape
    pairs = (
        (counts_hbm, counts_ref),
        (occ_hbm, occ_ref),
        (w1_hbm, w1_ref),
        (bias_hbm, bias_ref),
        (orbitals_hbm, orbitals_ref),
        (elements_hbm, elements_ref),
        (readout_hbm, readout_ref),
        (own_hbm, own_ref),
    )
    copies = [pltpu.make_async_copy(a, b, sems.at[i]) for i, (a, b) in enumerate(pairs)]
    for copy in copies:
        copy.start()
    chip, core = lax.axis_index("chip"), lax.axis_index("core")
    place = chip * 2 + core
    copies[0].wait()
    counts = counts_ref[...].astype(F32)
    row, col = iota((here, here), 0), iota((here, here), 1)
    ends = jnp.sum(jnp.where(col <= row, counts, 0.0), axis=1, keepdims=True)
    starts = jnp.sum(jnp.where(col < row, counts, 0.0), axis=1, keepdims=True)
    positions = (place + spread * iota((1, slots), 1)).astype(F32)
    owner = jnp.where((starts <= positions) & (positions < ends), 1.0, 0.0).astype(BF16)
    owner_ref[...] = owner
    copies[1].wait()
    occupied = occ_ref[...].astype(F32).astype(BF16)
    occupied_ref[...] = occupied
    copies[2].wait()
    copies[3].wait()
    w1 = w1_ref[...]
    bias = bias_ref[...]
    hidden_ref[slots:, :] = jnp.tanh(dot(occupied, w1, ((1,), (0,))) + bias).astype(BF16)
    copies[4].wait()
    for start in range(0, slots, ROWS):
        stop = min(start + ROWS, slots)
        parent_occ = dot(occupied, owner[:, start:stop], ((0,), (0,)))
        columns = iota((orbitals, stop - start), 0)
        flipped = columns == orbitals_ref[0:1, start:stop]
        for u in range(1, updates):
            flipped = flipped | (columns == orbitals_ref[u : u + 1, start:stop])
        slot_occ = jnp.where(flipped, 1.0 - parent_occ, parent_occ).astype(BF16)
        pre = dot(slot_occ, w1, ((0,), (0,))) + bias
        hidden_ref[start:stop, :] = jnp.tanh(pre).astype(BF16)
    copies[5].wait()
    copies[6].wait()
    copies[7].wait()


def sine_cosine(x):
    turns = jnp.floor(x * (2.0 / math.pi) + 0.5)
    rest = ((x - turns * 1.5703125) - turns * 4.837512969970703125e-4) - turns * 7.549789948768648e-8
    square = rest * rest
    sine = (-1.9515295891e-4 * square + 8.3321608736e-3) * square - 1.6666654611e-1
    sine = rest + rest * square * sine
    cosine = (2.443315711809948e-5 * square - 1.388731625493765e-3) * square + 4.166664568298827e-2
    cosine = 1.0 - 0.5 * square + square * square * cosine
    quarter = turns.astype(jnp.int32) & 3
    odd = (quarter & 1) == 1
    high_sine = jnp.where(odd, cosine, sine)
    high_cosine = jnp.where(odd, sine, cosine)
    sine = jnp.where(quarter >= 2, -high_sine, high_sine)
    cosine = jnp.where((quarter == 1) | (quarter == 2), -high_cosine, high_cosine)
    return sine, cosine


def slot_energy_kernel(
    shifts, field_ref, hidden_ref, owner_ref, elements_ref, readout_ref, *refs
):
    shard_refs, (send_ref, second_ref) = refs[: len(shifts)], refs[len(shifts) :]
    here, slots = owner_ref.shape
    chips = lax.axis_size("chip")
    chip, core = lax.axis_index("chip"), lax.axis_index("core")
    for (step, other), shard in zip(shifts, shard_refs):
        rows = shard.shape[0]
        source = lax.rem(chip + chips - step, chips) * 2 + (core ^ other)
        second_ref[pl.ds(pl.multiple_of(source * rows, rows), rows), :] = shard[...]
    mid = jnp.tanh(dot(second_ref[...], hidden_ref[...], ((0,), (1,))))
    readout = readout_ref[...].T
    logs_re = jnp.sum(mid * readout[:, 0:1], axis=0, keepdims=True)
    logs_im = jnp.sum(mid * readout[:, 1:2], axis=0, keepdims=True)
    owner = owner_ref[...]
    own = jnp.concatenate(parts(logs_re[:, slots:]) + parts(logs_im[:, slots:]), axis=0)
    parent = dot(own, owner, ((1,), (0,)))
    diff_re = logs_re[:, :slots] - (parent[0:1] + parent[1:2] + parent[2:3])
    diff_im = logs_im[:, :slots] - (parent[3:4] + parent[4:5] + parent[5:6])
    used = jnp.sum(owner.astype(F32), axis=0, keepdims=True) > 0.0
    weight = elements_ref[0:1, :] + field_ref[...] * elements_ref[1:2, :]
    scale = weight * jnp.exp(diff_re)
    sine, cosine = sine_cosine(diff_im)
    contrib_re = jnp.where(used, scale * cosine, 0.0)
    contrib_im = jnp.where(used, scale * sine, 0.0)
    contrib = jnp.concatenate(parts(contrib_re) + parts(contrib_im), axis=0)
    sums = dot(contrib, owner, ((1,), (1,)))
    partial_re = sums[0:1] + sums[1:2] + sums[2:3]
    partial_im = sums[3:4] + sums[4:5] + sums[5:6]
    row = jnp.concatenate([partial_re, partial_im], axis=1)
    send_ref[...] = jnp.broadcast_to(row[None], send_ref.shape)


def collect(entries, spread, received_ref):
    peers, here = received_ref.shape[0], received_ref.shape[2] // 2
    block = lax.axis_index("samples")
    out_re, out_im = [], []
    for entry in entries:
        first = lax.rem((block ^ entry) * spread + peers // 2, peers)
        row = received_ref[first]
        for k in range(1, spread):
            row = row + received_ref[first + k]
        out_re.append(row[:, :here])
        out_im.append(row[:, here:])
    return jnp.concatenate([jnp.concatenate(out_re, axis=1), jnp.concatenate(out_im, axis=1)], axis=0)


def collect_kernel(entries, spread, received_ref, after_ref, energy_ref):
    del after_ref
    energy_ref[...] = collect(entries, spread, received_ref)


def sample_values(packed_ref, w1_ref, bias_ref, second_ref, readout_ref, size):
    hidden = jnp.tanh(sample_pre(packed_ref, w1_ref, bias_ref, size)).astype(BF16)
    mid = jnp.tanh(dot(second_ref[...], hidden, ((0,), (1,))))
    slope = 1.0 - mid * mid
    readout = readout_ref[...].T
    return hidden, slope * readout[:, 0:1], slope * readout[:, 1:2]


def pack_kernel(mine_ref, moved_ref, after_ref, packed_ref):
    del after_ref
    blocks, here, orbitals = mine_ref.shape
    full = packed_ref.shape[1]
    pieces = [mine_ref[k] for k in range(blocks)] + [moved_ref[k] for k in range(blocks)]
    rest = orbitals - full
    for k, piece in enumerate(pieces):
        packed_ref[k * here : (k + 1) * here, :] = piece[:, :full]
    rests = [piece[:, full:].astype(F32) for piece in pieces]
    rests.append(jnp.zeros((here, full - rest * len(pieces)), F32))
    packed_ref[len(pieces) * here :, :] = jnp.concatenate(rests, axis=1).astype(BF16)


def sample_pre(packed_ref, w1_ref, bias_ref, size):
    full = packed_ref.shape[1]
    here = packed_ref.shape[0] - size
    rest = w1_ref.shape[0] - full
    tail = packed_ref[size:, :].astype(F32)
    rests = [tail[:, k * rest : (k + 1) * rest] for k in range(size // here)]
    tail = jnp.concatenate(rests, axis=0).astype(BF16)
    pre = dot(packed_ref[:size, :], w1_ref[:full, :], ((1,), (0,)))
    return pre + dot(tail, w1_ref[full:, :], ((1,), (0,))) + bias_ref[...]


def put(overlap_ref, overlap):
    size = overlap.shape[0]
    high = overlap.astype(BF16)
    overlap_ref[:size, :] = high
    overlap_ref[size : 2 * size, :] = (overlap - high.astype(F32)).astype(BF16)
    overlap_ref[2 * size :, :] = high


def near_half_kernel(
    packed_ref, w1_ref, bias_ref, second_ref, readout_ref, w1_again, hidden_ref, near_ref, re_ref, im_ref
):
    w1_again[...] = w1_ref[...]
    size = hidden_ref.shape[0]
    hidden, re_ref[...], im_ref[...] = sample_values(packed_ref, w1_ref, bias_ref, second_ref, readout_ref, size)
    hidden_ref[...] = hidden
    put(near_ref, dot(hidden, hidden, ((1,), (1,))))


def far_half_kernel(
    packed_ref,
    w1_ref,
    bias_ref,
    second_ref,
    readout_ref,
    hidden_ref,
    near_far_ref,
    far_near_ref,
    far_ref,
    re_ref,
    im_ref,
):
    size = hidden_ref.shape[0]
    hidden, re_ref[...], im_ref[...] = sample_values(packed_ref, w1_ref, bias_ref, second_ref, readout_ref, size)
    near = hidden_ref[...]
    put(near_far_ref, dot(near, hidden, ((1,), (1,))))
    put(far_near_ref, dot(hidden, near, ((1,), (1,))))
    put(far_ref, dot(hidden, hidden, ((1,), (1,))))


def solve(energy, gram):
    total = energy.shape[1]
    centered = energy - jnp.mean(energy, axis=1, keepdims=True)
    res_c = jnp.concatenate([centered[1:2], -centered[0:1]], axis=0) / total
    res_y = gram(res_c)
    dir_c, dir_y = res_c, res_y
    norm_now = full_sum(res_c * res_y)
    cross, square = norm_now, full_sum(res_y * res_y)
    change = jnp.zeros_like(res_y)
    for turn in range(ITERS):
        alpha = norm_now / (square / total + DIAG_SHIFT * cross)
        change = change + alpha * dir_y
        if turn + 1 < ITERS:
            img_c = dir_y / total + DIAG_SHIFT * dir_c
            img_y = gram(dir_y) / total + DIAG_SHIFT * dir_y
            res_c = res_c - alpha * img_c
            res_y = res_y - alpha * img_y
            norm_next = full_sum(res_c * res_y)
            mixed = full_sum(res_c * dir_y) + full_sum(dir_c * res_y)
            squares = full_sum(res_y * res_y), full_sum(res_y * dir_y)
            beta = norm_next / norm_now
            cross = norm_next + beta * mixed + beta * beta * cross
            square = squares[0] + 2.0 * beta * squares[1] + beta * beta * square
            dir_c = res_c + beta * dir_c
            dir_y = res_y + beta * dir_y
            norm_now = norm_next
    return change


def full_sum(x):
    return jnp.sum(jnp.sum(x, axis=1, keepdims=True), axis=0, keepdims=True)


def project(lifted, slope_re, slope_im):
    raw = jnp.concatenate(
        [jnp.sum(lifted * slope_re, axis=0, keepdims=True), jnp.sum(lifted * slope_im, axis=0, keepdims=True)],
        axis=0,
    )
    return raw - jnp.mean(raw, axis=1, keepdims=True)


def solve_kernel(
    energy_ref,
    near_ref,
    near_re_ref,
    near_im_ref,
    near_far_ref,
    far_near_ref,
    far_ref,
    far_re_ref,
    far_im_ref,
    local_ref,
    change_ref,
):
    width = local_ref.shape[1]
    half = near_ref.shape[1]
    energy = energy_ref[...]
    local_ref[...] = energy[:, :width]

    def scaled(c, re_ref, im_ref):
        back = re_ref[...] * c[0:1] + im_ref[...] * c[1:2]
        high = back.astype(BF16)
        low = (back - high.astype(F32)).astype(BF16)
        return jnp.concatenate([high, high, low], axis=1)

    def raw(lifted, re_ref, im_ref):
        re = jnp.sum(lifted * re_ref[...], axis=0, keepdims=True)
        return jnp.concatenate([re, jnp.sum(lifted * im_ref[...], axis=0, keepdims=True)], axis=0)

    def gram(c):
        near = scaled(c[:, :half], near_re_ref, near_im_ref)
        far = scaled(c[:, half:], far_re_ref, far_im_ref)
        to_near = dot(near, near_ref[...], ((1,), (0,))) + dot(far, far_near_ref[...], ((1,), (0,)))
        to_far = dot(near, near_far_ref[...], ((1,), (0,))) + dot(far, far_ref[...], ((1,), (0,)))
        both = jnp.concatenate(
            [raw(to_near, near_re_ref, near_im_ref), raw(to_far, far_re_ref, far_im_ref)], axis=1
        )
        return both - jnp.mean(both, axis=1, keepdims=True)

    change_ref[...] = solve(energy, gram)[:, :width]


def wide_solve(energy, occ_stack, first_weight, bias_row, second, readout):
    here = occ_stack.shape[1]
    occupied = occ_stack.reshape(-1, occ_stack.shape[2])
    pre = dot(occupied, first_weight, ((1,), (0,))) + bias_row
    hidden = jnp.tanh(pre).astype(BF16)
    mid = jnp.tanh(dot(second, hidden, ((0,), (1,))))
    slope = 1.0 - mid * mid
    slope_re = slope * readout[0][:, None]
    slope_im = slope * readout[1][:, None]

    def gram(c):
        high, low = split(slope_re * c[0:1] + slope_im * c[1:2])
        high, low = split(dot(high, hidden, ((1,), (0,))) + dot(low, hidden, ((1,), (0,))))
        lifted = dot(high, hidden, ((1,), (1,))) + dot(low, hidden, ((1,), (1,)))
        return project(lifted, slope_re, slope_im)

    return energy[:, :here], solve(energy, gram)[:, :here]


def swap(x, axis, bit):
    return lax.ppermute(x, axis, [(i, i ^ bit) for i in range(lax.axis_size(axis))])


def shift(x, axis, step):
    size = lax.axis_size(axis)
    return lax.ppermute(x, axis, [(i, (i + step) % size) for i in range(size)])


def exchange_all(send):
    peers = send.shape[0]
    return lax.all_to_all(
        send,
        ("samples", "chip", "core"),
        0,
        0,
        axis_index_groups=[[(k + peers // 2) % peers for k in range(peers)]],
        tiled=True,
    )


def powers(size):
    return [1 << k for k in reversed(range((size - 1).bit_length()))]


def body(
    occupations,
    connection_counts,
    connection_orbitals,
    connection_elements,
    laser_step,
    first_weight,
    first_bias,
    second_weight,
    readout,
):
    here, orbitals = occupations.shape
    slots = connection_orbitals.shape[1]
    wide, narrow = first_weight.shape[1], second_weight.shape[1]
    chips = lax.axis_size("chip")
    spread = chips * lax.axis_size("core")
    blocks = lax.axis_size("samples")
    total = here * blocks
    bias_row = first_bias[None, :]
    field = FIELD_SCALE * jnp.sin(FIELD_RATE * laser_step.astype(F32)[None, None])

    bits = powers(blocks)
    bits = bits[-1:] + bits[:-1]
    entries = [0]
    for bit in bits:
        entries = entries + [e ^ bit for e in entries]
    moved = swap(occupations[None], "samples", bits[0])

    shifts, shards = [], []
    for step in range(1, chips):
        shifts.append((step, 0))
        shards.append(shift(second_weight, "chip", step))
    shifts.append((0, 1))
    shards.append(shift(second_weight, "core", 1))

    hidden, owner, elements, w1, bias, readout_near, own_shard, occupied = call(
        functools.partial(slot_hidden_kernel, spread),
        8,
        (
            jax.ShapeDtypeStruct((slots + here, wide), BF16),
            jax.ShapeDtypeStruct((here, slots), BF16),
            jax.ShapeDtypeStruct(connection_elements.shape, F32),
            jax.ShapeDtypeStruct(first_weight.shape, BF16),
            jax.ShapeDtypeStruct(bias_row.shape, F32),
            jax.ShapeDtypeStruct(readout.shape, F32),
            jax.ShapeDtypeStruct(second_weight.shape, BF16),
            jax.ShapeDtypeStruct(occupations.shape, BF16),
        ),
        [
            pltpu.VMEM((1, here), jnp.int32),
            pltpu.VMEM(connection_orbitals.shape, jnp.int32),
            pltpu.VMEM(occupations.shape, jnp.int32),
            pltpu.SemaphoreType.DMA((8,)),
        ],
        name="slot_hidden",
        copies=True,
        flops=2 * (slots + here) * orbitals * wide,
        transcendentals=(slots + here) * wide,
    )(
        *(
            pltpu.with_memory_space_constraint(x, pltpu.HBM)
            for x in (
                connection_counts[None, :],
                connection_orbitals,
                occupations,
                first_weight,
                bias_row,
                connection_elements,
                readout,
                second_weight,
            )
        ),
    )
    relayed, occupied, field = lax.optimization_barrier((shards[: chips - 1], occupied, field))
    for step in range(1, chips):
        shifts.append((step, 1))
        shards.append(shift(relayed[step - 1], "core", 1))
    shifts.append((0, 0))
    stack = jnp.concatenate([occupied[None], moved.astype(BF16)], axis=0)
    moved = swap(stack, "samples", bits[1])

    send, second = call(
        functools.partial(slot_energy_kernel, tuple(shifts)),
        5 + len(shifts),
        (
            jax.ShapeDtypeStruct((blocks * spread, 1, 2 * here), F32),
            jax.ShapeDtypeStruct((wide, narrow), BF16),
        ),
        name="slot_energy",
        flops=2 * (slots + here) * wide * narrow,
        transcendentals=(slots + here) * narrow,
    )(field, hidden, owner, elements, readout_near, *shards, own_shard)
    received = exchange_all(send)

    def collected(after):
        return call(
            functools.partial(collect_kernel, entries, spread),
            2,
            jax.ShapeDtypeStruct((2, total), F32),
            name="collect",
            flops=COLLECT_WEIGHT,
        )(received, after)

    for bit in bits[2:-1]:
        stack = jnp.concatenate([stack, moved], axis=0)
        moved = swap(stack, "samples", bit)
    if total > wide:
        stack = jnp.concatenate([stack, moved], axis=0)
        stack = jnp.concatenate([stack, swap(stack, "samples", bits[-1])], axis=0)
        return wide_solve(collected(stack), stack, first_weight, bias_row, second, readout)

    half = total // 2
    weights = (w1, bias, second, readout_near)
    full = orbitals // 128 * 128
    packed = call(
        pack_kernel,
        3,
        jax.ShapeDtypeStruct((half + here, full), BF16),
        name="pack",
    )(stack, moved, second)
    far_packed = swap(packed, "samples", bits[-1])
    block = jax.ShapeDtypeStruct((3 * half, half), BF16)
    slopes = (jax.ShapeDtypeStruct((narrow, half), F32),) * 2
    w1, near_hidden, *near = call(
        near_half_kernel,
        5,
        (jax.ShapeDtypeStruct(w1.shape, BF16), jax.ShapeDtypeStruct((half, wide), BF16), block) + slopes,
        name="near_half",
        flops=NEAR_WEIGHT,
        transcendentals=half * (wide + narrow),
    )(packed, *weights)
    far = call(
        far_half_kernel,
        6,
        (block,) * 3 + slopes,
        name="far_half",
        flops=2 * half * wide * (orbitals + narrow + 3 * half),
        transcendentals=half * (wide + narrow),
    )(far_packed, w1, *weights[1:], near_hidden)
    return call(
        solve_kernel,
        9,
        (jax.ShapeDtypeStruct((2, here), F32),) * 2,
        name="solve",
        flops=ITERS * 6 * total * total * narrow,
    )(collected(far[0]), *near, *far)


def solution(mesh):
    blocks, spread = mesh.shape["samples"], mesh.shape["params"]
    fine = Mesh(mesh.devices.reshape(blocks, spread // 2, 2), ("samples", "chip", "core"))
    return jax.shard_map(
        body,
        mesh=fine,
        in_specs=(
            P("samples", None),
            P("samples"),
            P(None, ("samples", "chip", "core")),
            P(None, ("samples", "chip", "core")),
            P(),
            P(),
            P(),
            P(("chip", "core"), None),
            P(),
        ),
        out_specs=(P(None, "samples"), P(None, "samples")),
        check_vma=False,
    )
```

```python
import functools
import math

import jax
import jax.numpy as jnp
from jax import lax
from jax.experimental import pallas as pl
from jax.experimental.pallas import tpu as pltpu
from jax.sharding import Mesh, PartitionSpec as P

ITERS = 2


FIELD_SCALE = 0.8
FIELD_RATE = 0.0123
DIAG_SHIFT = 0.01
F32 = jnp.float32
BF16 = jnp.bfloat16
ROWS = 256
COLLECT_WEIGHT = 1e10
NEAR_WEIGHT = 1e10
VMEM_LIMIT = 48 * 1024 * 1024


def dot(a, b, dims):
    return lax.dot_general(a, b, (dims, ((), ())), preferred_element_type=F32)


def split(x):
    high = lax.reduce_precision(x, 8, 7)
    return high.astype(BF16), (x - high).astype(BF16)


def parts(x):
    high = x.astype(BF16)
    rest = x - high.astype(F32)
    middle = rest.astype(BF16)
    return high, middle, (rest - middle.astype(F32)).astype(BF16)


def iota(shape, dim):
    return lax.broadcasted_iota(jnp.int32, shape, dim)


def call(kernel, count, out_shape, scratch=(), name=None, copies=False, flops=0, transcendentals=0):
    vmem = pl.BlockSpec(memory_space=pltpu.VMEM)
    far = pl.BlockSpec(memory_space=pltpu.HBM)
    return pl.pallas_call(
        kernel,
        out_shape=out_shape,
        in_specs=[far if copies else vmem] * count,
        out_specs=jax.tree.map(lambda _: vmem, out_shape),
        scratch_shapes=scratch,
        compiler_params=pltpu.CompilerParams(vmem_limit_bytes=VMEM_LIMIT),
        cost_estimate=pl.CostEstimate(
            flops=int(flops),
            transcendentals=int(transcendentals),
            bytes_accessed=sum(x.size * x.dtype.itemsize for x in jax.tree.leaves(out_shape)),
        ),
        name=name,
    )


def slot_hidden_kernel(
    spread,
    counts_hbm,
    orbitals_hbm,
    occ_hbm,
    w1_hbm,
    bias_hbm,
    elements_hbm,
    readout_hbm,
    own_hbm,
    hidden_ref,
    owner_ref,
    elements_ref,
    w1_ref,
    bias_ref,
    readout_ref,
    own_ref,
    occupied_ref,
    counts_ref,
    orbitals_ref,
    occ_ref,
    sems,
):
    here, orbitals = occ_ref.shape
    updates, slots = orbitals_ref.shape
    pairs = (
        (counts_hbm, counts_ref),
        (occ_hbm, occ_ref),
        (w1_hbm, w1_ref),
        (bias_hbm, bias_ref),
        (orbitals_hbm, orbitals_ref),
        (elements_hbm, elements_ref),
        (readout_hbm, readout_ref),
        (own_hbm, own_ref),
    )
    copies = [pltpu.make_async_copy(a, b, sems.at[i]) for i, (a, b) in enumerate(pairs)]
    for copy in copies:
        copy.start()
    chip, core = lax.axis_index("chip"), lax.axis_index("core")
    place = chip * 2 + core
    copies[0].wait()
    counts = counts_ref[...].astype(F32)
    row, col = iota((here, here), 0), iota((here, here), 1)
    ends = jnp.sum(jnp.where(col <= row, counts, 0.0), axis=1, keepdims=True)
    starts = jnp.sum(jnp.where(col < row, counts, 0.0), axis=1, keepdims=True)
    positions = (place + spread * iota((1, slots), 1)).astype(F32)
    owner = jnp.where((starts <= positions) & (positions < ends), 1.0, 0.0).astype(BF16)
    owner_ref[...] = owner
    copies[1].wait()
    occupied = occ_ref[...].astype(F32).astype(BF16)
    occupied_ref[...] = occupied
    copies[2].wait()
    copies[3].wait()
    w1 = w1_ref[...]
    bias = bias_ref[...]
    hidden_ref[slots:, :] = jnp.tanh(dot(occupied, w1, ((1,), (0,))) + bias).astype(BF16)
    copies[4].wait()
    for start in range(0, slots, ROWS):
        stop = min(start + ROWS, slots)
        parent_occ = dot(occupied, owner[:, start:stop], ((0,), (0,)))
        columns = iota((orbitals, stop - start), 0)
        flipped = columns == orbitals_ref[0:1, start:stop]
        for u in range(1, updates):
            flipped = flipped | (columns == orbitals_ref[u : u + 1, start:stop])
        slot_occ = jnp.where(flipped, 1.0 - parent_occ, parent_occ).astype(BF16)
        pre = dot(slot_occ, w1, ((0,), (0,))) + bias
        hidden_ref[start:stop, :] = jnp.tanh(pre).astype(BF16)
    copies[5].wait()
    copies[6].wait()
    copies[7].wait()


def sine_cosine(x):
    turns = jnp.floor(x * (2.0 / math.pi) + 0.5)
    rest = ((x - turns * 1.5703125) - turns * 4.837512969970703125e-4) - turns * 7.549789948768648e-8
    square = rest * rest
    sine = (-1.9515295891e-4 * square + 8.3321608736e-3) * square - 1.6666654611e-1
    sine = rest + rest * square * sine
    cosine = (2.443315711809948e-5 * square - 1.388731625493765e-3) * square + 4.166664568298827e-2
    cosine = 1.0 - 0.5 * square + square * square * cosine
    quarter = turns.astype(jnp.int32) & 3
    odd = (quarter & 1) == 1
    high_sine = jnp.where(odd, cosine, sine)
    high_cosine = jnp.where(odd, sine, cosine)
    sine = jnp.where(quarter >= 2, -high_sine, high_sine)
    cosine = jnp.where((quarter == 1) | (quarter == 2), -high_cosine, high_cosine)
    return sine, cosine


def slot_energy_kernel(
    shifts, field_ref, hidden_ref, owner_ref, elements_ref, readout_ref, *refs
):
    shard_refs, (send_ref, second_ref) = refs[: len(shifts)], refs[len(shifts) :]
    here, slots = owner_ref.shape
    chips = lax.axis_size("chip")
    chip, core = lax.axis_index("chip"), lax.axis_index("core")
    for (step, other), shard in zip(shifts, shard_refs):
        rows = shard.shape[0]
        source = lax.rem(chip + chips - step, chips) * 2 + (core ^ other)
        second_ref[pl.ds(pl.multiple_of(source * rows, rows), rows), :] = shard[...]
    mid = jnp.tanh(dot(second_ref[...], hidden_ref[...], ((0,), (1,))))
    readout = readout_ref[...].T
    logs_re = jnp.sum(mid * readout[:, 0:1], axis=0, keepdims=True)
    logs_im = jnp.sum(mid * readout[:, 1:2], axis=0, keepdims=True)
    owner = owner_ref[...]
    own = jnp.concatenate(parts(logs_re[:, slots:]) + parts(logs_im[:, slots:]), axis=0)
    parent = dot(own, owner, ((1,), (0,)))
    diff_re = logs_re[:, :slots] - (parent[0:1] + parent[1:2] + parent[2:3])
    diff_im = logs_im[:, :slots] - (parent[3:4] + parent[4:5] + parent[5:6])
    used = jnp.sum(owner.astype(F32), axis=0, keepdims=True) > 0.0
    weight = elements_ref[0:1, :] + field_ref[...] * elements_ref[1:2, :]
    scale = weight * jnp.exp(diff_re)
    sine, cosine = sine_cosine(diff_im)
    contrib_re = jnp.where(used, scale * cosine, 0.0)
    contrib_im = jnp.where(used, scale * sine, 0.0)
    contrib = jnp.concatenate(parts(contrib_re) + parts(contrib_im), axis=0)
    sums = dot(contrib, owner, ((1,), (1,)))
    partial_re = sums[0:1] + sums[1:2] + sums[2:3]
    partial_im = sums[3:4] + sums[4:5] + sums[5:6]
    row = jnp.concatenate([partial_re, partial_im], axis=1)
    send_ref[...] = jnp.broadcast_to(row[None], send_ref.shape)


def collect(entries, spread, received_ref):
    peers, here = received_ref.shape[0], received_ref.shape[2] // 2
    block = lax.axis_index("samples")
    out_re, out_im = [], []
    for entry in entries:
        first = lax.rem((block ^ entry) * spread + peers // 2, peers)
        row = received_ref[first]
        for k in range(1, spread):
            row = row + received_ref[first + k]
        out_re.append(row[:, :here])
        out_im.append(row[:, here:])
    return jnp.concatenate([jnp.concatenate(out_re, axis=1), jnp.concatenate(out_im, axis=1)], axis=0)


def collect_kernel(entries, spread, received_ref, after_ref, energy_ref):
    del after_ref
    energy_ref[...] = collect(entries, spread, received_ref)


def sample_values(packed_ref, w1_ref, bias_ref, second_ref, readout_ref, size):
    hidden = jnp.tanh(sample_pre(packed_ref, w1_ref, bias_ref, size)).astype(BF16)
    mid = jnp.tanh(dot(second_ref[...], hidden, ((0,), (1,))))
    slope = 1.0 - mid * mid
    readout = readout_ref[...].T
    return hidden, slope * readout[:, 0:1], slope * readout[:, 1:2]


def pack_kernel(mine_ref, moved_ref, after_ref, packed_ref):
    del after_ref
    blocks, here, orbitals = mine_ref.shape
    full = packed_ref.shape[1]
    pieces = [mine_ref[k] for k in range(blocks)] + [moved_ref[k] for k in range(blocks)]
    rest = orbitals - full
    for k, piece in enumerate(pieces):
        packed_ref[k * here : (k + 1) * here, :] = piece[:, :full]
    rests = [piece[:, full:].astype(F32) for piece in pieces]
    rests.append(jnp.zeros((here, full - rest * len(pieces)), F32))
    packed_ref[len(pieces) * here :, :] = jnp.concatenate(rests, axis=1).astype(BF16)


def sample_pre(packed_ref, w1_ref, bias_ref, size):
    full = packed_ref.shape[1]
    here = packed_ref.shape[0] - size
    rest = w1_ref.shape[0] - full
    tail = packed_ref[size:, :].astype(F32)
    rests = [tail[:, k * rest : (k + 1) * rest] for k in range(size // here)]
    tail = jnp.concatenate(rests, axis=0).astype(BF16)
    pre = dot(packed_ref[:size, :], w1_ref[:full, :], ((1,), (0,)))
    return pre + dot(tail, w1_ref[full:, :], ((1,), (0,))) + bias_ref[...]


def put(overlap_ref, overlap):
    size = overlap.shape[0]
    high = overlap.astype(BF16)
    overlap_ref[:size, :] = high
    overlap_ref[size : 2 * size, :] = (overlap - high.astype(F32)).astype(BF16)
    overlap_ref[2 * size :, :] = high


def near_half_kernel(
    packed_ref, w1_ref, bias_ref, second_ref, readout_ref, w1_again, hidden_ref, near_ref, re_ref, im_ref
):
    w1_again[...] = w1_ref[...]
    size = hidden_ref.shape[0]
    hidden, re_ref[...], im_ref[...] = sample_values(packed_ref, w1_ref, bias_ref, second_ref, readout_ref, size)
    hidden_ref[...] = hidden
    put(near_ref, dot(hidden, hidden, ((1,), (1,))))


def far_half_kernel(
    packed_ref,
    w1_ref,
    bias_ref,
    second_ref,
    readout_ref,
    hidden_ref,
    near_far_ref,
    far_near_ref,
    far_ref,
    re_ref,
    im_ref,
):
    size = hidden_ref.shape[0]
    hidden, re_ref[...], im_ref[...] = sample_values(packed_ref, w1_ref, bias_ref, second_ref, readout_ref, size)
    near = hidden_ref[...]
    put(near_far_ref, dot(near, hidden, ((1,), (1,))))
    put(far_near_ref, dot(hidden, near, ((1,), (1,))))
    put(far_ref, dot(hidden, hidden, ((1,), (1,))))


def solve(energy, gram):
    total = energy.shape[1]
    centered = energy - jnp.mean(energy, axis=1, keepdims=True)
    res_c = jnp.concatenate([centered[1:2], -centered[0:1]], axis=0) / total
    res_y = gram(res_c)
    dir_c, dir_y = res_c, res_y
    norm_now = full_sum(res_c * res_y)
    cross, square = norm_now, full_sum(res_y * res_y)
    change = jnp.zeros_like(res_y)
    for turn in range(ITERS):
        alpha = norm_now / (square / total + DIAG_SHIFT * cross)
        change = change + alpha * dir_y
        if turn + 1 < ITERS:
            img_c = dir_y / total + DIAG_SHIFT * dir_c
            img_y = gram(dir_y) / total + DIAG_SHIFT * dir_y
            res_c = res_c - alpha * img_c
            res_y = res_y - alpha * img_y
            norm_next = full_sum(res_c * res_y)
            mixed = full_sum(res_c * dir_y) + full_sum(dir_c * res_y)
            squares = full_sum(res_y * res_y), full_sum(res_y * dir_y)
            beta = norm_next / norm_now
            cross = norm_next + beta * mixed + beta * beta * cross
            square = squares[0] + 2.0 * beta * squares[1] + beta * beta * square
            dir_c = res_c + beta * dir_c
            dir_y = res_y + beta * dir_y
            norm_now = norm_next
    return change


def full_sum(x):
    return jnp.sum(jnp.sum(x, axis=1, keepdims=True), axis=0, keepdims=True)


def project(lifted, slope_re, slope_im):
    raw = jnp.concatenate(
        [jnp.sum(lifted * slope_re, axis=0, keepdims=True), jnp.sum(lifted * slope_im, axis=0, keepdims=True)],
        axis=0,
    )
    return raw - jnp.mean(raw, axis=1, keepdims=True)


def solve_kernel(
    entries,
    spread,
    received_ref,
    near_ref,
    near_re_ref,
    near_im_ref,
    near_far_ref,
    far_near_ref,
    far_ref,
    far_re_ref,
    far_im_ref,
    local_ref,
    change_ref,
):
    width = local_ref.shape[1]
    half = near_ref.shape[1]
    energy = collect(entries, spread, received_ref)
    local_ref[...] = energy[:, :width]

    def scaled(c, re_ref, im_ref):
        back = re_ref[...] * c[0:1] + im_ref[...] * c[1:2]
        high = back.astype(BF16)
        low = (back - high.astype(F32)).astype(BF16)
        return jnp.concatenate([high, high, low], axis=1)

    def raw(lifted, re_ref, im_ref):
        re = jnp.sum(lifted * re_ref[...], axis=0, keepdims=True)
        return jnp.concatenate([re, jnp.sum(lifted * im_ref[...], axis=0, keepdims=True)], axis=0)

    def gram(c):
        near = scaled(c[:, :half], near_re_ref, near_im_ref)
        far = scaled(c[:, half:], far_re_ref, far_im_ref)
        to_near = dot(near, near_ref[...], ((1,), (0,))) + dot(far, far_near_ref[...], ((1,), (0,)))
        to_far = dot(near, near_far_ref[...], ((1,), (0,))) + dot(far, far_ref[...], ((1,), (0,)))
        both = jnp.concatenate(
            [raw(to_near, near_re_ref, near_im_ref), raw(to_far, far_re_ref, far_im_ref)], axis=1
        )
        return both - jnp.mean(both, axis=1, keepdims=True)

    change_ref[...] = solve(energy, gram)[:, :width]


def wide_solve(energy, occ_stack, first_weight, bias_row, second, readout):
    here = occ_stack.shape[1]
    occupied = occ_stack.reshape(-1, occ_stack.shape[2])
    pre = dot(occupied, first_weight, ((1,), (0,))) + bias_row
    hidden = jnp.tanh(pre).astype(BF16)
    mid = jnp.tanh(dot(second, hidden, ((0,), (1,))))
    slope = 1.0 - mid * mid
    slope_re = slope * readout[0][:, None]
    slope_im = slope * readout[1][:, None]

    def gram(c):
        high, low = split(slope_re * c[0:1] + slope_im * c[1:2])
        high, low = split(dot(high, hidden, ((1,), (0,))) + dot(low, hidden, ((1,), (0,))))
        lifted = dot(high, hidden, ((1,), (1,))) + dot(low, hidden, ((1,), (1,)))
        return project(lifted, slope_re, slope_im)

    return energy[:, :here], solve(energy, gram)[:, :here]


def swap(x, axis, bit):
    return lax.ppermute(x, axis, [(i, i ^ bit) for i in range(lax.axis_size(axis))])


def shift(x, axis, step):
    size = lax.axis_size(axis)
    return lax.ppermute(x, axis, [(i, (i + step) % size) for i in range(size)])


def exchange_all(send):
    peers = send.shape[0]
    return lax.all_to_all(
        send,
        ("samples", "chip", "core"),
        0,
        0,
        axis_index_groups=[[(k + peers // 2) % peers for k in range(peers)]],
        tiled=True,
    )


def powers(size):
    return [1 << k for k in reversed(range((size - 1).bit_length()))]


def body(
    occupations,
    connection_counts,
    connection_orbitals,
    connection_elements,
    laser_step,
    first_weight,
    first_bias,
    second_weight,
    readout,
):
    here, orbitals = occupations.shape
    slots = connection_orbitals.shape[1]
    wide, narrow = first_weight.shape[1], second_weight.shape[1]
    chips = lax.axis_size("chip")
    spread = chips * lax.axis_size("core")
    blocks = lax.axis_size("samples")
    total = here * blocks
    bias_row = first_bias[None, :]
    field = FIELD_SCALE * jnp.sin(FIELD_RATE * laser_step.astype(F32)[None, None])

    bits = powers(blocks)
    bits = bits[-1:] + bits[:-1]
    entries = [0]
    for bit in bits:
        entries = entries + [e ^ bit for e in entries]
    moved = swap(occupations[None], "samples", bits[0])

    shifts, shards = [], []
    for step in range(1, chips):
        shifts.append((step, 0))
        shards.append(shift(second_weight, "chip", step))
    shifts.append((0, 1))
    shards.append(shift(second_weight, "core", 1))

    hidden, owner, elements, w1, bias, readout_near, own_shard, occupied = call(
        functools.partial(slot_hidden_kernel, spread),
        8,
        (
            jax.ShapeDtypeStruct((slots + here, wide), BF16),
            jax.ShapeDtypeStruct((here, slots), BF16),
            jax.ShapeDtypeStruct(connection_elements.shape, F32),
            jax.ShapeDtypeStruct(first_weight.shape, BF16),
            jax.ShapeDtypeStruct(bias_row.shape, F32),
            jax.ShapeDtypeStruct(readout.shape, F32),
            jax.ShapeDtypeStruct(second_weight.shape, BF16),
            jax.ShapeDtypeStruct(occupations.shape, BF16),
        ),
        [
            pltpu.VMEM((1, here), jnp.int32),
            pltpu.VMEM(connection_orbitals.shape, jnp.int32),
            pltpu.VMEM(occupations.shape, jnp.int32),
            pltpu.SemaphoreType.DMA((8,)),
        ],
        name="slot_hidden",
        copies=True,
        flops=2 * (slots + here) * orbitals * wide,
        transcendentals=(slots + here) * wide,
    )(
        *(
            pltpu.with_memory_space_constraint(x, pltpu.HBM)
            for x in (
                connection_counts[None, :],
                connection_orbitals,
                occupations,
                first_weight,
                bias_row,
                connection_elements,
                readout,
                second_weight,
            )
        ),
    )
    relayed, occupied, field = lax.optimization_barrier((shards[: chips - 1], occupied, field))
    for step in range(1, chips):
        shifts.append((step, 1))
        shards.append(shift(relayed[step - 1], "core", 1))
    shifts.append((0, 0))
    stack = jnp.concatenate([occupied[None], moved.astype(BF16)], axis=0)
    moved = swap(stack, "samples", bits[1])

    send, second = call(
        functools.partial(slot_energy_kernel, tuple(shifts)),
        5 + len(shifts),
        (
            jax.ShapeDtypeStruct((blocks * spread, 1, 2 * here), F32),
            jax.ShapeDtypeStruct((wide, narrow), BF16),
        ),
        name="slot_energy",
        flops=2 * (slots + here) * wide * narrow,
        transcendentals=(slots + here) * narrow,
    )(field, hidden, owner, elements, readout_near, *shards, own_shard)
    received = exchange_all(send)

    def collected(after):
        return call(
            functools.partial(collect_kernel, entries, spread),
            2,
            jax.ShapeDtypeStruct((2, total), F32),
            name="collect",
            flops=COLLECT_WEIGHT,
        )(received, after)

    for bit in bits[2:-1]:
        stack = jnp.concatenate([stack, moved], axis=0)
        moved = swap(stack, "samples", bit)
    if total > wide:
        stack = jnp.concatenate([stack, moved], axis=0)
        stack = jnp.concatenate([stack, swap(stack, "samples", bits[-1])], axis=0)
        return wide_solve(collected(stack), stack, first_weight, bias_row, second, readout)

    half = total // 2
    weights = (w1, bias, second, readout_near)
    full = orbitals // 128 * 128
    packed = call(
        pack_kernel,
        3,
        jax.ShapeDtypeStruct((half + here, full), BF16),
        name="pack",
    )(stack, moved, second)
    far_packed = swap(packed, "samples", bits[-1])
    block = jax.ShapeDtypeStruct((3 * half, half), BF16)
    slopes = (jax.ShapeDtypeStruct((narrow, half), F32),) * 2
    w1, near_hidden, *near = call(
        near_half_kernel,
        5,
        (jax.ShapeDtypeStruct(w1.shape, BF16), jax.ShapeDtypeStruct((half, wide), BF16), block) + slopes,
        name="near_half",
        flops=NEAR_WEIGHT,
        transcendentals=half * (wide + narrow),
    )(packed, *weights)
    far = call(
        far_half_kernel,
        6,
        (block,) * 3 + slopes,
        name="far_half",
        flops=2 * half * wide * (orbitals + narrow + 3 * half),
        transcendentals=half * (wide + narrow),
    )(far_packed, w1, *weights[1:], near_hidden)
    return call(
        functools.partial(solve_kernel, entries, spread),
        9,
        (jax.ShapeDtypeStruct((2, here), F32),) * 2,
        name="solve",
        flops=COLLECT_WEIGHT,
    )(received, *near, *far)


def solution(mesh):
    blocks, spread = mesh.shape["samples"], mesh.shape["params"]
    fine = Mesh(mesh.devices.reshape(blocks, spread // 2, 2), ("samples", "chip", "core"))
    return jax.shard_map(
        body,
        mesh=fine,
        in_specs=(
            P("samples", None),
            P("samples"),
            P(None, ("samples", "chip", "core")),
            P(None, ("samples", "chip", "core")),
            P(),
            P(),
            P(),
            P(("chip", "core"), None),
            P(),
        ),
        out_specs=(P(None, "samples"), P(None, "samples")),
        check_vma=False,
    )
```

```python
import functools
import math

import jax
import jax.numpy as jnp
from jax import lax
from jax.experimental import pallas as pl
from jax.experimental.pallas import tpu as pltpu
from jax.sharding import Mesh, PartitionSpec as P

ITERS = 2


FIELD_SCALE = 0.8
FIELD_RATE = 0.0123
DIAG_SHIFT = 0.01
F32 = jnp.float32
BF16 = jnp.bfloat16
ROWS = 768
COLLECT_WEIGHT = 1e10
NEAR_WEIGHT = 1e10
VMEM_LIMIT = 48 * 1024 * 1024


def dot(a, b, dims):
    return lax.dot_general(a, b, (dims, ((), ())), preferred_element_type=F32)


def split(x):
    high = lax.reduce_precision(x, 8, 7)
    return high.astype(BF16), (x - high).astype(BF16)


def parts(x):
    high = x.astype(BF16)
    rest = x - high.astype(F32)
    middle = rest.astype(BF16)
    return high, middle, (rest - middle.astype(F32)).astype(BF16)


def iota(shape, dim):
    return lax.broadcasted_iota(jnp.int32, shape, dim)


def call(kernel, count, out_shape, scratch=(), name=None, copies=False, flops=0, transcendentals=0):
    vmem = pl.BlockSpec(memory_space=pltpu.VMEM)
    far = pl.BlockSpec(memory_space=pltpu.HBM)
    return pl.pallas_call(
        kernel,
        out_shape=out_shape,
        in_specs=[far if copies else vmem] * count,
        out_specs=jax.tree.map(lambda _: vmem, out_shape),
        scratch_shapes=scratch,
        compiler_params=pltpu.CompilerParams(vmem_limit_bytes=VMEM_LIMIT),
        cost_estimate=pl.CostEstimate(
            flops=int(flops),
            transcendentals=int(transcendentals),
            bytes_accessed=sum(x.size * x.dtype.itemsize for x in jax.tree.leaves(out_shape)),
        ),
        name=name,
    )


def slot_hidden_kernel(
    spread,
    counts_hbm,
    orbitals_hbm,
    occ_hbm,
    w1_hbm,
    bias_hbm,
    elements_hbm,
    readout_hbm,
    own_hbm,
    hidden_ref,
    owner_ref,
    elements_ref,
    w1_ref,
    bias_ref,
    readout_ref,
    own_ref,
    occupied_ref,
    counts_ref,
    orbitals_ref,
    occ_ref,
    sems,
):
    here, orbitals = occ_ref.shape
    updates, slots = orbitals_ref.shape
    pairs = (
        (counts_hbm, counts_ref),
        (occ_hbm, occ_ref),
        (w1_hbm, w1_ref),
        (bias_hbm, bias_ref),
        (orbitals_hbm, orbitals_ref),
        (elements_hbm, elements_ref),
        (readout_hbm, readout_ref),
        (own_hbm, own_ref),
    )
    copies = [pltpu.make_async_copy(a, b, sems.at[i]) for i, (a, b) in enumerate(pairs)]
    for copy in copies:
        copy.start()
    chip, core = lax.axis_index("chip"), lax.axis_index("core")
    place = chip * 2 + core
    copies[0].wait()
    counts = counts_ref[...].astype(F32)
    row, col = iota((here, here), 0), iota((here, here), 1)
    ends = jnp.sum(jnp.where(col <= row, counts, 0.0), axis=1, keepdims=True)
    starts = jnp.sum(jnp.where(col < row, counts, 0.0), axis=1, keepdims=True)
    positions = (place + spread * iota((1, slots), 1)).astype(F32)
    owner = jnp.where((starts <= positions) & (positions < ends), 1.0, 0.0).astype(BF16)
    owner_ref[...] = owner
    copies[1].wait()
    occupied = occ_ref[...].astype(F32).astype(BF16)
    occupied_ref[...] = occupied
    copies[2].wait()
    copies[3].wait()
    w1 = w1_ref[...]
    bias = bias_ref[...]
    hidden_ref[slots:, :] = jnp.tanh(dot(occupied, w1, ((1,), (0,))) + bias).astype(BF16)
    copies[4].wait()
    for start in range(0, slots, ROWS):
        stop = min(start + ROWS, slots)
        parent_occ = dot(occupied, owner[:, start:stop], ((0,), (0,)))
        columns = iota((orbitals, stop - start), 0)
        flipped = columns == orbitals_ref[0:1, start:stop]
        for u in range(1, updates):
            flipped = flipped | (columns == orbitals_ref[u : u + 1, start:stop])
        slot_occ = jnp.where(flipped, 1.0 - parent_occ, parent_occ).astype(BF16)
        pre = dot(slot_occ, w1, ((0,), (0,))) + bias
        hidden_ref[start:stop, :] = jnp.tanh(pre).astype(BF16)
    copies[5].wait()
    copies[6].wait()
    copies[7].wait()


def sine_cosine(x):
    turns = jnp.floor(x * (2.0 / math.pi) + 0.5)
    rest = ((x - turns * 1.5703125) - turns * 4.837512969970703125e-4) - turns * 7.549789948768648e-8
    square = rest * rest
    sine = (-1.9515295891e-4 * square + 8.3321608736e-3) * square - 1.6666654611e-1
    sine = rest + rest * square * sine
    cosine = (2.443315711809948e-5 * square - 1.388731625493765e-3) * square + 4.166664568298827e-2
    cosine = 1.0 - 0.5 * square + square * square * cosine
    quarter = turns.astype(jnp.int32) & 3
    odd = (quarter & 1) == 1
    high_sine = jnp.where(odd, cosine, sine)
    high_cosine = jnp.where(odd, sine, cosine)
    sine = jnp.where(quarter >= 2, -high_sine, high_sine)
    cosine = jnp.where((quarter == 1) | (quarter == 2), -high_cosine, high_cosine)
    return sine, cosine


def slot_energy_kernel(
    shifts, field_ref, hidden_ref, owner_ref, elements_ref, readout_ref, *refs
):
    shard_refs, (send_ref, second_ref) = refs[: len(shifts)], refs[len(shifts) :]
    here, slots = owner_ref.shape
    chips = lax.axis_size("chip")
    chip, core = lax.axis_index("chip"), lax.axis_index("core")
    for (step, other), shard in zip(shifts, shard_refs):
        rows = shard.shape[0]
        source = lax.rem(chip + chips - step, chips) * 2 + (core ^ other)
        second_ref[pl.ds(pl.multiple_of(source * rows, rows), rows), :] = shard[...]
    mid = jnp.tanh(dot(second_ref[...], hidden_ref[...], ((0,), (1,))))
    readout = readout_ref[...].T
    logs_re = jnp.sum(mid * readout[:, 0:1], axis=0, keepdims=True)
    logs_im = jnp.sum(mid * readout[:, 1:2], axis=0, keepdims=True)
    owner = owner_ref[...]
    own = jnp.concatenate(parts(logs_re[:, slots:]) + parts(logs_im[:, slots:]), axis=0)
    parent = dot(own, owner, ((1,), (0,)))
    diff_re = logs_re[:, :slots] - (parent[0:1] + parent[1:2] + parent[2:3])
    diff_im = logs_im[:, :slots] - (parent[3:4] + parent[4:5] + parent[5:6])
    used = jnp.sum(owner.astype(F32), axis=0, keepdims=True) > 0.0
    weight = elements_ref[0:1, :] + field_ref[...] * elements_ref[1:2, :]
    scale = weight * jnp.exp(diff_re)
    sine, cosine = sine_cosine(diff_im)
    contrib_re = jnp.where(used, scale * cosine, 0.0)
    contrib_im = jnp.where(used, scale * sine, 0.0)
    contrib = jnp.concatenate(parts(contrib_re) + parts(contrib_im), axis=0)
    sums = dot(contrib, owner, ((1,), (1,)))
    partial_re = sums[0:1] + sums[1:2] + sums[2:3]
    partial_im = sums[3:4] + sums[4:5] + sums[5:6]
    row = jnp.concatenate([partial_re, partial_im], axis=1)
    send_ref[...] = jnp.broadcast_to(row[None], send_ref.shape)


def collect(entries, spread, received_ref):
    peers, here = received_ref.shape[0], received_ref.shape[2] // 2
    block = lax.axis_index("samples")
    out_re, out_im = [], []
    for entry in entries:
        first = lax.rem((block ^ entry) * spread + peers // 2, peers)
        row = received_ref[first]
        for k in range(1, spread):
            row = row + received_ref[first + k]
        out_re.append(row[:, :here])
        out_im.append(row[:, here:])
    return jnp.concatenate([jnp.concatenate(out_re, axis=1), jnp.concatenate(out_im, axis=1)], axis=0)


def collect_kernel(entries, spread, received_ref, after_ref, energy_ref):
    del after_ref
    energy_ref[...] = collect(entries, spread, received_ref)


def sample_values(packed_ref, w1_ref, bias_ref, second_ref, readout_ref, size):
    hidden = jnp.tanh(sample_pre(packed_ref, w1_ref, bias_ref, size)).astype(BF16)
    mid = jnp.tanh(dot(second_ref[...], hidden, ((0,), (1,))))
    slope = 1.0 - mid * mid
    readout = readout_ref[...].T
    return hidden, slope * readout[:, 0:1], slope * readout[:, 1:2]


def pack_kernel(mine_ref, moved_ref, after_ref, packed_ref):
    del after_ref
    blocks, here, orbitals = mine_ref.shape
    full = packed_ref.shape[1]
    pieces = [mine_ref[k] for k in range(blocks)] + [moved_ref[k] for k in range(blocks)]
    rest = orbitals - full
    for k, piece in enumerate(pieces):
        packed_ref[k * here : (k + 1) * here, :] = piece[:, :full]
    rests = [piece[:, full:].astype(F32) for piece in pieces]
    rests.append(jnp.zeros((here, full - rest * len(pieces)), F32))
    packed_ref[len(pieces) * here :, :] = jnp.concatenate(rests, axis=1).astype(BF16)


def sample_pre(packed_ref, w1_ref, bias_ref, size):
    full = packed_ref.shape[1]
    here = packed_ref.shape[0] - size
    rest = w1_ref.shape[0] - full
    tail = packed_ref[size:, :].astype(F32)
    rests = [tail[:, k * rest : (k + 1) * rest] for k in range(size // here)]
    tail = jnp.concatenate(rests, axis=0).astype(BF16)
    pre = dot(packed_ref[:size, :], w1_ref[:full, :], ((1,), (0,)))
    return pre + dot(tail, w1_ref[full:, :], ((1,), (0,))) + bias_ref[...]


def put(overlap_ref, overlap):
    size = overlap.shape[0]
    high = overlap.astype(BF16)
    overlap_ref[:size, :] = high
    overlap_ref[size : 2 * size, :] = (overlap - high.astype(F32)).astype(BF16)
    overlap_ref[2 * size :, :] = high


def near_half_kernel(
    packed_ref, w1_ref, bias_ref, second_ref, readout_ref, w1_again, hidden_ref, near_ref, re_ref, im_ref
):
    w1_again[...] = w1_ref[...]
    size = hidden_ref.shape[0]
    hidden, re_ref[...], im_ref[...] = sample_values(packed_ref, w1_ref, bias_ref, second_ref, readout_ref, size)
    hidden_ref[...] = hidden
    put(near_ref, dot(hidden, hidden, ((1,), (1,))))


def far_half_kernel(
    packed_ref,
    w1_ref,
    bias_ref,
    second_ref,
    readout_ref,
    hidden_ref,
    near_far_ref,
    far_near_ref,
    far_ref,
    re_ref,
    im_ref,
):
    size = hidden_ref.shape[0]
    hidden, re_ref[...], im_ref[...] = sample_values(packed_ref, w1_ref, bias_ref, second_ref, readout_ref, size)
    near = hidden_ref[...]
    put(near_far_ref, dot(near, hidden, ((1,), (1,))))
    put(far_near_ref, dot(hidden, near, ((1,), (1,))))
    put(far_ref, dot(hidden, hidden, ((1,), (1,))))


def solve(energy, gram):
    total = energy.shape[1]
    centered = energy - jnp.mean(energy, axis=1, keepdims=True)
    res_c = jnp.concatenate([centered[1:2], -centered[0:1]], axis=0) / total
    res_y = gram(res_c)
    dir_c, dir_y = res_c, res_y
    norm_now = full_sum(res_c * res_y)
    cross, square = norm_now, full_sum(res_y * res_y)
    change = jnp.zeros_like(res_y)
    for turn in range(ITERS):
        alpha = norm_now / (square / total + DIAG_SHIFT * cross)
        change = change + alpha * dir_y
        if turn + 1 < ITERS:
            img_c = dir_y / total + DIAG_SHIFT * dir_c
            img_y = gram(dir_y) / total + DIAG_SHIFT * dir_y
            res_c = res_c - alpha * img_c
            res_y = res_y - alpha * img_y
            norm_next = full_sum(res_c * res_y)
            mixed = full_sum(res_c * dir_y) + full_sum(dir_c * res_y)
            squares = full_sum(res_y * res_y), full_sum(res_y * dir_y)
            beta = norm_next / norm_now
            cross = norm_next + beta * mixed + beta * beta * cross
            square = squares[0] + 2.0 * beta * squares[1] + beta * beta * square
            dir_c = res_c + beta * dir_c
            dir_y = res_y + beta * dir_y
            norm_now = norm_next
    return change


def full_sum(x):
    return jnp.sum(jnp.sum(x, axis=1, keepdims=True), axis=0, keepdims=True)


def project(lifted, slope_re, slope_im):
    raw = jnp.concatenate(
        [jnp.sum(lifted * slope_re, axis=0, keepdims=True), jnp.sum(lifted * slope_im, axis=0, keepdims=True)],
        axis=0,
    )
    return raw - jnp.mean(raw, axis=1, keepdims=True)


def solve_kernel(
    energy_ref,
    near_ref,
    near_re_ref,
    near_im_ref,
    near_far_ref,
    far_near_ref,
    far_ref,
    far_re_ref,
    far_im_ref,
    local_ref,
    change_ref,
):
    width = local_ref.shape[1]
    half = near_ref.shape[1]
    energy = energy_ref[...]
    local_ref[...] = energy[:, :width]

    def scaled(c, re_ref, im_ref):
        back = re_ref[...] * c[0:1] + im_ref[...] * c[1:2]
        high = back.astype(BF16)
        low = (back - high.astype(F32)).astype(BF16)
        return jnp.concatenate([high, high, low], axis=1)

    def raw(lifted, re_ref, im_ref):
        re = jnp.sum(lifted * re_ref[...], axis=0, keepdims=True)
        return jnp.concatenate([re, jnp.sum(lifted * im_ref[...], axis=0, keepdims=True)], axis=0)

    def gram(c):
        near = scaled(c[:, :half], near_re_ref, near_im_ref)
        far = scaled(c[:, half:], far_re_ref, far_im_ref)
        to_near = dot(near, near_ref[...], ((1,), (0,))) + dot(far, far_near_ref[...], ((1,), (0,)))
        to_far = dot(near, near_far_ref[...], ((1,), (0,))) + dot(far, far_ref[...], ((1,), (0,)))
        both = jnp.concatenate(
            [raw(to_near, near_re_ref, near_im_ref), raw(to_far, far_re_ref, far_im_ref)], axis=1
        )
        return both - jnp.mean(both, axis=1, keepdims=True)

    change_ref[...] = solve(energy, gram)[:, :width]


def wide_solve(energy, occ_stack, first_weight, bias_row, second, readout):
    here = occ_stack.shape[1]
    occupied = occ_stack.reshape(-1, occ_stack.shape[2])
    pre = dot(occupied, first_weight, ((1,), (0,))) + bias_row
    hidden = jnp.tanh(pre).astype(BF16)
    mid = jnp.tanh(dot(second, hidden, ((0,), (1,))))
    slope = 1.0 - mid * mid
    slope_re = slope * readout[0][:, None]
    slope_im = slope * readout[1][:, None]

    def gram(c):
        high, low = split(slope_re * c[0:1] + slope_im * c[1:2])
        high, low = split(dot(high, hidden, ((1,), (0,))) + dot(low, hidden, ((1,), (0,))))
        lifted = dot(high, hidden, ((1,), (1,))) + dot(low, hidden, ((1,), (1,)))
        return project(lifted, slope_re, slope_im)

    return energy[:, :here], solve(energy, gram)[:, :here]


def swap(x, axis, bit):
    return lax.ppermute(x, axis, [(i, i ^ bit) for i in range(lax.axis_size(axis))])


def shift(x, axis, step):
    size = lax.axis_size(axis)
    return lax.ppermute(x, axis, [(i, (i + step) % size) for i in range(size)])


def exchange_all(send):
    peers = send.shape[0]
    return lax.all_to_all(
        send,
        ("samples", "chip", "core"),
        0,
        0,
        axis_index_groups=[[(k + peers // 2) % peers for k in range(peers)]],
        tiled=True,
    )


def powers(size):
    return [1 << k for k in reversed(range((size - 1).bit_length()))]


def body(
    occupations,
    connection_counts,
    connection_orbitals,
    connection_elements,
    laser_step,
    first_weight,
    first_bias,
    second_weight,
    readout,
):
    here, orbitals = occupations.shape
    slots = connection_orbitals.shape[1]
    wide, narrow = first_weight.shape[1], second_weight.shape[1]
    chips = lax.axis_size("chip")
    spread = chips * lax.axis_size("core")
    blocks = lax.axis_size("samples")
    total = here * blocks
    bias_row = first_bias[None, :]
    field = FIELD_SCALE * jnp.sin(FIELD_RATE * laser_step.astype(F32)[None, None])

    bits = powers(blocks)
    bits = bits[-1:] + bits[:-1]
    entries = [0]
    for bit in bits:
        entries = entries + [e ^ bit for e in entries]
    moved = swap(occupations[None], "samples", bits[0])

    shifts, shards = [], []
    for step in range(1, chips):
        shifts.append((step, 0))
        shards.append(shift(second_weight, "chip", step))
    shifts.append((0, 1))
    shards.append(shift(second_weight, "core", 1))

    hidden, owner, elements, w1, bias, readout_near, own_shard, occupied = call(
        functools.partial(slot_hidden_kernel, spread),
        8,
        (
            jax.ShapeDtypeStruct((slots + here, wide), BF16),
            jax.ShapeDtypeStruct((here, slots), BF16),
            jax.ShapeDtypeStruct(connection_elements.shape, F32),
            jax.ShapeDtypeStruct(first_weight.shape, BF16),
            jax.ShapeDtypeStruct(bias_row.shape, F32),
            jax.ShapeDtypeStruct(readout.shape, F32),
            jax.ShapeDtypeStruct(second_weight.shape, BF16),
            jax.ShapeDtypeStruct(occupations.shape, BF16),
        ),
        [
            pltpu.VMEM((1, here), jnp.int32),
            pltpu.VMEM(connection_orbitals.shape, jnp.int32),
            pltpu.VMEM(occupations.shape, jnp.int32),
            pltpu.SemaphoreType.DMA((8,)),
        ],
        name="slot_hidden",
        copies=True,
        flops=2 * (slots + here) * orbitals * wide,
        transcendentals=(slots + here) * wide,
    )(
        *(
            pltpu.with_memory_space_constraint(x, pltpu.HBM)
            for x in (
                connection_counts[None, :],
                connection_orbitals,
                occupations,
                first_weight,
                bias_row,
                connection_elements,
                readout,
                second_weight,
            )
        ),
    )
    relayed, occupied, field = lax.optimization_barrier((shards[: chips - 1], occupied, field))
    for step in range(1, chips):
        shifts.append((step, 1))
        shards.append(shift(relayed[step - 1], "core", 1))
    shifts.append((0, 0))
    stack = jnp.concatenate([occupied[None], moved.astype(BF16)], axis=0)
    moved = swap(stack, "samples", bits[1])

    send, second = call(
        functools.partial(slot_energy_kernel, tuple(shifts)),
        5 + len(shifts),
        (
            jax.ShapeDtypeStruct((blocks * spread, 1, 2 * here), F32),
            jax.ShapeDtypeStruct((wide, narrow), BF16),
        ),
        name="slot_energy",
        flops=2 * (slots + here) * wide * narrow,
        transcendentals=(slots + here) * narrow,
    )(field, hidden, owner, elements, readout_near, *shards, own_shard)
    received = exchange_all(send)

    def collected(after):
        return call(
            functools.partial(collect_kernel, entries, spread),
            2,
            jax.ShapeDtypeStruct((2, total), F32),
            name="collect",
            flops=COLLECT_WEIGHT,
        )(received, after)

    for bit in bits[2:-1]:
        stack = jnp.concatenate([stack, moved], axis=0)
        moved = swap(stack, "samples", bit)
    if total > wide:
        stack = jnp.concatenate([stack, moved], axis=0)
        stack = jnp.concatenate([stack, swap(stack, "samples", bits[-1])], axis=0)
        return wide_solve(collected(stack), stack, first_weight, bias_row, second, readout)

    half = total // 2
    weights = (w1, bias, second, readout_near)
    full = orbitals // 128 * 128
    packed = call(
        pack_kernel,
        3,
        jax.ShapeDtypeStruct((half + here, full), BF16),
        name="pack",
    )(stack, moved, second)
    far_packed = swap(packed, "samples", bits[-1])
    block = jax.ShapeDtypeStruct((3 * half, half), BF16)
    slopes = (jax.ShapeDtypeStruct((narrow, half), F32),) * 2
    w1, near_hidden, *near = call(
        near_half_kernel,
        5,
        (jax.ShapeDtypeStruct(w1.shape, BF16), jax.ShapeDtypeStruct((half, wide), BF16), block) + slopes,
        name="near_half",
        flops=NEAR_WEIGHT,
        transcendentals=half * (wide + narrow),
    )(packed, *weights)
    far = call(
        far_half_kernel,
        6,
        (block,) * 3 + slopes,
        name="far_half",
        flops=2 * half * wide * (orbitals + narrow + 3 * half),
        transcendentals=half * (wide + narrow),
    )(far_packed, w1, *weights[1:], near_hidden)
    return call(
        solve_kernel,
        9,
        (jax.ShapeDtypeStruct((2, here), F32),) * 2,
        name="solve",
        flops=ITERS * 6 * total * total * narrow,
    )(collected(far[0]), *near, *far)


def solution(mesh):
    blocks, spread = mesh.shape["samples"], mesh.shape["params"]
    fine = Mesh(mesh.devices.reshape(blocks, spread // 2, 2), ("samples", "chip", "core"))
    return jax.shard_map(
        body,
        mesh=fine,
        in_specs=(
            P("samples", None),
            P("samples"),
            P(None, ("samples", "chip", "core")),
            P(None, ("samples", "chip", "core")),
            P(),
            P(),
            P(),
            P(("chip", "core"), None),
            P(),
        ),
        out_specs=(P(None, "samples"), P(None, "samples")),
        check_vma=False,
    )
```

```python
import functools
import math

import jax
import jax.numpy as jnp
from jax import lax
from jax.experimental import pallas as pl
from jax.experimental.pallas import tpu as pltpu
from jax.sharding import Mesh, PartitionSpec as P

ITERS = 2


FIELD_SCALE = 0.8
FIELD_RATE = 0.0123
DIAG_SHIFT = 0.01
F32 = jnp.float32
BF16 = jnp.bfloat16
ROWS = 768
COLLECT_WEIGHT = 1e10
NEAR_WEIGHT = 1e10
VMEM_LIMIT = 48 * 1024 * 1024


def dot(a, b, dims):
    return lax.dot_general(a, b, (dims, ((), ())), preferred_element_type=F32)


def split(x):
    high = lax.reduce_precision(x, 8, 7)
    return high.astype(BF16), (x - high).astype(BF16)


def parts(x):
    high = x.astype(BF16)
    rest = x - high.astype(F32)
    middle = rest.astype(BF16)
    return high, middle, (rest - middle.astype(F32)).astype(BF16)


def iota(shape, dim):
    return lax.broadcasted_iota(jnp.int32, shape, dim)


def call(kernel, count, out_shape, scratch=(), name=None, copies=False, flops=0, transcendentals=0):
    vmem = pl.BlockSpec(memory_space=pltpu.VMEM)
    far = pl.BlockSpec(memory_space=pltpu.HBM)
    return pl.pallas_call(
        kernel,
        out_shape=out_shape,
        in_specs=[far if copies else vmem] * count,
        out_specs=jax.tree.map(lambda _: vmem, out_shape),
        scratch_shapes=scratch,
        compiler_params=pltpu.CompilerParams(vmem_limit_bytes=VMEM_LIMIT),
        cost_estimate=pl.CostEstimate(
            flops=int(flops),
            transcendentals=int(transcendentals),
            bytes_accessed=sum(x.size * x.dtype.itemsize for x in jax.tree.leaves(out_shape)),
        ),
        name=name,
    )


def slot_hidden_kernel(
    spread,
    counts_hbm,
    orbitals_hbm,
    occ_hbm,
    w1_hbm,
    bias_hbm,
    elements_hbm,
    readout_hbm,
    own_hbm,
    hidden_ref,
    owner_ref,
    elements_ref,
    w1_ref,
    bias_ref,
    readout_ref,
    own_ref,
    occupied_ref,
    counts_ref,
    orbitals_ref,
    occ_ref,
    sems,
):
    here, orbitals = occ_ref.shape
    updates, slots = orbitals_ref.shape
    pairs = (
        (counts_hbm, counts_ref),
        (occ_hbm, occ_ref),
        (w1_hbm, w1_ref),
        (bias_hbm, bias_ref),
        (orbitals_hbm, orbitals_ref),
        (elements_hbm, elements_ref),
        (readout_hbm, readout_ref),
        (own_hbm, own_ref),
    )
    copies = [pltpu.make_async_copy(a, b, sems.at[i]) for i, (a, b) in enumerate(pairs)]
    for copy in copies:
        copy.start()
    chip, core = lax.axis_index("chip"), lax.axis_index("core")
    place = chip * 2 + core
    copies[0].wait()
    counts = counts_ref[...].astype(F32)
    row, col = iota((here, here), 0), iota((here, here), 1)
    ends = jnp.sum(jnp.where(col <= row, counts, 0.0), axis=1, keepdims=True)
    starts = jnp.sum(jnp.where(col < row, counts, 0.0), axis=1, keepdims=True)
    positions = (place + spread * iota((1, slots), 1)).astype(F32)
    owner = jnp.where((starts <= positions) & (positions < ends), 1.0, 0.0).astype(BF16)
    owner_ref[...] = owner
    copies[1].wait()
    occupied = occ_ref[...].astype(F32).astype(BF16)
    occupied_ref[...] = occupied
    copies[2].wait()
    copies[3].wait()
    w1 = w1_ref[...]
    bias = bias_ref[...]
    hidden_ref[slots:, :] = jnp.tanh(dot(occupied, w1, ((1,), (0,))) + bias).astype(BF16)
    copies[4].wait()
    for start in range(0, slots, ROWS):
        stop = min(start + ROWS, slots)
        parent_occ = dot(occupied, owner[:, start:stop], ((0,), (0,)))
        columns = iota((orbitals, stop - start), 0)
        flipped = columns == orbitals_ref[0:1, start:stop]
        for u in range(1, updates):
            flipped = flipped | (columns == orbitals_ref[u : u + 1, start:stop])
        slot_occ = jnp.where(flipped, 1.0 - parent_occ, parent_occ).astype(BF16)
        pre = dot(slot_occ, w1, ((0,), (0,))) + bias
        hidden_ref[start:stop, :] = jnp.tanh(pre).astype(BF16)
    copies[5].wait()
    copies[6].wait()
    copies[7].wait()


def sine_cosine(x):
    turns = jnp.floor(x * (2.0 / math.pi) + 0.5)
    rest = ((x - turns * 1.5703125) - turns * 4.837512969970703125e-4) - turns * 7.549789948768648e-8
    square = rest * rest
    sine = (-1.9515295891e-4 * square + 8.3321608736e-3) * square - 1.6666654611e-1
    sine = rest + rest * square * sine
    cosine = (2.443315711809948e-5 * square - 1.388731625493765e-3) * square + 4.166664568298827e-2
    cosine = 1.0 - 0.5 * square + square * square * cosine
    quarter = turns.astype(jnp.int32) & 3
    odd = (quarter & 1) == 1
    high_sine = jnp.where(odd, cosine, sine)
    high_cosine = jnp.where(odd, sine, cosine)
    sine = jnp.where(quarter >= 2, -high_sine, high_sine)
    cosine = jnp.where((quarter == 1) | (quarter == 2), -high_cosine, high_cosine)
    return sine, cosine


def slot_energy_kernel(
    shifts, field_ref, hidden_ref, owner_ref, elements_ref, readout_ref, *refs
):
    shard_refs, (send_ref, second_ref) = refs[: len(shifts)], refs[len(shifts) :]
    here, slots = owner_ref.shape
    chips = lax.axis_size("chip")
    chip, core = lax.axis_index("chip"), lax.axis_index("core")
    for (step, other), shard in zip(shifts, shard_refs):
        rows = shard.shape[0]
        source = lax.rem(chip + chips - step, chips) * 2 + (core ^ other)
        second_ref[pl.ds(pl.multiple_of(source * rows, rows), rows), :] = shard[...]
    mid = jnp.tanh(dot(hidden_ref[...], second_ref[...], ((1,), (0,)))).T
    readout = readout_ref[...].T
    logs_re = jnp.sum(mid * readout[:, 0:1], axis=0, keepdims=True)
    logs_im = jnp.sum(mid * readout[:, 1:2], axis=0, keepdims=True)
    owner = owner_ref[...]
    own = jnp.concatenate(parts(logs_re[:, slots:]) + parts(logs_im[:, slots:]), axis=0)
    parent = dot(own, owner, ((1,), (0,)))
    diff_re = logs_re[:, :slots] - (parent[0:1] + parent[1:2] + parent[2:3])
    diff_im = logs_im[:, :slots] - (parent[3:4] + parent[4:5] + parent[5:6])
    used = jnp.sum(owner.astype(F32), axis=0, keepdims=True) > 0.0
    weight = elements_ref[0:1, :] + field_ref[...] * elements_ref[1:2, :]
    scale = weight * jnp.exp(diff_re)
    sine, cosine = sine_cosine(diff_im)
    contrib_re = jnp.where(used, scale * cosine, 0.0)
    contrib_im = jnp.where(used, scale * sine, 0.0)
    contrib = jnp.concatenate(parts(contrib_re) + parts(contrib_im), axis=0)
    sums = dot(contrib, owner, ((1,), (1,)))
    partial_re = sums[0:1] + sums[1:2] + sums[2:3]
    partial_im = sums[3:4] + sums[4:5] + sums[5:6]
    row = jnp.concatenate([partial_re, partial_im], axis=1)
    send_ref[...] = jnp.broadcast_to(row[None], send_ref.shape)


def collect(entries, spread, received_ref):
    peers, here = received_ref.shape[0], received_ref.shape[2] // 2
    block = lax.axis_index("samples")
    out_re, out_im = [], []
    for entry in entries:
        first = lax.rem((block ^ entry) * spread + peers // 2, peers)
        row = received_ref[first]
        for k in range(1, spread):
            row = row + received_ref[first + k]
        out_re.append(row[:, :here])
        out_im.append(row[:, here:])
    return jnp.concatenate([jnp.concatenate(out_re, axis=1), jnp.concatenate(out_im, axis=1)], axis=0)


def collect_kernel(entries, spread, received_ref, after_ref, energy_ref):
    del after_ref
    energy_ref[...] = collect(entries, spread, received_ref)


def sample_values(packed_ref, w1_ref, bias_ref, second_ref, readout_ref, size):
    hidden = jnp.tanh(sample_pre(packed_ref, w1_ref, bias_ref, size)).astype(BF16)
    mid = jnp.tanh(dot(second_ref[...], hidden, ((0,), (1,))))
    slope = 1.0 - mid * mid
    readout = readout_ref[...].T
    return hidden, slope * readout[:, 0:1], slope * readout[:, 1:2]


def pack_kernel(mine_ref, moved_ref, after_ref, packed_ref):
    del after_ref
    blocks, here, orbitals = mine_ref.shape
    full = packed_ref.shape[1]
    pieces = [mine_ref[k] for k in range(blocks)] + [moved_ref[k] for k in range(blocks)]
    rest = orbitals - full
    for k, piece in enumerate(pieces):
        packed_ref[k * here : (k + 1) * here, :] = piece[:, :full]
    rests = [piece[:, full:].astype(F32) for piece in pieces]
    rests.append(jnp.zeros((here, full - rest * len(pieces)), F32))
    packed_ref[len(pieces) * here :, :] = jnp.concatenate(rests, axis=1).astype(BF16)


def sample_pre(packed_ref, w1_ref, bias_ref, size):
    full = packed_ref.shape[1]
    here = packed_ref.shape[0] - size
    rest = w1_ref.shape[0] - full
    tail = packed_ref[size:, :].astype(F32)
    rests = [tail[:, k * rest : (k + 1) * rest] for k in range(size // here)]
    tail = jnp.concatenate(rests, axis=0).astype(BF16)
    pre = dot(packed_ref[:size, :], w1_ref[:full, :], ((1,), (0,)))
    return pre + dot(tail, w1_ref[full:, :], ((1,), (0,))) + bias_ref[...]


def put(overlap_ref, overlap):
    size = overlap.shape[0]
    high = overlap.astype(BF16)
    overlap_ref[:size, :] = high
    overlap_ref[size : 2 * size, :] = (overlap - high.astype(F32)).astype(BF16)
    overlap_ref[2 * size :, :] = high


def near_half_kernel(
    packed_ref, w1_ref, bias_ref, second_ref, readout_ref, w1_again, hidden_ref, near_ref, re_ref, im_ref
):
    w1_again[...] = w1_ref[...]
    size = hidden_ref.shape[0]
    hidden, re_ref[...], im_ref[...] = sample_values(packed_ref, w1_ref, bias_ref, second_ref, readout_ref, size)
    hidden_ref[...] = hidden
    put(near_ref, dot(hidden, hidden, ((1,), (1,))))


def far_half_kernel(
    packed_ref,
    w1_ref,
    bias_ref,
    second_ref,
    readout_ref,
    hidden_ref,
    near_far_ref,
    far_near_ref,
    far_ref,
    re_ref,
    im_ref,
):
    size = hidden_ref.shape[0]
    hidden, re_ref[...], im_ref[...] = sample_values(packed_ref, w1_ref, bias_ref, second_ref, readout_ref, size)
    near = hidden_ref[...]
    put(near_far_ref, dot(near, hidden, ((1,), (1,))))
    put(far_near_ref, dot(hidden, near, ((1,), (1,))))
    put(far_ref, dot(hidden, hidden, ((1,), (1,))))


def solve(energy, gram):
    total = energy.shape[1]
    centered = energy - jnp.mean(energy, axis=1, keepdims=True)
    res_c = jnp.concatenate([centered[1:2], -centered[0:1]], axis=0) / total
    res_y = gram(res_c)
    dir_c, dir_y = res_c, res_y
    norm_now = full_sum(res_c * res_y)
    cross, square = norm_now, full_sum(res_y * res_y)
    change = jnp.zeros_like(res_y)
    for turn in range(ITERS):
        alpha = norm_now / (square / total + DIAG_SHIFT * cross)
        change = change + alpha * dir_y
        if turn + 1 < ITERS:
            img_c = dir_y / total + DIAG_SHIFT * dir_c
            img_y = gram(dir_y) / total + DIAG_SHIFT * dir_y
            res_c = res_c - alpha * img_c
            res_y = res_y - alpha * img_y
            norm_next = full_sum(res_c * res_y)
            mixed = full_sum(res_c * dir_y) + full_sum(dir_c * res_y)
            squares = full_sum(res_y * res_y), full_sum(res_y * dir_y)
            beta = norm_next / norm_now
            cross = norm_next + beta * mixed + beta * beta * cross
            square = squares[0] + 2.0 * beta * squares[1] + beta * beta * square
            dir_c = res_c + beta * dir_c
            dir_y = res_y + beta * dir_y
            norm_now = norm_next
    return change


def full_sum(x):
    return jnp.sum(jnp.sum(x, axis=1, keepdims=True), axis=0, keepdims=True)


def project(lifted, slope_re, slope_im):
    raw = jnp.concatenate(
        [jnp.sum(lifted * slope_re, axis=0, keepdims=True), jnp.sum(lifted * slope_im, axis=0, keepdims=True)],
        axis=0,
    )
    return raw - jnp.mean(raw, axis=1, keepdims=True)


def solve_kernel(
    energy_ref,
    near_ref,
    near_re_ref,
    near_im_ref,
    near_far_ref,
    far_near_ref,
    far_ref,
    far_re_ref,
    far_im_ref,
    local_ref,
    change_ref,
):
    width = local_ref.shape[1]
    half = near_ref.shape[1]
    energy = energy_ref[...]
    local_ref[...] = energy[:, :width]

    def scaled(c, re_ref, im_ref):
        back = re_ref[...] * c[0:1] + im_ref[...] * c[1:2]
        high = back.astype(BF16)
        low = (back - high.astype(F32)).astype(BF16)
        return jnp.concatenate([high, high, low], axis=1)

    def raw(lifted, re_ref, im_ref):
        re = jnp.sum(lifted * re_ref[...], axis=0, keepdims=True)
        return jnp.concatenate([re, jnp.sum(lifted * im_ref[...], axis=0, keepdims=True)], axis=0)

    def gram(c):
        near = scaled(c[:, :half], near_re_ref, near_im_ref)
        far = scaled(c[:, half:], far_re_ref, far_im_ref)
        to_near = dot(near, near_ref[...], ((1,), (0,))) + dot(far, far_near_ref[...], ((1,), (0,)))
        to_far = dot(near, near_far_ref[...], ((1,), (0,))) + dot(far, far_ref[...], ((1,), (0,)))
        both = jnp.concatenate(
            [raw(to_near, near_re_ref, near_im_ref), raw(to_far, far_re_ref, far_im_ref)], axis=1
        )
        return both - jnp.mean(both, axis=1, keepdims=True)

    change_ref[...] = solve(energy, gram)[:, :width]


def wide_solve(energy, occ_stack, first_weight, bias_row, second, readout):
    here = occ_stack.shape[1]
    occupied = occ_stack.reshape(-1, occ_stack.shape[2])
    pre = dot(occupied, first_weight, ((1,), (0,))) + bias_row
    hidden = jnp.tanh(pre).astype(BF16)
    mid = jnp.tanh(dot(second, hidden, ((0,), (1,))))
    slope = 1.0 - mid * mid
    slope_re = slope * readout[0][:, None]
    slope_im = slope * readout[1][:, None]

    def gram(c):
        high, low = split(slope_re * c[0:1] + slope_im * c[1:2])
        high, low = split(dot(high, hidden, ((1,), (0,))) + dot(low, hidden, ((1,), (0,))))
        lifted = dot(high, hidden, ((1,), (1,))) + dot(low, hidden, ((1,), (1,)))
        return project(lifted, slope_re, slope_im)

    return energy[:, :here], solve(energy, gram)[:, :here]


def swap(x, axis, bit):
    return lax.ppermute(x, axis, [(i, i ^ bit) for i in range(lax.axis_size(axis))])


def shift(x, axis, step):
    size = lax.axis_size(axis)
    return lax.ppermute(x, axis, [(i, (i + step) % size) for i in range(size)])


def exchange_all(send):
    peers = send.shape[0]
    return lax.all_to_all(
        send,
        ("samples", "chip", "core"),
        0,
        0,
        axis_index_groups=[[(k + peers // 2) % peers for k in range(peers)]],
        tiled=True,
    )


def powers(size):
    return [1 << k for k in reversed(range((size - 1).bit_length()))]


def body(
    occupations,
    connection_counts,
    connection_orbitals,
    connection_elements,
    laser_step,
    first_weight,
    first_bias,
    second_weight,
    readout,
):
    here, orbitals = occupations.shape
    slots = connection_orbitals.shape[1]
    wide, narrow = first_weight.shape[1], second_weight.shape[1]
    chips = lax.axis_size("chip")
    spread = chips * lax.axis_size("core")
    blocks = lax.axis_size("samples")
    total = here * blocks
    bias_row = first_bias[None, :]
    field = FIELD_SCALE * jnp.sin(FIELD_RATE * laser_step.astype(F32)[None, None])

    bits = powers(blocks)
    bits = bits[-1:] + bits[:-1]
    entries = [0]
    for bit in bits:
        entries = entries + [e ^ bit for e in entries]
    moved = swap(occupations[None], "samples", bits[0])

    shifts, shards = [], []
    for step in range(1, chips):
        shifts.append((step, 0))
        shards.append(shift(second_weight, "chip", step))
    shifts.append((0, 1))
    shards.append(shift(second_weight, "core", 1))

    hidden, owner, elements, w1, bias, readout_near, own_shard, occupied = call(
        functools.partial(slot_hidden_kernel, spread),
        8,
        (
            jax.ShapeDtypeStruct((slots + here, wide), BF16),
            jax.ShapeDtypeStruct((here, slots), BF16),
            jax.ShapeDtypeStruct(connection_elements.shape, F32),
            jax.ShapeDtypeStruct(first_weight.shape, BF16),
            jax.ShapeDtypeStruct(bias_row.shape, F32),
            jax.ShapeDtypeStruct(readout.shape, F32),
            jax.ShapeDtypeStruct(second_weight.shape, BF16),
            jax.ShapeDtypeStruct(occupations.shape, BF16),
        ),
        [
            pltpu.VMEM((1, here), jnp.int32),
            pltpu.VMEM(connection_orbitals.shape, jnp.int32),
            pltpu.VMEM(occupations.shape, jnp.int32),
            pltpu.SemaphoreType.DMA((8,)),
        ],
        name="slot_hidden",
        copies=True,
        flops=2 * (slots + here) * orbitals * wide,
        transcendentals=(slots + here) * wide,
    )(
        *(
            pltpu.with_memory_space_constraint(x, pltpu.HBM)
            for x in (
                connection_counts[None, :],
                connection_orbitals,
                occupations,
                first_weight,
                bias_row,
                connection_elements,
                readout,
                second_weight,
            )
        ),
    )
    relayed, occupied, field = lax.optimization_barrier((shards[: chips - 1], occupied, field))
    for step in range(1, chips):
        shifts.append((step, 1))
        shards.append(shift(relayed[step - 1], "core", 1))
    shifts.append((0, 0))
    stack = jnp.concatenate([occupied[None], moved.astype(BF16)], axis=0)
    moved = swap(stack, "samples", bits[1])

    send, second = call(
        functools.partial(slot_energy_kernel, tuple(shifts)),
        5 + len(shifts),
        (
            jax.ShapeDtypeStruct((blocks * spread, 1, 2 * here), F32),
            jax.ShapeDtypeStruct((wide, narrow), BF16),
        ),
        name="slot_energy",
        flops=2 * (slots + here) * wide * narrow,
        transcendentals=(slots + here) * narrow,
    )(field, hidden, owner, elements, readout_near, *shards, own_shard)
    received = exchange_all(send)

    def collected(after):
        return call(
            functools.partial(collect_kernel, entries, spread),
            2,
            jax.ShapeDtypeStruct((2, total), F32),
            name="collect",
            flops=COLLECT_WEIGHT,
        )(received, after)

    for bit in bits[2:-1]:
        stack = jnp.concatenate([stack, moved], axis=0)
        moved = swap(stack, "samples", bit)
    if total > wide:
        stack = jnp.concatenate([stack, moved], axis=0)
        stack = jnp.concatenate([stack, swap(stack, "samples", bits[-1])], axis=0)
        return wide_solve(collected(stack), stack, first_weight, bias_row, second, readout)

    half = total // 2
    weights = (w1, bias, second, readout_near)
    full = orbitals // 128 * 128
    packed = call(
        pack_kernel,
        3,
        jax.ShapeDtypeStruct((half + here, full), BF16),
        name="pack",
    )(stack, moved, second)
    far_packed = swap(packed, "samples", bits[-1])
    block = jax.ShapeDtypeStruct((3 * half, half), BF16)
    slopes = (jax.ShapeDtypeStruct((narrow, half), F32),) * 2
    w1, near_hidden, *near = call(
        near_half_kernel,
        5,
        (jax.ShapeDtypeStruct(w1.shape, BF16), jax.ShapeDtypeStruct((half, wide), BF16), block) + slopes,
        name="near_half",
        flops=NEAR_WEIGHT,
        transcendentals=half * (wide + narrow),
    )(packed, *weights)
    far = call(
        far_half_kernel,
        6,
        (block,) * 3 + slopes,
        name="far_half",
        flops=2 * half * wide * (orbitals + narrow + 3 * half),
        transcendentals=half * (wide + narrow),
    )(far_packed, w1, *weights[1:], near_hidden)
    return call(
        solve_kernel,
        9,
        (jax.ShapeDtypeStruct((2, here), F32),) * 2,
        name="solve",
        flops=ITERS * 6 * total * total * narrow,
    )(collected(far[0]), *near, *far)


def solution(mesh):
    blocks, spread = mesh.shape["samples"], mesh.shape["params"]
    fine = Mesh(mesh.devices.reshape(blocks, spread // 2, 2), ("samples", "chip", "core"))
    return jax.shard_map(
        body,
        mesh=fine,
        in_specs=(
            P("samples", None),
            P("samples"),
            P(None, ("samples", "chip", "core")),
            P(None, ("samples", "chip", "core")),
            P(),
            P(),
            P(),
            P(("chip", "core"), None),
            P(),
        ),
        out_specs=(P(None, "samples"), P(None, "samples")),
        check_vma=False,
    )
```

```python
import functools
import math

import jax
import jax.numpy as jnp
from jax import lax
from jax.experimental import pallas as pl
from jax.experimental.pallas import tpu as pltpu
from jax.sharding import Mesh, PartitionSpec as P

ITERS = 2


FIELD_SCALE = 0.8
FIELD_RATE = 0.0123
DIAG_SHIFT = 0.01
F32 = jnp.float32
BF16 = jnp.bfloat16
ROWS = 768
COLLECT_WEIGHT = 1e10
NEAR_WEIGHT = 1e10
VMEM_LIMIT = 48 * 1024 * 1024


def dot(a, b, dims):
    return lax.dot_general(a, b, (dims, ((), ())), preferred_element_type=F32)


def split(x):
    high = lax.reduce_precision(x, 8, 7)
    return high.astype(BF16), (x - high).astype(BF16)


def parts(x):
    high = x.astype(BF16)
    rest = x - high.astype(F32)
    middle = rest.astype(BF16)
    return high, middle, (rest - middle.astype(F32)).astype(BF16)


def iota(shape, dim):
    return lax.broadcasted_iota(jnp.int32, shape, dim)


def call(kernel, count, out_shape, scratch=(), name=None, copies=False, flops=0, transcendentals=0):
    vmem = pl.BlockSpec(memory_space=pltpu.VMEM)
    far = pl.BlockSpec(memory_space=pltpu.HBM)
    return pl.pallas_call(
        kernel,
        out_shape=out_shape,
        in_specs=[far if copies else vmem] * count,
        out_specs=jax.tree.map(lambda _: vmem, out_shape),
        scratch_shapes=scratch,
        compiler_params=pltpu.CompilerParams(vmem_limit_bytes=VMEM_LIMIT),
        cost_estimate=pl.CostEstimate(
            flops=int(flops),
            transcendentals=int(transcendentals),
            bytes_accessed=sum(x.size * x.dtype.itemsize for x in jax.tree.leaves(out_shape)),
        ),
        name=name,
    )


def slot_hidden_kernel(
    spread,
    counts_hbm,
    orbitals_hbm,
    occ_hbm,
    w1_hbm,
    bias_hbm,
    elements_hbm,
    readout_hbm,
    own_hbm,
    hidden_ref,
    owner_ref,
    elements_ref,
    w1_ref,
    bias_ref,
    readout_ref,
    own_ref,
    occupied_ref,
    counts_ref,
    orbitals_ref,
    occ_ref,
    sems,
):
    here, orbitals = occ_ref.shape
    updates, slots = orbitals_ref.shape
    pairs = (
        (counts_hbm, counts_ref),
        (occ_hbm, occ_ref),
        (w1_hbm, w1_ref),
        (bias_hbm, bias_ref),
        (orbitals_hbm, orbitals_ref),
        (elements_hbm, elements_ref),
        (readout_hbm, readout_ref),
        (own_hbm, own_ref),
    )
    copies = [pltpu.make_async_copy(a, b, sems.at[i]) for i, (a, b) in enumerate(pairs)]
    for copy in copies:
        copy.start()
    chip, core = lax.axis_index("chip"), lax.axis_index("core")
    place = chip * 2 + core
    copies[0].wait()
    counts = counts_ref[...].astype(F32)
    row, col = iota((here, here), 0), iota((here, here), 1)
    ends = jnp.sum(jnp.where(col <= row, counts, 0.0), axis=1, keepdims=True)
    starts = jnp.sum(jnp.where(col < row, counts, 0.0), axis=1, keepdims=True)
    positions = (place + spread * iota((1, slots), 1)).astype(F32)
    owner = jnp.where((starts <= positions) & (positions < ends), 1.0, 0.0).astype(BF16)
    owner_ref[...] = owner
    copies[1].wait()
    occupied = occ_ref[...].astype(F32).astype(BF16)
    occupied_ref[...] = occupied
    copies[2].wait()
    copies[3].wait()
    w1 = w1_ref[...]
    bias = bias_ref[...]
    own = occ_ref[...].astype(F32).T
    copies[4].wait()
    parent_occ = dot(occupied, owner, ((0,), (0,)))
    columns = iota((orbitals, slots), 0)
    flipped = columns == orbitals_ref[0:1, :]
    for u in range(1, updates):
        flipped = flipped | (columns == orbitals_ref[u : u + 1, :])
    slot_occ = jnp.where(flipped, 1.0 - parent_occ, parent_occ)
    all_occ = jnp.concatenate([slot_occ, own], axis=1).astype(BF16)
    hidden_ref[...] = jnp.tanh(dot(all_occ, w1, ((0,), (0,))) + bias).astype(BF16)
    copies[5].wait()
    copies[6].wait()
    copies[7].wait()


def sine_cosine(x):
    turns = jnp.floor(x * (2.0 / math.pi) + 0.5)
    rest = ((x - turns * 1.5703125) - turns * 4.837512969970703125e-4) - turns * 7.549789948768648e-8
    square = rest * rest
    sine = (-1.9515295891e-4 * square + 8.3321608736e-3) * square - 1.6666654611e-1
    sine = rest + rest * square * sine
    cosine = (2.443315711809948e-5 * square - 1.388731625493765e-3) * square + 4.166664568298827e-2
    cosine = 1.0 - 0.5 * square + square * square * cosine
    quarter = turns.astype(jnp.int32) & 3
    odd = (quarter & 1) == 1
    high_sine = jnp.where(odd, cosine, sine)
    high_cosine = jnp.where(odd, sine, cosine)
    sine = jnp.where(quarter >= 2, -high_sine, high_sine)
    cosine = jnp.where((quarter == 1) | (quarter == 2), -high_cosine, high_cosine)
    return sine, cosine


def slot_energy_kernel(
    shifts, field_ref, hidden_ref, owner_ref, elements_ref, readout_ref, *refs
):
    shard_refs, (send_ref, second_ref) = refs[: len(shifts)], refs[len(shifts) :]
    here, slots = owner_ref.shape
    chips = lax.axis_size("chip")
    chip, core = lax.axis_index("chip"), lax.axis_index("core")
    for (step, other), shard in zip(shifts, shard_refs):
        rows = shard.shape[0]
        source = lax.rem(chip + chips - step, chips) * 2 + (core ^ other)
        second_ref[pl.ds(pl.multiple_of(source * rows, rows), rows), :] = shard[...]
    mid = jnp.tanh(dot(hidden_ref[...], second_ref[...], ((1,), (0,)))).T
    readout = readout_ref[...].T
    logs_re = jnp.sum(mid * readout[:, 0:1], axis=0, keepdims=True)
    logs_im = jnp.sum(mid * readout[:, 1:2], axis=0, keepdims=True)
    owner = owner_ref[...]
    own = jnp.concatenate(parts(logs_re[:, slots:]) + parts(logs_im[:, slots:]), axis=0)
    parent = dot(own, owner, ((1,), (0,)))
    diff_re = logs_re[:, :slots] - (parent[0:1] + parent[1:2] + parent[2:3])
    diff_im = logs_im[:, :slots] - (parent[3:4] + parent[4:5] + parent[5:6])
    used = jnp.sum(owner.astype(F32), axis=0, keepdims=True) > 0.0
    weight = elements_ref[0:1, :] + field_ref[...] * elements_ref[1:2, :]
    scale = weight * jnp.exp(diff_re)
    sine, cosine = sine_cosine(diff_im)
    contrib_re = jnp.where(used, scale * cosine, 0.0)
    contrib_im = jnp.where(used, scale * sine, 0.0)
    contrib = jnp.concatenate(parts(contrib_re) + parts(contrib_im), axis=0)
    sums = dot(contrib, owner, ((1,), (1,)))
    partial_re = sums[0:1] + sums[1:2] + sums[2:3]
    partial_im = sums[3:4] + sums[4:5] + sums[5:6]
    row = jnp.concatenate([partial_re, partial_im], axis=1)
    send_ref[...] = jnp.broadcast_to(row[None], send_ref.shape)


def collect(entries, spread, received_ref):
    peers, here = received_ref.shape[0], received_ref.shape[2] // 2
    block = lax.axis_index("samples")
    out_re, out_im = [], []
    for entry in entries:
        first = lax.rem((block ^ entry) * spread + peers // 2, peers)
        row = received_ref[first]
        for k in range(1, spread):
            row = row + received_ref[first + k]
        out_re.append(row[:, :here])
        out_im.append(row[:, here:])
    return jnp.concatenate([jnp.concatenate(out_re, axis=1), jnp.concatenate(out_im, axis=1)], axis=0)


def collect_kernel(entries, spread, received_ref, after_ref, energy_ref):
    del after_ref
    energy_ref[...] = collect(entries, spread, received_ref)


def sample_values(packed_ref, w1_ref, bias_ref, second_ref, readout_ref, size):
    hidden = jnp.tanh(sample_pre(packed_ref, w1_ref, bias_ref, size)).astype(BF16)
    mid = jnp.tanh(dot(second_ref[...], hidden, ((0,), (1,))))
    slope = 1.0 - mid * mid
    readout = readout_ref[...].T
    return hidden, slope * readout[:, 0:1], slope * readout[:, 1:2]


def pack_kernel(mine_ref, moved_ref, after_ref, packed_ref):
    del after_ref
    blocks, here, orbitals = mine_ref.shape
    full = packed_ref.shape[1]
    pieces = [mine_ref[k] for k in range(blocks)] + [moved_ref[k] for k in range(blocks)]
    rest = orbitals - full
    for k, piece in enumerate(pieces):
        packed_ref[k * here : (k + 1) * here, :] = piece[:, :full]
    rests = [piece[:, full:].astype(F32) for piece in pieces]
    rests.append(jnp.zeros((here, full - rest * len(pieces)), F32))
    packed_ref[len(pieces) * here :, :] = jnp.concatenate(rests, axis=1).astype(BF16)


def sample_pre(packed_ref, w1_ref, bias_ref, size):
    full = packed_ref.shape[1]
    here = packed_ref.shape[0] - size
    rest = w1_ref.shape[0] - full
    tail = packed_ref[size:, :].astype(F32)
    rests = [tail[:, k * rest : (k + 1) * rest] for k in range(size // here)]
    tail = jnp.concatenate(rests, axis=0).astype(BF16)
    pre = dot(packed_ref[:size, :], w1_ref[:full, :], ((1,), (0,)))
    return pre + dot(tail, w1_ref[full:, :], ((1,), (0,))) + bias_ref[...]


def put(overlap_ref, overlap):
    size = overlap.shape[0]
    high = overlap.astype(BF16)
    overlap_ref[:size, :] = high
    overlap_ref[size : 2 * size, :] = (overlap - high.astype(F32)).astype(BF16)
    overlap_ref[2 * size :, :] = high


def near_half_kernel(
    packed_ref, w1_ref, bias_ref, second_ref, readout_ref, w1_again, hidden_ref, near_ref, re_ref, im_ref
):
    w1_again[...] = w1_ref[...]
    size = hidden_ref.shape[0]
    hidden, re_ref[...], im_ref[...] = sample_values(packed_ref, w1_ref, bias_ref, second_ref, readout_ref, size)
    hidden_ref[...] = hidden
    put(near_ref, dot(hidden, hidden, ((1,), (1,))))


def far_half_kernel(
    packed_ref,
    w1_ref,
    bias_ref,
    second_ref,
    readout_ref,
    hidden_ref,
    near_far_ref,
    far_near_ref,
    far_ref,
    re_ref,
    im_ref,
):
    size = hidden_ref.shape[0]
    hidden, re_ref[...], im_ref[...] = sample_values(packed_ref, w1_ref, bias_ref, second_ref, readout_ref, size)
    near = hidden_ref[...]
    put(near_far_ref, dot(near, hidden, ((1,), (1,))))
    put(far_near_ref, dot(hidden, near, ((1,), (1,))))
    put(far_ref, dot(hidden, hidden, ((1,), (1,))))


def solve(energy, gram):
    total = energy.shape[1]
    centered = energy - jnp.mean(energy, axis=1, keepdims=True)
    res_c = jnp.concatenate([centered[1:2], -centered[0:1]], axis=0) / total
    res_y = gram(res_c)
    dir_c, dir_y = res_c, res_y
    norm_now = full_sum(res_c * res_y)
    cross, square = norm_now, full_sum(res_y * res_y)
    change = jnp.zeros_like(res_y)
    for turn in range(ITERS):
        alpha = norm_now / (square / total + DIAG_SHIFT * cross)
        change = change + alpha * dir_y
        if turn + 1 < ITERS:
            img_c = dir_y / total + DIAG_SHIFT * dir_c
            img_y = gram(dir_y) / total + DIAG_SHIFT * dir_y
            res_c = res_c - alpha * img_c
            res_y = res_y - alpha * img_y
            norm_next = full_sum(res_c * res_y)
            mixed = full_sum(res_c * dir_y) + full_sum(dir_c * res_y)
            squares = full_sum(res_y * res_y), full_sum(res_y * dir_y)
            beta = norm_next / norm_now
            cross = norm_next + beta * mixed + beta * beta * cross
            square = squares[0] + 2.0 * beta * squares[1] + beta * beta * square
            dir_c = res_c + beta * dir_c
            dir_y = res_y + beta * dir_y
            norm_now = norm_next
    return change


def full_sum(x):
    return jnp.sum(jnp.sum(x, axis=1, keepdims=True), axis=0, keepdims=True)


def project(lifted, slope_re, slope_im):
    raw = jnp.concatenate(
        [jnp.sum(lifted * slope_re, axis=0, keepdims=True), jnp.sum(lifted * slope_im, axis=0, keepdims=True)],
        axis=0,
    )
    return raw - jnp.mean(raw, axis=1, keepdims=True)


def solve_kernel(
    energy_ref,
    near_ref,
    near_re_ref,
    near_im_ref,
    near_far_ref,
    far_near_ref,
    far_ref,
    far_re_ref,
    far_im_ref,
    local_ref,
    change_ref,
):
    width = local_ref.shape[1]
    half = near_ref.shape[1]
    energy = energy_ref[...]
    local_ref[...] = energy[:, :width]

    def scaled(c, re_ref, im_ref):
        back = re_ref[...] * c[0:1] + im_ref[...] * c[1:2]
        high = back.astype(BF16)
        low = (back - high.astype(F32)).astype(BF16)
        return jnp.concatenate([high, high, low], axis=1)

    def raw(lifted, re_ref, im_ref):
        re = jnp.sum(lifted * re_ref[...], axis=0, keepdims=True)
        return jnp.concatenate([re, jnp.sum(lifted * im_ref[...], axis=0, keepdims=True)], axis=0)

    def gram(c):
        near = scaled(c[:, :half], near_re_ref, near_im_ref)
        far = scaled(c[:, half:], far_re_ref, far_im_ref)
        to_near = dot(near, near_ref[...], ((1,), (0,))) + dot(far, far_near_ref[...], ((1,), (0,)))
        to_far = dot(near, near_far_ref[...], ((1,), (0,))) + dot(far, far_ref[...], ((1,), (0,)))
        both = jnp.concatenate(
            [raw(to_near, near_re_ref, near_im_ref), raw(to_far, far_re_ref, far_im_ref)], axis=1
        )
        return both - jnp.mean(both, axis=1, keepdims=True)

    change_ref[...] = solve(energy, gram)[:, :width]


def wide_solve(energy, occ_stack, first_weight, bias_row, second, readout):
    here = occ_stack.shape[1]
    occupied = occ_stack.reshape(-1, occ_stack.shape[2])
    pre = dot(occupied, first_weight, ((1,), (0,))) + bias_row
    hidden = jnp.tanh(pre).astype(BF16)
    mid = jnp.tanh(dot(second, hidden, ((0,), (1,))))
    slope = 1.0 - mid * mid
    slope_re = slope * readout[0][:, None]
    slope_im = slope * readout[1][:, None]

    def gram(c):
        high, low = split(slope_re * c[0:1] + slope_im * c[1:2])
        high, low = split(dot(high, hidden, ((1,), (0,))) + dot(low, hidden, ((1,), (0,))))
        lifted = dot(high, hidden, ((1,), (1,))) + dot(low, hidden, ((1,), (1,)))
        return project(lifted, slope_re, slope_im)

    return energy[:, :here], solve(energy, gram)[:, :here]


def swap(x, axis, bit):
    return lax.ppermute(x, axis, [(i, i ^ bit) for i in range(lax.axis_size(axis))])


def shift(x, axis, step):
    size = lax.axis_size(axis)
    return lax.ppermute(x, axis, [(i, (i + step) % size) for i in range(size)])


def exchange_all(send):
    peers = send.shape[0]
    return lax.all_to_all(
        send,
        ("samples", "chip", "core"),
        0,
        0,
        axis_index_groups=[[(k + peers // 2) % peers for k in range(peers)]],
        tiled=True,
    )


def powers(size):
    return [1 << k for k in reversed(range((size - 1).bit_length()))]


def body(
    occupations,
    connection_counts,
    connection_orbitals,
    connection_elements,
    laser_step,
    first_weight,
    first_bias,
    second_weight,
    readout,
):
    here, orbitals = occupations.shape
    slots = connection_orbitals.shape[1]
    wide, narrow = first_weight.shape[1], second_weight.shape[1]
    chips = lax.axis_size("chip")
    spread = chips * lax.axis_size("core")
    blocks = lax.axis_size("samples")
    total = here * blocks
    bias_row = first_bias[None, :]
    field = FIELD_SCALE * jnp.sin(FIELD_RATE * laser_step.astype(F32)[None, None])

    bits = powers(blocks)
    bits = bits[-1:] + bits[:-1]
    entries = [0]
    for bit in bits:
        entries = entries + [e ^ bit for e in entries]
    moved = swap(occupations[None], "samples", bits[0])

    shifts, shards = [], []
    for step in range(1, chips):
        shifts.append((step, 0))
        shards.append(shift(second_weight, "chip", step))
    shifts.append((0, 1))
    shards.append(shift(second_weight, "core", 1))

    hidden, owner, elements, w1, bias, readout_near, own_shard, occupied = call(
        functools.partial(slot_hidden_kernel, spread),
        8,
        (
            jax.ShapeDtypeStruct((slots + here, wide), BF16),
            jax.ShapeDtypeStruct((here, slots), BF16),
            jax.ShapeDtypeStruct(connection_elements.shape, F32),
            jax.ShapeDtypeStruct(first_weight.shape, BF16),
            jax.ShapeDtypeStruct(bias_row.shape, F32),
            jax.ShapeDtypeStruct(readout.shape, F32),
            jax.ShapeDtypeStruct(second_weight.shape, BF16),
            jax.ShapeDtypeStruct(occupations.shape, BF16),
        ),
        [
            pltpu.VMEM((1, here), jnp.int32),
            pltpu.VMEM(connection_orbitals.shape, jnp.int32),
            pltpu.VMEM(occupations.shape, jnp.int32),
            pltpu.SemaphoreType.DMA((8,)),
        ],
        name="slot_hidden",
        copies=True,
        flops=2 * (slots + here) * orbitals * wide,
        transcendentals=(slots + here) * wide,
    )(
        *(
            pltpu.with_memory_space_constraint(x, pltpu.HBM)
            for x in (
                connection_counts[None, :],
                connection_orbitals,
                occupations,
                first_weight,
                bias_row,
                connection_elements,
                readout,
                second_weight,
            )
        ),
    )
    relayed, occupied, field = lax.optimization_barrier((shards[: chips - 1], occupied, field))
    for step in range(1, chips):
        shifts.append((step, 1))
        shards.append(shift(relayed[step - 1], "core", 1))
    shifts.append((0, 0))
    stack = jnp.concatenate([occupied[None], moved.astype(BF16)], axis=0)
    moved = swap(stack, "samples", bits[1])

    send, second = call(
        functools.partial(slot_energy_kernel, tuple(shifts)),
        5 + len(shifts),
        (
            jax.ShapeDtypeStruct((blocks * spread, 1, 2 * here), F32),
            jax.ShapeDtypeStruct((wide, narrow), BF16),
        ),
        name="slot_energy",
        flops=2 * (slots + here) * wide * narrow,
        transcendentals=(slots + here) * narrow,
    )(field, hidden, owner, elements, readout_near, *shards, own_shard)
    received = exchange_all(send)

    def collected(after):
        return call(
            functools.partial(collect_kernel, entries, spread),
            2,
            jax.ShapeDtypeStruct((2, total), F32),
            name="collect",
            flops=COLLECT_WEIGHT,
        )(received, after)

    for bit in bits[2:-1]:
        stack = jnp.concatenate([stack, moved], axis=0)
        moved = swap(stack, "samples", bit)
    if total > wide:
        stack = jnp.concatenate([stack, moved], axis=0)
        stack = jnp.concatenate([stack, swap(stack, "samples", bits[-1])], axis=0)
        return wide_solve(collected(stack), stack, first_weight, bias_row, second, readout)

    half = total // 2
    weights = (w1, bias, second, readout_near)
    full = orbitals // 128 * 128
    packed = call(
        pack_kernel,
        3,
        jax.ShapeDtypeStruct((half + here, full), BF16),
        name="pack",
    )(stack, moved, second)
    far_packed = swap(packed, "samples", bits[-1])
    block = jax.ShapeDtypeStruct((3 * half, half), BF16)
    slopes = (jax.ShapeDtypeStruct((narrow, half), F32),) * 2
    w1, near_hidden, *near = call(
        near_half_kernel,
        5,
        (jax.ShapeDtypeStruct(w1.shape, BF16), jax.ShapeDtypeStruct((half, wide), BF16), block) + slopes,
        name="near_half",
        flops=NEAR_WEIGHT,
        transcendentals=half * (wide + narrow),
    )(packed, *weights)
    far = call(
        far_half_kernel,
        6,
        (block,) * 3 + slopes,
        name="far_half",
        flops=2 * half * wide * (orbitals + narrow + 3 * half),
        transcendentals=half * (wide + narrow),
    )(far_packed, w1, *weights[1:], near_hidden)
    return call(
        solve_kernel,
        9,
        (jax.ShapeDtypeStruct((2, here), F32),) * 2,
        name="solve",
        flops=ITERS * 6 * total * total * narrow,
    )(collected(far[0]), *near, *far)


def solution(mesh):
    blocks, spread = mesh.shape["samples"], mesh.shape["params"]
    fine = Mesh(mesh.devices.reshape(blocks, spread // 2, 2), ("samples", "chip", "core"))
    return jax.shard_map(
        body,
        mesh=fine,
        in_specs=(
            P("samples", None),
            P("samples"),
            P(None, ("samples", "chip", "core")),
            P(None, ("samples", "chip", "core")),
            P(),
            P(),
            P(),
            P(("chip", "core"), None),
            P(),
        ),
        out_specs=(P(None, "samples"), P(None, "samples")),
        check_vma=False,
    )
```
